32 devices in a mesh: seq: 8 (over z, y), chan: 4 (over x, core).
Axes of the slice: x: 2, y: 2, z: 4, core: 2. Of those that a mesh axis runs over, the one named last changes fastest.
Arguments:
- tokens: bfloat16 [4, 1024, 1152], P(None, 'seq'), may hold values from -6 to 6
- teacher: bfloat16 [4, 1024, 1152], P(None, 'seq'), may hold values from -6 to 6
- true_lengths: int32 [4], replicated, may hold values from 512 to 1024
- doc_lengths: int32 [4, 3], replicated, may hold values from 1 to 960, 1024 in all within a row
- routes: int32 [4, 1024], P(None, 'seq'), may hold values from 0 to 7, as said below
- norm1_gain: bfloat16 [1152], replicated, may hold values from 0.5 to 1.5
- in_weight: bfloat16 [1152, 2, 2304], P(None, None, 'chan'), may hold values from -0.1875 to 0.1875
- conv_weight: bfloat16 [4, 2304], P(None, 'chan'), may hold values from -3 to 3
- conv_bias: bfloat16 [2304], P('chan'), may hold values from -3 to 3
- xproj_weight: bfloat16 [2304, 104], P('chan'), may hold values from -0.125 to 0.125
- dt_weight: bfloat16 [72, 2304], P(None, 'chan'), may hold values from -0.75 to 0.75
- dt_bias: float32 [2304], P('chan'), may hold values from -6 to -2
- a_log: float32 [2304, 16], P('chan'), may hold values from -9 to 0
- skip_weight: float32 [2304], P('chan'), may hold values from 0.5 to 1.5
- out_weight: bfloat16 [2304, 1152], P('chan'), may hold values from -0.25 to 0.25
- norm2_gain: bfloat16 [1152], replicated, may hold values from 0.5 to 1.5
- router_weight: bfloat16 [1152, 8], replicated, may hold values from -0.109375 to 0.109375
- expert_in: bfloat16 [8, 1152, 3072], P('seq'), may hold values from -0.1875 to 0.1875
- expert_out: bfloat16 [8, 3072, 1152], P('seq'), may hold values from -0.3125 to 0.3125
Outputs:
- layer_out: bfloat16 [4, 1024, 1152], P(None, 'seq')
- loss: float32 [], replicated
- grad_tokens: float32 [4, 1024, 1152], P(None, 'seq')
- grad_norm1_gain: float32 [1152], replicated
- grad_in_weight: float32 [1152, 2, 2304], P(None, None, 'chan')
- grad_conv_weight: float32 [4, 2304], P(None, 'chan')
- grad_conv_bias: float32 [2304], P('chan')
- grad_xproj_weight: float32 [2304, 104], P('chan')
- grad_dt_weight: float32 [72, 2304], P(None, 'chan')
- grad_dt_bias: float32 [2304], P('chan')
- grad_a_log: float32 [2304, 16], P('chan')
- grad_skip_weight: float32 [2304], P('chan')
- grad_out_weight: float32 [2304, 1152], P('chan')
- grad_norm2_gain: float32 [1152], replicated
- grad_router_weight: float32 [1152, 8], replicated
- grad_expert_in: float32 [8, 1152, 3072], P('seq', None, 'chan')
- grad_expert_out: float32 [8, 3072, 1152], P('seq', 'chan')
The draws below stay inside these ranges and needn't reach their ends.
Inputs may be any that keep to these rules, and one draw needn't show every extreme that they name: `routes`: each position names one expert. In every aligned block of 128 positions of a sequence no expert is named more than 32 times, and one expert, the same in all blocks, is named exactly 32 times in every block. `doc_lengths`: the documents of each sequence, in order; their lengths sum to 1024.
All inputs are finite; a program needn't handle non-finite values.
Results may differ from the reference program's by a relative error of at most 0.013.
Values may be sent and summed in bfloat16 or wider, within the bound.
A program may use at most 448 MiB of HBM per device.

```python
import math
import jax
import jax.numpy as jnp
import numpy as np
from jax import lax

D = 1152
E = 2304
NST = 16
RANK = 72
KCONV = 4
EXPERTS = 8
FF = 3072
GROUP = 128
SEQS = 4
DOCS = 3
LENGTH = 1024
MOST = 32
FFS = 3072
SLABS = 8
N_SEQ = 8


def draw_routes(key, part):
    key = jax.random.fold_in(key, 7)
    blocks = SEQS * (LENGTH // GROUP)
    hot_key, pool_key, order_key = jax.random.split(key, 3)
    hottest = jax.random.randint(hot_key, (), 0, EXPERTS)
    others = (hottest + 1 + jnp.arange(EXPERTS - 1, dtype=jnp.int32)) % EXPERTS
    pooled = jnp.repeat(others, MOST)

    def take_rest(block_key):
        return jax.random.permutation(block_key, pooled)[:GROUP - MOST]

    def shuffle_block(block_key, labels):
        return jax.random.permutation(block_key, labels)
    picked = jax.vmap(take_rest)(jax.random.split(pool_key, blocks))
    labels = jnp.concatenate([jnp.full((blocks, MOST), hottest, jnp.int32), picked.astype(jnp.int32)], axis=1)
    ordered = jax.vmap(shuffle_block)(jax.random.split(order_key, blocks), labels)
    return ordered.reshape(SEQS, LENGTH).astype(jnp.int32)


def set_ends(values, own_key, low, high):
    longest = values.shape.index(max(values.shape))
    spots = []
    for shift in (0, 1):
        where = [jax.random.randint(jax.random.fold_in(own_key, axis), (), 0, length) for axis, length in enumerate(values.shape)]
        where[longest] = (where[longest] + shift) % values.shape[longest]
        spots.append(tuple(where))
    return values.at[spots[0]].set(low).at[spots[1]].set(high)


def level_of(own_key, shape, cuts, smallest, largest):
    gain, own = 1.0, jax.random.fold_in(own_key, 6)
    for dim, blocks in cuts:
        steps = jnp.exp(jax.random.uniform(jax.random.fold_in(own, dim), (blocks,), jnp.float32, smallest / len(cuts), largest / len(cuts)))
        gain = gain * jnp.repeat(steps, shape[dim] // blocks).reshape([-1 if axis == dim else 1 for axis in range(len(shape))])
    return gain


def length_profile(number_of, total, most, lean):
    loads = [(1 << 20) // math.isqrt(rank ** lean) + 1 for rank in range(2, number_of + 1)]
    surplus, given = total - most - (number_of - 1), [1] * (number_of - 1)
    while surplus > 0:
        candidates = [i for i in range(number_of - 1) if given[i] < most]
        whole, left = sum([loads[i] for i in candidates]), surplus
        for i in candidates:
            more = min(most - given[i], max(1, left * loads[i] // whole), surplus)
            given[i] = given[i] + more
            surplus = surplus - more
    return np.array([most] + given)


def ragged(own_key, number_of, total, reach, skew):
    if number_of == 2:
        one = jax.random.randint(own_key, (), max(1, total - reach), min(reach, total - 1) + 1)
        return jnp.stack([one, total - one])
    tallies = jnp.asarray(length_profile(number_of, total, reach, skew), jnp.int32)
    couples = (number_of - 1) // 2
    giver, sink = tallies[1:1 + 2 * couples:2], tallies[2:2 + 2 * couples:2]
    margin = jnp.minimum(giver - 1, reach - sink)
    passed = jax.random.randint(jax.random.fold_in(own_key, 1), (couples,), 0, 1 << 20) % (margin + 1)
    tallies = tallies.at[1:1 + 2 * couples:2].set(giver - passed).at[2:2 + 2 * couples:2].set(sink + passed)
    return tallies[jax.random.permutation(jax.random.fold_in(own_key, 2), number_of)]


def noise(key, dims, deviation, reach, cuts=(), held_as=jnp.bfloat16):
    entries = jax.random.normal(key, dims, jnp.float32) * deviation
    if len(cuts) > 0:
        entries = level_of(key, dims, cuts, -0.22, 0.18) * entries
    return jnp.clip(entries, min=-reach, max=reach).astype(held_as)


def setup_inputs(seed: int = 0) -> dict:
    streams_of = jax.random.split(jax.random.key(seed), 20)
    tokens = noise(streams_of[0], (SEQS, LENGTH, D), 1.0, 6.0, ((1, 8),))
    teacher = noise(streams_of[1], (SEQS, LENGTH, D), 1.0, 6.0, ((1, 8),))
    true_lengths = set_ends(jax.random.randint(streams_of[2], (SEQS,), LENGTH // 2, LENGTH + 1), jax.random.fold_in(streams_of[2], 1), LENGTH // 2, LENGTH).astype(jnp.int32)
    doc_lengths = jax.vmap(lambda own: ragged(own, DOCS, LENGTH, LENGTH - GROUP // 2, 2))(jax.random.split(streams_of[3], SEQS)).reshape((SEQS, DOCS)).astype(jnp.int32)
    routes = draw_routes(jax.random.fold_in(streams_of[19], 71), 0)
    norm1_gain = jnp.clip(1.0 + 0.1 * jax.random.normal(streams_of[5], (D,), jnp.float32), 0.5, 1.5).astype(jnp.bfloat16)
    in_weight = noise(streams_of[6], (D, 2, E), D ** -0.5, 0.1875, ((2, 4),))
    conv_weight = noise(streams_of[7], (KCONV, E), 0.5, 3.0, ((1, 4),))
    conv_bias = noise(streams_of[8], (E,), 0.3, 3.0, ((0, 4),))
    xproj_weight = noise(streams_of[9], (E, RANK + 2 * NST), E ** -0.5, 0.125, ((0, 4),))
    dt_weight = noise(streams_of[10], (RANK, E), RANK ** -0.5, 0.75, ((1, 4),))
    dt_bias = jnp.clip(-6.0 + 4.0 * jax.random.uniform(streams_of[11], (E,), jnp.float32) ** level_of(streams_of[11], (E,), ((0, 4),), -0.2, 0.2), -6.0, -2.0)
    a_log = jnp.clip(-9.0 + 9.0 * jax.random.uniform(streams_of[12], (E, NST), jnp.float32) ** level_of(streams_of[12], (E, NST), ((0, 4),), -0.2, 0.2), -9.0, 0.0)
    skip_weight = jnp.clip(0.5 + 1.0 * jax.random.uniform(streams_of[13], (E,), jnp.float32) ** level_of(streams_of[13], (E,), ((0, 4),), -0.2, 0.2), 0.5, 1.5)
    out_weight = noise(streams_of[14], (E, D), (E // 4) ** -0.5, 0.25, ((0, 4),))
    norm2_gain = jnp.clip(1.0 + 0.1 * jax.random.normal(streams_of[15], (D,), jnp.float32), 0.5, 1.5).astype(jnp.bfloat16)
    router_weight = noise(streams_of[16], (D, EXPERTS), (3 * D) ** -0.5, 0.109375)
    expert_in = noise(streams_of[17], (SLABS, D, FFS), D ** -0.5, 0.1875, ((0, 8),))
    expert_out = noise(streams_of[18], (SLABS, FFS, D), (FF // 8) ** -0.5, 0.3125, ((0, 8),))
    return dict(tokens=tokens, teacher=teacher, true_lengths=true_lengths, doc_lengths=doc_lengths, routes=routes, norm1_gain=norm1_gain, in_weight=in_weight, conv_weight=conv_weight, conv_bias=conv_bias, xproj_weight=xproj_weight, dt_weight=dt_weight, dt_bias=dt_bias, a_log=a_log, skip_weight=skip_weight, out_weight=out_weight, norm2_gain=norm2_gain, router_weight=router_weight, expert_in=expert_in, expert_out=expert_out)


@jax.custom_vjp
def low(v):
    return lax.optimization_barrier(v.astype(jnp.bfloat16)).astype(jnp.float32)

@jax.custom_vjp
def low_back(v):
    return v

def low_keep(v):
    return (low(v), None)

def low_pass(kept, grad):
    return (grad,)

def back_keep(v):
    return (v, None)

def back_low(kept, grad):
    return (low(grad),)
low.defvjp(low_keep, low_pass)
low_back.defvjp(back_keep, back_low)
epsilon = 1e-05
highest = lax.Precision.HIGHEST

def matmul(left, right):
    return jnp.dot(left, right, precision=highest)

def rms_norm(values, weight_gain):
    mean_sq = lax.optimization_barrier(jnp.mean(values * values, axis=-1, keepdims=True))
    return values * lax.rsqrt(mean_sq + epsilon) * weight_gain

def segment_ids(doc_lengths, positions):
    ends = jnp.cumsum(doc_lengths, axis=-1)[:, :-1]
    return lax.optimization_barrier(jnp.sum((positions[None, :, None] >= ends[:, None, :]).astype(jnp.int32), axis=-1))

def silu(values):
    return values * jax.nn.sigmoid(values)

def mixer_sequence(normed, doc_ids, params):
    in_weight, conv_weight, conv_bias, xproj_weight, dt_weight, dt_bias, a_log, skip_weight, out_weight = params
    projected = low_back(matmul(normed, in_weight.reshape(D, 2 * E)))
    conv_in = low(projected[:, :E])
    gate_z = projected[:, E:]
    padded = jnp.concatenate([jnp.zeros((KCONV - 1, E), jnp.float32), conv_in], axis=0)
    ids_pad = jnp.concatenate([jnp.full((KCONV - 1,), -1, jnp.int32), doc_ids], axis=0)
    pre_act = conv_bias + jnp.zeros((LENGTH, E), jnp.float32)
    for offset in range(KCONV):
        valid = (ids_pad[offset:offset + LENGTH] == doc_ids).astype(jnp.float32)
        pre_act = pre_act + conv_weight[offset] * padded[offset:offset + LENGTH] * valid[:, None]
    act = silu(pre_act)
    act_low = low(act)
    mapped = matmul(act_low, xproj_weight)
    dt_low = low(mapped[:, :RANK])
    input_map = mapped[:, RANK:RANK + NST]
    read_map = mapped[:, RANK + NST:]
    delta = jax.nn.softplus(matmul(dt_low, dt_weight) + dt_bias)
    rate = -jnp.exp(a_log)
    keep = jnp.concatenate([jnp.zeros((1,), jnp.float32), (doc_ids[1:] == doc_ids[:-1]).astype(jnp.float32)])

    def advance(state, inputs):
        step_delta, step_input, step_read, step_act, step_keep = inputs
        decay = jnp.exp(step_delta[:, None] * rate) * step_keep
        state = decay * state + (step_delta * step_act)[:, None] * step_input[None, :]
        return (state, lax.optimization_barrier(jnp.sum(state * step_read[None, :], axis=-1)))
    unused, y_val = lax.scan(advance, jnp.zeros((E, NST), jnp.float32), (delta, input_map, read_map, act, keep))
    y_full = y_val + skip_weight * act
    gated = low(y_full * silu(gate_z))
    return low_back(matmul(gated, out_weight))

def forward(tokens, gain_one, in_weight, conv_weight, conv_bias, xproj_weight, dt_weight, dt_bias, a_log, skip_weight, out_weight, gain_two, router_weight, expert_in, expert_out, teacher, loss_mask, total_true, doc_ids, route_flat):
    normed = low(rms_norm(tokens, gain_one))
    params = (in_weight, conv_weight, conv_bias, xproj_weight, dt_weight, dt_bias, a_log, skip_weight, out_weight)

    def one_sequence(pieces):
        return mixer_sequence(pieces[0], pieces[1], params)
    mixed = lax.map(jax.checkpoint(one_sequence), (normed, doc_ids))
    hidden_one = tokens + mixed
    normed_two = low(rms_norm(hidden_one, gain_two)).reshape(-1, D)
    logits = matmul(normed_two, router_weight)
    probs = jax.nn.softmax(logits, axis=-1)
    chosen = (route_flat[:, None] == jnp.arange(EXPERTS, dtype=jnp.int32)[None, :]).astype(jnp.float32)
    gate_value = lax.optimization_barrier(jnp.sum(probs * chosen, axis=-1))
    first_all = expert_in.reshape(EXPERTS, N_SEQ // EXPERTS, D, FFS).transpose(0, 2, 1, 3).reshape(EXPERTS, D, FF)
    second_all = expert_out.reshape(EXPERTS, FF, D)
    capacity = route_flat.shape[0] // 4
    expert_total = jnp.zeros_like(normed_two)
    for expert in range(EXPERTS):
        members = route_flat == expert
        row_index = jnp.nonzero(members, size=capacity, fill_value=0)[0]
        filled = (jnp.arange(capacity) < jnp.sum(members)).astype(jnp.float32)
        rows_in = normed_two[row_index]
        pre_hidden = low_back(matmul(rows_in, first_all[expert]))
        hidden_low = low(jax.nn.gelu(pre_hidden, approximate=False))
        result = low_back(matmul(hidden_low, second_all[expert])) * filled[:, None]
        expert_total = expert_total.at[row_index].add(result)
    layer = hidden_one + (gate_value[:, None] * expert_total).reshape(hidden_one.shape)
    error = layer - teacher
    loss = jnp.sum(loss_mask[:, :, None] * error * error) / total_true
    return (loss, layer)

def reference(tokens, teacher, true_lengths, doc_lengths, routes, norm1_gain, in_weight, conv_weight, conv_bias, xproj_weight, dt_weight, dt_bias, a_log, skip_weight, out_weight, norm2_gain, router_weight, expert_in, expert_out):
    positions = jnp.arange(LENGTH, dtype=jnp.int32)
    loss_mask = (positions[None, :] < true_lengths[:, None]).astype(jnp.float32)
    total_true = jnp.sum(true_lengths).astype(jnp.float32)
    doc_ids = segment_ids(doc_lengths, positions)
    route_flat = routes.reshape(-1)
    teacher_full = teacher.astype(jnp.float32)
    inputs = tuple((member.astype(jnp.float32) for member in (tokens, norm1_gain, in_weight, conv_weight, conv_bias, xproj_weight, dt_weight, dt_bias, a_log, skip_weight, out_weight, norm2_gain, router_weight, expert_in, expert_out)))

    def objective(*values):
        return forward(*values, teacher_full, loss_mask, total_true, doc_ids, route_flat)
    loss, pullback, layer = jax.vjp(objective, *inputs, has_aux=True)
    grads = pullback(jnp.ones((), jnp.float32))
    return (layer.astype(jnp.bfloat16), loss, grads[0], grads[1], grads[2], grads[3], grads[4], grads[5], grads[6], grads[7], grads[8], grads[9], grads[10], grads[11], grads[12], grads[13], grads[14])
```

```python
import functools

import jax
import jax.numpy as jnp
from jax import lax
from jax.experimental import pallas as pl
from jax.experimental.pallas import tpu as pltpu
from jax.sharding import PartitionSpec as P

epsilon = 1e-05
log2e = 1.4426950408889634
cut = 1e30
MESH = pl.DeviceIdType.MESH
f32 = jnp.float32
bf16 = jnp.bfloat16
LANES = 128
MIB = 1024 * 1024


def exchange_kernel(axis, count, gather, x_ref, o_ref, own_sem, send_sem, recv_sem):
    me = lax.axis_index(axis)
    barrier = pltpu.get_barrier_semaphore()
    for k in range(1, count):
        pl.semaphore_signal(
            barrier, inc=1, device_id={axis: lax.rem(me + k, count)}, device_id_type=MESH
        )
    own = pltpu.make_async_copy(x_ref if gather else x_ref.at[me], o_ref.at[me], own_sem)
    own.start()
    pl.semaphore_wait(barrier, count - 1)
    copies = []
    for k in range(1, count):
        to = lax.rem(me + k, count)
        copies.append(
            pltpu.make_async_remote_copy(
                src_ref=x_ref if gather else x_ref.at[to],
                dst_ref=o_ref.at[me],
                send_sem=send_sem.at[k - 1],
                recv_sem=recv_sem.at[k - 1],
                device_id={axis: to},
                device_id_type=MESH,
            )
        )
        copies[-1].start()
    own.wait()
    for copy in copies:
        copy.wait()


def exchange(x, axis, gather, number):
    count = lax.axis_size(axis)
    shape = (count,) + x.shape if gather else x.shape
    return pl.pallas_call(
        functools.partial(exchange_kernel, axis, count, gather),
        out_shape=jax.ShapeDtypeStruct(shape, x.dtype),
        in_specs=[pl.BlockSpec(memory_space=pl.ANY)],
        out_specs=pl.BlockSpec(memory_space=pl.ANY),
        scratch_shapes=[
            pltpu.SemaphoreType.DMA,
            pltpu.SemaphoreType.DMA((count - 1,)),
            pltpu.SemaphoreType.DMA((count - 1,)),
        ],
        compiler_params=pltpu.CompilerParams(
            collective_id=number, has_side_effects=True, vmem_limit_bytes=16 * MIB
        ),
    )(x)


def turned(value):
    return pltpu.roll(value, value.shape[0] // 2, 0)


def carry_kernel(axis, count, back, local_ref, sums_ref, rate_ref, o_ref, send, got, send_sum, got_sum, total, enter,
                 send_sem, recv_sem, send_sum_sem, recv_sum_sem):
    me = lax.axis_index(axis)
    states, rows, width = local_ref.shape
    half = rows // 2
    spans = []
    span = 1
    while span < count:
        spans.append(span)
        span *= 2
    sign = -1 if back else 1
    barrier = pltpu.get_barrier_semaphore()
    greeted = 0
    for span in spans:
        for by in (span, -span):
            there = me + by
            greeted = greeted + jnp.where((there >= 0) & (there < count), 1, 0)

            @pl.when((there >= 0) & (there < count))
            def _():
                pl.semaphore_signal(barrier, inc=1, device_id={axis: there}, device_id_type=MESH)

    upper = lax.broadcasted_iota(jnp.int32, (rows, width), 0) >= half
    first = upper if back else jnp.logical_not(upper)
    sums = sums_ref[...]
    sums_turned = turned(sums)
    sums_both = sums + sums_turned
    sums_first = jnp.where(first, sums, sums_turned)
    sums_last = jnp.where(first, sums_turned, sums)

    def packed_rate(j):
        return jnp.where(upper, rate_ref[pl.ds(2 * j + 1, 1), :], rate_ref[pl.ds(2 * j, 1), :])

    def both(j):
        even, odd = local_ref[2 * j], local_ref[2 * j + 1]
        low = jnp.where(upper, turned(odd), even)
        high = jnp.where(upper, odd, turned(even))
        return (high, low) if back else (low, high)

    for j in range(states // 2):
        begin, end = both(j)
        total[j] = jnp.exp2(packed_rate(j) * sums_last) * begin + end
        enter[j] = jnp.zeros((rows, width), f32)

    pl.semaphore_wait(barrier, greeted)

    sums_total = sums_both
    sums_enter = jnp.zeros((rows, width), f32)
    for turn, span in enumerate(spans):
        to = me + sign * span
        origin = me - sign * span
        sends = (to >= 0) & (to < count)
        takes = (origin >= 0) & (origin < count)
        for j in range(0, states // 2, 2):
            send[turn, pl.ds(j * rows, 2 * rows), :] = jnp.concatenate([total[j], total[j + 1]], axis=0).astype(bf16)
        send_sum[turn] = sums_total
        copies = [
            pltpu.make_async_remote_copy(
                src_ref=source.at[turn],
                dst_ref=target.at[turn],
                send_sem=ssem.at[turn],
                recv_sem=rsem.at[turn],
                device_id={axis: to},
                device_id_type=MESH,
            )
            for source, target, ssem, rsem in (
                (send, got, send_sem, recv_sem),
                (send_sum, got_sum, send_sum_sem, recv_sum_sem),
            )
        ]

        @pl.when(sends)
        def _():
            for copy in copies:
                copy.start()

        @pl.when(jnp.logical_not(takes))
        def _():
            got[turn] = jnp.zeros(got.shape[1:], bf16)
            got_sum[turn] = jnp.zeros(got_sum.shape[1:], f32)

        @pl.when(takes)
        def _():
            for copy in copies:
                copy.wait_recv()

        for j in range(0, states // 2, 2):
            pair = got[turn, pl.ds(j * rows, 2 * rows), :].astype(f32)
            for i in (j, j + 1):
                came = pair[(i - j) * rows : (i - j + 1) * rows]
                rate = packed_rate(i)
                enter[i] = jnp.exp2(rate * sums_enter) * came + enter[i]
                total[i] = jnp.exp2(rate * sums_total) * came + total[i]
        sums_enter = sums_enter + got_sum[turn]
        sums_total = sums_total + got_sum[turn]

        @pl.when(sends)
        def _():
            for copy in copies:
                copy.wait_send()

    for j in range(states // 2):
        begin, _ = both(j)
        outer = enter[j]
        inner = jnp.exp2(packed_rate(j) * sums_first) * outer + begin
        low, high = (inner, outer) if back else (outer, inner)
        o_ref[2 * j] = jnp.where(upper, turned(high), low)
        o_ref[2 * j + 1] = jnp.where(upper, high, turned(low))


def carried(local, sums, rate, axis, back, number):
    count = lax.axis_size(axis)
    states, rows, width = local.shape
    turns = max(1, (count - 1).bit_length())
    return pl.pallas_call(
        functools.partial(carry_kernel, axis, count, back),
        out_shape=jax.ShapeDtypeStruct(local.shape, f32),
        in_specs=[pl.BlockSpec(memory_space=pltpu.VMEM)] * 3,
        out_specs=pl.BlockSpec(memory_space=pltpu.VMEM),
        scratch_shapes=[
            pltpu.VMEM((turns, states // 2 * rows, width), bf16),
            pltpu.VMEM((turns, states // 2 * rows, width), bf16),
            pltpu.VMEM((turns, rows, width), f32),
            pltpu.VMEM((turns, rows, width), f32),
            pltpu.VMEM((states // 2, rows, width), f32),
            pltpu.VMEM((states // 2, rows, width), f32),
            pltpu.SemaphoreType.DMA((turns,)),
            pltpu.SemaphoreType.DMA((turns,)),
            pltpu.SemaphoreType.DMA((turns,)),
            pltpu.SemaphoreType.DMA((turns,)),
        ],
        compiler_params=pltpu.CompilerParams(
            collective_id=number, has_side_effects=True, vmem_limit_bytes=24 * MIB
        ),
    )(local, sums, rate)


def spread(mapped_ref, first, wide_ref):
    steps, count, rows, lanes = wide_ref.shape

    def one(p, _):
        values = mapped_ref[p]
        for n in range(count):
            wide_ref[p, n] = jnp.broadcast_to(values[:, first + n : first + n + 1], (rows, lanes))
        return 0

    lax.fori_loop(0, steps, one, 0)


def rows_of(rate_ref, n, rows):
    return jnp.broadcast_to(rate_ref[n : n + 1, :], (rows, rate_ref.shape[1]))


def totals_kernel(rank, delta_ref, drive_ref, mapped_ref, rate_ref, last_ref, sums_ref, wide):
    steps, count, rows, lanes = wide.shape

    @pl.when(pl.program_id(0) == 0)
    def _():
        spread(mapped_ref, rank, wide)

    rates = [rows_of(rate_ref, n, rows) for n in range(count)]
    zero = jnp.zeros((rows, lanes), f32)

    def one(p, held):
        states, sums = held
        step, drive = delta_ref[p], drive_ref[p]
        states = tuple(
            jnp.exp2(step * rates[n]) * states[n] + drive * wide[p, n] for n in range(count)
        )
        return states, sums + step

    states, sums = lax.fori_loop(0, steps, one, ((zero,) * count, zero))
    for n in range(count):
        last_ref[n] = states[n]
    sums_ref[...] = sums


def states_kernel(rank, delta_ref, drive_ref, mapped_ref, rate_ref, enter_ref, y_ref, state_ref, wide_in, wide_read):
    steps, count, rows, lanes = wide_in.shape

    @pl.when(pl.program_id(0) == 0)
    def _():
        spread(mapped_ref, rank, wide_in)
        spread(mapped_ref, rank + count, wide_read)

    rates = [rows_of(rate_ref, n, rows) for n in range(count)]

    def one(p, states):
        step, drive = delta_ref[p], drive_ref[p]
        states = tuple(
            jnp.exp2(step * rates[n]) * states[n] + drive * wide_in[p, n] for n in range(count)
        )
        terms = [states[n] * wide_read[p, n] for n in range(count)]
        while len(terms) > 1:
            terms = [a + b for a, b in zip(terms[::2], terms[1::2])]
        y_ref[p] = terms[0]
        for n in range(count):
            state_ref[p, n] = states[n]
        return states

    lax.fori_loop(0, steps, one, tuple(enter_ref[n] for n in range(count)))


def back_totals_kernel(rank, delta_ref, grad_y_ref, mapped_ref, rate_ref, last_ref, wide):
    steps, count, rows, lanes = wide.shape

    @pl.when(pl.program_id(0) == 0)
    def _():
        spread(mapped_ref, rank + count, wide)

    rates = [rows_of(rate_ref, n, rows) for n in range(count)]
    zero = jnp.zeros((rows, lanes), f32)

    def one(turn, held):
        p = steps - 1 - turn
        step, grad_y = delta_ref[p], grad_y_ref[p]
        return tuple(
            jnp.exp2(step * rates[n]) * (held[n] + grad_y * wide[p, n]) for n in range(count)
        )

    held = lax.fori_loop(0, steps, one, (zero,) * count)
    for n in range(count):
        last_ref[n] = held[n]


def back_kernel(rank, width, delta_ref, drive_ref, grad_y_ref, mapped_ref, rate_ref, first_ref, state_ref, enter_ref,
                input_ref, decay_ref, log_ref, maps_ref, wide_in, wide_read, sum_in, sum_read):
    steps, count, rows, lanes = wide_in.shape
    place = pl.program_id(0)

    @pl.when(place == 0)
    def _():
        spread(mapped_ref, rank, wide_in)
        spread(mapped_ref, rank + count, wide_read)

    rates = [rows_of(rate_ref, n, rows) for n in range(count)]
    held = lax.broadcasted_iota(jnp.int32, (rows, lanes), 1) < width - place * lanes
    fresh = place == 0
    for n in range(count):
        log_ref[n] = jnp.zeros((rows, lanes), f32)

    def one(turn, carry):
        p = steps - 1 - turn
        before = jnp.maximum(p - 1, 0)
        opening = p == 0
        step, drive, grad_y = delta_ref[p], drive_ref[p], grad_y_ref[p]
        to_input = jnp.zeros((rows, lanes), f32)
        to_decay = jnp.zeros((rows, lanes), f32)
        new = []
        for n in range(count):
            grad = grad_y * wide_read[p, n] + carry[n]
            passed = jnp.exp2(step * rates[n]) * grad
            new.append(passed)
            prior = jnp.where(opening, first_ref[n], state_ref[before, n])
            grad_decay = passed * prior
            to_decay = to_decay + grad_decay * rates[n]
            log_ref[n] += grad_decay * step
            to_input = to_input + grad * wide_in[p, n]
            part_in = jnp.where(held, grad * drive, 0.0)
            part_read = jnp.where(held, grad_y * state_ref[p, n], 0.0)
            sum_in[p, n] = jnp.where(fresh, 0.0, sum_in[p, n]) + part_in
            sum_read[p, n] = jnp.where(fresh, 0.0, sum_read[p, n]) + part_read
        input_ref[p] = to_input
        decay_ref[p] = to_decay
        return tuple(new)

    lax.fori_loop(0, steps, one, tuple(enter_ref[n] for n in range(count)))

    @pl.when(place == pl.num_programs(0) - 1)
    def _():
        ones = jnp.ones((8, lanes), bf16)

        def flat(p, _):
            for which, source in enumerate((sum_in, sum_read)):
                block = source[p].reshape(count * rows, lanes).astype(bf16)
                out = lax.dot_general(ones, block, (((1,), (1,)), ((), ())), preferred_element_type=f32)
                maps_ref[which, p] = out
            return 0

        lax.fori_loop(0, steps, flat, 0)


def tiles(shape, last):
    return pl.BlockSpec(shape[:-1] + (last,), lambda i: (0,) * (len(shape) - 1) + (i,))


def whole(shape):
    return pl.BlockSpec(shape, lambda i: (0,) * len(shape))


def scan_call(kernel, ins, outs, scratch, cost):
    width = ins[0][0].shape[-1]
    return pl.pallas_call(
        kernel,
        grid=(pl.cdiv(width, LANES),),
        in_specs=[whole(a.shape) if full else tiles(a.shape, LANES) for a, full in ins],
        out_specs=[whole(s) if full else tiles(s, LANES) for s, full in outs],
        out_shape=[jax.ShapeDtypeStruct(s, f32) for s, _ in outs],
        scratch_shapes=[pltpu.VMEM(s, f32) for s in scratch],
        compiler_params=pltpu.CompilerParams(vmem_limit_bytes=56 * MIB),
        cost_estimate=cost,
    )(*[a for a, _ in ins])


def dot(a, b):
    return jnp.dot(a, b, preferred_element_type=f32)


def dot_nt(a, b):
    return lax.dot_general(a, b, (((1,), (1,)), ((), ())), preferred_element_type=f32)


def dot_tn(a, b):
    return lax.dot_general(a, b, (((0,), (0,)), ((), ())), preferred_element_type=f32)


def shifted(x, axis, by):
    length = lax.axis_size(axis)
    pairs = [(i, i + by) for i in range(length) if 0 <= i + by < length]
    return lax.ppermute(x, axis, pairs)


def turns_of(x, axis):
    count = lax.axis_size(axis)
    return [
        lax.ppermute(x, axis, [(i, (i + k) % count) for i in range(count)]) for k in range(1, count)
    ]


def turned_parts(x, axis):
    count = lax.axis_size(axis)
    me = lax.axis_index(axis)
    parts = [lax.dynamic_index_in_dim(x, me, 0, False)]
    for k in range(1, count):
        mine = lax.dynamic_index_in_dim(x, lax.rem(me + k, count), 0, False)
        parts.append(lax.ppermute(mine, axis, [(i, (i + k) % count) for i in range(count)]))
    return parts


def silu_slope(values):
    sigma = jax.nn.sigmoid(values)
    return sigma * (1.0 + values * (1.0 - sigma))


def norm_back(grad_normed, unit_rows, inverse, weight_gain):
    scaled = grad_normed * weight_gain
    return inverse * (scaled - unit_rows * jnp.mean(scaled * unit_rows, axis=-1, keepdims=True))


def local(
    tokens,
    teacher,
    true_lengths,
    doc_lengths,
    routes,
    norm1_gain,
    in_weight,
    conv_weight,
    conv_bias,
    xproj_weight,
    dt_weight,
    dt_bias,
    a_log,
    skip_weight,
    out_weight,
    norm2_gain,
    router_weight,
    expert_in,
    expert_out,
):
    seqs, group, width = tokens.shape
    inner = in_weight.shape[2]
    rank = dt_weight.shape[0]
    states = a_log.shape[1]
    experts = router_weight.shape[1]
    n_seq = lax.axis_size("seq")
    n_chan = lax.axis_size("chan")
    shards = n_seq // experts
    most = group // 4
    taps = conv_weight.shape[0]
    rim = taps - 1
    lines = 8
    chunks = lines // seqs
    steps = group // chunks
    owned = seqs * group // n_chan
    part = min(group, owned)
    most = min(most, part)
    parts = owned // part
    place = lax.axis_index("chan")
    first_pos = lax.axis_index("seq") * group

    def laid(x):
        x = x.reshape((seqs, chunks, steps) + x.shape[2:])
        return x.transpose((2, 1, 0) + tuple(range(3, x.ndim))).reshape((steps, lines) + x.shape[3:])

    def unlaid(x):
        x = x.reshape((steps, chunks, seqs) + x.shape[2:])
        return x.transpose((2, 1, 0) + tuple(range(3, x.ndim))).reshape((seqs, group) + x.shape[3:])

    at = (
        first_pos
        + jnp.arange(steps, dtype=jnp.int32)[:, None]
        + (jnp.arange(lines, dtype=jnp.int32) // seqs * steps)[None, :]
    )
    ends = []
    for k in range(doc_lengths.shape[1] - 1):
        ends.append(doc_lengths[:, k] + (ends[-1] if ends else 0))
    ends = [jnp.tile(end, chunks)[None, :] for end in ends]

    def doc_at(pos):
        return sum((pos >= end).astype(jnp.int32) for end in ends)

    doc_ids = doc_at(at)
    keep = (doc_ids == doc_at(at - 1)) & (at > 0)
    valid = [(doc_at(at - rim + k) == doc_ids).astype(f32)[..., None] for k in range(taps)]

    gain_one = norm1_gain.astype(f32)

    def normed_of(rows):
        full = rows.astype(f32)
        inverse = lax.rsqrt(jnp.mean(full * full, axis=-1, keepdims=True) + epsilon)
        return (full * inverse * gain_one).astype(bf16)

    conv_w_in, gate_w_in = in_weight[:, 0, :], in_weight[:, 1, :]
    prior_rows = shifted(tokens[:, group - rim :, :], "seq", 1)
    normed_one = normed_of(laid(tokens)).reshape(steps * lines, width)
    conv_in = dot(normed_one, conv_w_in).astype(bf16).reshape(steps, lines, inner)
    gate_z = dot(normed_one, gate_w_in).reshape(steps, lines, inner)
    prior_normed = normed_of(prior_rows.transpose(1, 0, 2)).reshape(rim * seqs, width)
    prior_in = dot(prior_normed, conv_w_in).astype(bf16).reshape(rim, seqs, inner)
    halo = jnp.concatenate([prior_in, conv_in[steps - rim :, : lines - seqs]], axis=1)
    extended = jnp.concatenate([halo, conv_in], axis=0)
    taps_full = conv_weight.astype(f32)

    def tapped(k):
        return extended[k : k + steps].astype(f32) * valid[k]

    pre_act = conv_bias.astype(f32) + sum(taps_full[k] * tapped(k) for k in range(taps))
    act = pre_act * jax.nn.sigmoid(pre_act)
    act_low = act.astype(bf16).reshape(steps * lines, inner)
    mapped_part = dot(act_low, xproj_weight).astype(bf16)
    mapped = jnp.sum(exchange(mapped_part, "chan", True, 1).astype(f32), axis=0)
    dt_low = mapped[:, :rank].astype(bf16)
    mapped_laid = mapped.reshape(steps, lines, rank + 2 * states)
    dt_pre = (dot(dt_low, dt_weight) + dt_bias).reshape(steps, lines, inner)
    delta = jax.nn.softplus(dt_pre)
    rate = -jnp.exp(a_log).T
    rate_two = rate * log2e
    step_size = jnp.where(keep[..., None], delta, cut)
    drive = delta * act

    flat = steps * lines * states * inner
    wide_shape = (steps, states, lines, LANES)
    last, sums = scan_call(
        functools.partial(totals_kernel, rank),
        [(step_size, False), (drive, False), (mapped_laid, True), (rate_two, False)],
        [((states, lines, inner), False), ((lines, inner), False)],
        [wide_shape],
        pl.CostEstimate(flops=5 * flat, bytes_accessed=8 * steps * lines * inner, transcendentals=flat),
    )
    enter = carried(last, sums, rate_two, "seq", False, 2)
    y_scan, state = scan_call(
        functools.partial(states_kernel, rank),
        [
            (step_size, False),
            (drive, False),
            (mapped_laid, True),
            (rate_two, False),
            (enter, False),
        ],
        [((steps, lines, inner), False), ((steps, states, lines, inner), False)],
        [wide_shape] * 2,
        pl.CostEstimate(flops=7 * flat, bytes_accessed=4 * flat, transcendentals=flat),
    )
    y_full = y_scan + skip_weight * act
    silu_z = gate_z * jax.nn.sigmoid(gate_z)
    gated = (y_full * silu_z).astype(bf16)
    gated_rows = gated.reshape(steps * lines, inner)
    out_part = dot(unlaid(gated).reshape(seqs * group, inner), out_weight).astype(bf16)
    mixed = jnp.sum(
        exchange(out_part.reshape(n_chan, owned, width), "chan", False, 3).astype(f32), axis=0
    )

    def own(x):
        rows = x.reshape((seqs * group,) + x.shape[2:])
        return lax.dynamic_slice_in_dim(rows, place * owned, owned, 0)

    tokens_own = own(tokens).astype(f32)
    inverse_one = lax.rsqrt(jnp.mean(tokens_own * tokens_own, axis=-1, keepdims=True) + epsilon)
    unit_one = tokens_own * inverse_one
    hidden_one = tokens_own + mixed
    inverse_two = lax.rsqrt(jnp.mean(hidden_one * hidden_one, axis=-1, keepdims=True) + epsilon)
    unit_two = hidden_one * inverse_two
    gain_two = norm2_gain.astype(f32)
    normed_two = (unit_two * gain_two).astype(bf16)
    probs = jax.nn.softmax(dot(normed_two, router_weight), axis=-1)
    routes_own = own(routes)
    chosen = routes_own[..., None] == jnp.arange(experts, dtype=jnp.int32)
    chosen_rows = chosen.astype(f32)
    gate_value = jnp.sum(probs * chosen_rows, axis=-1, keepdims=True)
    row = jnp.arange(owned, dtype=jnp.int32)
    earlier = (row[None, :] < row[:, None]) & (row[None, :] // part == row[:, None] // part)
    rank_in = dot(earlier.astype(bf16), chosen.astype(bf16))
    slots = parts * most
    wanted = rank_in + (row // part * most).astype(f32)[:, None]
    hit = (wanted[..., None] == jnp.arange(slots, dtype=f32)) & chosen[..., None]
    hit = hit.astype(bf16)
    hit_send = hit.reshape(owned, experts * slots)
    hit_back = jnp.repeat(hit, shards, axis=1).reshape(owned, n_seq * slots)

    def to_slabs(rows, number):
        packed = dot_tn(hit_send, rows).astype(bf16).reshape(experts, slots, width)
        came = exchange(jnp.repeat(packed, shards, axis=0), "seq", False, number)
        return came.reshape(n_seq * slots, width)

    def from_slabs(rows, number):
        came = exchange(rows.reshape(n_seq, slots, width), "seq", False, number)
        return dot(hit_back, came.reshape(n_seq * slots, width))

    first_slab, second_slab = expert_in[0], expert_out[0]
    units = first_slab.shape[1] // n_chan
    arrived = to_slabs(normed_two, 4)
    pre_hidden = dot(arrived, first_slab)
    cdf = 0.5 * (1.0 + lax.erf(pre_hidden * 0.7071067811865476))
    hidden_low = (pre_hidden * cdf).astype(bf16)
    density = jnp.exp(-0.5 * pre_hidden * pre_hidden) * 0.3989422804014327
    slope = cdf + pre_hidden * density
    result = dot(hidden_low, second_slab).astype(bf16)
    expert_total = from_slabs(result, 5)
    layer = hidden_one + gate_value * expert_total
    layer_low = layer.astype(bf16)

    flat_row = place * owned + row
    seq_of = flat_row // group
    lengths_own = sum(
        jnp.where(seq_of == s, true_lengths[s], 0) for s in range(seqs)
    )
    total_true = jnp.sum(true_lengths).astype(f32)
    loss_mask = (first_pos + flat_row % group < lengths_own).astype(f32)[:, None]
    error = layer - own(teacher).astype(f32)
    loss_part = jnp.sum(loss_mask * error * error) / total_true
    grad_layer = 2.0 / total_true * loss_mask * error
    grad_gate = jnp.sum(grad_layer * expert_total, axis=-1, keepdims=True)
    grad_result = (gate_value * grad_layer).astype(bf16)
    grad_rows = to_slabs(grad_result, 6)
    grad_pre = (dot_nt(grad_rows, second_slab) * slope).astype(bf16)
    grad_slab_rows = dot_nt(grad_pre, first_slab).astype(bf16)
    grad_expert = from_slabs(grad_slab_rows, 7)

    def by_units(x):
        return x.reshape(n_seq * slots, n_chan, units).transpose(1, 0, 2)

    rows_all = jnp.concatenate([arrived] + turns_of(arrived, "chan"), axis=0)
    hidden_all = jnp.concatenate(turned_parts(by_units(hidden_low), "chan"), axis=0)
    grad_rows_all = jnp.concatenate([grad_rows] + turns_of(grad_rows, "chan"), axis=0)
    grad_pre_all = jnp.concatenate(turned_parts(by_units(grad_pre), "chan"), axis=0)
    grad_first = dot_tn(rows_all, grad_pre_all)
    grad_second = dot_tn(hidden_all, grad_rows_all)

    grad_logit = grad_gate * gate_value * (chosen_rows - probs)
    grad_router = dot_tn(normed_two, grad_logit.astype(bf16))
    grad_normed_two = grad_expert + dot_nt(grad_logit.astype(bf16), router_weight)
    grad_gain_two = jnp.sum(grad_normed_two * unit_two, axis=0)
    grad_hidden_one = grad_layer + norm_back(grad_normed_two, unit_two, inverse_two, gain_two)

    grad_mixed = exchange(grad_hidden_one.astype(bf16), "chan", True, 8)
    grad_mixed = laid(grad_mixed.reshape(seqs, group, width)).reshape(steps * lines, width)
    grad_out_w = dot_tn(gated_rows, grad_mixed)
    grad_gated = dot_nt(grad_mixed, out_weight).reshape(steps, lines, inner)
    grad_y = grad_gated * silu_z
    grad_z = (grad_gated * y_full * silu_slope(gate_z)).astype(bf16)
    grad_z_rows = grad_z.reshape(steps * lines, inner)
    grad_in_gate = dot_tn(normed_one, grad_z_rows)
    grad_skip = jnp.sum(grad_y * act, axis=(0, 1))
    (back_last,) = scan_call(
        functools.partial(back_totals_kernel, rank),
        [(step_size, False), (grad_y, False), (mapped_laid, True), (rate_two, False)],
        [((states, lines, inner), False)],
        [wide_shape],
        pl.CostEstimate(flops=5 * flat, bytes_accessed=8 * steps * lines * inner, transcendentals=flat),
    )
    back_enter = carried(back_last, sums, rate_two, "seq", True, 9)
    state_input, from_decay, log_sums, maps = scan_call(
        functools.partial(back_kernel, rank, inner),
        [
            (step_size, False),
            (drive, False),
            (grad_y, False),
            (mapped_laid, True),
            (rate_two, False),
            (enter, False),
            (state, False),
            (back_enter, False),
        ],
        [
            ((steps, lines, inner), False),
            ((steps, lines, inner), False),
            ((states, lines, inner), False),
            ((2, steps, 8, states * lines), True),
        ],
        [wide_shape] * 4,
        pl.CostEstimate(flops=17 * flat, bytes_accessed=4 * flat, transcendentals=flat),
    )
    grad_a_log = (jnp.sum(log_sums, axis=1) * rate).T
    grad_maps = maps[:, :, 0].reshape(2, steps, states, lines).transpose(1, 3, 0, 2)
    grad_maps = grad_maps.reshape(steps * lines, 2 * states)
    grad_delta = from_decay * (1.0 / log2e) + state_input * act
    grad_dt_pre = grad_delta * jax.nn.sigmoid(dt_pre)
    grad_dt_bias = jnp.sum(grad_dt_pre, axis=(0, 1))
    grad_dt_low = grad_dt_pre.astype(bf16).reshape(steps * lines, inner)
    grad_dt_w = dot_tn(dt_low, grad_dt_low)
    low_part = jnp.concatenate([dot_nt(grad_dt_low, dt_weight), grad_maps], axis=1).astype(bf16)
    grad_mapped = jnp.sum(exchange(low_part, "chan", True, 10).astype(f32), axis=0).astype(bf16)
    grad_xproj = dot_tn(act_low, grad_mapped)
    grad_act = (
        grad_y * skip_weight
        + state_input * delta
        + dot_nt(grad_mapped, xproj_weight).reshape(steps, lines, inner)
    )
    grad_pre_act = grad_act * silu_slope(pre_act)
    grad_conv_b = jnp.sum(grad_pre_act, axis=(0, 1))
    grad_conv_w = jnp.stack([jnp.sum(grad_pre_act * tapped(k), axis=(0, 1)) for k in range(taps)])
    rims = sum(
        jnp.pad(
            (grad_pre_act[: rim - k] * taps_full[k] * valid[k][: rim - k]),
            ((k, 0), (0, 0), (0, 0)),
        )
        for k in range(rim)
    )
    next_rims = shifted(rims[:, :seqs], "seq", -1)
    after = jnp.concatenate([rims[:, seqs:], next_rims], axis=1)
    grad_conv_in = sum(
        jnp.pad(
            (grad_pre_act * taps_full[k] * valid[k])[rim - k :],
            ((0, rim - k), (0, 0), (0, 0)),
        )
        for k in range(taps)
    ) + jnp.pad(after, ((steps - rim, 0), (0, 0), (0, 0)))
    grad_conv_low = grad_conv_in.astype(bf16)
    grad_in_conv = dot_tn(normed_one, grad_conv_low.reshape(steps * lines, inner))

    def natural(x):
        return unlaid(x).reshape(seqs * group, inner)

    normed_part = dot_nt(natural(grad_conv_low), conv_w_in) + dot_nt(natural(grad_z), gate_w_in)
    normed_part = normed_part.astype(bf16).reshape(n_chan, owned, width)
    grad_normed_one = jnp.sum(exchange(normed_part, "chan", False, 11).astype(f32), axis=0)
    grad_gain_one = jnp.sum(grad_normed_one * unit_one, axis=0)
    grad_own = grad_hidden_one + norm_back(grad_normed_one, unit_one, inverse_one, gain_one)
    grad_tokens = exchange(grad_own.astype(bf16), "chan", True, 12)
    layer_out = exchange(layer_low, "chan", True, 13)

    summed_out, summed_gate = lax.psum((grad_out_w.astype(bf16), grad_in_gate.astype(bf16)), "seq")
    summed_conv, summed_xproj, summed_dt = lax.psum(
        (grad_in_conv.astype(bf16), grad_xproj.astype(bf16), grad_dt_w.astype(bf16)), "seq"
    )
    small = lax.psum(
        (grad_conv_w, grad_conv_b, grad_dt_bias, grad_a_log, grad_skip), "seq"
    )
    tiny = lax.psum((grad_gain_one, grad_gain_two, grad_router, loss_part), ("seq", "chan"))
    return (
        layer_out.reshape(seqs, group, width),
        tiny[3],
        grad_tokens.reshape(seqs, group, width).astype(f32),
        tiny[0],
        jnp.stack([summed_conv.astype(f32), summed_gate.astype(f32)], axis=1),
        small[0],
        small[1],
        summed_xproj.astype(f32),
        summed_dt.astype(f32),
        small[2],
        small[3],
        small[4],
        summed_out.astype(f32),
        tiny[1],
        tiny[2],
        grad_first[None],
        grad_second[None],
    )


def solution(mesh):
    placed = (
        P(None, "seq", None),
        P(None, "seq", None),
        P(),
        P(),
        P(None, "seq"),
        P(),
        P(None, None, "chan"),
        P(None, "chan"),
        P("chan"),
        P("chan", None),
        P(None, "chan"),
        P("chan"),
        P("chan", None),
        P("chan"),
        P("chan", None),
        P(),
        P(),
        P("seq", None, None),
        P("seq", None, None),
    )
    return jax.shard_map(
        local,
        mesh=mesh,
        in_specs=placed,
        out_specs=(
            P(None, "seq", None),
            P(),
            P(None, "seq", None),
            P(),
            P(None, None, "chan"),
            P(None, "chan"),
            P("chan"),
            P("chan", None),
            P(None, "chan"),
            P("chan"),
            P("chan", None),
            P("chan"),
            P("chan", None),
            P(),
            P(),
            P("seq", None, "chan"),
            P("seq", "chan", None),
        ),
        check_vma=False,
    )
```

```python
import functools
import math

import jax
import jax.numpy as jnp
from jax import lax
from jax.experimental import pallas as pl
from jax.experimental.pallas import tpu as pltpu
from jax.sharding import PartitionSpec as P

epsilon = 1e-05
log2e = 1.4426950408889634
cut = 1e30
MESH = pl.DeviceIdType.MESH
f32 = jnp.float32
bf16 = jnp.bfloat16
LANES = 128
MIB = 1024 * 1024


def greet(axes):
    barrier = pltpu.get_barrier_semaphore()
    told = 0
    for axis, count in axes:
        me = lax.axis_index(axis)
        for k in range(1, count):
            pl.semaphore_signal(
                barrier, inc=1, device_id={axis: lax.rem(me + k, count)}, device_id_type=MESH
            )
        told += count - 1
    return told


def sems_of(item):
    count = item[2]
    return [pltpu.SemaphoreType.DMA] + [pltpu.SemaphoreType.DMA((count - 1,))] * 2


def begin(item, x_ref, o_ref, own_sem, send_sem, recv_sem):
    mode, axis, count = item
    me = lax.axis_index(axis)

    def remote(source, row, slot, to):
        return pltpu.make_async_remote_copy(
            src_ref=source,
            dst_ref=o_ref.at[row],
            send_sem=send_sem.at[slot],
            recv_sem=recv_sem.at[slot],
            device_id={axis: to},
            device_id_type=MESH,
        )

    own = pltpu.make_async_copy(x_ref.at[me] if mode == "scatter" else x_ref, o_ref.at[me], own_sem)
    copies, later = [], []
    if mode == "relay":
        beside = me + 1 - 2 * lax.rem(me, 2)
        for k in range(1, count // 2):
            first = remote(x_ref, me, k - 1, lax.rem(me + 2 * k, count))
            row = lax.rem(me + count - 2 * k, count)
            later.append((first, remote(o_ref.at[row], row, count // 2 - 1 + k, beside)))
        copies.append(remote(x_ref, me, count // 2 - 1, beside))
    else:
        for k in range(1, count):
            to = lax.rem(me + k, count)
            copies.append(remote(x_ref.at[to] if mode == "scatter" else x_ref, me, k - 1, to))
    for copy in [first for first, _ in later] + copies:
        copy.start()
    own.start()
    return own, copies, later


def finish(under_way):
    for _, _, later in under_way:
        for first, second in later:
            first.wait_recv()
            second.start()
    for own, copies, later in under_way:
        own.wait()
        for copy in copies:
            copy.wait()
        for first, second in later:
            first.wait_send()
            second.wait()


def items_of(exchanges):
    return [(mode, axis, lax.axis_size(axis)) for _, mode, axis in exchanges]


def axes_of(items):
    return sorted({(axis, count) for _, axis, count in items})


def landed(x, item):
    shape = x.shape if item[0] == "scatter" else (item[2],) + x.shape
    return jax.ShapeDtypeStruct(shape, x.dtype)


def exchange_kernel(items, *refs):
    number = len(items)
    sems = refs[2 * number :]
    pl.semaphore_wait(pltpu.get_barrier_semaphore(), greet(axes_of(items)))
    finish(
        [
            begin(item, refs[i], refs[number + i], *sems[3 * i : 3 * i + 3])
            for i, item in enumerate(items)
        ]
    )


def exchange(number, *exchanges):
    items = items_of(exchanges)
    return pl.pallas_call(
        functools.partial(exchange_kernel, items),
        out_shape=[landed(x, item) for (x, _, _), item in zip(exchanges, items)],
        in_specs=[pl.BlockSpec(memory_space=pl.ANY)] * len(items),
        out_specs=[pl.BlockSpec(memory_space=pl.ANY)] * len(items),
        scratch_shapes=[sem for item in items for sem in sems_of(item)],
        compiler_params=pltpu.CompilerParams(
            collective_id=number, has_side_effects=True, vmem_limit_bytes=16 * MIB
        ),
    )(*[x for x, _, _ in exchanges])


def greet_near(axis, count):
    barrier = pltpu.get_barrier_semaphore()
    me = lax.axis_index(axis)
    beside = me + 1 - 2 * lax.rem(me, 2)
    pl.semaphore_signal(barrier, inc=1, device_id={axis: beside}, device_id_type=MESH)
    for k in range(1, count // 2):
        pl.semaphore_signal(
            barrier, inc=1, device_id={axis: lax.rem(me + 2 * k, count)}, device_id_type=MESH
        )
    pl.semaphore_wait(barrier, count // 2)


def sum_kernel(axis, count, x_ref, o_ref, beside_in, pair, far_in, send_sem, recv_sem):
    me = lax.axis_index(axis)
    beside = me + 1 - 2 * lax.rem(me, 2)
    greet_near(axis, count)
    near = pltpu.make_async_remote_copy(
        src_ref=x_ref,
        dst_ref=beside_in,
        send_sem=send_sem.at[0],
        recv_sem=recv_sem.at[0],
        device_id={axis: beside},
        device_id_type=MESH,
    )
    near.start()
    near.wait_recv()
    pair[...] = (x_ref[...].astype(f32) + beside_in[...].astype(f32)).astype(bf16)
    copies = []
    for k in range(1, count // 2):
        copies.append(
            pltpu.make_async_remote_copy(
                src_ref=pair,
                dst_ref=far_in.at[k - 1],
                send_sem=send_sem.at[k],
                recv_sem=recv_sem.at[k],
                device_id={axis: lax.rem(me + 2 * k, count)},
                device_id_type=MESH,
            )
        )
        copies[-1].start()
    for copy in copies:
        copy.wait_recv()
    total = pair[...].astype(f32)
    for k in range(count // 2 - 1):
        total = total + far_in[k].astype(f32)
    o_ref[...] = total
    near.wait_send()
    for copy in copies:
        copy.wait_send()


def summed_over(x, axis, number):
    count = lax.axis_size(axis)
    return pl.pallas_call(
        functools.partial(sum_kernel, axis, count),
        out_shape=jax.ShapeDtypeStruct(x.shape, f32),
        in_specs=[pl.BlockSpec(memory_space=pltpu.VMEM)],
        out_specs=pl.BlockSpec(memory_space=pltpu.VMEM),
        scratch_shapes=[
            pltpu.VMEM(x.shape, bf16),
            pltpu.VMEM(x.shape, bf16),
            pltpu.VMEM((count // 2 - 1,) + x.shape, bf16),
            pltpu.SemaphoreType.DMA((count // 2,)),
            pltpu.SemaphoreType.DMA((count // 2,)),
        ],
        compiler_params=pltpu.CompilerParams(
            collective_id=number, has_side_effects=True, vmem_limit_bytes=16 * MIB
        ),
    )(x)


def share_kernel(axis, count, items, *refs):
    number = len(items)
    x_ref, xs = refs[0], refs[1 : 1 + number]
    o_ref, outs = refs[1 + number], refs[2 + number : 2 + 2 * number]
    near_in, pairs, far_in, near_send, near_recv, far_send, far_recv = refs[2 + 2 * number : 9 + 2 * number]
    sems = refs[9 + 2 * number :]
    me = lax.axis_index(axis)
    half = count // 2
    side, place = lax.rem(me, 2), me // 2
    beside = me + 1 - 2 * side
    if items:
        pl.semaphore_wait(
            pltpu.get_barrier_semaphore(), greet(sorted(set(axes_of(items)) | {(axis, count)}))
        )
    else:
        greet_near(axis, count)
    near = []
    for k in range(half):
        to = lax.rem(place + k + 1, half)
        near.append(
            pltpu.make_async_remote_copy(
                src_ref=x_ref.at[2 * to + 1 - side],
                dst_ref=near_in.at[k],
                send_sem=near_send.at[k],
                recv_sem=near_recv.at[k],
                device_id={axis: beside},
                device_id_type=MESH,
            )
        )
        near[-1].start()
    under_way = [
        begin(item, xs[i], outs[i], *sems[3 * i : 3 * i + 3]) for i, item in enumerate(items)
    ]
    far = []
    for k in range(half - 1):
        to = 2 * lax.rem(place + k + 1, half) + side
        near[k].wait_recv()
        pairs[k] = (x_ref[to].astype(f32) + near_in[k].astype(f32)).astype(bf16)
        far.append(
            pltpu.make_async_remote_copy(
                src_ref=pairs.at[k],
                dst_ref=far_in.at[k],
                send_sem=far_send.at[k],
                recv_sem=far_recv.at[k],
                device_id={axis: to},
                device_id_type=MESH,
            )
        )
        far[-1].start()
    near[half - 1].wait_recv()
    total = x_ref[me].astype(f32) + near_in[half - 1].astype(f32)
    for k, copy in enumerate(far):
        copy.wait_recv()
        total = total + far_in[k].astype(f32)
    o_ref[...] = total
    for copy in near + far:
        copy.wait_send()
    finish(under_way)


def share_of(x, axis, number, *exchanges):
    count = lax.axis_size(axis)
    items = items_of(exchanges)
    part = x.shape[1:]
    anywhere = [pl.BlockSpec(memory_space=pl.ANY)] * len(items)
    return pl.pallas_call(
        functools.partial(share_kernel, axis, count, items),
        out_shape=[jax.ShapeDtypeStruct(part, f32)]
        + [landed(x, item) for (x, _, _), item in zip(exchanges, items)],
        in_specs=[pl.BlockSpec(memory_space=pltpu.VMEM)] + anywhere,
        out_specs=[pl.BlockSpec(memory_space=pltpu.VMEM)] + anywhere,
        scratch_shapes=[
            pltpu.VMEM((count // 2,) + part, bf16),
            pltpu.VMEM((count // 2 - 1,) + part, bf16),
            pltpu.VMEM((count // 2 - 1,) + part, bf16),
            pltpu.SemaphoreType.DMA((count // 2,)),
            pltpu.SemaphoreType.DMA((count // 2,)),
            pltpu.SemaphoreType.DMA((count // 2 - 1,)),
            pltpu.SemaphoreType.DMA((count // 2 - 1,)),
        ]
        + [sem for item in items for sem in sems_of(item)],
        compiler_params=pltpu.CompilerParams(
            collective_id=number, has_side_effects=True, vmem_limit_bytes=24 * MIB
        ),
    )(x, *[x for x, _, _ in exchanges])


def turned(value):
    return pltpu.roll(value, value.shape[0] // 2, 0)


def carry_kernel(axis, count, back, items, *refs):
    number = len(items)
    local_ref, sums_ref, rate_ref = refs[:3]
    xs, o_ref, outs = refs[3 : 3 + number], refs[3 + number], refs[4 + number : 4 + 2 * number]
    send, got, send_sum, got_sum, total, enter = refs[4 + 2 * number : 10 + 2 * number]
    send_sem, recv_sem, send_sum_sem, recv_sum_sem = refs[10 + 2 * number : 14 + 2 * number]
    sems = refs[14 + 2 * number :]
    me = lax.axis_index(axis)
    states, rows, width = local_ref.shape
    half = rows // 2
    spans = []
    span = 1
    while span < count:
        spans.append(span)
        span *= 2
    sign = -1 if back else 1
    barrier = pltpu.get_barrier_semaphore()
    greeted = greet(axes_of(items))
    for span in spans:
        for by in (span, -span):
            there = me + by
            greeted = greeted + jnp.where((there >= 0) & (there < count), 1, 0)

            @pl.when((there >= 0) & (there < count))
            def _():
                pl.semaphore_signal(barrier, inc=1, device_id={axis: there}, device_id_type=MESH)

    upper = lax.broadcasted_iota(jnp.int32, (rows, width), 0) >= half
    first = upper if back else jnp.logical_not(upper)
    sums = sums_ref[...]
    sums_turned = turned(sums)
    sums_both = sums + sums_turned
    sums_first = jnp.where(first, sums, sums_turned)
    sums_last = jnp.where(first, sums_turned, sums)

    def packed_rate(j):
        return jnp.where(upper, rate_ref[pl.ds(2 * j + 1, 1), :], rate_ref[pl.ds(2 * j, 1), :])

    def both(j):
        even, odd = local_ref[2 * j], local_ref[2 * j + 1]
        low = jnp.where(upper, turned(odd), even)
        high = jnp.where(upper, odd, turned(even))
        return (high, low) if back else (low, high)

    for j in range(states // 2):
        opening, closing = both(j)
        total[j] = jnp.exp2(packed_rate(j) * sums_last) * opening + closing
        enter[j] = jnp.zeros((rows, width), f32)

    pl.semaphore_wait(barrier, greeted)
    under_way = [
        begin(item, xs[i], outs[i], *sems[3 * i : 3 * i + 3]) for i, item in enumerate(items)
    ]
    sums_total = sums_both
    sums_enter = jnp.zeros((rows, width), f32)
    for turn, span in enumerate(spans):
        to = me + sign * span
        origin = me - sign * span
        sends = (to >= 0) & (to < count)
        takes = (origin >= 0) & (origin < count)
        for j in range(0, states // 2, 2):
            send[turn, pl.ds(j * rows, 2 * rows), :] = jnp.concatenate([total[j], total[j + 1]], axis=0).astype(bf16)
        send_sum[turn] = sums_total
        copies = [
            pltpu.make_async_remote_copy(
                src_ref=source.at[turn],
                dst_ref=target.at[turn],
                send_sem=ssem.at[turn],
                recv_sem=rsem.at[turn],
                device_id={axis: to},
                device_id_type=MESH,
            )
            for source, target, ssem, rsem in (
                (send, got, send_sem, recv_sem),
                (send_sum, got_sum, send_sum_sem, recv_sum_sem),
            )
        ]

        @pl.when(sends)
        def _():
            for copy in copies:
                copy.start()

        @pl.when(jnp.logical_not(takes))
        def _():
            got[turn] = jnp.zeros(got.shape[1:], bf16)
            got_sum[turn] = jnp.zeros(got_sum.shape[1:], f32)

        @pl.when(takes)
        def _():
            for copy in copies:
                copy.wait_recv()

        for j in range(0, states // 2, 2):
            pair = got[turn, pl.ds(j * rows, 2 * rows), :].astype(f32)
            for i in (j, j + 1):
                came = pair[(i - j) * rows : (i - j + 1) * rows]
                rate = packed_rate(i)
                enter[i] = jnp.exp2(rate * sums_enter) * came + enter[i]
                total[i] = jnp.exp2(rate * sums_total) * came + total[i]
        sums_enter = sums_enter + got_sum[turn]
        sums_total = sums_total + got_sum[turn]

        @pl.when(sends)
        def _():
            for copy in copies:
                copy.wait_send()

    for j in range(states // 2):
        opening, _ = both(j)
        outer = enter[j]
        inner = jnp.exp2(packed_rate(j) * sums_first) * outer + opening
        low, high = (inner, outer) if back else (outer, inner)
        o_ref[2 * j] = jnp.where(upper, turned(high), low)
        o_ref[2 * j + 1] = jnp.where(upper, high, turned(low))
    finish(under_way)


def carried(local, sums, rate, axis, back, number, *exchanges):
    count = lax.axis_size(axis)
    states, rows, width = local.shape
    turns = max(1, (count - 1).bit_length())
    items = items_of(exchanges)
    anywhere = [pl.BlockSpec(memory_space=pl.ANY)] * len(items)
    return pl.pallas_call(
        functools.partial(carry_kernel, axis, count, back, items),
        out_shape=[jax.ShapeDtypeStruct(local.shape, f32)]
        + [landed(x, item) for (x, _, _), item in zip(exchanges, items)],
        in_specs=[pl.BlockSpec(memory_space=pltpu.VMEM)] * 3 + anywhere,
        out_specs=[pl.BlockSpec(memory_space=pltpu.VMEM)] + anywhere,
        scratch_shapes=[
            pltpu.VMEM((turns, states // 2 * rows, width), bf16),
            pltpu.VMEM((turns, states // 2 * rows, width), bf16),
            pltpu.VMEM((turns, rows, width), f32),
            pltpu.VMEM((turns, rows, width), f32),
            pltpu.VMEM((states // 2, rows, width), f32),
            pltpu.VMEM((states // 2, rows, width), f32),
            pltpu.SemaphoreType.DMA((turns,)),
            pltpu.SemaphoreType.DMA((turns,)),
            pltpu.SemaphoreType.DMA((turns,)),
            pltpu.SemaphoreType.DMA((turns,)),
        ]
        + [sem for item in items for sem in sems_of(item)],
        compiler_params=pltpu.CompilerParams(
            collective_id=number, has_side_effects=True, vmem_limit_bytes=24 * MIB
        ),
    )(local, sums, rate, *[x for x, _, _ in exchanges])


def spread(mapped_ref, first, wide_ref):
    count, steps, rows, lanes = wide_ref.shape
    column = lax.broadcasted_iota(jnp.int32, (mapped_ref.shape[1], lanes), 0)
    values = mapped_ref[...]
    for n in range(count):
        pick = (column == first + n).astype(bf16)
        wide_ref[n] = jnp.dot(values, pick, preferred_element_type=f32).reshape(steps, rows, lanes)


def rows_of(rate_ref, n, rows):
    return jnp.broadcast_to(rate_ref[n : n + 1, :], (rows, rate_ref.shape[1]))


def totals_kernel(rank, delta_ref, drive_ref, mapped_ref, rate_ref, last_ref, sums_ref, wide):
    count, steps, rows, lanes = wide.shape

    @pl.when(pl.program_id(0) == 0)
    def _():
        spread(mapped_ref, rank, wide)

    rates = [rows_of(rate_ref, n, rows) for n in range(count)]
    zero = jnp.zeros((rows, lanes), f32)

    def one(p, held):
        states, sums = held
        step, drive = delta_ref[p], drive_ref[p]
        states = tuple(
            jnp.exp2(step * rates[n]) * states[n] + drive * wide[n, p] for n in range(count)
        )
        return states, sums + step

    states, sums = lax.fori_loop(0, steps, one, ((zero,) * count, zero))
    for n in range(count):
        last_ref[n] = states[n]
    sums_ref[...] = sums


def states_kernel(rank, delta_ref, drive_ref, mapped_ref, rate_ref, enter_ref, y_ref, state_ref, wide_in, wide_read):
    count, steps, rows, lanes = wide_in.shape

    @pl.when(pl.program_id(0) == 0)
    def _():
        spread(mapped_ref, rank, wide_in)
        spread(mapped_ref, rank + count, wide_read)

    rates = [rows_of(rate_ref, n, rows) for n in range(count)]

    def one(p, states):
        step, drive = delta_ref[p], drive_ref[p]
        states = tuple(
            jnp.exp2(step * rates[n]) * states[n] + drive * wide_in[n, p] for n in range(count)
        )
        terms = [states[n] * wide_read[n, p] for n in range(count)]
        while len(terms) > 1:
            terms = [a + b for a, b in zip(terms[::2], terms[1::2])]
        y_ref[p] = terms[0]
        for n in range(count):
            state_ref[p, n] = states[n]
        return states

    lax.fori_loop(0, steps, one, tuple(enter_ref[n] for n in range(count)))


def back_totals_kernel(rank, delta_ref, grad_y_ref, mapped_ref, rate_ref, last_ref, wide):
    count, steps, rows, lanes = wide.shape

    @pl.when(pl.program_id(0) == 0)
    def _():
        spread(mapped_ref, rank + count, wide)

    rates = [rows_of(rate_ref, n, rows) for n in range(count)]
    zero = jnp.zeros((rows, lanes), f32)

    def one(turn, held):
        p = steps - 1 - turn
        step, grad_y = delta_ref[p], grad_y_ref[p]
        return tuple(
            jnp.exp2(step * rates[n]) * (held[n] + grad_y * wide[n, p]) for n in range(count)
        )

    held = lax.fori_loop(0, steps, one, (zero,) * count)
    for n in range(count):
        last_ref[n] = held[n]


def back_kernel(rank, width, delta_ref, drive_ref, grad_y_ref, mapped_ref, rate_ref, first_ref, state_ref, enter_ref,
                input_ref, decay_ref, log_ref, maps_ref, wide_in, wide_read, sum_in, sum_read):
    count, steps, rows, lanes = wide_in.shape
    place = pl.program_id(0)

    @pl.when(place == 0)
    def _():
        spread(mapped_ref, rank, wide_in)
        spread(mapped_ref, rank + count, wide_read)

    rates = [rows_of(rate_ref, n, rows) for n in range(count)]
    held = lax.broadcasted_iota(jnp.int32, (rows, lanes), 1) < width - place * lanes
    fresh = place == 0
    for n in range(count):
        log_ref[n] = jnp.zeros((rows, lanes), f32)

    def one(turn, carry):
        p = steps - 1 - turn
        before = jnp.maximum(p - 1, 0)
        opening = p == 0
        step, drive, grad_y = delta_ref[p], drive_ref[p], grad_y_ref[p]
        to_input = jnp.zeros((rows, lanes), f32)
        to_decay = jnp.zeros((rows, lanes), f32)
        new = []
        for n in range(count):
            grad = grad_y * wide_read[n, p] + carry[n]
            passed = jnp.exp2(step * rates[n]) * grad
            new.append(passed)
            prior = jnp.where(opening, first_ref[n], state_ref[before, n])
            grad_decay = passed * prior
            to_decay = to_decay + grad_decay * rates[n]
            log_ref[n] += grad_decay * step
            to_input = to_input + grad * wide_in[n, p]
            part_in = jnp.where(held, grad * drive, 0.0)
            part_read = jnp.where(held, grad_y * state_ref[p, n], 0.0)
            sum_in[p, n] = jnp.where(fresh, 0.0, sum_in[p, n]) + part_in
            sum_read[p, n] = jnp.where(fresh, 0.0, sum_read[p, n]) + part_read
        input_ref[p] = to_input
        decay_ref[p] = to_decay
        return tuple(new)

    lax.fori_loop(0, steps, one, tuple(enter_ref[n] for n in range(count)))

    @pl.when(place == pl.num_programs(0) - 1)
    def _():
        ones = jnp.ones((8, lanes), bf16)

        def flat(p, _):
            for which, source in enumerate((sum_in, sum_read)):
                block = source[p].reshape(count * rows, lanes).astype(bf16)
                out = lax.dot_general(ones, block, (((1,), (1,)), ((), ())), preferred_element_type=f32)
                maps_ref[which, p] = out
            return 0

        lax.fori_loop(0, steps, flat, 0)


def tiles(shape, last):
    return pl.BlockSpec(shape[:-1] + (last,), lambda i: (0,) * (len(shape) - 1) + (i,))


def whole(shape):
    return pl.BlockSpec(shape, lambda i: (0,) * len(shape))


def scan_call(kernel, ins, outs, scratch, cost):
    width = ins[0][0].shape[-1]
    return pl.pallas_call(
        kernel,
        grid=(pl.cdiv(width, LANES),),
        in_specs=[whole(a.shape) if full else tiles(a.shape, LANES) for a, full in ins],
        out_specs=[whole(s) if full else tiles(s, LANES) for s, full in outs],
        out_shape=[jax.ShapeDtypeStruct(s, f32) for s, _ in outs],
        scratch_shapes=[pltpu.VMEM(s, f32) for s in scratch],
        compiler_params=pltpu.CompilerParams(vmem_limit_bytes=56 * MIB),
        cost_estimate=cost,
    )(*[a for a, _ in ins])


def dot(a, b):
    return jnp.dot(a, b, preferred_element_type=f32)


def dot_nt(a, b):
    return lax.dot_general(a, b, (((1,), (1,)), ((), ())), preferred_element_type=f32)


def dot_tn(a, b):
    return lax.dot_general(a, b, (((0,), (0,)), ((), ())), preferred_element_type=f32)


def shifted(x, axis, by):
    length = lax.axis_size(axis)
    pairs = [(i, i + by) for i in range(length) if 0 <= i + by < length]
    return lax.ppermute(x, axis, pairs)


def packed_size(arrays, rows):
    total = -(-sum(a.size for a in arrays) // LANES)
    return -(-total // rows) * rows


def packed_rows(arrays, rows):
    total = packed_size(arrays, rows)
    joined = jnp.concatenate([a.reshape(-1) for a in arrays])
    return jnp.pad(joined, (0, total * LANES - joined.size)).reshape(total, LANES)


def unpacked_rows(packed, shapes):
    packed = packed.reshape(-1)
    arrays, at = [], 0
    for shape in shapes:
        size = math.prod(shape)
        arrays.append(packed[at : at + size].reshape(shape))
        at += size
    return arrays


def silu_slope(values):
    sigma = jax.nn.sigmoid(values)
    return sigma * (1.0 + values * (1.0 - sigma))


def norm_back(grad_normed, unit_rows, inverse, weight_gain):
    scaled = grad_normed * weight_gain
    return inverse * (scaled - unit_rows * jnp.mean(scaled * unit_rows, axis=-1, keepdims=True))


def local(
    tokens,
    teacher,
    true_lengths,
    doc_lengths,
    routes,
    norm1_gain,
    in_weight,
    conv_weight,
    conv_bias,
    xproj_weight,
    dt_weight,
    dt_bias,
    a_log,
    skip_weight,
    out_weight,
    norm2_gain,
    router_weight,
    expert_in,
    expert_out,
):
    seqs, group, width = tokens.shape
    inner = in_weight.shape[2]
    rank = dt_weight.shape[0]
    states = a_log.shape[1]
    experts = router_weight.shape[1]
    n_seq = lax.axis_size("seq")
    n_chan = lax.axis_size("chan")
    shards = n_seq // experts
    most = group // 4
    taps = conv_weight.shape[0]
    rim = taps - 1
    lines = 8
    chunks = lines // seqs
    steps = group // chunks
    owned = seqs * group // n_chan
    part = min(group, owned)
    most = min(most, part)
    parts = owned // part
    place = lax.axis_index("chan")
    first_pos = lax.axis_index("seq") * group

    def laid(x):
        x = x.reshape((seqs, chunks, steps) + x.shape[2:])
        return x.transpose((2, 1, 0) + tuple(range(3, x.ndim))).reshape((steps, lines) + x.shape[3:])

    def unlaid(x):
        x = x.reshape((steps, chunks, seqs) + x.shape[2:])
        return x.transpose((2, 1, 0) + tuple(range(3, x.ndim))).reshape((seqs, group) + x.shape[3:])

    at = (
        first_pos
        + jnp.arange(steps, dtype=jnp.int32)[:, None]
        + (jnp.arange(lines, dtype=jnp.int32) // seqs * steps)[None, :]
    )
    ends = []
    for k in range(doc_lengths.shape[1] - 1):
        ends.append(doc_lengths[:, k] + (ends[-1] if ends else 0))
    ends = [jnp.tile(end, chunks)[None, :] for end in ends]

    def doc_at(pos):
        return sum((pos >= end).astype(jnp.int32) for end in ends)

    doc_ids = doc_at(at)
    keep = (doc_ids == doc_at(at - 1)) & (at > 0)
    valid = [(doc_at(at - rim + k) == doc_ids).astype(f32)[..., None] for k in range(taps)]

    gain_one = norm1_gain.astype(f32)

    def normed_of(rows):
        full = rows.astype(f32)
        inverse = lax.rsqrt(jnp.mean(full * full, axis=-1, keepdims=True) + epsilon)
        return (full * inverse * gain_one).astype(bf16)

    conv_w_in, gate_w_in = in_weight[:, 0, :], in_weight[:, 1, :]
    prior_rows = shifted(tokens[:, group - rim :, :], "seq", 1)
    normed_one = normed_of(laid(tokens)).reshape(steps * lines, width)
    conv_in = dot(normed_one, conv_w_in).astype(bf16).reshape(steps, lines, inner)
    gate_z = dot(normed_one, gate_w_in).reshape(steps, lines, inner)
    prior_normed = normed_of(prior_rows.transpose(1, 0, 2)).reshape(rim * seqs, width)
    prior_in = dot(prior_normed, conv_w_in).astype(bf16).reshape(rim, seqs, inner)
    halo = jnp.concatenate([prior_in, conv_in[steps - rim :, : lines - seqs]], axis=1)
    extended = jnp.concatenate([halo, conv_in], axis=0)
    taps_full = conv_weight.astype(f32)

    def tapped(k):
        return extended[k : k + steps].astype(f32) * valid[k]

    pre_act = conv_bias.astype(f32) + sum(taps_full[k] * tapped(k) for k in range(taps))
    act = pre_act * jax.nn.sigmoid(pre_act)
    act_low = act.astype(bf16).reshape(steps * lines, inner)
    mapped_part = dot(act_low, xproj_weight).astype(bf16)
    mapped = summed_over(mapped_part, "chan", 1)
    dt_low = mapped[:, :rank].astype(bf16)
    mapped_low = mapped.astype(bf16)
    dt_pre = (dot(dt_low, dt_weight) + dt_bias).reshape(steps, lines, inner)
    delta = jax.nn.softplus(dt_pre)
    rate = -jnp.exp(a_log).T
    rate_two = rate * log2e
    step_size = jnp.where(keep[..., None], delta, cut)
    drive = delta * act

    work = steps * lines * states * inner
    wide_shape = (states, steps, lines, LANES)
    last, sums = scan_call(
        functools.partial(totals_kernel, rank),
        [(step_size, False), (drive, False), (mapped_low, True), (rate_two, False)],
        [((states, lines, inner), False), ((lines, inner), False)],
        [wide_shape],
        pl.CostEstimate(flops=5 * work, bytes_accessed=8 * steps * lines * inner, transcendentals=work),
    )
    (enter,) = carried(last, sums, rate_two, "seq", False, 2)
    y_scan, state = scan_call(
        functools.partial(states_kernel, rank),
        [
            (step_size, False),
            (drive, False),
            (mapped_low, True),
            (rate_two, False),
            (enter, False),
        ],
        [((steps, lines, inner), False), ((steps, states, lines, inner), False)],
        [wide_shape] * 2,
        pl.CostEstimate(flops=7 * work, bytes_accessed=4 * work, transcendentals=work),
    )
    y_full = y_scan + skip_weight * act
    silu_z = gate_z * jax.nn.sigmoid(gate_z)
    gated = (y_full * silu_z).astype(bf16)
    gated_rows = gated.reshape(steps * lines, inner)
    out_part = dot(unlaid(gated).reshape(seqs * group, inner), out_weight).astype(bf16)
    (mixed,) = share_of(out_part.reshape(n_chan, owned, width), "chan", 3)

    def own(x):
        rows = x.reshape((seqs * group,) + x.shape[2:])
        return lax.dynamic_slice_in_dim(rows, place * owned, owned, 0)

    tokens_own = own(tokens).astype(f32)
    inverse_one = lax.rsqrt(jnp.mean(tokens_own * tokens_own, axis=-1, keepdims=True) + epsilon)
    unit_one = tokens_own * inverse_one
    hidden_one = tokens_own + mixed
    inverse_two = lax.rsqrt(jnp.mean(hidden_one * hidden_one, axis=-1, keepdims=True) + epsilon)
    unit_two = hidden_one * inverse_two
    gain_two = norm2_gain.astype(f32)
    normed_two = (unit_two * gain_two).astype(bf16)
    probs = jax.nn.softmax(dot(normed_two, router_weight), axis=-1)
    routes_own = own(routes)
    chosen = routes_own[..., None] == jnp.arange(experts, dtype=jnp.int32)
    chosen_rows = chosen.astype(f32)
    gate_value = jnp.sum(probs * chosen_rows, axis=-1, keepdims=True)
    row = jnp.arange(owned, dtype=jnp.int32)
    earlier = (row[None, :] < row[:, None]) & (row[None, :] // part == row[:, None] // part)
    rank_in = dot(earlier.astype(bf16), chosen.astype(bf16))
    slots = parts * most
    wanted = rank_in + (row // part * most).astype(f32)[:, None]
    hit = (wanted[..., None] == jnp.arange(slots, dtype=f32)) & chosen[..., None]
    hit = hit.astype(bf16)
    hit_send = hit.reshape(owned, experts * slots)
    hit_back = jnp.repeat(hit, shards, axis=1).reshape(owned, n_seq * slots)

    def to_slabs(rows):
        packed = dot_tn(hit_send, rows).astype(bf16).reshape(experts, slots, width)
        return jnp.repeat(packed, shards, axis=0), "scatter", "seq"

    def to_rows(x):
        return x.reshape(n_seq, slots, width), "scatter", "seq"

    def by_units(x):
        return x.reshape(n_seq * slots, n_chan, units).transpose(1, 0, 2), "scatter", "chan"

    def flat(x):
        return x.reshape(-1, x.shape[-1])

    first_slab, second_slab = expert_in[0], expert_out[0]
    units = first_slab.shape[1] // n_chan
    arrived = flat(exchange(4, to_slabs(normed_two))[0])
    pre_hidden = dot(arrived, first_slab)
    cdf = 0.5 * (1.0 + lax.erf(pre_hidden * 0.7071067811865476))
    hidden_low = (pre_hidden * cdf).astype(bf16)
    density = jnp.exp(-0.5 * pre_hidden * pre_hidden) * 0.3989422804014327
    slope = cdf + pre_hidden * density
    result = dot(hidden_low, second_slab).astype(bf16)
    result_rows, rows_all = exchange(5, to_rows(result), (arrived, "relay", "chan"))
    expert_total = dot(hit_back, flat(result_rows))
    layer = hidden_one + gate_value * expert_total
    layer_low = layer.astype(bf16)

    flat_row = place * owned + row
    seq_of = flat_row // group
    lengths_own = sum(
        jnp.where(seq_of == s, true_lengths[s], 0) for s in range(seqs)
    )
    total_true = jnp.sum(true_lengths).astype(f32)
    loss_mask = (first_pos + flat_row % group < lengths_own).astype(f32)[:, None]
    error = layer - own(teacher).astype(f32)
    loss_part = jnp.sum(loss_mask * error * error) / total_true
    grad_layer = 2.0 / total_true * loss_mask * error
    grad_gate = jnp.sum(grad_layer * expert_total, axis=-1, keepdims=True)
    grad_result = (gate_value * grad_layer).astype(bf16)
    grad_rows, hidden_all = exchange(6, to_slabs(grad_result), by_units(hidden_low))
    grad_rows = flat(grad_rows)
    grad_pre = (dot_nt(grad_rows, second_slab) * slope).astype(bf16)
    grad_slab_rows = dot_nt(grad_pre, first_slab).astype(bf16)
    grad_expert, grad_rows_all = exchange(7, to_rows(grad_slab_rows), (grad_rows, "relay", "chan"))
    grad_expert = dot(hit_back, flat(grad_expert))

    grad_logit = grad_gate * gate_value * (chosen_rows - probs)
    grad_router = dot_tn(normed_two, grad_logit.astype(bf16))
    grad_normed_two = grad_expert + dot_nt(grad_logit.astype(bf16), router_weight)
    grad_gain_two = jnp.sum(grad_normed_two * unit_two, axis=0)
    grad_hidden_one = grad_layer + norm_back(grad_normed_two, unit_two, inverse_two, gain_two)

    shared = packed_rows([grad_gain_two, grad_router, loss_part], 8)
    grad_mixed, shared = exchange(
        8, (grad_hidden_one.astype(bf16), "relay", "chan"), (shared, "gather", "chan")
    )
    shared = jnp.sum(shared, axis=0)
    grad_mixed = laid(grad_mixed.reshape(seqs, group, width)).reshape(steps * lines, width)
    grad_out_w = dot_tn(gated_rows, grad_mixed)
    grad_gated = dot_nt(grad_mixed, out_weight).reshape(steps, lines, inner)
    grad_y = grad_gated * silu_z
    grad_z = (grad_gated * y_full * silu_slope(gate_z)).astype(bf16)
    grad_z_rows = grad_z.reshape(steps * lines, inner)
    grad_in_gate = dot_tn(normed_one, grad_z_rows)
    summed_out, summed_gate = lax.psum((grad_out_w.astype(bf16), grad_in_gate.astype(bf16)), "seq")
    grad_skip = jnp.sum(grad_y * act, axis=(0, 1))
    (back_last,) = scan_call(
        functools.partial(back_totals_kernel, rank),
        [(step_size, False), (grad_y, False), (mapped_low, True), (rate_two, False)],
        [((states, lines, inner), False)],
        [wide_shape],
        pl.CostEstimate(flops=5 * work, bytes_accessed=8 * steps * lines * inner, transcendentals=work),
    )
    back_enter, grad_pre_all = carried(
        back_last, sums, rate_two, "seq", True, 9, by_units(grad_pre)
    )
    grad_first = dot_tn(flat(rows_all), flat(grad_pre_all))
    grad_second = dot_tn(flat(hidden_all), flat(grad_rows_all))
    state_input, from_decay, log_sums, maps = scan_call(
        functools.partial(back_kernel, rank, inner),
        [
            (step_size, False),
            (drive, False),
            (grad_y, False),
            (mapped_low, True),
            (rate_two, False),
            (enter, False),
            (state, False),
            (back_enter, False),
        ],
        [
            ((steps, lines, inner), False),
            ((steps, lines, inner), False),
            ((states, lines, inner), False),
            ((2, steps, 8, states * lines), True),
        ],
        [wide_shape] * 2 + [(steps, states, lines, LANES)] * 2,
        pl.CostEstimate(flops=17 * work, bytes_accessed=4 * work, transcendentals=work),
    )
    grad_a_log = (jnp.sum(log_sums, axis=1) * rate).T
    grad_maps = maps[:, :, 0].reshape(2, steps, states, lines).transpose(1, 3, 0, 2)
    grad_maps = grad_maps.reshape(steps * lines, 2 * states)
    grad_delta = from_decay * (1.0 / log2e) + state_input * act
    grad_dt_pre = grad_delta * jax.nn.sigmoid(dt_pre)
    grad_dt_bias = jnp.sum(grad_dt_pre, axis=(0, 1))
    grad_dt_low = grad_dt_pre.astype(bf16).reshape(steps * lines, inner)
    grad_dt_w = dot_tn(dt_low, grad_dt_low)
    low_part = jnp.concatenate([dot_nt(grad_dt_low, dt_weight), grad_maps], axis=1).astype(bf16)
    grad_mapped = summed_over(low_part, "chan", 10).astype(bf16)
    grad_xproj = dot_tn(grad_mapped, act_low)
    grad_act = (
        grad_y * skip_weight
        + state_input * delta
        + dot_nt(grad_mapped, xproj_weight).reshape(steps, lines, inner)
    )
    grad_pre_act = grad_act * silu_slope(pre_act)
    grad_conv_b = jnp.sum(grad_pre_act, axis=(0, 1))
    grad_conv_w = jnp.stack([jnp.sum(grad_pre_act * tapped(k), axis=(0, 1)) for k in range(taps)])
    rims = sum(
        jnp.pad(
            (grad_pre_act[: rim - k] * taps_full[k] * valid[k][: rim - k]),
            ((k, 0), (0, 0), (0, 0)),
        )
        for k in range(rim)
    )
    next_rims = shifted(rims[:, :seqs], "seq", -1)
    after = jnp.concatenate([rims[:, seqs:], next_rims], axis=1)
    grad_conv_in = sum(
        jnp.pad(
            (grad_pre_act * taps_full[k] * valid[k])[rim - k :],
            ((0, rim - k), (0, 0), (0, 0)),
        )
        for k in range(taps)
    ) + jnp.pad(after, ((steps - rim, 0), (0, 0), (0, 0)))
    grad_conv_low = grad_conv_in.astype(bf16)
    grad_in_conv = dot_tn(normed_one, grad_conv_low.reshape(steps * lines, inner))

    def natural(x):
        return unlaid(x).reshape(seqs * group, inner)

    normed_part = dot_nt(natural(grad_conv_low), conv_w_in) + dot_nt(natural(grad_z), gate_w_in)
    unit_all = tokens.reshape(seqs * group, width).astype(f32)
    unit_all = unit_all * lax.rsqrt(jnp.mean(unit_all * unit_all, axis=-1, keepdims=True) + epsilon)
    grad_gain_one = packed_rows([jnp.sum(normed_part * unit_all, axis=0)], 8)
    normed_part = normed_part.astype(bf16).reshape(n_chan, owned, width)
    large = jnp.concatenate([grad_in_conv, grad_xproj, grad_dt_w], axis=0).astype(bf16)
    large_rows = large.shape[0]
    each = -(-large_rows // (16 * n_seq)) * 16
    large = jnp.pad(large, ((0, each * n_seq - large_rows), (0, 0))).reshape(n_seq, each, inner)
    small = [grad_conv_w, grad_conv_b, grad_dt_bias, grad_a_log, grad_skip]
    small_flat = jnp.concatenate([packed_rows(small, 1), shared], axis=0)
    small_rows = small_flat.shape[0]
    each_small = -(-small_rows // (8 * n_seq)) * 8
    small_flat = jnp.pad(small_flat, ((0, each_small * n_seq - small_rows), (0, 0)))
    small_flat = small_flat.reshape(n_seq, each_small, LANES)
    grad_normed_one, large, small_flat, grad_gain_one = share_of(
        normed_part,
        "chan",
        11,
        (large, "scatter", "seq"),
        (small_flat, "scatter", "seq"),
        (grad_gain_one, "gather", "chan"),
    )
    large = jnp.sum(large.astype(f32), axis=0).astype(bf16)
    small_flat = jnp.sum(small_flat, axis=0)
    grad_gain_one = jnp.sum(grad_gain_one, axis=0)
    grad_own = grad_hidden_one + norm_back(grad_normed_one, unit_one, inverse_one, gain_one)
    grad_tokens, layer_out, large, small_flat, grad_gain_one = exchange(
        12,
        (grad_own.astype(bf16), "relay", "chan"),
        (layer_low, "relay", "chan"),
        (large, "gather", "seq"),
        (small_flat, "gather", "seq"),
        (grad_gain_one, "gather", "seq"),
    )
    (grad_gain_one,) = unpacked_rows(jnp.sum(grad_gain_one, axis=0), [(width,)])
    large = flat(large).astype(f32)
    summed_conv, summed_xproj, summed_dt, _ = jnp.split(
        large, [width, width + grad_xproj.shape[0], large_rows]
    )
    small_flat = flat(small_flat)
    mid = packed_size(small, 1)
    small = unpacked_rows(small_flat[:mid], [a.shape for a in small])
    tiny = unpacked_rows(small_flat[mid:small_rows], [(width,), grad_router.shape, ()])
    return (
        layer_out.reshape(seqs, group, width),
        tiny[2],
        grad_tokens.reshape(seqs, group, width).astype(f32),
        grad_gain_one,
        jnp.stack([summed_conv, summed_gate.astype(f32)], axis=1),
        small[0],
        small[1],
        summed_xproj.T,
        summed_dt,
        small[2],
        small[3],
        small[4],
        summed_out.astype(f32),
        tiny[0],
        tiny[1],
        grad_first[None],
        grad_second[None],
    )


def solution(mesh):
    placed = (
        P(None, "seq", None),
        P(None, "seq", None),
        P(),
        P(),
        P(None, "seq"),
        P(),
        P(None, None, "chan"),
        P(None, "chan"),
        P("chan"),
        P("chan", None),
        P(None, "chan"),
        P("chan"),
        P("chan", None),
        P("chan"),
        P("chan", None),
        P(),
        P(),
        P("seq", None, None),
        P("seq", None, None),
    )
    return jax.shard_map(
        local,
        mesh=mesh,
        in_specs=placed,
        out_specs=(
            P(None, "seq", None),
            P(),
            P(None, "seq", None),
            P(),
            P(None, None, "chan"),
            P(None, "chan"),
            P("chan"),
            P("chan", None),
            P(None, "chan"),
            P("chan"),
            P("chan", None),
            P("chan"),
            P("chan", None),
            P(),
            P(),
            P("seq", None, "chan"),
            P("seq", "chan", None),
        ),
        check_vma=False,
    )
```

```python
import functools
import math

import jax
import jax.numpy as jnp
from jax import lax
from jax.experimental import pallas as pl
from jax.experimental.pallas import tpu as pltpu
from jax.sharding import PartitionSpec as P

epsilon = 1e-05
log2e = 1.4426950408889634
cut = 1e30
MESH = pl.DeviceIdType.MESH
f32 = jnp.float32
bf16 = jnp.bfloat16
LANES = 128
MIB = 1024 * 1024


def greet(axes):
    barrier = pltpu.get_barrier_semaphore()
    told = 0
    for axis, count in axes:
        me = lax.axis_index(axis)
        for k in range(1, count):
            pl.semaphore_signal(
                barrier, inc=1, device_id={axis: lax.rem(me + k, count)}, device_id_type=MESH
            )
        told += count - 1
    return told


def sems_of(item):
    count = item[2]
    return [pltpu.SemaphoreType.DMA] + [pltpu.SemaphoreType.DMA((count - 1,))] * 2


def flipped(i, mask):
    bit = 1
    while bit <= mask:
        if mask & bit:
            i = i + bit - 2 * bit * lax.rem(i // bit, 2)
        bit *= 2
    return i


def begin(item, x_ref, o_ref, own_sem, send_sem, recv_sem):
    mode, axis, count = item
    me = lax.axis_index(axis)

    def remote(source, row, slot, to):
        return pltpu.make_async_remote_copy(
            src_ref=source,
            dst_ref=o_ref.at[row],
            send_sem=send_sem.at[slot],
            recv_sem=recv_sem.at[slot],
            device_id={axis: to},
            device_id_type=MESH,
        )

    own = pltpu.make_async_copy(x_ref.at[me] if mode == "scatter" else x_ref, o_ref.at[me], own_sem)
    copies, later = [], []
    if mode in ("gather", "scatter"):
        for mask in range(count - 1, 0, -1):
            to = flipped(me, mask)
            copies.append(remote(x_ref.at[to] if mode == "scatter" else x_ref, me, mask - 1, to))
    else:
        groups = count // mode
        side, place = lax.rem(me, mode), me // mode
        mates = [place * mode + lax.rem(side + j, mode) for j in range(1, mode)]
        slot = groups - 1
        for mate in mates:
            copies.append(remote(x_ref, me, slot, mate))
            slot += 1
        for mask in range(groups - 1, 0, -1):
            row = flipped(place, mask) * mode + side
            first = remote(x_ref, me, mask - 1, row)
            passed = []
            for mate in mates:
                passed.append(remote(o_ref.at[row], row, slot, mate))
                slot += 1
            later.append((first, passed))
    for copy in [first for first, _ in later] + copies:
        copy.start()
    own.start()
    return own, copies, later


def finish(under_way):
    for _, _, later in under_way:
        for first, passed in later:
            first.wait_recv()
            for second in passed:
                second.start()
    for own, copies, later in under_way:
        own.wait()
        for copy in copies:
            copy.wait()
        for first, passed in later:
            first.wait_send()
            for second in passed:
                second.wait()


def items_of(exchanges):
    return [(mode, axis, lax.axis_size(axis)) for _, mode, axis in exchanges]


def axes_of(items):
    return sorted({(axis, count) for _, axis, count in items})


def landed(x, item):
    shape = x.shape if item[0] == "scatter" else (item[2],) + x.shape
    return jax.ShapeDtypeStruct(shape, x.dtype)


def exchange_kernel(items, *refs):
    number = len(items)
    sems = refs[2 * number :]
    pl.semaphore_wait(pltpu.get_barrier_semaphore(), greet(axes_of(items)))
    finish(
        [
            begin(item, refs[i], refs[number + i], *sems[3 * i : 3 * i + 3])
            for i, item in enumerate(items)
        ]
    )


def exchange(number, *exchanges):
    items = items_of(exchanges)
    return pl.pallas_call(
        functools.partial(exchange_kernel, items),
        out_shape=[landed(x, item) for (x, _, _), item in zip(exchanges, items)],
        in_specs=[pl.BlockSpec(memory_space=pl.ANY)] * len(items),
        out_specs=[pl.BlockSpec(memory_space=pl.ANY)] * len(items),
        scratch_shapes=[sem for item in items for sem in sems_of(item)],
        compiler_params=pltpu.CompilerParams(
            collective_id=number, has_side_effects=True, vmem_limit_bytes=16 * MIB
        ),
    )(*[x for x, _, _ in exchanges])


def greet_near(axis, count):
    barrier = pltpu.get_barrier_semaphore()
    me = lax.axis_index(axis)
    beside = me + 1 - 2 * lax.rem(me, 2)
    pl.semaphore_signal(barrier, inc=1, device_id={axis: beside}, device_id_type=MESH)
    for k in range(1, count // 2):
        pl.semaphore_signal(
            barrier, inc=1, device_id={axis: lax.rem(me + 2 * k, count)}, device_id_type=MESH
        )
    pl.semaphore_wait(barrier, count // 2)


def sum_kernel(axis, count, x_ref, o_ref, beside_in, pair, far_in, send_sem, recv_sem):
    me = lax.axis_index(axis)
    beside = me + 1 - 2 * lax.rem(me, 2)
    greet_near(axis, count)
    near = pltpu.make_async_remote_copy(
        src_ref=x_ref,
        dst_ref=beside_in,
        send_sem=send_sem.at[0],
        recv_sem=recv_sem.at[0],
        device_id={axis: beside},
        device_id_type=MESH,
    )
    near.start()
    near.wait_recv()
    pair[...] = (x_ref[...].astype(f32) + beside_in[...].astype(f32)).astype(bf16)
    copies = []
    for k in range(1, count // 2):
        copies.append(
            pltpu.make_async_remote_copy(
                src_ref=pair,
                dst_ref=far_in.at[k - 1],
                send_sem=send_sem.at[k],
                recv_sem=recv_sem.at[k],
                device_id={axis: lax.rem(me + 2 * k, count)},
                device_id_type=MESH,
            )
        )
        copies[-1].start()
    for copy in copies:
        copy.wait_recv()
    total = pair[...].astype(f32)
    for k in range(count // 2 - 1):
        total = total + far_in[k].astype(f32)
    o_ref[...] = total
    near.wait_send()
    for copy in copies:
        copy.wait_send()


def summed_over(x, axis, number):
    count = lax.axis_size(axis)
    return pl.pallas_call(
        functools.partial(sum_kernel, axis, count),
        out_shape=jax.ShapeDtypeStruct(x.shape, f32),
        in_specs=[pl.BlockSpec(memory_space=pltpu.VMEM)],
        out_specs=pl.BlockSpec(memory_space=pltpu.VMEM),
        scratch_shapes=[
            pltpu.VMEM(x.shape, bf16),
            pltpu.VMEM(x.shape, bf16),
            pltpu.VMEM((count // 2 - 1,) + x.shape, bf16),
            pltpu.SemaphoreType.DMA((count // 2,)),
            pltpu.SemaphoreType.DMA((count // 2,)),
        ],
        compiler_params=pltpu.CompilerParams(
            collective_id=number, has_side_effects=True, vmem_limit_bytes=16 * MIB
        ),
    )(x)


class Share:
    def __init__(self, axis, count, size, x_ref, near_in, pairs, far_in, near_send, near_recv, far_send, far_recv):
        self.groups, self.size, self.x = count // size, size, x_ref
        self.near_in, self.pairs, self.far_in = near_in, pairs, far_in
        me = lax.axis_index(axis)
        side, place = lax.rem(me, size), me // size
        self.rows, self.near, self.far = [], [], []
        for k in range(self.groups):
            group = flipped(place, self.groups - 1 - k)
            self.rows.append(group * size + side)
            self.near.append(
                [
                    pltpu.make_async_remote_copy(
                        src_ref=x_ref.at[group * size + lax.rem(side + j, size)],
                        dst_ref=near_in.at[k, j - 1],
                        send_sem=near_send.at[k, j - 1],
                        recv_sem=near_recv.at[k, j - 1],
                        device_id={axis: place * size + lax.rem(side + j, size)},
                        device_id_type=MESH,
                    )
                    for j in range(1, size)
                ]
            )
            if k < self.groups - 1:
                self.far.append(
                    pltpu.make_async_remote_copy(
                        src_ref=pairs.at[k],
                        dst_ref=far_in.at[k],
                        send_sem=far_send.at[k],
                        recv_sem=far_recv.at[k],
                        device_id={axis: self.rows[k]},
                        device_id_type=MESH,
                    )
                )

    def begin(self):
        for copies in self.near:
            for copy in copies:
                copy.start()

    def near_sum(self, k):
        total = self.x[self.rows[k]].astype(f32)
        for j, copy in enumerate(self.near[k]):
            copy.wait_recv()
            total = total + self.near_in[k, j].astype(f32)
        return total

    def pass_on(self):
        for k, copy in enumerate(self.far):
            self.pairs[k] = self.near_sum(k).astype(bf16)
            copy.start()

    def total(self):
        total = self.near_sum(self.groups - 1)
        for k, copy in enumerate(self.far):
            copy.wait_recv()
            total = total + self.far_in[k].astype(f32)
        return total

    def close(self):
        for copy in [copy for copies in self.near for copy in copies] + self.far:
            copy.wait_send()


def share_kernel(shares, items, *refs):
    many, number = len(shares), len(items)
    at = 0

    def take(k):
        nonlocal at
        at += k
        return refs[at - k : at]

    xs, riders, outs, rider_outs = take(many), take(number), take(many), take(number)
    tasks = [Share(axis, count, size, x, *take(7)) for (axis, count, size), x in zip(shares, xs)]
    axes = set(axes_of(items)) | {(axis, count) for axis, count, _ in shares}
    pl.semaphore_wait(pltpu.get_barrier_semaphore(), greet(sorted(axes)))
    for task in tasks:
        task.begin()
    under_way = [begin(item, riders[i], rider_outs[i], *take(3)) for i, item in enumerate(items)]
    for task in tasks:
        task.pass_on()
    for task, out in zip(tasks, outs):
        out[...] = task.total().astype(out.dtype)
    for task in tasks:
        task.close()
    finish(under_way)


def share_of(number, shares, *exchanges):
    items = items_of(exchanges)
    anywhere = [pl.BlockSpec(memory_space=pl.ANY)] * len(items)
    held = [pl.BlockSpec(memory_space=pltpu.VMEM)] * len(shares)
    scratch = []
    for x, axis, size, _ in shares:
        groups = lax.axis_size(axis) // size
        part = x.shape[1:]
        scratch += [
            pltpu.VMEM((groups, size - 1) + part, bf16),
            pltpu.VMEM((groups - 1,) + part, bf16),
            pltpu.VMEM((groups - 1,) + part, bf16),
            pltpu.SemaphoreType.DMA((groups, size - 1)),
            pltpu.SemaphoreType.DMA((groups, size - 1)),
            pltpu.SemaphoreType.DMA((groups - 1,)),
            pltpu.SemaphoreType.DMA((groups - 1,)),
        ]
    return pl.pallas_call(
        functools.partial(
            share_kernel, [(axis, lax.axis_size(axis), size) for _, axis, size, _ in shares], items
        ),
        out_shape=[jax.ShapeDtypeStruct(x.shape[1:], kind) for x, _, _, kind in shares]
        + [landed(x, item) for (x, _, _), item in zip(exchanges, items)],
        in_specs=held + anywhere,
        out_specs=held + anywhere,
        scratch_shapes=scratch + [sem for item in items for sem in sems_of(item)],
        compiler_params=pltpu.CompilerParams(
            collective_id=number, has_side_effects=True, vmem_limit_bytes=32 * MIB
        ),
    )(*[share[0] for share in shares], *[x for x, _, _ in exchanges])


def turned(value):
    return pltpu.roll(value, value.shape[0] // 2, 0)


def carry_kernel(axis, count, back, items, *refs):
    number = len(items)
    local_ref, sums_ref, rate_ref = refs[:3]
    xs, o_ref, outs = refs[3 : 3 + number], refs[3 + number], refs[4 + number : 4 + 2 * number]
    send, got, send_sum, got_sum, total, enter = refs[4 + 2 * number : 10 + 2 * number]
    send_sem, recv_sem, send_sum_sem, recv_sum_sem = refs[10 + 2 * number : 14 + 2 * number]
    sems = refs[14 + 2 * number :]
    me = lax.axis_index(axis)
    states, rows, width = local_ref.shape
    half = rows // 2
    spans = []
    span = 1
    while span < count:
        spans.append(span)
        span *= 2
    sign = -1 if back else 1
    barrier = pltpu.get_barrier_semaphore()
    greeted = greet(axes_of(items))
    for span in spans:
        for by in (span, -span):
            there = me + by
            greeted = greeted + jnp.where((there >= 0) & (there < count), 1, 0)

            @pl.when((there >= 0) & (there < count))
            def _():
                pl.semaphore_signal(barrier, inc=1, device_id={axis: there}, device_id_type=MESH)

    upper = lax.broadcasted_iota(jnp.int32, (rows, width), 0) >= half
    first = upper if back else jnp.logical_not(upper)
    sums = sums_ref[...]
    sums_turned = turned(sums)
    sums_both = sums + sums_turned
    sums_first = jnp.where(first, sums, sums_turned)
    sums_last = jnp.where(first, sums_turned, sums)

    def packed_rate(j):
        return jnp.where(upper, rate_ref[pl.ds(2 * j + 1, 1), :], rate_ref[pl.ds(2 * j, 1), :])

    def both(j):
        even, odd = local_ref[2 * j], local_ref[2 * j + 1]
        low = jnp.where(upper, turned(odd), even)
        high = jnp.where(upper, odd, turned(even))
        return (high, low) if back else (low, high)

    for j in range(states // 2):
        opening, closing = both(j)
        total[j] = jnp.exp2(packed_rate(j) * sums_last) * opening + closing
        enter[j] = jnp.zeros((rows, width), f32)

    pl.semaphore_wait(barrier, greeted)
    under_way = [
        begin(item, xs[i], outs[i], *sems[3 * i : 3 * i + 3]) for i, item in enumerate(items)
    ]
    sums_total = sums_both
    sums_enter = jnp.zeros((rows, width), f32)
    for turn, span in enumerate(spans):
        to = me + sign * span
        origin = me - sign * span
        sends = (to >= 0) & (to < count)
        takes = (origin >= 0) & (origin < count)
        for j in range(0, states // 2, 2):
            send[turn, pl.ds(j * rows, 2 * rows), :] = jnp.concatenate([total[j], total[j + 1]], axis=0).astype(bf16)
        send_sum[turn] = sums_total
        copies = [
            pltpu.make_async_remote_copy(
                src_ref=source.at[turn],
                dst_ref=target.at[turn],
                send_sem=ssem.at[turn],
                recv_sem=rsem.at[turn],
                device_id={axis: to},
                device_id_type=MESH,
            )
            for source, target, ssem, rsem in (
                (send, got, send_sem, recv_sem),
                (send_sum, got_sum, send_sum_sem, recv_sum_sem),
            )
        ]

        @pl.when(sends)
        def _():
            for copy in copies:
                copy.start()

        @pl.when(jnp.logical_not(takes))
        def _():
            got[turn] = jnp.zeros(got.shape[1:], bf16)
            got_sum[turn] = jnp.zeros(got_sum.shape[1:], f32)

        @pl.when(takes)
        def _():
            for copy in copies:
                copy.wait_recv()

        for j in range(0, states // 2, 2):
            pair = got[turn, pl.ds(j * rows, 2 * rows), :].astype(f32)
            for i in (j, j + 1):
                came = pair[(i - j) * rows : (i - j + 1) * rows]
                rate = packed_rate(i)
                enter[i] = jnp.exp2(rate * sums_enter) * came + enter[i]
                total[i] = jnp.exp2(rate * sums_total) * came + total[i]
        sums_enter = sums_enter + got_sum[turn]
        sums_total = sums_total + got_sum[turn]

        @pl.when(sends)
        def _():
            for copy in copies:
                copy.wait_send()

    for j in range(states // 2):
        opening, _ = both(j)
        outer = enter[j]
        inner = jnp.exp2(packed_rate(j) * sums_first) * outer + opening
        low, high = (inner, outer) if back else (outer, inner)
        o_ref[2 * j] = jnp.where(upper, turned(high), low)
        o_ref[2 * j + 1] = jnp.where(upper, high, turned(low))
    finish(under_way)


def carried(local, sums, rate, axis, back, number, *exchanges):
    count = lax.axis_size(axis)
    states, rows, width = local.shape
    turns = max(1, (count - 1).bit_length())
    items = items_of(exchanges)
    anywhere = [pl.BlockSpec(memory_space=pl.ANY)] * len(items)
    return pl.pallas_call(
        functools.partial(carry_kernel, axis, count, back, items),
        out_shape=[jax.ShapeDtypeStruct(local.shape, f32)]
        + [landed(x, item) for (x, _, _), item in zip(exchanges, items)],
        in_specs=[pl.BlockSpec(memory_space=pltpu.VMEM)] * 3 + anywhere,
        out_specs=[pl.BlockSpec(memory_space=pltpu.VMEM)] + anywhere,
        scratch_shapes=[
            pltpu.VMEM((turns, states // 2 * rows, width), bf16),
            pltpu.VMEM((turns, states // 2 * rows, width), bf16),
            pltpu.VMEM((turns, rows, width), f32),
            pltpu.VMEM((turns, rows, width), f32),
            pltpu.VMEM((states // 2, rows, width), f32),
            pltpu.VMEM((states // 2, rows, width), f32),
            pltpu.SemaphoreType.DMA((turns,)),
            pltpu.SemaphoreType.DMA((turns,)),
            pltpu.SemaphoreType.DMA((turns,)),
            pltpu.SemaphoreType.DMA((turns,)),
        ]
        + [sem for item in items for sem in sems_of(item)],
        compiler_params=pltpu.CompilerParams(
            collective_id=number, has_side_effects=True, vmem_limit_bytes=24 * MIB
        ),
    )(local, sums, rate, *[x for x, _, _ in exchanges])


def spread(mapped_ref, first, wide_ref):
    count, steps, rows, lanes = wide_ref.shape
    column = lax.broadcasted_iota(jnp.int32, (mapped_ref.shape[1], lanes), 0)
    values = mapped_ref[...]
    for n in range(count):
        pick = (column == first + n).astype(bf16)
        wide_ref[n] = jnp.dot(values, pick, preferred_element_type=f32).reshape(steps, rows, lanes)


def rows_of(rate_ref, n, rows):
    return jnp.broadcast_to(rate_ref[n : n + 1, :], (rows, rate_ref.shape[1]))


def perm_of(steps, lines, seqs):
    rows = steps * lines
    laid = lax.broadcasted_iota(jnp.int32, (rows, rows), 0)
    natural = lax.broadcasted_iota(jnp.int32, (rows, rows), 1)
    line = laid % lines
    wanted = (line % seqs) * (rows // seqs) + (line // seqs) * steps + laid // lines
    return (natural == wanted).astype(bf16)


def unit_of(rows):
    return rows * lax.rsqrt(jnp.mean(rows * rows, axis=-1, keepdims=True) + epsilon)


def softplus(x):
    return jnp.maximum(x, 0.0) + jnp.log1p(jnp.exp(-jnp.abs(x)))


def sigmoid(x):
    return 1.0 / (1.0 + jnp.exp(-x))


def silu_slope(values, sigma):
    return sigma * (1.0 + values * (1.0 - sigma))


def dot(a, b):
    return jnp.dot(a, b, preferred_element_type=f32)


def dot_nt(a, b):
    return lax.dot_general(a, b, (((1,), (1,)), ((), ())), preferred_element_type=f32)


def dot_tn(a, b):
    return lax.dot_general(a, b, (((0,), (0,)), ((), ())), preferred_element_type=f32)


def front_kernel(seq_count, chan_count, tokens_ref, gain_ref, w_ref, taps_ref, bias_ref, xproj_ref, valid_ref,
                 normed_ref, ext_ref, pre_ref, gate_ref, mapped_ref,
                 halo, part, beside_in, pair, far_in, halo_send, halo_recv, send_sem, recv_sem):
    seqs, group, width = tokens_ref.shape
    steps, lines, full = pre_ref.shape
    taps, inner = taps_ref.shape[0], w_ref.shape[1]
    rim, rows, tail = taps - 1, steps * lines, halo.shape[1]
    here, me = lax.axis_index("seq"), lax.axis_index("chan")
    beside = me + 1 - 2 * lax.rem(me, 2)
    barrier = pltpu.get_barrier_semaphore()
    told = chan_count // 2
    for by in (1, -1):
        there = here + by
        near = (there >= 0) & (there < seq_count)
        told = told + jnp.where(near, 1, 0)

        @pl.when(near)
        def _():
            pl.semaphore_signal(barrier, inc=1, device_id={"seq": there}, device_id_type=MESH)

    pl.semaphore_signal(barrier, inc=1, device_id={"chan": beside}, device_id_type=MESH)
    for k in range(1, chan_count // 2):
        to = lax.rem(me + 2 * k, chan_count)
        pl.semaphore_signal(barrier, inc=1, device_id={"chan": to}, device_id_type=MESH)
    pl.semaphore_wait(barrier, told)
    ends = pltpu.make_async_remote_copy(
        src_ref=tokens_ref.at[:, pl.ds(group - tail, tail), :],
        dst_ref=halo,
        send_sem=halo_send,
        recv_sem=halo_recv,
        device_id={"seq": here + 1},
        device_id_type=MESH,
    )

    @pl.when(here + 1 < seq_count)
    def _():
        ends.start()

    def normed_of(rows_low):
        return (unit_of(rows_low.astype(f32)) * gain_ref[...]).astype(bf16)

    perm = perm_of(steps, lines, seqs)
    normed = dot(perm, normed_of(tokens_ref[...].reshape(rows, width))).astype(bf16)
    normed_ref[...] = normed
    conv_in = dot_nt(normed, w_ref[0]).astype(bf16).astype(f32)
    ext_ref[pl.ds(rim, steps), :, pl.ds(0, inner)] = conv_in.reshape(steps, lines, inner)
    gate_ref[:, :, pl.ds(0, inner)] = dot_nt(normed, w_ref[1]).reshape(steps, lines, inner)
    if full > inner:
        ext_ref[:, :, pl.ds(inner, full - inner)] = jnp.zeros((steps + rim, lines, full - inner), f32)
        gate_ref[:, :, pl.ds(inner, full - inner)] = jnp.zeros((steps, lines, full - inner), f32)

    @pl.when(here == 0)
    def _():
        halo[...] = jnp.zeros(halo.shape, bf16)

    @pl.when(here > 0)
    def _():
        ends.wait_recv()

    prior = dot_nt(normed_of(halo[...].reshape(seqs * tail, width)), w_ref[0]).astype(bf16)
    to = lax.broadcasted_iota(jnp.int32, (rim * lines, seqs * tail), 0)
    origin = lax.broadcasted_iota(jnp.int32, (rim * lines, seqs * tail), 1)
    pick = (to % lines < seqs) & (origin == (to % lines) * tail + tail - rim + to // lines)
    prior = dot(pick.astype(bf16), prior).reshape(rim, lines, inner)
    upper = lax.broadcasted_iota(jnp.int32, (lines, inner), 0) >= seqs
    for j in range(rim):
        own = turned(ext_ref[steps + j, :, pl.ds(0, inner)])
        ext_ref[j, :, pl.ds(0, inner)] = jnp.where(upper, own, prior[j])
    pre = jnp.broadcast_to(bias_ref[...], (steps, lines, full))
    for k in range(taps):
        pre = pre + taps_ref[k : k + 1, :] * ext_ref[pl.ds(k, steps)] * valid_ref[:, :, k : k + 1]
    pre_ref[...] = pre
    act_low = (pre * sigmoid(pre)).astype(bf16).reshape(rows, full)
    part[...] = dot_nt(act_low, xproj_ref[...]).astype(bf16)
    near = pltpu.make_async_remote_copy(
        src_ref=part,
        dst_ref=beside_in,
        send_sem=send_sem.at[0],
        recv_sem=recv_sem.at[0],
        device_id={"chan": beside},
        device_id_type=MESH,
    )
    near.start()
    near.wait_recv()
    pair[...] = (part[...].astype(f32) + beside_in[...].astype(f32)).astype(bf16)
    copies = []
    for k in range(1, chan_count // 2):
        copies.append(
            pltpu.make_async_remote_copy(
                src_ref=pair,
                dst_ref=far_in.at[k - 1],
                send_sem=send_sem.at[k],
                recv_sem=recv_sem.at[k],
                device_id={"chan": lax.rem(me + 2 * k, chan_count)},
                device_id_type=MESH,
            )
        )
        copies[-1].start()
    for copy in copies:
        copy.wait_recv()
    total = pair[...].astype(f32)
    for k in range(chan_count // 2 - 1):
        total = total + far_in[k].astype(f32)
    mapped_ref[...] = total.astype(bf16)
    near.wait_send()
    for copy in copies:
        copy.wait_send()

    @pl.when(here + 1 < seq_count)
    def _():
        ends.wait_send()


def front(tokens, gain, w_in, taps, bias, xproj, valid, full, number):
    seqs, group, width = tokens.shape
    steps, lines = valid.shape[:2]
    count, rows, maps = lax.axis_size("chan"), steps * lines, xproj.shape[0]
    tail = min(16, group)
    return pl.pallas_call(
        functools.partial(front_kernel, lax.axis_size("seq"), count),
        out_shape=[
            jax.ShapeDtypeStruct((rows, width), bf16),
            jax.ShapeDtypeStruct((steps + taps.shape[0] - 1, lines, full), f32),
            jax.ShapeDtypeStruct((steps, lines, full), f32),
            jax.ShapeDtypeStruct((steps, lines, full), f32),
            jax.ShapeDtypeStruct((rows, maps), bf16),
        ],
        in_specs=[pl.BlockSpec(memory_space=pltpu.VMEM)] * 7,
        out_specs=[pl.BlockSpec(memory_space=pltpu.VMEM)] * 5,
        scratch_shapes=[
            pltpu.VMEM((seqs, tail, width), bf16),
            pltpu.VMEM((rows, maps), bf16),
            pltpu.VMEM((rows, maps), bf16),
            pltpu.VMEM((rows, maps), bf16),
            pltpu.VMEM((count // 2 - 1, rows, maps), bf16),
            pltpu.SemaphoreType.DMA,
            pltpu.SemaphoreType.DMA,
            pltpu.SemaphoreType.DMA((count // 2,)),
            pltpu.SemaphoreType.DMA((count // 2,)),
        ],
        compiler_params=pltpu.CompilerParams(
            collective_id=number, has_side_effects=True, vmem_limit_bytes=48 * MIB
        ),
    )(tokens, gain, w_in, taps, bias, xproj, valid)


def totals_kernel(rank, taps, pre_ref, mapped_ref, dtw_ref, bias_ref, valid_ref, rate_ref,
                  dt_ref, step_ref, drive_ref, last_ref, sums_ref, wide):
    count, steps, rows, lanes = wide.shape

    @pl.when(pl.program_id(0) == 0)
    def _():
        spread(mapped_ref, rank, wide)

    dt_pre = (dot(mapped_ref[...], dtw_ref[...]) + bias_ref[...]).reshape(steps, rows, lanes)
    delta = softplus(dt_pre)
    pre = pre_ref[...]
    dt_ref[...] = dt_pre
    step_ref[...] = jnp.where(valid_ref[:, :, taps : taps + 1] > 0.5, delta, cut)
    drive_ref[...] = delta * pre * sigmoid(pre)
    rates = [rows_of(rate_ref, n, rows) for n in range(count)]
    zero = jnp.zeros((rows, lanes), f32)

    def one(p, held):
        states, sums = held
        step, drive = step_ref[p], drive_ref[p]
        states = tuple(
            jnp.exp2(step * rates[n]) * states[n] + drive * wide[n, p] for n in range(count)
        )
        return states, sums + step

    states, sums = lax.fori_loop(0, steps, one, ((zero,) * count, zero), unroll=2)
    for n in range(count):
        last_ref[n] = states[n]
    sums_ref[...] = sums


def states_kernel(rank, seqs, step_ref, drive_ref, mapped_ref, rate_ref, enter_ref, pre_ref, gate_ref, skip_ref, out_w_ref,
                  y_ref, gated_ref, state_ref, out_ref, wide_in, wide_read, total):
    count, steps, rows, lanes = wide_in.shape
    place = pl.program_id(0)

    @pl.when(place == 0)
    def _():
        spread(mapped_ref, rank, wide_in)
        spread(mapped_ref, rank + count, wide_read)
        total[...] = jnp.zeros_like(total)

    rates = [rows_of(rate_ref, n, rows) for n in range(count)]

    def one(p, states):
        step, drive = step_ref[p], drive_ref[p]
        states = tuple(
            jnp.exp2(step * rates[n]) * states[n] + drive * wide_in[n, p] for n in range(count)
        )
        terms = [states[n] * wide_read[n, p] for n in range(count)]
        while len(terms) > 1:
            terms = [a + b for a, b in zip(terms[::2], terms[1::2])]
        y_ref[p] = terms[0]
        for n in range(count):
            state_ref[p, n] = states[n]
        return states

    lax.fori_loop(0, steps, one, tuple(enter_ref[n] for n in range(count)), unroll=2)
    pre, gate = pre_ref[...], gate_ref[...]
    y_full = y_ref[...] + skip_ref[...] * (pre * sigmoid(pre))
    y_ref[...] = y_full
    gated = (y_full * (gate * sigmoid(gate))).astype(bf16).reshape(steps * rows, lanes)
    gated_ref[...] = gated
    total[...] += dot(gated, out_w_ref[...])

    @pl.when(place == pl.num_programs(0) - 1)
    def _():
        perm = perm_of(steps, rows, seqs)
        out_ref[...] = dot_tn(perm, total[...].astype(bf16)).astype(bf16)


def back_totals_kernel(rank, seqs, step_ref, mapped_ref, rate_ref, mixed_ref, normed_ref, out_w_ref, gate_ref, y_ref, gated_ref,
                       pre_ref, grad_y_ref, grad_z_ref, grad_out_ref, grad_gate_ref, skip_ref, last_ref,
                       wide, mixed):
    count, steps, rows, lanes = wide.shape

    @pl.when(pl.program_id(0) == 0)
    def _():
        spread(mapped_ref, rank + count, wide)
        mixed[...] = dot(perm_of(steps, rows, seqs), mixed_ref[...]).astype(bf16)

    grad_gated = dot_nt(mixed[...], out_w_ref[...]).reshape(steps, rows, lanes)
    gate, pre = gate_ref[...], pre_ref[...]
    sigma = sigmoid(gate)
    grad_y = grad_gated * (gate * sigma)
    grad_y_ref[...] = grad_y
    grad_z = (grad_gated * y_ref[...] * silu_slope(gate, sigma)).astype(bf16)
    grad_z = grad_z.reshape(steps * rows, lanes)
    grad_z_ref[...] = grad_z
    skip_ref[...] = jnp.sum(grad_y * (pre * sigmoid(pre)), axis=0)
    grad_out_ref[...] = dot_tn(gated_ref[...], mixed[...]).astype(bf16)
    grad_gate_ref[...] = dot_tn(grad_z, normed_ref[...]).astype(bf16)
    rates = [rows_of(rate_ref, n, rows) for n in range(count)]
    zero = jnp.zeros((rows, lanes), f32)

    def one(turn, held):
        p = steps - 1 - turn
        step, grad_y = step_ref[p], grad_y_ref[p]
        return tuple(
            jnp.exp2(step * rates[n]) * (held[n] + grad_y * wide[n, p]) for n in range(count)
        )

    held = lax.fori_loop(0, steps, one, (zero,) * count, unroll=2)
    for n in range(count):
        last_ref[n] = held[n]


def back_kernel(rank, step_ref, drive_ref, grad_y_ref, mapped_ref, rate_ref, first_ref, state_ref, enter_ref, dt_ref, pre_ref,
                dtw_ref, side_ref, log_ref, bias_ref, grad_dtw_ref, low_ref,
                wide_in, wide_read, sum_in, sum_read, to_input, to_decay, total):
    count, steps, rows, lanes = wide_in.shape
    place = pl.program_id(0)

    @pl.when(place == 0)
    def _():
        spread(mapped_ref, rank, wide_in)
        spread(mapped_ref, rank + count, wide_read)
        sum_in[...] = jnp.zeros_like(sum_in)
        sum_read[...] = jnp.zeros_like(sum_read)
        total[...] = jnp.zeros_like(total)

    rates = [rows_of(rate_ref, n, rows) for n in range(count)]
    for n in range(count):
        log_ref[n] = jnp.zeros((rows, lanes), f32)

    def step_back(p, carry, prior_of):
        step, drive, grad_y = step_ref[p], drive_ref[p], grad_y_ref[p]
        inputs = jnp.zeros((rows, lanes), f32)
        decays = jnp.zeros((rows, lanes), f32)
        new = []
        for n in range(count):
            grad = grad_y * wide_read[n, p] + carry[n]
            passed = jnp.exp2(step * rates[n]) * grad
            new.append(passed)
            grad_decay = passed * prior_of(n)
            decays = decays + grad_decay * rates[n]
            log_ref[n] += grad_decay * step
            inputs = inputs + grad * wide_in[n, p]
            sum_in[n, p] += grad * drive
            sum_read[n, p] += grad_y * state_ref[p, n]
        to_input[p] = inputs
        to_decay[p] = decays
        return tuple(new)

    def one(turn, carry):
        p = steps - 1 - turn
        return step_back(p, carry, lambda n: state_ref[p - 1, n])

    carry = lax.fori_loop(0, steps - 1, one, tuple(enter_ref[n] for n in range(count)))
    step_back(0, carry, lambda n: first_ref[n])
    dt_pre, pre = dt_ref[...], pre_ref[...]
    inputs = to_input[...]
    side_ref[...] = inputs * softplus(dt_pre)
    grad_delta = to_decay[...] * (1.0 / log2e) + inputs * (pre * sigmoid(pre))
    grad_dt = grad_delta * sigmoid(dt_pre)
    bias_ref[...] = jnp.sum(grad_dt, axis=0)
    grad_dt = grad_dt.astype(bf16).reshape(steps * rows, lanes)
    grad_dtw_ref[...] = dot_tn(mapped_ref[...], grad_dt)
    total[...] += dot_nt(grad_dt, dtw_ref[...])

    @pl.when(place == pl.num_programs(0) - 1)
    def _():
        column = lax.broadcasted_iota(jnp.int32, (lanes, total.shape[1]), 1)
        sums = total[...]
        for which, source in enumerate((sum_in, sum_read)):
            for n in range(count):
                pick = (column == rank + which * count + n).astype(bf16)
                sums = sums + dot(source[n].reshape(steps * rows, lanes).astype(bf16), pick)
        low_ref[...] = sums.astype(bf16)


def conv_back_kernel(taps, grad_mapped_ref, grad_y_ref, side_ref, pre_ref, ext_ref, skip_ref, xproj_ref, taps_ref, valid_ref,
                     grad_ref, rim_ref, grad_xproj_ref, sums_ref, ext_grad):
    steps, rows, lanes = pre_ref.shape
    rim = taps - 1
    pre = pre_ref[...]
    sigma = sigmoid(pre)
    grad_act = dot(grad_mapped_ref[...], xproj_ref[...]).reshape(steps, rows, lanes)
    grad_act = grad_act + grad_y_ref[...] * skip_ref[...] + side_ref[...]
    grad_pre = grad_act * silu_slope(pre, sigma)
    act_low = (pre * sigma).astype(bf16).reshape(steps * rows, lanes)
    grad_xproj_ref[...] = dot_tn(grad_mapped_ref[...], act_low)
    ext_grad[...] = jnp.zeros_like(ext_grad)
    for k in range(taps):
        masked = grad_pre * valid_ref[:, :, k : k + 1]
        sums_ref[k] = jnp.sum(masked * ext_ref[pl.ds(k, steps)], axis=0)
        ext_grad[pl.ds(k, steps)] += masked * taps_ref[k : k + 1, :]
    sums_ref[taps] = jnp.sum(grad_pre, axis=0)
    upper = lax.broadcasted_iota(jnp.int32, (rows, lanes), 0) >= rows // 2
    for j in range(rim):
        edge = ext_grad[j]
        rim_ref[j] = edge
        ext_grad[steps + j] += jnp.where(upper, 0.0, turned(edge))
    grad_ref[...] = ext_grad[pl.ds(rim, steps)]


def ends_kernel(count, tokens_ref, grad_ref, rim_ref, grad_z_ref, normed_ref, w_ref, grad_conv_ref, part_ref, gain_ref,
                came, send_sem, recv_sem):
    steps, lines, full = grad_ref.shape
    seqs, group, width = tokens_ref.shape
    rows, inner, rim = steps * lines, w_ref.shape[1], rim_ref.shape[0]
    here = lax.axis_index("seq")
    barrier = pltpu.get_barrier_semaphore()
    told = 0
    for by in (1, -1):
        there = here + by
        near = (there >= 0) & (there < count)
        told = told + jnp.where(near, 1, 0)

        @pl.when(near)
        def _():
            pl.semaphore_signal(barrier, inc=1, device_id={"seq": there}, device_id_type=MESH)

    pl.semaphore_wait(barrier, told)
    edge = pltpu.make_async_remote_copy(
        src_ref=rim_ref,
        dst_ref=came,
        send_sem=send_sem,
        recv_sem=recv_sem,
        device_id={"seq": here - 1},
        device_id_type=MESH,
    )

    @pl.when(here > 0)
    def _():
        edge.start()

    unit = unit_of(tokens_ref[...].reshape(rows, width).astype(f32))
    by_gate = dot(grad_z_ref[:, pl.ds(0, inner)], w_ref[1])

    @pl.when(here == count - 1)
    def _():
        came[...] = jnp.zeros(came.shape, f32)

    @pl.when(here < count - 1)
    def _():
        edge.wait_recv()

    upper = lax.broadcasted_iota(jnp.int32, (lines, full), 0) >= lines // 2
    last = [
        (grad_ref[steps - rim + j] + jnp.where(upper, turned(came[j]), 0.0))[None] for j in range(rim)
    ]
    grad = jnp.concatenate([grad_ref[pl.ds(0, steps - rim)]] + last, axis=0)
    grad = grad.reshape(rows, full).astype(bf16)
    grad_conv_ref[...] = dot_tn(grad, normed_ref[...]).astype(bf16)
    part = (dot(grad[:, :inner], w_ref[0]) + by_gate).astype(bf16)
    part = dot_tn(perm_of(steps, lines, seqs), part)
    part_ref[...] = part.astype(bf16)
    gain_ref[...] = jnp.sum(part * unit, axis=0, keepdims=True)

    @pl.when(here > 0)
    def _():
        edge.wait_send()


def ends(tokens, grad, rim, grad_z, normed, w_in, number):
    steps, lines, full = grad.shape
    rows, width = normed.shape
    return pl.pallas_call(
        functools.partial(ends_kernel, lax.axis_size("seq")),
        out_shape=[
            jax.ShapeDtypeStruct((full, width), bf16),
            jax.ShapeDtypeStruct((rows, width), bf16),
            jax.ShapeDtypeStruct((1, width), f32),
        ],
        in_specs=[pl.BlockSpec(memory_space=pltpu.VMEM)] * 6,
        out_specs=[pl.BlockSpec(memory_space=pltpu.VMEM)] * 3,
        scratch_shapes=[
            pltpu.VMEM(rim.shape, f32),
            pltpu.SemaphoreType.DMA,
            pltpu.SemaphoreType.DMA,
        ],
        compiler_params=pltpu.CompilerParams(
            collective_id=number, has_side_effects=True, vmem_limit_bytes=48 * MIB
        ),
    )(tokens, grad, rim, grad_z, normed, w_in)


def block_of(shape, kind):
    if kind == "tile":
        return pl.BlockSpec(shape[:-1] + (LANES,), lambda i: (0,) * (len(shape) - 1) + (i,))
    if kind == "rows":
        return pl.BlockSpec((LANES,) + shape[1:], lambda i: (i,) + (0,) * (len(shape) - 1))
    return pl.BlockSpec(shape, lambda i: (0,) * len(shape))


def by_tiles(kernel, full, ins, outs, scratch):
    return pl.pallas_call(
        kernel,
        grid=(full // LANES,),
        in_specs=[block_of(a.shape, kind) for a, kind in ins],
        out_specs=[block_of(shape, kind) for shape, _, kind in outs],
        out_shape=[jax.ShapeDtypeStruct(shape, dtype) for shape, dtype, _ in outs],
        scratch_shapes=[pltpu.VMEM(shape, dtype) for shape, dtype in scratch],
        compiler_params=pltpu.CompilerParams(vmem_limit_bytes=58 * MIB),
        cost_estimate=pl.CostEstimate(flops=1000, bytes_accessed=1000, transcendentals=0),
    )(*[a for a, _ in ins])


def packed_size(arrays, rows):
    total = -(-sum(a.size for a in arrays) // LANES)
    return -(-total // rows) * rows


def packed_rows(arrays, rows):
    total = packed_size(arrays, rows)
    joined = jnp.concatenate([a.reshape(-1) for a in arrays])
    return jnp.pad(joined, (0, total * LANES - joined.size)).reshape(total, LANES)


def unpacked_rows(packed, shapes):
    packed = packed.reshape(-1)
    arrays, at = [], 0
    for shape in shapes:
        size = math.prod(shape)
        arrays.append(packed[at : at + size].reshape(shape))
        at += size
    return arrays


def norm_back(grad_normed, unit_rows, inverse, weight_gain):
    scaled = grad_normed * weight_gain
    return inverse * (scaled - unit_rows * jnp.mean(scaled * unit_rows, axis=-1, keepdims=True))


def local(
    tokens,
    teacher,
    true_lengths,
    doc_lengths,
    routes,
    norm1_gain,
    in_weight,
    conv_weight,
    conv_bias,
    xproj_weight,
    dt_weight,
    dt_bias,
    a_log,
    skip_weight,
    out_weight,
    norm2_gain,
    router_weight,
    expert_in,
    expert_out,
):
    seqs, group, width = tokens.shape
    inner = in_weight.shape[2]
    rank = dt_weight.shape[0]
    states = a_log.shape[1]
    experts = router_weight.shape[1]
    n_seq = lax.axis_size("seq")
    n_chan = lax.axis_size("chan")
    shards = n_seq // experts
    most = group // 4
    taps = conv_weight.shape[0]
    rim = taps - 1
    lines = 8
    chunks = lines // seqs
    steps = group // chunks
    owned = seqs * group // n_chan
    part = min(group, owned)
    most = min(most, part)
    parts = owned // part
    place = lax.axis_index("chan")
    first_pos = lax.axis_index("seq") * group

    full = -(-inner // LANES) * LANES
    rows = steps * lines
    maps = rank + 2 * states

    def padded(x):
        return jnp.pad(x, ((0, 0),) * (x.ndim - 1) + ((0, full - inner),))

    at = (
        first_pos
        + jnp.arange(steps, dtype=jnp.int32)[:, None]
        + (jnp.arange(lines, dtype=jnp.int32) // seqs * steps)[None, :]
    )
    stops = []
    for k in range(doc_lengths.shape[1] - 1):
        stops.append(doc_lengths[:, k] + (stops[-1] if stops else 0))
    stops = [jnp.tile(stop, chunks)[None, :] for stop in stops]

    def doc_at(pos):
        return sum((pos >= stop).astype(jnp.int32) for stop in stops)

    doc_ids = doc_at(at)
    keep = (doc_ids == doc_at(at - 1)) & (at > 0)
    valid = [doc_at(at - rim + k) == doc_ids for k in range(taps)] + [keep]
    valid = jnp.stack(valid + [keep] * (lines - taps - 1), axis=-1).astype(f32)

    w_in = in_weight.transpose(1, 2, 0)
    router_rows = router_weight.T
    gain_one = norm1_gain.astype(f32)
    taps_full = padded(conv_weight.astype(f32))
    xproj_rows = padded(xproj_weight.T)
    dt_rows = jnp.pad(padded(dt_weight), ((0, maps - rank), (0, 0)))
    skip_row = padded(skip_weight[None])
    out_rows = jnp.pad(out_weight, ((0, full - inner), (0, 0)))
    rate = -jnp.exp(a_log.T)
    rate_two = padded(rate * log2e)
    normed_one, extended, pre_act, gate_z, mapped = front(
        tokens,
        gain_one[None],
        w_in,
        taps_full,
        padded(conv_bias.astype(f32)[None]),
        xproj_rows,
        valid,
        full,
        1,
    )
    act_shape, state_shape, wide_shape = (steps, lines, full), (states, lines, full), (states, steps, lines, LANES)
    dt_pre, step_size, drive, last, sums = by_tiles(
        functools.partial(totals_kernel, rank, taps),
        full,
        [
            (pre_act, "tile"),
            (mapped, "whole"),
            (dt_rows, "tile"),
            (padded(dt_bias[None]), "tile"),
            (valid, "whole"),
            (rate_two, "tile"),
        ],
        [
            (act_shape, f32, "tile"),
            (act_shape, f32, "tile"),
            (act_shape, f32, "tile"),
            (state_shape, f32, "tile"),
            ((lines, full), f32, "tile"),
        ],
        [(wide_shape, f32)],
    )
    (enter,) = carried(last, sums, rate_two, "seq", False, 2)
    y_full, gated, state, out_part = by_tiles(
        functools.partial(states_kernel, rank, seqs),
        full,
        [
            (step_size, "tile"),
            (drive, "tile"),
            (mapped, "whole"),
            (rate_two, "tile"),
            (enter, "tile"),
            (pre_act, "tile"),
            (gate_z, "tile"),
            (skip_row, "tile"),
            (out_rows, "rows"),
        ],
        [
            (act_shape, f32, "tile"),
            ((rows, full), bf16, "tile"),
            ((steps, states, lines, full), f32, "tile"),
            ((rows, width), bf16, "whole"),
        ],
        [(wide_shape, f32)] * 2 + [((rows, width), f32)],
    )
    (mixed,) = share_of(3, [(out_part.reshape(n_chan, owned, width), "chan", 2, f32)])

    def own(x):
        return lax.dynamic_slice_in_dim(x.reshape((rows,) + x.shape[2:]), place * owned, owned, 0)

    tokens_own = own(tokens).astype(f32)
    inverse_one = lax.rsqrt(jnp.mean(tokens_own * tokens_own, axis=-1, keepdims=True) + epsilon)
    unit_one = tokens_own * inverse_one
    hidden_one = tokens_own + mixed
    inverse_two = lax.rsqrt(jnp.mean(hidden_one * hidden_one, axis=-1, keepdims=True) + epsilon)
    unit_two = hidden_one * inverse_two
    gain_two = norm2_gain.astype(f32)
    normed_two = (unit_two * gain_two).astype(bf16)
    probs = jax.nn.softmax(dot_nt(normed_two, router_rows), axis=-1)
    routes_own = own(routes)
    chosen = routes_own[..., None] == jnp.arange(experts, dtype=jnp.int32)
    chosen_rows = chosen.astype(f32)
    gate_value = jnp.sum(probs * chosen_rows, axis=-1, keepdims=True)
    row = jnp.arange(owned, dtype=jnp.int32)
    earlier = (row[None, :] < row[:, None]) & (row[None, :] // part == row[:, None] // part)
    rank_in = dot(earlier.astype(bf16), chosen.astype(bf16))
    slots = parts * most
    wanted = rank_in + (row // part * most).astype(f32)[:, None]
    hit = (wanted[..., None] == jnp.arange(slots, dtype=f32)) & chosen[..., None]
    hit = hit.astype(bf16)
    hit_send = hit.reshape(owned, experts * slots)
    hit_back = jnp.repeat(hit, shards, axis=1).reshape(owned, n_seq * slots)

    def to_slabs(x):
        packed = dot_tn(hit_send, x).astype(bf16).reshape(experts, slots, width)
        return jnp.repeat(packed, shards, axis=0), "scatter", "seq"

    def to_rows(x):
        return x.reshape(n_seq, slots, width), "scatter", "seq"

    def by_units(x):
        return x.reshape(n_seq * slots, n_chan, units).transpose(1, 0, 2), "scatter", "chan"

    def flat(x):
        return x.reshape(-1, x.shape[-1])

    first_slab, second_slab = expert_in[0], expert_out[0]
    units = first_slab.shape[1] // n_chan
    arrived = flat(exchange(4, to_slabs(normed_two))[0])
    pre_hidden = dot(arrived, first_slab)
    cdf = 0.5 * (1.0 + lax.erf(pre_hidden * 0.7071067811865476))
    hidden_low = (pre_hidden * cdf).astype(bf16)
    density = jnp.exp(-0.5 * pre_hidden * pre_hidden) * 0.3989422804014327
    slope = cdf + pre_hidden * density
    result = dot(hidden_low, second_slab).astype(bf16)
    result_rows, rows_all = exchange(5, to_rows(result), (arrived, 2, "chan"))
    expert_total = dot(hit_back, flat(result_rows))
    layer = hidden_one + gate_value * expert_total
    layer_low = layer.astype(bf16)

    flat_row = place * owned + row
    seq_of = flat_row // group
    lengths_own = sum(
        jnp.where(seq_of == s, true_lengths[s], 0) for s in range(seqs)
    )
    total_true = jnp.sum(true_lengths).astype(f32)
    loss_mask = (first_pos + flat_row % group < lengths_own).astype(f32)[:, None]
    error = layer - own(teacher).astype(f32)
    loss_part = jnp.sum(loss_mask * error * error) / total_true
    grad_layer = 2.0 / total_true * loss_mask * error
    grad_gate = jnp.sum(grad_layer * expert_total, axis=-1, keepdims=True)
    grad_result = (gate_value * grad_layer).astype(bf16)
    grad_rows, hidden_all = exchange(6, to_slabs(grad_result), by_units(hidden_low))
    grad_rows = flat(grad_rows)
    grad_pre = (dot_nt(grad_rows, second_slab) * slope).astype(bf16)
    grad_slab_rows = dot_nt(grad_pre, first_slab).astype(bf16)
    grad_expert, grad_rows_all = exchange(7, to_rows(grad_slab_rows), (grad_rows, 2, "chan"))
    grad_expert = dot(hit_back, flat(grad_expert))

    grad_logit = grad_gate * gate_value * (chosen_rows - probs)
    grad_router = dot_tn(grad_logit.astype(bf16), normed_two)
    grad_normed_two = grad_expert + dot(grad_logit.astype(bf16), router_rows)
    grad_gain_two = jnp.sum(grad_normed_two * unit_two, axis=0)
    grad_hidden_one = grad_layer + norm_back(grad_normed_two, unit_two, inverse_two, gain_two)

    shared = packed_rows([grad_gain_two, grad_router, loss_part], 8)
    grad_mixed, shared = exchange(
        8, (grad_hidden_one.astype(bf16), 2, "chan"), (shared, "gather", "chan")
    )
    shared = jnp.sum(shared, axis=0)
    grad_y, grad_z, grad_out_w, grad_in_gate, skip_sums, back_last = by_tiles(
        functools.partial(back_totals_kernel, rank, seqs),
        full,
        [
            (step_size, "tile"),
            (mapped, "whole"),
            (rate_two, "tile"),
            (grad_mixed.reshape(rows, width), "whole"),
            (normed_one, "whole"),
            (out_rows, "rows"),
            (gate_z, "tile"),
            (y_full, "tile"),
            (gated, "tile"),
            (pre_act, "tile"),
        ],
        [
            (act_shape, f32, "tile"),
            ((rows, full), bf16, "tile"),
            ((full, width), bf16, "rows"),
            ((full, width), bf16, "rows"),
            ((lines, full), f32, "tile"),
            (state_shape, f32, "tile"),
        ],
        [(wide_shape, f32), ((rows, width), bf16)],
    )
    summed_out, summed_gate = lax.psum((grad_out_w, grad_in_gate), "seq")
    (back_enter,) = carried(back_last, sums, rate_two, "seq", True, 9)
    side, log_sums, bias_sums, grad_dt_w, low_part = by_tiles(
        functools.partial(back_kernel, rank),
        full,
        [
            (step_size, "tile"),
            (drive, "tile"),
            (grad_y, "tile"),
            (mapped, "whole"),
            (rate_two, "tile"),
            (enter, "tile"),
            (state, "tile"),
            (back_enter, "tile"),
            (dt_pre, "tile"),
            (pre_act, "tile"),
            (dt_rows, "tile"),
        ],
        [
            (act_shape, f32, "tile"),
            (state_shape, f32, "tile"),
            ((lines, full), f32, "tile"),
            ((maps, full), f32, "tile"),
            ((rows, maps), bf16, "whole"),
        ],
        [(wide_shape, f32)] * 4 + [((steps, lines, LANES), f32)] * 2 + [((rows, maps), f32)],
    )
    grad_mapped = summed_over(low_part, "chan", 10).astype(bf16)
    grad_conv_in, rims, grad_xproj, conv_sums = by_tiles(
        functools.partial(conv_back_kernel, taps),
        full,
        [
            (grad_mapped, "whole"),
            (grad_y, "tile"),
            (side, "tile"),
            (pre_act, "tile"),
            (extended, "tile"),
            (skip_row, "tile"),
            (xproj_rows, "tile"),
            (taps_full, "tile"),
            (valid, "whole"),
        ],
        [
            (act_shape, f32, "tile"),
            ((rim, lines, full), f32, "tile"),
            ((maps, full), f32, "tile"),
            ((taps + 1, lines, full), f32, "tile"),
        ],
        [((steps + rim, lines, LANES), f32)],
    )
    grad_in_conv, normed_part, grad_gain_one = ends(
        tokens, grad_conv_in, rims, grad_z, normed_one, w_in, 14
    )
    normed_part = normed_part.reshape(n_chan, owned, width)
    sums_all = jnp.concatenate([conv_sums, bias_sums[None], skip_sums[None], log_sums], axis=0)
    sums_all = jnp.sum(sums_all, axis=1)

    def cut_rows(x, unit):
        each = -(-x.shape[0] // (unit * n_seq)) * unit
        return jnp.pad(x, ((0, each * n_seq - x.shape[0]), (0, 0))).reshape(n_seq, each, -1)

    large = cut_rows(grad_in_conv, 16)
    middle = cut_rows(jnp.concatenate([grad_xproj, grad_dt_w[:rank]], axis=0).astype(bf16), 16)
    across = n_chan // 2
    grad_normed_one, large, middle, sums_all, shared, grad_gain_one, grad_pre_all = share_of(
        11,
        [
            (normed_part, "chan", 2, f32),
            (large, "seq", across, bf16),
            (middle, "seq", across, bf16),
        ],
        (cut_rows(sums_all, 8), "scatter", "seq"),
        (cut_rows(shared, 8), "scatter", "seq"),
        (grad_gain_one, "gather", "chan"),
        by_units(grad_pre),
    )
    sums_all = jnp.sum(sums_all, axis=0)
    shared = jnp.sum(shared, axis=0)
    grad_gain_one = jnp.sum(grad_gain_one, axis=0)
    grad_own = grad_hidden_one + norm_back(grad_normed_one, unit_one, inverse_one, gain_one)
    large, grad_tokens, layer_out, middle, sums_all, shared, grad_gain_one = exchange(
        12,
        (large, across, "seq"),
        (grad_own.astype(bf16), 2, "chan"),
        (layer_low, 2, "chan"),
        (middle, across, "seq"),
        (sums_all, "gather", "seq"),
        (shared, "gather", "seq"),
        (grad_gain_one, "gather", "seq"),
    )
    grad_first = dot_tn(flat(rows_all), flat(grad_pre_all))
    grad_second = dot_tn(flat(hidden_all), flat(grad_rows_all))
    grad_gain_one = jnp.sum(grad_gain_one, axis=(0, 1))
    summed_in = jnp.stack([flat(large)[:inner], summed_gate[:inner]]).astype(f32)
    middle = flat(middle)[:, :inner].astype(f32)
    small = flat(sums_all)[:, :inner]
    tiny = unpacked_rows(flat(shared), [(width,), grad_router.shape, ()])
    return (
        layer_out.reshape(seqs, group, width),
        tiny[2],
        grad_tokens.reshape(seqs, group, width).astype(f32),
        grad_gain_one,
        summed_in.transpose(2, 0, 1),
        small[:taps],
        small[taps],
        middle[:maps].T,
        middle[maps : maps + rank],
        small[taps + 1],
        (small[taps + 3 : taps + 3 + states] * rate).T,
        small[taps + 2],
        summed_out[:inner].astype(f32),
        tiny[0],
        tiny[1].T,
        grad_first[None],
        grad_second[None],
    )


def solution(mesh):
    placed = (
        P(None, "seq", None),
        P(None, "seq", None),
        P(),
        P(),
        P(None, "seq"),
        P(),
        P(None, None, "chan"),
        P(None, "chan"),
        P("chan"),
        P("chan", None),
        P(None, "chan"),
        P("chan"),
        P("chan", None),
        P("chan"),
        P("chan", None),
        P(),
        P(),
        P("seq", None, None),
        P("seq", None, None),
    )
    return jax.shard_map(
        local,
        mesh=mesh,
        in_specs=placed,
        out_specs=(
            P(None, "seq", None),
            P(),
            P(None, "seq", None),
            P(),
            P(None, None, "chan"),
            P(None, "chan"),
            P("chan"),
            P("chan", None),
            P(None, "chan"),
            P("chan"),
            P("chan", None),
            P("chan"),
            P("chan", None),
            P(),
            P(),
            P("seq", None, "chan"),
            P("seq", "chan", None),
        ),
        check_vma=False,
    )
```

```python
import functools

import jax
import jax.numpy as jnp
from jax import lax
from jax.experimental import pallas as pl
from jax.experimental.pallas import tpu as pltpu
from jax.sharding import PartitionSpec as P

epsilon = 1e-05
log2e = 1.4426950408889634
cut = 1e30
MESH = pl.DeviceIdType.MESH
f32 = jnp.float32
bf16 = jnp.bfloat16
LANES = 128
MIB = 1024 * 1024


def greet(axes):
    barrier = pltpu.get_barrier_semaphore()
    told = 0
    for axis, count in axes:
        me = lax.axis_index(axis)
        for k in range(1, count):
            pl.semaphore_signal(
                barrier, inc=1, device_id={axis: lax.rem(me + k, count)}, device_id_type=MESH
            )
        told += count - 1
    return told


def sems_of(item):
    count = item[2]
    return [pltpu.SemaphoreType.DMA] + [pltpu.SemaphoreType.DMA((count - 1,))] * 2


def flipped(i, mask):
    bit = 1
    while bit <= mask:
        if mask & bit:
            i = i + bit - 2 * bit * lax.rem(i // bit, 2)
        bit *= 2
    return i


def order_of(groups):
    masks, low, high = [], 1, groups - 1
    while low <= high:
        masks += [high] if low == high else [high, low]
        low, high = low + 1, high - 1
    return masks


class Riders:
    def __init__(self, items, xs, outs, sems):
        self.own, self.copies, self.chains = [], [], {}
        for i, item in enumerate(items):
            self.add(item, xs[i], outs[i], *sems[3 * i : 3 * i + 3])
        self.at = {axis: 0 for axis in self.chains}

    def start(self):
        for copy in self.copies + self.own:
            copy.start()
        for chain in self.chains.values():
            for first, _ in chain[:2]:
                first.start()
        return self

    def add(self, item, x_ref, o_ref, own_sem, send_sem, recv_sem):
        mode, axis, count = item
        me = lax.axis_index(axis)

        def remote(source, row, slot, to):
            return pltpu.make_async_remote_copy(
                src_ref=source,
                dst_ref=o_ref.at[row],
                send_sem=send_sem.at[slot],
                recv_sem=recv_sem.at[slot],
                device_id={axis: to},
                device_id_type=MESH,
            )

        source = x_ref.at[me] if mode == "scatter" else x_ref
        self.own.append(pltpu.make_async_copy(source, o_ref.at[me], own_sem))
        if mode in ("gather", "scatter"):
            for mask in range(count - 1, 0, -1):
                to = flipped(me, mask)
                source = x_ref.at[to] if mode == "scatter" else x_ref
                self.copies.append(remote(source, me, mask - 1, to))
            return
        groups = count // mode
        side, place = lax.rem(me, mode), me // mode
        mates = [place * mode + lax.rem(side + j, mode) for j in range(1, mode)]
        slot = groups - 1
        for mate in mates:
            self.copies.append(remote(x_ref, me, slot, mate))
            slot += 1
        chain = self.chains.setdefault(axis, [])
        for mask in order_of(groups):
            row = flipped(place, mask) * mode + side
            first = remote(x_ref, me, mask - 1, row)
            passed = []
            for mate in mates:
                passed.append(remote(o_ref.at[row], row, slot, mate))
                slot += 1
            chain.append((first, passed))

    def left(self):
        return max([len(chain) - self.at[axis] for axis, chain in self.chains.items()] + [0])

    def step(self):
        for axis, chain in self.chains.items():
            i = self.at[axis]
            if i == len(chain):
                continue
            self.at[axis] = i + 1
            first, passed = chain[i]
            first.wait_recv()
            for copy in passed:
                copy.start()
            if i + 2 < len(chain):
                chain[i + 2][0].start()

    def finish(self):
        while self.left():
            self.step()
        for copy in self.own + self.copies:
            copy.wait()
        for chain in self.chains.values():
            for first, passed in chain:
                first.wait_send()
                for copy in passed:
                    copy.wait()


def items_of(exchanges):
    return [(mode, axis, lax.axis_size(axis)) for _, mode, axis in exchanges]


def axes_of(items):
    return sorted({(axis, count) for _, axis, count in items})


def landed(x, item):
    shape = x.shape if item[0] == "scatter" else (item[2],) + x.shape
    return jax.ShapeDtypeStruct(shape, x.dtype)


def exchange_kernel(items, *refs):
    number = len(items)
    sems = refs[2 * number :]
    pl.semaphore_wait(pltpu.get_barrier_semaphore(), greet(axes_of(items)))
    Riders(items, refs[:number], refs[number : 2 * number], sems).start().finish()


def exchange(number, *exchanges):
    items = items_of(exchanges)
    return pl.pallas_call(
        functools.partial(exchange_kernel, items),
        out_shape=[landed(x, item) for (x, _, _), item in zip(exchanges, items)],
        in_specs=[pl.BlockSpec(memory_space=pl.ANY)] * len(items),
        out_specs=[pl.BlockSpec(memory_space=pl.ANY)] * len(items),
        scratch_shapes=[sem for item in items for sem in sems_of(item)],
        compiler_params=pltpu.CompilerParams(
            collective_id=number, has_side_effects=True, vmem_limit_bytes=16 * MIB
        ),
    )(*[x for x, _, _ in exchanges])


def greet_near(axis, count):
    barrier = pltpu.get_barrier_semaphore()
    me = lax.axis_index(axis)
    beside = me + 1 - 2 * lax.rem(me, 2)
    pl.semaphore_signal(barrier, inc=1, device_id={axis: beside}, device_id_type=MESH)
    for k in range(1, count // 2):
        pl.semaphore_signal(
            barrier, inc=1, device_id={axis: lax.rem(me + 2 * k, count)}, device_id_type=MESH
        )
    pl.semaphore_wait(barrier, count // 2)


def sum_kernel(axis, count, x_ref, o_ref, beside_in, pair, far_in, send_sem, recv_sem):
    me = lax.axis_index(axis)
    beside = me + 1 - 2 * lax.rem(me, 2)
    greet_near(axis, count)
    near = pltpu.make_async_remote_copy(
        src_ref=x_ref,
        dst_ref=beside_in,
        send_sem=send_sem.at[0],
        recv_sem=recv_sem.at[0],
        device_id={axis: beside},
        device_id_type=MESH,
    )
    near.start()
    near.wait_recv()
    pair[...] = (x_ref[...].astype(f32) + beside_in[...].astype(f32)).astype(bf16)
    copies = []
    for k in range(1, count // 2):
        copies.append(
            pltpu.make_async_remote_copy(
                src_ref=pair,
                dst_ref=far_in.at[k - 1],
                send_sem=send_sem.at[k],
                recv_sem=recv_sem.at[k],
                device_id={axis: lax.rem(me + 2 * k, count)},
                device_id_type=MESH,
            )
        )
        copies[-1].start()
    for copy in copies:
        copy.wait_recv()
    total = pair[...].astype(f32)
    for k in range(count // 2 - 1):
        total = total + far_in[k].astype(f32)
    o_ref[...] = total
    near.wait_send()
    for copy in copies:
        copy.wait_send()


def summed_over(x, axis, number):
    count = lax.axis_size(axis)
    return pl.pallas_call(
        functools.partial(sum_kernel, axis, count),
        out_shape=jax.ShapeDtypeStruct(x.shape, f32),
        in_specs=[pl.BlockSpec(memory_space=pltpu.VMEM)],
        out_specs=pl.BlockSpec(memory_space=pltpu.VMEM),
        scratch_shapes=[
            pltpu.VMEM(x.shape, bf16),
            pltpu.VMEM(x.shape, bf16),
            pltpu.VMEM((count // 2 - 1,) + x.shape, bf16),
            pltpu.SemaphoreType.DMA((count // 2,)),
            pltpu.SemaphoreType.DMA((count // 2,)),
        ],
        compiler_params=pltpu.CompilerParams(
            collective_id=number, has_side_effects=True, vmem_limit_bytes=16 * MIB
        ),
    )(x)


class Share:
    def __init__(self, axis, count, size, x_ref, near_in, pairs, far_in, near_send, near_recv, far_send, far_recv):
        self.groups, self.size, self.x = count // size, size, x_ref
        self.near_in, self.pairs, self.far_in = near_in, pairs, far_in
        me = lax.axis_index(axis)
        side, place = lax.rem(me, size), me // size
        self.rows, self.near, self.far = [], [], []
        for k in range(self.groups):
            group = flipped(place, (order_of(self.groups) + [0])[k])
            self.rows.append(group * size + side)
            self.near.append(
                [
                    pltpu.make_async_remote_copy(
                        src_ref=x_ref.at[group * size + lax.rem(side + j, size)],
                        dst_ref=near_in.at[k, j - 1],
                        send_sem=near_send.at[k, j - 1],
                        recv_sem=near_recv.at[k, j - 1],
                        device_id={axis: place * size + lax.rem(side + j, size)},
                        device_id_type=MESH,
                    )
                    for j in range(1, size)
                ]
            )
            if k < self.groups - 1:
                self.far.append(
                    pltpu.make_async_remote_copy(
                        src_ref=pairs.at[k],
                        dst_ref=far_in.at[k],
                        send_sem=far_send.at[k],
                        recv_sem=far_recv.at[k],
                        device_id={axis: self.rows[k]},
                        device_id_type=MESH,
                    )
                )

    def begin(self, k):
        for copy in self.near[k]:
            copy.start()

    def near_sum(self, k, wait=True):
        total = self.x[self.rows[k]].astype(f32)
        for j, copy in enumerate(self.near[k]):
            if wait:
                copy.wait_recv()
            total = total + self.near_in[k, j].astype(f32)
        return total

    def pass_on(self, k):
        if k < self.groups - 1:
            self.pairs[k] = self.near_sum(k).astype(bf16)
            self.far[k].start()
        else:
            for copy in self.near[k]:
                copy.wait_recv()

    def total(self):
        total = self.near_sum(self.groups - 1, False)
        for k, copy in enumerate(self.far):
            copy.wait_recv()
            total = total + self.far_in[k].astype(f32)
        return total

    def close(self):
        for copy in [copy for copies in self.near for copy in copies] + self.far:
            copy.wait_send()


def share_kernel(shares, items, *refs):
    many, number = len(shares), len(items)
    at = 0

    def take(k):
        nonlocal at
        at += k
        return refs[at - k : at]

    xs, riders, outs, rider_outs = take(many), take(number), take(many), take(number)
    tasks = [Share(axis, count, size, x, *take(7)) for (axis, count, size), x in zip(shares, xs)]
    axes = set(axes_of(items)) | {(axis, count) for axis, count, _ in shares}
    pl.semaphore_wait(pltpu.get_barrier_semaphore(), greet(sorted(axes)))
    turns = {}
    for (axis, _, _), task in zip(shares, tasks):
        turns.setdefault(axis, []).extend((task, k) for k in range(task.groups))
    for turn in turns.values():
        for task, k in turn[:2]:
            task.begin(k)
    under_way = Riders(items, riders, rider_outs, take(3 * number)).start()
    for i in range(max(len(turn) for turn in turns.values())):
        for turn in turns.values():
            if i < len(turn):
                task, k = turn[i]
                task.pass_on(k)
                if i + 2 < len(turn):
                    task, k = turn[i + 2]
                    task.begin(k)
        under_way.step()
    for task, out in zip(tasks, outs):
        out[...] = task.total().astype(out.dtype)
    for task in tasks:
        task.close()
    under_way.finish()


def share_of(number, shares, *exchanges):
    items = items_of(exchanges)
    anywhere = [pl.BlockSpec(memory_space=pl.ANY)] * len(items)
    held = [pl.BlockSpec(memory_space=pltpu.VMEM)] * len(shares)
    scratch = []
    for x, axis, size, _ in shares:
        scratch += share_scratch(x, axis, size)
    return pl.pallas_call(
        functools.partial(
            share_kernel, [(axis, lax.axis_size(axis), size) for _, axis, size, _ in shares], items
        ),
        out_shape=[jax.ShapeDtypeStruct(x.shape[1:], kind) for x, _, _, kind in shares]
        + [landed(x, item) for (x, _, _), item in zip(exchanges, items)],
        in_specs=held + anywhere,
        out_specs=held + anywhere,
        scratch_shapes=scratch + [sem for item in items for sem in sems_of(item)],
        compiler_params=pltpu.CompilerParams(
            collective_id=number, has_side_effects=True, vmem_limit_bytes=32 * MIB
        ),
    )(*[share[0] for share in shares], *[x for x, _, _ in exchanges])


def turned(value):
    return pltpu.roll(value, value.shape[0] // 2, 0)


def carry_kernel(axis, count, back, items, *refs):
    number = len(items)
    local_ref, sums_ref, rate_ref = refs[:3]
    xs, o_ref, outs = refs[3 : 3 + number], refs[3 + number], refs[4 + number : 4 + 2 * number]
    send, got, send_sum, got_sum, total, enter = refs[4 + 2 * number : 10 + 2 * number]
    send_sem, recv_sem, send_sum_sem, recv_sum_sem = refs[10 + 2 * number : 14 + 2 * number]
    sems = refs[14 + 2 * number :]
    me = lax.axis_index(axis)
    states, rows, width = local_ref.shape
    half = rows // 2
    spans = []
    span = 1
    while span < count:
        spans.append(span)
        span *= 2
    sign = -1 if back else 1
    barrier = pltpu.get_barrier_semaphore()
    greeted = greet(axes_of(items))
    for span in spans:
        for by in (span, -span):
            there = me + by
            greeted = greeted + jnp.where((there >= 0) & (there < count), 1, 0)

            @pl.when((there >= 0) & (there < count))
            def _():
                pl.semaphore_signal(barrier, inc=1, device_id={axis: there}, device_id_type=MESH)

    upper = lax.broadcasted_iota(jnp.int32, (rows, width), 0) >= half
    first = upper if back else jnp.logical_not(upper)
    sums = sums_ref[...]
    sums_turned = turned(sums)
    sums_both = sums + sums_turned
    sums_first = jnp.where(first, sums, sums_turned)
    sums_last = jnp.where(first, sums_turned, sums)

    def packed_rate(j):
        return jnp.where(upper, rate_ref[pl.ds(2 * j + 1, 1), :], rate_ref[pl.ds(2 * j, 1), :])

    def both(j):
        even, odd = local_ref[2 * j], local_ref[2 * j + 1]
        low = jnp.where(upper, turned(odd), even)
        high = jnp.where(upper, odd, turned(even))
        return (high, low) if back else (low, high)

    for j in range(states // 2):
        opening, closing = both(j)
        total[j] = jnp.exp2(packed_rate(j) * sums_last) * opening + closing
        enter[j] = jnp.zeros((rows, width), f32)

    pl.semaphore_wait(barrier, greeted)
    under_way = Riders(items, xs, outs, sems).start()
    sums_total = sums_both
    sums_enter = jnp.zeros((rows, width), f32)
    for turn, span in enumerate(spans):
        to = me + sign * span
        origin = me - sign * span
        sends = (to >= 0) & (to < count)
        takes = (origin >= 0) & (origin < count)
        for j in range(0, states // 2, 2):
            send[turn, pl.ds(j * rows, 2 * rows), :] = jnp.concatenate([total[j], total[j + 1]], axis=0).astype(bf16)
        send_sum[turn] = sums_total
        copies = [
            pltpu.make_async_remote_copy(
                src_ref=source.at[turn],
                dst_ref=target.at[turn],
                send_sem=ssem.at[turn],
                recv_sem=rsem.at[turn],
                device_id={axis: to},
                device_id_type=MESH,
            )
            for source, target, ssem, rsem in (
                (send, got, send_sem, recv_sem),
                (send_sum, got_sum, send_sum_sem, recv_sum_sem),
            )
        ]

        @pl.when(sends)
        def _():
            for copy in copies:
                copy.start()

        @pl.when(jnp.logical_not(takes))
        def _():
            got[turn] = jnp.zeros(got.shape[1:], bf16)
            got_sum[turn] = jnp.zeros(got_sum.shape[1:], f32)

        @pl.when(takes)
        def _():
            for copy in copies:
                copy.wait_recv()

        for j in range(0, states // 2, 2):
            pair = got[turn, pl.ds(j * rows, 2 * rows), :].astype(f32)
            for i in (j, j + 1):
                came = pair[(i - j) * rows : (i - j + 1) * rows]
                rate = packed_rate(i)
                enter[i] = jnp.exp2(rate * sums_enter) * came + enter[i]
                total[i] = jnp.exp2(rate * sums_total) * came + total[i]
        sums_enter = sums_enter + got_sum[turn]
        sums_total = sums_total + got_sum[turn]

        @pl.when(sends)
        def _():
            for copy in copies:
                copy.wait_send()

    for j in range(states // 2):
        opening, _ = both(j)
        outer = enter[j]
        inner = jnp.exp2(packed_rate(j) * sums_first) * outer + opening
        low, high = (inner, outer) if back else (outer, inner)
        o_ref[2 * j] = jnp.where(upper, turned(high), low)
        o_ref[2 * j + 1] = jnp.where(upper, high, turned(low))
    under_way.finish()


def carried(local, sums, rate, axis, back, number, *exchanges):
    count = lax.axis_size(axis)
    states, rows, width = local.shape
    turns = max(1, (count - 1).bit_length())
    items = items_of(exchanges)
    anywhere = [pl.BlockSpec(memory_space=pl.ANY)] * len(items)
    return pl.pallas_call(
        functools.partial(carry_kernel, axis, count, back, items),
        out_shape=[jax.ShapeDtypeStruct(local.shape, f32)]
        + [landed(x, item) for (x, _, _), item in zip(exchanges, items)],
        in_specs=[pl.BlockSpec(memory_space=pltpu.VMEM)] * 3 + anywhere,
        out_specs=[pl.BlockSpec(memory_space=pltpu.VMEM)] + anywhere,
        scratch_shapes=[
            pltpu.VMEM((turns, states // 2 * rows, width), bf16),
            pltpu.VMEM((turns, states // 2 * rows, width), bf16),
            pltpu.VMEM((turns, rows, width), f32),
            pltpu.VMEM((turns, rows, width), f32),
            pltpu.VMEM((states // 2, rows, width), f32),
            pltpu.VMEM((states // 2, rows, width), f32),
            pltpu.SemaphoreType.DMA((turns,)),
            pltpu.SemaphoreType.DMA((turns,)),
            pltpu.SemaphoreType.DMA((turns,)),
            pltpu.SemaphoreType.DMA((turns,)),
        ]
        + [sem for item in items for sem in sems_of(item)],
        compiler_params=pltpu.CompilerParams(
            collective_id=number, has_side_effects=True, vmem_limit_bytes=24 * MIB
        ),
    )(local, sums, rate, *[x for x, _, _ in exchanges])


def spread(mapped_ref, first, wide_ref):
    count, steps, rows, lanes = wide_ref.shape
    column = lax.broadcasted_iota(jnp.int32, (mapped_ref.shape[1], lanes), 0)
    values = mapped_ref[...]
    for n in range(count):
        pick = (column == first + n).astype(bf16)
        wide_ref[n] = jnp.dot(values, pick, preferred_element_type=f32).reshape(steps, rows, lanes)


def rows_of(rate_ref, n, rows):
    return jnp.broadcast_to(rate_ref[n : n + 1, :], (rows, rate_ref.shape[1]))


def perm_of(steps, lines, seqs):
    rows = steps * lines
    laid = lax.broadcasted_iota(jnp.int32, (rows, rows), 0)
    natural = lax.broadcasted_iota(jnp.int32, (rows, rows), 1)
    line = laid % lines
    wanted = (line % seqs) * (rows // seqs) + (line // seqs) * steps + laid // lines
    return (natural == wanted).astype(bf16)


def unit_of(rows):
    return rows * lax.rsqrt(jnp.mean(rows * rows, axis=-1, keepdims=True) + epsilon)


def softplus(x):
    return jnp.maximum(x, 0.0) + jnp.log1p(jnp.exp(-jnp.abs(x)))


def sigmoid(x):
    return 1.0 / (1.0 + jnp.exp(-x))


def silu_slope(values, sigma):
    return sigma * (1.0 + values * (1.0 - sigma))


def dot(a, b):
    return jnp.dot(a, b, preferred_element_type=f32)


def dot_nt(a, b):
    return lax.dot_general(a, b, (((1,), (1,)), ((), ())), preferred_element_type=f32)


def dot_tn(a, b):
    return lax.dot_general(a, b, (((0,), (0,)), ((), ())), preferred_element_type=f32)


def front_kernel(seq_count, chan_count, tokens_ref, gain_ref, w_ref, taps_ref, bias_ref, xproj_ref, valid_ref,
                 normed_ref, ext_ref, pre_ref, gate_ref, mapped_ref,
                 halo, part, beside_in, pair, far_in, halo_send, halo_recv, send_sem, recv_sem):
    seqs, group, width = tokens_ref.shape
    steps, lines, full = pre_ref.shape
    taps, inner = taps_ref.shape[0], w_ref.shape[1]
    rim, rows, tail = taps - 1, steps * lines, halo.shape[1]
    here, me = lax.axis_index("seq"), lax.axis_index("chan")
    beside = me + 1 - 2 * lax.rem(me, 2)
    barrier = pltpu.get_barrier_semaphore()
    told = chan_count // 2
    for by in (1, -1):
        there = here + by
        near = (there >= 0) & (there < seq_count)
        told = told + jnp.where(near, 1, 0)

        @pl.when(near)
        def _():
            pl.semaphore_signal(barrier, inc=1, device_id={"seq": there}, device_id_type=MESH)

    pl.semaphore_signal(barrier, inc=1, device_id={"chan": beside}, device_id_type=MESH)
    for k in range(1, chan_count // 2):
        to = lax.rem(me + 2 * k, chan_count)
        pl.semaphore_signal(barrier, inc=1, device_id={"chan": to}, device_id_type=MESH)
    pl.semaphore_wait(barrier, told)
    ends = pltpu.make_async_remote_copy(
        src_ref=tokens_ref.at[:, pl.ds(group - tail, tail), :],
        dst_ref=halo,
        send_sem=halo_send,
        recv_sem=halo_recv,
        device_id={"seq": here + 1},
        device_id_type=MESH,
    )

    @pl.when(here + 1 < seq_count)
    def _():
        ends.start()

    def normed_of(rows_low):
        return (unit_of(rows_low.astype(f32)) * gain_ref[...]).astype(bf16)

    perm = perm_of(steps, lines, seqs)
    normed = dot(perm, normed_of(tokens_ref[...].reshape(rows, width))).astype(bf16)
    normed_ref[...] = normed
    conv_in = dot_nt(normed, w_ref[0]).astype(bf16).astype(f32)
    ext_ref[pl.ds(rim, steps), :, pl.ds(0, inner)] = conv_in.reshape(steps, lines, inner)
    gate_ref[:, :, pl.ds(0, inner)] = dot_nt(normed, w_ref[1]).reshape(steps, lines, inner)
    if full > inner:
        ext_ref[:, :, pl.ds(inner, full - inner)] = jnp.zeros((steps + rim, lines, full - inner), f32)
        gate_ref[:, :, pl.ds(inner, full - inner)] = jnp.zeros((steps, lines, full - inner), f32)

    @pl.when(here == 0)
    def _():
        halo[...] = jnp.zeros(halo.shape, bf16)

    @pl.when(here > 0)
    def _():
        ends.wait_recv()

    prior = dot_nt(normed_of(halo[...].reshape(seqs * tail, width)), w_ref[0]).astype(bf16)
    to = lax.broadcasted_iota(jnp.int32, (rim * lines, seqs * tail), 0)
    origin = lax.broadcasted_iota(jnp.int32, (rim * lines, seqs * tail), 1)
    pick = (to % lines < seqs) & (origin == (to % lines) * tail + tail - rim + to // lines)
    prior = dot(pick.astype(bf16), prior).reshape(rim, lines, inner)
    upper = lax.broadcasted_iota(jnp.int32, (lines, inner), 0) >= seqs
    for j in range(rim):
        own = turned(ext_ref[steps + j, :, pl.ds(0, inner)])
        ext_ref[j, :, pl.ds(0, inner)] = jnp.where(upper, own, prior[j])
    pre = jnp.broadcast_to(bias_ref[...], (steps, lines, full))
    for k in range(taps):
        pre = pre + taps_ref[k : k + 1, :] * ext_ref[pl.ds(k, steps)] * valid_ref[:, :, k : k + 1]
    pre_ref[...] = pre
    act_low = (pre * sigmoid(pre)).astype(bf16).reshape(rows, full)
    part[...] = dot_nt(act_low, xproj_ref[...]).astype(bf16)
    near = pltpu.make_async_remote_copy(
        src_ref=part,
        dst_ref=beside_in,
        send_sem=send_sem.at[0],
        recv_sem=recv_sem.at[0],
        device_id={"chan": beside},
        device_id_type=MESH,
    )
    near.start()
    near.wait_recv()
    pair[...] = (part[...].astype(f32) + beside_in[...].astype(f32)).astype(bf16)
    copies = []
    for k in range(1, chan_count // 2):
        copies.append(
            pltpu.make_async_remote_copy(
                src_ref=pair,
                dst_ref=far_in.at[k - 1],
                send_sem=send_sem.at[k],
                recv_sem=recv_sem.at[k],
                device_id={"chan": lax.rem(me + 2 * k, chan_count)},
                device_id_type=MESH,
            )
        )
        copies[-1].start()
    for copy in copies:
        copy.wait_recv()
    total = pair[...].astype(f32)
    for k in range(chan_count // 2 - 1):
        total = total + far_in[k].astype(f32)
    mapped_ref[...] = total.astype(bf16)
    near.wait_send()
    for copy in copies:
        copy.wait_send()

    @pl.when(here + 1 < seq_count)
    def _():
        ends.wait_send()


def front(tokens, gain, w_in, taps, bias, xproj, valid, full, number):
    seqs, group, width = tokens.shape
    steps, lines = valid.shape[:2]
    count, rows, maps = lax.axis_size("chan"), steps * lines, xproj.shape[0]
    tail = min(16, group)
    return pl.pallas_call(
        functools.partial(front_kernel, lax.axis_size("seq"), count),
        out_shape=[
            jax.ShapeDtypeStruct((rows, width), bf16),
            jax.ShapeDtypeStruct((steps + taps.shape[0] - 1, lines, full), f32),
            jax.ShapeDtypeStruct((steps, lines, full), f32),
            jax.ShapeDtypeStruct((steps, lines, full), f32),
            jax.ShapeDtypeStruct((rows, maps), bf16),
        ],
        in_specs=[pl.BlockSpec(memory_space=pltpu.VMEM)] * 7,
        out_specs=[pl.BlockSpec(memory_space=pltpu.VMEM)] * 5,
        scratch_shapes=[
            pltpu.VMEM((seqs, tail, width), bf16),
            pltpu.VMEM((rows, maps), bf16),
            pltpu.VMEM((rows, maps), bf16),
            pltpu.VMEM((rows, maps), bf16),
            pltpu.VMEM((count // 2 - 1, rows, maps), bf16),
            pltpu.SemaphoreType.DMA,
            pltpu.SemaphoreType.DMA,
            pltpu.SemaphoreType.DMA((count // 2,)),
            pltpu.SemaphoreType.DMA((count // 2,)),
        ],
        compiler_params=pltpu.CompilerParams(
            collective_id=number, has_side_effects=True, vmem_limit_bytes=48 * MIB
        ),
    )(tokens, gain, w_in, taps, bias, xproj, valid)


def totals_kernel(rank, taps, pre_ref, mapped_ref, dtw_ref, bias_ref, valid_ref, rate_ref,
                  dt_ref, step_ref, drive_ref, last_ref, sums_ref, wide):
    count, steps, rows, lanes = wide.shape

    @pl.when(pl.program_id(0) == 0)
    def _():
        spread(mapped_ref, rank, wide)

    dt_pre = (dot(mapped_ref[...], dtw_ref[...]) + bias_ref[...]).reshape(steps, rows, lanes)
    delta = softplus(dt_pre)
    pre = pre_ref[...]
    dt_ref[...] = dt_pre
    step_ref[...] = jnp.where(valid_ref[:, :, taps : taps + 1] > 0.5, delta, cut)
    drive_ref[...] = delta * pre * sigmoid(pre)
    rates = [rows_of(rate_ref, n, rows) for n in range(count)]
    zero = jnp.zeros((rows, lanes), f32)

    def one(p, held):
        states, sums = held
        step, drive = step_ref[p], drive_ref[p]
        states = tuple(
            jnp.exp2(step * rates[n]) * states[n] + drive * wide[n, p] for n in range(count)
        )
        return states, sums + step

    states, sums = lax.fori_loop(0, steps, one, ((zero,) * count, zero), unroll=2)
    for n in range(count):
        last_ref[n] = states[n]
    sums_ref[...] = sums


def states_kernel(rank, seqs, step_ref, drive_ref, mapped_ref, rate_ref, enter_ref, pre_ref, gate_ref, skip_ref, out_w_ref,
                  y_ref, gated_ref, state_ref, out_ref, wide_in, wide_read, total):
    count, steps, rows, lanes = wide_in.shape
    place = pl.program_id(0)

    @pl.when(place == 0)
    def _():
        spread(mapped_ref, rank, wide_in)
        spread(mapped_ref, rank + count, wide_read)
        total[...] = jnp.zeros_like(total)

    rates = [rows_of(rate_ref, n, rows) for n in range(count)]

    def one(p, states):
        step, drive = step_ref[p], drive_ref[p]
        states = tuple(
            jnp.exp2(step * rates[n]) * states[n] + drive * wide_in[n, p] for n in range(count)
        )
        terms = [states[n] * wide_read[n, p] for n in range(count)]
        while len(terms) > 1:
            terms = [a + b for a, b in zip(terms[::2], terms[1::2])]
        y_ref[p] = terms[0]
        for n in range(count):
            state_ref[p, n] = states[n]
        return states

    lax.fori_loop(0, steps, one, tuple(enter_ref[n] for n in range(count)), unroll=2)
    pre, gate = pre_ref[...], gate_ref[...]
    y_full = y_ref[...] + skip_ref[...] * (pre * sigmoid(pre))
    y_ref[...] = y_full
    gated = (y_full * (gate * sigmoid(gate))).astype(bf16).reshape(steps * rows, lanes)
    gated_ref[...] = gated
    total[...] += dot(gated, out_w_ref[...])

    @pl.when(place == pl.num_programs(0) - 1)
    def _():
        perm = perm_of(steps, rows, seqs)
        out_ref[...] = dot_tn(perm, total[...].astype(bf16)).astype(bf16)


def back_totals_kernel(rank, seqs, step_ref, mapped_ref, rate_ref, mixed_ref, normed_ref, out_w_ref, gate_ref, y_ref, gated_ref,
                       pre_ref, grad_y_ref, grad_z_ref, grad_out_ref, grad_gate_ref, skip_ref, last_ref,
                       wide, mixed):
    count, steps, rows, lanes = wide.shape

    @pl.when(pl.program_id(0) == 0)
    def _():
        spread(mapped_ref, rank + count, wide)
        mixed[...] = dot(perm_of(steps, rows, seqs), mixed_ref[...]).astype(bf16)

    grad_gated = dot_nt(mixed[...], out_w_ref[...]).reshape(steps, rows, lanes)
    gate, pre = gate_ref[...], pre_ref[...]
    sigma = sigmoid(gate)
    grad_y = grad_gated * (gate * sigma)
    grad_y_ref[...] = grad_y
    grad_z = (grad_gated * y_ref[...] * silu_slope(gate, sigma)).astype(bf16)
    grad_z = grad_z.reshape(steps * rows, lanes)
    grad_z_ref[...] = grad_z
    skip_ref[...] = jnp.sum(grad_y * (pre * sigmoid(pre)), axis=0)
    grad_out_ref[...] = dot_tn(gated_ref[...], mixed[...]).astype(bf16)
    grad_gate_ref[...] = dot_tn(grad_z, normed_ref[...]).astype(bf16)
    rates = [rows_of(rate_ref, n, rows) for n in range(count)]
    zero = jnp.zeros((rows, lanes), f32)

    def one(turn, held):
        p = steps - 1 - turn
        step, grad_y = step_ref[p], grad_y_ref[p]
        return tuple(
            jnp.exp2(step * rates[n]) * (held[n] + grad_y * wide[n, p]) for n in range(count)
        )

    held = lax.fori_loop(0, steps, one, (zero,) * count, unroll=2)
    for n in range(count):
        last_ref[n] = held[n]


def back_kernel(rank, pieces, shares, items, step_ref, drive_ref, grad_y_ref, mapped_ref, rate_ref, first_ref, state_ref, enter_ref, dt_ref,
                pre_ref, dtw_ref, *refs):
    many, number = len(shares), len(items)
    at = 0

    def take(k):
        nonlocal at
        at += k
        return refs[at - k : at]

    xs, riders = take(many), take(number)
    side_ref, log_ref, bias_ref, grad_dtw_ref, low_ref = take(5)
    parts, rider_outs = take(many), take(number)
    wide_in, wide_read, sum_in, sum_read, to_input, to_decay, total = take(7)
    count, steps, rows, lanes = wide_in.shape
    place, tiles = pl.program_id(0), pl.num_programs(0)
    kept, kept_sem = take(many), take(1)[0]
    tasks = [Share(*share, held, *take(7)) for share, held in zip(shares, kept)]
    under_way = Riders(items, riders, rider_outs, take(3 * number))
    turn = [(task, k) for task in tasks for k in range(task.groups)]

    @pl.when(place == 0)
    def _():
        copies = [
            pltpu.make_async_copy(x, held, kept_sem.at[i]) for i, (x, held) in enumerate(zip(xs, kept))
        ]
        for copy in copies:
            copy.start()
        axes = {share[:2] for share in shares} | set(axes_of(items))
        pl.semaphore_wait(pltpu.get_barrier_semaphore(), greet(sorted(axes)))
        for copy in copies:
            copy.wait()
        for task, k in turn[:2]:
            task.begin(k)
        under_way.start()
        spread(mapped_ref, rank, wide_in)
        spread(mapped_ref, rank + count, wide_read)
        sum_in[...] = jnp.zeros_like(sum_in)
        sum_read[...] = jnp.zeros_like(sum_read)
        total[...] = jnp.zeros_like(total)

    each = -(-len(turn) // (pieces - 1))
    for piece in range(1, pieces):

        @pl.when(place == piece)
        def _():
            for i in range((piece - 1) * each, min(piece * each, len(turn))):
                turn[i][0].pass_on(turn[i][1])
                if i + 2 < len(turn):
                    turn[i + 2][0].begin(turn[i + 2][1])

    rates = [rows_of(rate_ref, n, rows) for n in range(count)]
    for n in range(count):
        log_ref[n] = jnp.zeros((rows, lanes), f32)

    def step_back(p, carry, prior_of):
        step, drive, grad_y = step_ref[p], drive_ref[p], grad_y_ref[p]
        inputs = jnp.zeros((rows, lanes), f32)
        decays = jnp.zeros((rows, lanes), f32)
        new, grads = [], []
        for n in range(count):
            grad = grad_y * wide_read[n, p] + carry[n]
            passed = jnp.exp2(step * rates[n]) * grad
            new.append(passed)
            grad_decay = passed * prior_of(n)
            decays = decays + grad_decay * rates[n]
            log_ref[n] += grad_decay * step
            inputs = inputs + grad * wide_in[n, p]
            grads.append(grad)
        to_input[p] = inputs
        to_decay[p] = decays
        grads = jnp.concatenate(grads, axis=0).astype(bf16)
        held_states = state_ref[p].reshape(count * rows, lanes).astype(bf16)
        sum_in[p] += dot_nt(drive.astype(bf16), grads)
        sum_read[p] += dot_nt(grad_y.astype(bf16), held_states)
        return tuple(new)

    def one(turn, carry):
        p = steps - 1 - turn
        return step_back(p, carry, lambda n: state_ref[p - 1, n])

    carry = lax.fori_loop(0, steps - 1, one, tuple(enter_ref[n] for n in range(count)), unroll=7 if (steps - 1) % 7 == 0 else 1)
    step_back(0, carry, lambda n: first_ref[n])
    dt_pre, pre = dt_ref[...], pre_ref[...]
    inputs = to_input[...]
    side_ref[...] = inputs * softplus(dt_pre)
    grad_delta = to_decay[...] * (1.0 / log2e) + inputs * (pre * sigmoid(pre))
    grad_dt = grad_delta * sigmoid(dt_pre)
    bias_ref[...] = jnp.sum(grad_dt, axis=0)
    grad_dt = grad_dt.astype(bf16).reshape(steps * rows, lanes)
    grad_dtw_ref[...] = dot_tn(mapped_ref[...], grad_dt)
    total[...] += dot_nt(grad_dt, dtw_ref[...])

    @pl.when(place == tiles - 1)
    def _():
        wide = count * rows
        line = lax.broadcasted_iota(jnp.int32, (steps * rows, wide), 0) % rows
        lane = lax.broadcasted_iota(jnp.int32, (steps * rows, wide), 1)
        state = lax.broadcasted_iota(jnp.int32, (wide, total.shape[1]), 0) // rows
        column = lax.broadcasted_iota(jnp.int32, (wide, total.shape[1]), 1)
        sums = total[...]
        for which, source in enumerate((sum_in, sum_read)):
            values = jnp.where(lane % rows == line, source[...].reshape(steps * rows, wide), 0.0)
            pick = (column == rank + which * count + state).astype(bf16)
            sums = sums + dot(values.astype(bf16), pick)
        low_ref[...] = sums.astype(bf16)
        for task, part in zip(tasks, parts):
            part[...] = task.total().astype(bf16)
            task.close()
        under_way.finish()


def conv_back_kernel(taps, grad_mapped_ref, grad_y_ref, side_ref, pre_ref, ext_ref, skip_ref, xproj_ref, taps_ref, valid_ref,
                     grad_ref, rim_ref, grad_xproj_ref, sums_ref, ext_grad):
    steps, rows, lanes = pre_ref.shape
    rim = taps - 1
    pre = pre_ref[...]
    sigma = sigmoid(pre)
    grad_act = dot(grad_mapped_ref[...], xproj_ref[...]).reshape(steps, rows, lanes)
    grad_act = grad_act + grad_y_ref[...] * skip_ref[...] + side_ref[...]
    grad_pre = grad_act * silu_slope(pre, sigma)
    act_low = (pre * sigma).astype(bf16).reshape(steps * rows, lanes)
    grad_xproj_ref[...] = dot_tn(grad_mapped_ref[...], act_low)
    ext_grad[...] = jnp.zeros_like(ext_grad)
    for k in range(taps):
        masked = grad_pre * valid_ref[:, :, k : k + 1]
        sums_ref[k] = jnp.sum(masked * ext_ref[pl.ds(k, steps)], axis=0)
        ext_grad[pl.ds(k, steps)] += masked * taps_ref[k : k + 1, :]
    sums_ref[taps] = jnp.sum(grad_pre, axis=0)
    upper = lax.broadcasted_iota(jnp.int32, (rows, lanes), 0) >= rows // 2
    for j in range(rim):
        edge = ext_grad[j]
        rim_ref[j] = edge
        ext_grad[steps + j] += jnp.where(upper, 0.0, turned(edge))
    grad_ref[...] = ext_grad[pl.ds(rim, steps)]


def ends_kernel(count, items, tokens_ref, grad_ref, rim_ref, grad_z_ref, normed_ref, w_ref, *refs):
    number = len(items)
    xs, refs = refs[:number], refs[number:]
    grad_conv_ref, part_ref, gain_ref = refs[:3]
    outs, (came, send_sem, recv_sem), sems = refs[3 : 3 + number], refs[3 + number : 6 + number], refs[6 + number :]
    steps, lines, full = grad_ref.shape
    seqs, group, width = tokens_ref.shape
    rows, inner, rim = steps * lines, w_ref.shape[1], rim_ref.shape[0]
    here = lax.axis_index("seq")
    told = greet(sorted({("seq", count)} | set(axes_of(items))))
    pl.semaphore_wait(pltpu.get_barrier_semaphore(), told)
    edge = pltpu.make_async_remote_copy(
        src_ref=rim_ref,
        dst_ref=came,
        send_sem=send_sem,
        recv_sem=recv_sem,
        device_id={"seq": here - 1},
        device_id_type=MESH,
    )

    @pl.when(here > 0)
    def _():
        edge.start()

    under_way = Riders(items, xs, outs, sems).start()
    unit = unit_of(tokens_ref[...].reshape(rows, width).astype(f32))
    by_gate = dot(grad_z_ref[:, pl.ds(0, inner)], w_ref[1])

    @pl.when(here == count - 1)
    def _():
        came[...] = jnp.zeros(came.shape, f32)

    @pl.when(here < count - 1)
    def _():
        edge.wait_recv()

    upper = lax.broadcasted_iota(jnp.int32, (lines, full), 0) >= lines // 2
    last = [
        (grad_ref[steps - rim + j] + jnp.where(upper, turned(came[j]), 0.0))[None] for j in range(rim)
    ]
    grad = jnp.concatenate([grad_ref[pl.ds(0, steps - rim)]] + last, axis=0)
    grad = grad.reshape(rows, full).astype(bf16)
    under_way.step()
    grad_conv_ref[...] = dot_tn(grad, normed_ref[...]).astype(bf16)
    under_way.step()
    part = (dot(grad[:, :inner], w_ref[0]) + by_gate).astype(bf16)
    part = dot_tn(perm_of(steps, lines, seqs), part)
    part_ref[...] = part.astype(bf16)
    gain_ref[...] = jnp.sum(part * unit, axis=0, keepdims=True)
    under_way.finish()

    @pl.when(here > 0)
    def _():
        edge.wait_send()


def ends(tokens, grad, rim, grad_z, normed, w_in, number, *exchanges):
    steps, lines, full = grad.shape
    rows, width = normed.shape
    items = items_of(exchanges)
    anywhere = [pl.BlockSpec(memory_space=pl.ANY)] * len(items)
    return pl.pallas_call(
        functools.partial(ends_kernel, lax.axis_size("seq"), items),
        out_shape=[
            jax.ShapeDtypeStruct((full, width), bf16),
            jax.ShapeDtypeStruct((rows, width), bf16),
            jax.ShapeDtypeStruct((1, width), f32),
        ]
        + [landed(x, item) for (x, _, _), item in zip(exchanges, items)],
        in_specs=[pl.BlockSpec(memory_space=pltpu.VMEM)] * 6 + anywhere,
        out_specs=[pl.BlockSpec(memory_space=pltpu.VMEM)] * 3 + anywhere,
        scratch_shapes=[
            pltpu.VMEM(rim.shape, f32),
            pltpu.SemaphoreType.DMA,
            pltpu.SemaphoreType.DMA,
        ]
        + [sem for item in items for sem in sems_of(item)],
        compiler_params=pltpu.CompilerParams(
            collective_id=number, has_side_effects=True, vmem_limit_bytes=48 * MIB
        ),
    )(tokens, grad, rim, grad_z, normed, w_in, *[x for x, _, _ in exchanges])


def hits_of(routes, experts, part, most, slots):
    rows = routes.shape[0]
    chosen = (lax.broadcasted_iota(jnp.int32, (rows, experts), 1) == routes).astype(f32)
    row = lax.broadcasted_iota(jnp.int32, (rows, rows), 0)
    other = lax.broadcasted_iota(jnp.int32, (rows, rows), 1)
    earlier = (other < row) & (row // part == other // part)
    ranks = jnp.sum(dot(earlier.astype(bf16), chosen.astype(bf16)) * chosen, axis=1, keepdims=True)
    slot = lax.broadcasted_iota(jnp.int32, (rows, 1), 0) // part * most + ranks.astype(jnp.int32)
    column = lax.broadcasted_iota(jnp.int32, (rows, experts * slots), 1)
    return chosen, (column == routes * slots + slot).astype(bf16)


def route_kernel(part, most, slots, tokens_ref, mixed_ref, gain_ref, routes_ref, router_ref,
                 hidden_ref, normed_ref, probs_ref, chosen_ref, hit_ref, packed_ref):
    hidden = tokens_ref[...].astype(f32) + mixed_ref[...]
    hidden_ref[...] = hidden
    normed = (unit_of(hidden) * gain_ref[...]).astype(bf16)
    normed_ref[...] = normed
    logits = dot_nt(normed, router_ref[...])
    raised = jnp.exp(logits - jnp.max(logits, axis=1, keepdims=True))
    probs_ref[...] = raised / jnp.sum(raised, axis=1, keepdims=True)
    chosen, hit = hits_of(routes_ref[...], router_ref.shape[0], part, most, slots)
    chosen_ref[...] = chosen
    hit_ref[...] = hit
    packed_ref[...] = dot_tn(hit, normed).astype(bf16)


def loss_kernel(group, lengths_ref, came_ref, back_ref, hit_ref, hidden_ref, probs_ref, chosen_ref, teacher_ref,
                layer_ref, grad_layer_ref, grad_logit_ref, loss_ref, packed_ref):
    rows, width = hidden_ref.shape
    seqs = lengths_ref.shape[0]
    expert = dot(back_ref[...], came_ref[...])
    probs, chosen = probs_ref[...], chosen_ref[...]
    gate = jnp.sum(probs * chosen, axis=1, keepdims=True)
    layer = hidden_ref[...] + gate * expert
    layer_ref[...] = layer.astype(bf16)
    flat_row = lax.axis_index("chan") * rows + lax.broadcasted_iota(jnp.int32, (rows, 1), 0)
    length = jnp.zeros((rows, 1), jnp.int32)
    total = 0
    for s in range(seqs):
        length = jnp.where(flat_row // group == s, lengths_ref[s], length)
        total = total + lengths_ref[s]
    scale = 1.0 / jnp.broadcast_to(total, (rows, 1)).astype(f32)
    at = lax.axis_index("seq") * group + flat_row % group
    mask = jnp.where(at < length, scale, 0.0)
    error = layer - teacher_ref[...].astype(f32)
    scaled = mask * error
    lost = jnp.sum(scaled * error, axis=0, keepdims=True)
    loss_ref[...] = jnp.broadcast_to(jnp.sum(lost, axis=1, keepdims=True), (1, width))
    grad_layer = 2.0 * scaled
    grad_layer_ref[...] = grad_layer
    grad_gate = jnp.sum(grad_layer * expert, axis=1, keepdims=True)
    grad_logit_ref[...] = grad_gate * gate * (chosen - probs)
    packed_ref[...] = dot_tn(hit_ref[...], (gate * grad_layer).astype(bf16)).astype(bf16)


def norm_back_kernel(came_ref, back_ref, grad_logit_ref, router_ref, normed_ref, hidden_ref, grad_layer_ref, gain_ref, loss_ref,
                     grad_ref, low_ref, shared_ref):
    experts = router_ref.shape[0]
    grad_logit = grad_logit_ref[...].astype(bf16)
    grad_normed = dot(back_ref[...], came_ref[...]) + dot(grad_logit, router_ref[...])
    hidden = hidden_ref[...]
    inverse = lax.rsqrt(jnp.mean(hidden * hidden, axis=1, keepdims=True) + epsilon)
    unit = hidden * inverse
    shared_ref[...] = jnp.zeros_like(shared_ref)
    shared_ref[pl.ds(0, experts), :] = dot_tn(grad_logit, normed_ref[...])
    shared_ref[pl.ds(experts, 1), :] = jnp.sum(grad_normed * unit, axis=0, keepdims=True)
    shared_ref[pl.ds(experts + 1, 1), :] = loss_ref[...]
    grad = grad_layer_ref[...] + norm_back(grad_normed, unit, inverse, gain_ref[...])
    grad_ref[...] = grad
    low_ref[...] = grad.astype(bf16)


def at_once(kernel, ins, outs, scalars=0):
    spaces = [pltpu.SMEM] * scalars + [pltpu.VMEM] * (len(ins) - scalars)
    return pl.pallas_call(
        kernel,
        in_specs=[pl.BlockSpec(memory_space=space) for space in spaces],
        out_specs=[pl.BlockSpec(memory_space=pltpu.VMEM)] * len(outs),
        out_shape=[jax.ShapeDtypeStruct(shape, dtype) for shape, dtype in outs],
        compiler_params=pltpu.CompilerParams(vmem_limit_bytes=32 * MIB),
        cost_estimate=pl.CostEstimate(flops=1000, bytes_accessed=1000, transcendentals=0),
    )(*ins)


def expert_kernel(x_ref, first_ref, second_ref, hidden_ref, slope_ref, result_ref, total):
    place = pl.program_id(0)

    @pl.when(place == 0)
    def _():
        total[...] = jnp.zeros_like(total)

    pre = dot(x_ref[...], first_ref[...])
    cdf = 0.5 * (1.0 + lax.erf(pre * 0.7071067811865476))
    hidden = (pre * cdf).astype(bf16)
    hidden_ref[0] = hidden
    slope = cdf + pre * (jnp.exp(-0.5 * pre * pre) * 0.3989422804014327)
    slope_ref[...] = slope.astype(bf16)
    total[...] += dot(hidden, second_ref[...])

    @pl.when(place == pl.num_programs(0) - 1)
    def _():
        result_ref[...] = total[...].astype(bf16)


def expert_back_kernel(grad_ref, first_ref, second_ref, slope_ref, grad_pre_ref, result_ref, total):
    place = pl.program_id(0)

    @pl.when(place == 0)
    def _():
        total[...] = jnp.zeros_like(total)

    grad = dot_nt(grad_ref[...], second_ref[...]) * slope_ref[...].astype(f32)
    grad = grad.astype(bf16)
    grad_pre_ref[0] = grad
    total[...] += dot_nt(grad, first_ref[...])

    @pl.when(place == pl.num_programs(0) - 1)
    def _():
        result_ref[...] = total[...].astype(bf16)


def expert(x, first, second, parts, slope=None):
    rows, width = x.shape
    units = first.shape[1] // parts
    tile = next((t for t in (768, 384, 256, 128) if units % t == 0), None)
    low = jax.ShapeDtypeStruct((rows, width), bf16)
    if tile is None:

        def split(h):
            return h.reshape(rows, parts, units).transpose(1, 0, 2)

        if slope is not None:
            grad = (dot_nt(x, second) * slope.astype(f32)).astype(bf16)
            return split(grad), dot_nt(grad, first).astype(bf16)
        pre = dot(x, first)
        cdf = 0.5 * (1.0 + lax.erf(pre * 0.7071067811865476))
        hidden = (pre * cdf).astype(bf16)
        slope = cdf + pre * (jnp.exp(-0.5 * pre * pre) * 0.3989422804014327)
        return split(hidden), slope.astype(bf16), dot(hidden, second).astype(bf16)
    each = units // tile
    columns = pl.BlockSpec((width, tile), lambda i: (0, i))
    lines = pl.BlockSpec((tile, width), lambda i: (i, 0))
    everything = pl.BlockSpec((rows, width), lambda i: (0, 0))
    slopes = pl.BlockSpec((rows, tile), lambda i: (0, i))
    hiddens = pl.BlockSpec((1, rows, tile), lambda i: (i // each, 0, i % each))
    hidden_shape = jax.ShapeDtypeStruct((parts, rows, units), bf16)
    back = slope is not None
    return pl.pallas_call(
        expert_back_kernel if back else expert_kernel,
        grid=(parts * each,),
        in_specs=[everything, columns, lines] + ([slopes] if back else []),
        out_specs=[hiddens] + ([] if back else [slopes]) + [everything],
        out_shape=[hidden_shape]
        + ([] if back else [jax.ShapeDtypeStruct((rows, first.shape[1]), bf16)])
        + [low],
        scratch_shapes=[pltpu.VMEM((rows, width), f32)],
        compiler_params=pltpu.CompilerParams(vmem_limit_bytes=60 * MIB),
        cost_estimate=pl.CostEstimate(flops=1000, bytes_accessed=1000, transcendentals=0),
    )(x, first, second, *([slope] if back else []))


def block_of(shape, kind):
    if kind == "tile":
        return pl.BlockSpec(shape[:-1] + (LANES,), lambda i: (0,) * (len(shape) - 1) + (i,))
    if kind == "rows":
        return pl.BlockSpec((LANES,) + shape[1:], lambda i: (i,) + (0,) * (len(shape) - 1))
    if kind == "any":
        return pl.BlockSpec(memory_space=pl.ANY)
    return pl.BlockSpec(shape, lambda i: (0,) * len(shape))


def share_scratch(x, axis, size):
    groups = lax.axis_size(axis) // size
    part = x.shape[1:]
    return [
        pltpu.VMEM((groups, size - 1) + part, bf16),
        pltpu.VMEM((groups - 1,) + part, bf16),
        pltpu.VMEM((groups - 1,) + part, bf16),
        pltpu.SemaphoreType.DMA((groups, size - 1)),
        pltpu.SemaphoreType.DMA((groups, size - 1)),
        pltpu.SemaphoreType.DMA((groups - 1,)),
        pltpu.SemaphoreType.DMA((groups - 1,)),
    ]


def by_tiles(kernel, full, ins, outs, scratch, more=(), params=None):
    return pl.pallas_call(
        kernel,
        grid=(full // LANES,),
        in_specs=[block_of(a.shape, kind) for a, kind in ins],
        out_specs=[block_of(shape, kind) for shape, _, kind in outs],
        out_shape=[jax.ShapeDtypeStruct(shape, dtype) for shape, dtype, _ in outs],
        scratch_shapes=[pltpu.VMEM(shape, dtype) for shape, dtype in scratch] + list(more),
        compiler_params=pltpu.CompilerParams(vmem_limit_bytes=58 * MIB, **(params or {})),
        cost_estimate=pl.CostEstimate(flops=1000, bytes_accessed=1000, transcendentals=0),
    )(*[a for a, _ in ins])


def norm_back(grad_normed, unit_rows, inverse, weight_gain):
    scaled = grad_normed * weight_gain
    return inverse * (scaled - unit_rows * jnp.mean(scaled * unit_rows, axis=-1, keepdims=True))


def local(
    tokens,
    teacher,
    true_lengths,
    doc_lengths,
    routes,
    norm1_gain,
    in_weight,
    conv_weight,
    conv_bias,
    xproj_weight,
    dt_weight,
    dt_bias,
    a_log,
    skip_weight,
    out_weight,
    norm2_gain,
    router_weight,
    expert_in,
    expert_out,
):
    seqs, group, width = tokens.shape
    inner = in_weight.shape[2]
    rank = dt_weight.shape[0]
    states = a_log.shape[1]
    experts = router_weight.shape[1]
    n_seq = lax.axis_size("seq")
    n_chan = lax.axis_size("chan")
    shards = n_seq // experts
    most = group // 4
    taps = conv_weight.shape[0]
    rim = taps - 1
    lines = 8
    chunks = lines // seqs
    steps = group // chunks
    owned = seqs * group // n_chan
    part = min(group, owned)
    most = min(most, part)
    parts = owned // part
    place = lax.axis_index("chan")
    first_pos = lax.axis_index("seq") * group

    full = -(-inner // LANES) * LANES
    rows = steps * lines
    maps = rank + 2 * states

    def padded(x):
        return jnp.pad(x, ((0, 0),) * (x.ndim - 1) + ((0, full - inner),))

    at = (
        first_pos
        + jnp.arange(steps, dtype=jnp.int32)[:, None]
        + (jnp.arange(lines, dtype=jnp.int32) // seqs * steps)[None, :]
    )
    stops = []
    for k in range(doc_lengths.shape[1] - 1):
        stops.append(doc_lengths[:, k] + (stops[-1] if stops else 0))
    stops = [jnp.tile(stop, chunks)[None, :] for stop in stops]

    def doc_at(pos):
        return sum((pos >= stop).astype(jnp.int32) for stop in stops)

    doc_ids = doc_at(at)
    keep = (doc_ids == doc_at(at - 1)) & (at > 0)
    valid = [doc_at(at - rim + k) == doc_ids for k in range(taps)] + [keep]
    valid = jnp.stack(valid + [keep] * (lines - taps - 1), axis=-1).astype(f32)

    w_in = in_weight.transpose(1, 2, 0)
    router_rows = router_weight.T
    gain_one = norm1_gain.astype(f32)
    taps_full = padded(conv_weight.astype(f32))
    xproj_rows = padded(xproj_weight.T)
    dt_rows = jnp.pad(padded(dt_weight), ((0, maps - rank), (0, 0)))
    skip_row = padded(skip_weight[None])
    out_rows = jnp.pad(out_weight, ((0, full - inner), (0, 0)))
    rate = -jnp.exp(a_log.T)
    rate_two = padded(rate * log2e)
    normed_one, extended, pre_act, gate_z, mapped = front(
        tokens,
        gain_one[None],
        w_in,
        taps_full,
        padded(conv_bias.astype(f32)[None]),
        xproj_rows,
        valid,
        full,
        1,
    )
    act_shape, state_shape, wide_shape = (steps, lines, full), (states, lines, full), (states, steps, lines, LANES)
    dt_pre, step_size, drive, own_states, sums = by_tiles(
        functools.partial(totals_kernel, rank, taps),
        full,
        [
            (pre_act, "tile"),
            (mapped, "whole"),
            (dt_rows, "tile"),
            (padded(dt_bias[None]), "tile"),
            (valid, "whole"),
            (rate_two, "tile"),
        ],
        [
            (act_shape, f32, "tile"),
            (act_shape, f32, "tile"),
            (act_shape, f32, "tile"),
            (state_shape, f32, "tile"),
            ((lines, full), f32, "tile"),
        ],
        [(wide_shape, f32)],
    )
    (enter,) = carried(own_states, sums, rate_two, "seq", False, 2)
    y_full, gated, state, out_part = by_tiles(
        functools.partial(states_kernel, rank, seqs),
        full,
        [
            (step_size, "tile"),
            (drive, "tile"),
            (mapped, "whole"),
            (rate_two, "tile"),
            (enter, "tile"),
            (pre_act, "tile"),
            (gate_z, "tile"),
            (skip_row, "tile"),
            (out_rows, "rows"),
        ],
        [
            (act_shape, f32, "tile"),
            ((rows, full), bf16, "tile"),
            ((steps, states, lines, full), f32, "tile"),
            ((rows, width), bf16, "whole"),
        ],
        [(wide_shape, f32)] * 2 + [((rows, width), f32)],
    )
    (mixed,) = share_of(3, [(out_part.reshape(n_chan, owned, width), "chan", 2, f32)])

    def own(x):
        return lax.dynamic_slice_in_dim(x.reshape((rows,) + x.shape[2:]), place * owned, owned, 0)

    slots = parts * most
    tokens_own, gain_two = own(tokens), norm2_gain.astype(f32)[None]
    line, low = (owned, width), ((owned, width), bf16)
    hidden_one, normed_two, probs, chosen, hit, packed = at_once(
        functools.partial(route_kernel, part, most, slots),
        [tokens_own, mixed, gain_two, own(routes)[:, None], router_rows],
        [
            (line, f32),
            low,
            ((owned, experts), f32),
            ((owned, experts), f32),
            ((owned, experts * slots), bf16),
            ((experts * slots, width), bf16),
        ],
    )
    hit_back = hit
    if shards > 1:
        hit_back = hit.reshape(owned, experts, slots)
        hit_back = jnp.repeat(hit_back, shards, axis=1).reshape(owned, n_seq * slots)

    def to_slabs(x):
        x = x.reshape(experts, slots, width)
        return x if shards == 1 else jnp.repeat(x, shards, axis=0), "scatter", "seq"

    def to_rows(x):
        return x.reshape(n_seq, slots, width), "scatter", "seq"

    def flat(x):
        return x.reshape(-1, x.shape[-1])

    first_slab, second_slab = expert_in[0], expert_out[0]
    arrived = flat(exchange(4, to_slabs(packed))[0])
    hidden, slope, result = expert(arrived, first_slab, second_slab, n_chan)
    result_rows, rows_all = exchange(5, to_rows(result), (arrived, 2, "chan"))
    layer_low, grad_layer, grad_logit, loss_row, packed = at_once(
        functools.partial(loss_kernel, group),
        [
            true_lengths,
            flat(result_rows),
            hit_back,
            hit,
            hidden_one,
            probs,
            chosen,
            own(teacher),
        ],
        [
            low,
            (line, f32),
            ((owned, experts), f32),
            ((1, width), f32),
            ((experts * slots, width), bf16),
        ],
        scalars=1,
    )
    grad_rows, hidden_all = exchange(6, to_slabs(packed), (hidden, "scatter", "chan"))
    grad_rows = flat(grad_rows)
    grad_pre, grad_slab_rows = expert(grad_rows, first_slab, second_slab, n_chan, slope)
    grad_expert, grad_rows_all = exchange(7, to_rows(grad_slab_rows), (grad_rows, 2, "chan"))
    shared_rows = -(-(experts + 2) // 8) * 8
    grad_hidden_one, grad_low, shared = at_once(
        norm_back_kernel,
        [
            flat(grad_expert),
            hit_back,
            grad_logit,
            router_rows,
            normed_two,
            hidden_one,
            grad_layer,
            gain_two,
            loss_row,
        ],
        [(line, f32), low, ((shared_rows, width), f32)],
    )

    (grad_mixed,) = exchange(8, (grad_low, 2, "chan"))
    grad_y, grad_z, grad_out_w, grad_in_gate, skip_sums, back_last = by_tiles(
        functools.partial(back_totals_kernel, rank, seqs),
        full,
        [
            (step_size, "tile"),
            (mapped, "whole"),
            (rate_two, "tile"),
            (grad_mixed.reshape(rows, width), "whole"),
            (normed_one, "whole"),
            (out_rows, "rows"),
            (gate_z, "tile"),
            (y_full, "tile"),
            (gated, "tile"),
            (pre_act, "tile"),
        ],
        [
            (act_shape, f32, "tile"),
            ((rows, full), bf16, "tile"),
            ((full, width), bf16, "rows"),
            ((full, width), bf16, "rows"),
            ((lines, full), f32, "tile"),
            (state_shape, f32, "tile"),
        ],
        [(wide_shape, f32), ((rows, width), bf16)],
    )
    back_enter, shared = carried(
        back_last, sums, rate_two, "seq", True, 9, (shared, "gather", "chan")
    )
    shared = jnp.sum(shared, axis=0).reshape(-1, LANES)
    def cut_rows(x, unit):
        each = -(-x.shape[0] // (unit * n_seq)) * unit
        return jnp.pad(x, ((0, each * n_seq - x.shape[0]), (0, 0))).reshape(n_seq, each, -1)

    across = n_chan // 2
    by_out, by_gate = cut_rows(grad_out_w, 16), cut_rows(grad_in_gate, 16)
    rider = (grad_pre, "scatter", "chan")
    side, log_sums, bias_sums, grad_dt_w, low_part, by_out, by_gate, grad_pre_all = by_tiles(
        functools.partial(
            back_kernel, rank, full // LANES, [("seq", n_seq, across)] * 2, items_of([rider])
        ),
        full,
        [
            (step_size, "tile"),
            (drive, "tile"),
            (grad_y, "tile"),
            (mapped, "whole"),
            (rate_two, "tile"),
            (enter, "tile"),
            (state, "tile"),
            (back_enter, "tile"),
            (dt_pre, "tile"),
            (pre_act, "tile"),
            (dt_rows, "tile"),
            (by_out, "any"),
            (by_gate, "any"),
            (grad_pre, "any"),
        ],
        [
            (act_shape, f32, "tile"),
            (state_shape, f32, "tile"),
            ((lines, full), f32, "tile"),
            ((maps, full), f32, "tile"),
            ((rows, maps), bf16, "whole"),
            (by_out.shape[1:], bf16, "whole"),
            (by_gate.shape[1:], bf16, "whole"),
            (grad_pre.shape, bf16, "any"),
        ],
        [(wide_shape, f32)] * 2
        + [((steps, lines, states * lines), f32)] * 2
        + [((steps, lines, LANES), f32)] * 2
        + [((rows, maps), f32)]
        + [(by_out.shape, bf16)] * 2,
        [pltpu.SemaphoreType.DMA((2,))]
        + share_scratch(by_out, "seq", across)
        + share_scratch(by_gate, "seq", across)
        + sems_of(items_of([rider])[0]),
        {"collective_id": 15, "has_side_effects": True},
    )
    grad_mapped = summed_over(low_part, "chan", 10).astype(bf16)
    grad_conv_in, rims, grad_xproj, conv_sums = by_tiles(
        functools.partial(conv_back_kernel, taps),
        full,
        [
            (grad_mapped, "whole"),
            (grad_y, "tile"),
            (side, "tile"),
            (pre_act, "tile"),
            (extended, "tile"),
            (skip_row, "tile"),
            (xproj_rows, "tile"),
            (taps_full, "tile"),
            (valid, "whole"),
        ],
        [
            (act_shape, f32, "tile"),
            ((rim, lines, full), f32, "tile"),
            ((maps, full), f32, "tile"),
            ((taps + 1, lines, full), f32, "tile"),
        ],
        [((steps + rim, lines, LANES), f32)],
    )
    grad_in_conv, normed_part, grad_gain_one, by_gate = ends(
        tokens, grad_conv_in, rims, grad_z, normed_one, w_in, 14, (by_gate, across, "seq")
    )
    normed_part = normed_part.reshape(n_chan, owned, width)
    sums_all = jnp.concatenate([conv_sums, bias_sums[None], skip_sums[None], log_sums], axis=0)
    sums_all = jnp.sum(sums_all, axis=1)
    small_rows = sums_all.shape[0] * full // LANES
    small = jnp.concatenate([sums_all.reshape(small_rows, LANES), shared], axis=0)

    by_conv = cut_rows(grad_in_conv, 16)
    middle = cut_rows(jnp.concatenate([grad_xproj, grad_dt_w[:rank]], axis=0).astype(bf16), 16)
    grad_normed_one, by_conv, middle, small, grad_gain_one, by_out = share_of(
        11,
        [
            (normed_part, "chan", 2, f32),
            (by_conv, "seq", across, bf16),
            (middle, "seq", across, bf16),
        ],
        (cut_rows(small, 8), "scatter", "seq"),
        (grad_gain_one, "gather", "chan"),
        (by_out, across, "seq"),
    )
    small = jnp.sum(small, axis=0)
    grad_gain_one = jnp.sum(grad_gain_one, axis=0)
    tokens_full = tokens_own.astype(f32)
    inverse_one = lax.rsqrt(jnp.mean(tokens_full * tokens_full, axis=-1, keepdims=True) + epsilon)
    grad_own = grad_hidden_one + norm_back(
        grad_normed_one, tokens_full * inverse_one, inverse_one, gain_one
    )
    moved = [
        (grad_own.astype(bf16), 2, "chan"),
        (layer_low, 2, "chan"),
        (by_conv, across, "seq"),
        (middle, across, "seq"),
        (small, "gather", "seq"),
        (grad_gain_one, "gather", "seq"),
    ]
    moved = exchange(12, *moved)
    grad_first = dot_tn(flat(rows_all), flat(grad_pre_all))
    grad_second = dot_tn(flat(hidden_all), flat(grad_rows_all))
    grad_tokens, layer_out, by_conv, middle, small, grad_gain_one = moved
    grad_gain_one = jnp.sum(grad_gain_one, axis=(0, 1))
    summed_in = jnp.stack([flat(by_conv)[:inner], flat(by_gate)[:inner]]).astype(f32)
    middle = flat(middle)[:, :inner].astype(f32)
    small = flat(small)
    shared = small[small_rows : small_rows + shared_rows * width // LANES].reshape(shared_rows, width)
    small = small[:small_rows].reshape(-1, full)[:, :inner]
    return (
        layer_out.reshape(seqs, group, width),
        shared[experts + 1, 0],
        grad_tokens.reshape(seqs, group, width).astype(f32),
        grad_gain_one,
        summed_in.transpose(2, 0, 1),
        small[:taps],
        small[taps],
        middle[:maps].T,
        middle[maps : maps + rank],
        small[taps + 1],
        (small[taps + 3 : taps + 3 + states] * rate).T,
        small[taps + 2],
        flat(by_out)[:inner].astype(f32),
        shared[experts],
        shared[:experts].T,
        grad_first[None],
        grad_second[None],
    )


def solution(mesh):
    placed = (
        P(None, "seq", None),
        P(None, "seq", None),
        P(),
        P(),
        P(None, "seq"),
        P(),
        P(None, None, "chan"),
        P(None, "chan"),
        P("chan"),
        P("chan", None),
        P(None, "chan"),
        P("chan"),
        P("chan", None),
        P("chan"),
        P("chan", None),
        P(),
        P(),
        P("seq", None, None),
        P("seq", None, None),
    )
    return jax.shard_map(
        local,
        mesh=mesh,
        in_specs=placed,
        out_specs=(
            P(None, "seq", None),
            P(),
            P(None, "seq", None),
            P(),
            P(None, None, "chan"),
            P(None, "chan"),
            P("chan"),
            P("chan", None),
            P(None, "chan"),
            P("chan"),
            P("chan", None),
            P("chan"),
            P("chan", None),
            P(),
            P(),
            P("seq", None, "chan"),
            P("seq", "chan", None),
        ),
        check_vma=False,
    )
```

```python
import functools

import jax
import jax.numpy as jnp
from jax import lax
from jax.experimental import pallas as pl
from jax.experimental.pallas import tpu as pltpu
from jax.sharding import PartitionSpec as P

epsilon = 1e-05
log2e = 1.4426950408889634
cut = 1e30
MESH = pl.DeviceIdType.MESH
f32 = jnp.float32
bf16 = jnp.bfloat16
LANES = 128
MIB = 1024 * 1024
AHEAD = 12


def greet(axes):
    barrier = pltpu.get_barrier_semaphore()
    told = 0
    for axis, count in axes:
        me = lax.axis_index(axis)
        for k in range(1, count):
            pl.semaphore_signal(
                barrier, inc=1, device_id={axis: lax.rem(me + k, count)}, device_id_type=MESH
            )
        told += count - 1
    return told


def cuts_of(size):
    half = -(-size // 32) * 16
    return [(0, half), (half, size - half)] if half < size and size % 16 == 0 else [(0, size)]


def sems_of(item):
    copies = 2 * (item[2] - 1)
    return [pltpu.SemaphoreType.DMA] + [pltpu.SemaphoreType.DMA((copies,))] * 2


def flipped(i, mask):
    bit = 1
    while bit <= mask:
        if mask & bit:
            i = i + bit - 2 * bit * lax.rem(i // bit, 2)
        bit *= 2
    return i


def order_of(groups):
    masks, low, high = [], 1, groups - 1
    while low <= high:
        masks += [high] if low == high else [high, low]
        low, high = low + 1, high - 1
    return masks


class Riders:
    def __init__(self, items, xs, outs, sems):
        self.own, self.copies, self.chains = [], [], {}
        for i, item in enumerate(items):
            self.add(item, xs[i], outs[i], *sems[3 * i : 3 * i + 3])
        self.at = {axis: 0 for axis in self.chains}

    def start(self):
        for copy in self.copies + self.own:
            copy.start()
        for chain in self.chains.values():
            for first, _ in chain[:AHEAD]:
                first.start()
        return self

    def add(self, item, x_ref, o_ref, own_sem, send_sem, recv_sem):
        mode, axis, count = item
        me = lax.axis_index(axis)

        def remote(source, row, slot, to, cut=None):
            target = o_ref.at[row]
            if cut is not None:
                source, target = source.at[pl.ds(*cut)], o_ref.at[row, pl.ds(*cut)]
            return pltpu.make_async_remote_copy(
                src_ref=source,
                dst_ref=target,
                send_sem=send_sem.at[slot],
                recv_sem=recv_sem.at[slot],
                device_id={axis: to},
                device_id_type=MESH,
            )

        source = x_ref.at[me] if mode == "scatter" else x_ref
        self.own.append(pltpu.make_async_copy(source, o_ref.at[me], own_sem))
        if mode in ("gather", "scatter"):
            for mask in range(count - 1, 0, -1):
                to = flipped(me, mask)
                source = x_ref.at[to] if mode == "scatter" else x_ref
                self.copies.append(remote(source, me, mask - 1, to))
            return
        groups = count // mode
        side, place = lax.rem(me, mode), me // mode
        mates = [place * mode + lax.rem(side + j, mode) for j in range(1, mode)]
        slot = 0
        for mate in mates:
            self.copies.append(remote(x_ref, me, slot, mate))
            slot += 1
        chain = self.chains.setdefault(axis, [])
        for mask in order_of(groups):
            row = flipped(place, mask) * mode + side
            for cut in cuts_of(x_ref.shape[0]):
                first = remote(x_ref, me, slot, row, cut)
                slot += 1
                passed = []
                for mate in mates:
                    passed.append(remote(o_ref.at[row], row, slot, mate, cut))
                    slot += 1
                chain.append((first, passed))

    def left(self):
        return any(self.at[axis] < len(chain) for axis, chain in self.chains.items())

    def step(self):
        for axis in sorted(self.chains, reverse=True):
            i, chain = self.at[axis], self.chains[axis]
            if i == len(chain):
                continue
            self.at[axis] = i + 1
            first, passed = chain[i]
            first.wait_recv()
            for copy in passed:
                copy.start()
            if i + AHEAD < len(chain):
                chain[i + AHEAD][0].start()
            return

    def finish(self):
        while self.left():
            self.step()
        for copy in self.own + self.copies:
            copy.wait()
        for chain in self.chains.values():
            for first, passed in chain:
                first.wait_send()
                for copy in passed:
                    copy.wait()


def items_of(exchanges):
    return [(mode, axis, lax.axis_size(axis)) for _, mode, axis in exchanges]


def axes_of(items):
    return sorted({(axis, count) for _, axis, count in items})


def landed(x, item):
    shape = x.shape if item[0] == "scatter" else (item[2],) + x.shape
    return jax.ShapeDtypeStruct(shape, x.dtype)


def exchange_kernel(items, *refs):
    number = len(items)
    sems = refs[2 * number :]
    pl.semaphore_wait(pltpu.get_barrier_semaphore(), greet(axes_of(items)))
    Riders(items, refs[:number], refs[number : 2 * number], sems).start().finish()


def exchange(number, *exchanges):
    items = items_of(exchanges)
    return pl.pallas_call(
        functools.partial(exchange_kernel, items),
        out_shape=[landed(x, item) for (x, _, _), item in zip(exchanges, items)],
        in_specs=[pl.BlockSpec(memory_space=pl.ANY)] * len(items),
        out_specs=[pl.BlockSpec(memory_space=pl.ANY)] * len(items),
        scratch_shapes=[sem for item in items for sem in sems_of(item)],
        compiler_params=pltpu.CompilerParams(
            collective_id=number, has_side_effects=True, vmem_limit_bytes=16 * MIB
        ),
    )(*[x for x, _, _ in exchanges])


def greet_near(axis, count):
    barrier = pltpu.get_barrier_semaphore()
    me = lax.axis_index(axis)
    beside = me + 1 - 2 * lax.rem(me, 2)
    pl.semaphore_signal(barrier, inc=1, device_id={axis: beside}, device_id_type=MESH)
    for k in range(1, count // 2):
        pl.semaphore_signal(
            barrier, inc=1, device_id={axis: lax.rem(me + 2 * k, count)}, device_id_type=MESH
        )
    pl.semaphore_wait(barrier, count // 2)


def sum_kernel(axis, count, x_ref, o_ref, beside_in, pair, far_in, send_sem, recv_sem):
    me = lax.axis_index(axis)
    beside = me + 1 - 2 * lax.rem(me, 2)
    greet_near(axis, count)
    near = pltpu.make_async_remote_copy(
        src_ref=x_ref,
        dst_ref=beside_in,
        send_sem=send_sem.at[0],
        recv_sem=recv_sem.at[0],
        device_id={axis: beside},
        device_id_type=MESH,
    )
    near.start()
    near.wait_recv()
    pair[...] = (x_ref[...].astype(f32) + beside_in[...].astype(f32)).astype(bf16)
    copies = []
    for k in range(1, count // 2):
        copies.append(
            pltpu.make_async_remote_copy(
                src_ref=pair,
                dst_ref=far_in.at[k - 1],
                send_sem=send_sem.at[k],
                recv_sem=recv_sem.at[k],
                device_id={axis: lax.rem(me + 2 * k, count)},
                device_id_type=MESH,
            )
        )
        copies[-1].start()
    for copy in copies:
        copy.wait_recv()
    total = pair[...].astype(f32)
    for k in range(count // 2 - 1):
        total = total + far_in[k].astype(f32)
    o_ref[...] = total
    near.wait_send()
    for copy in copies:
        copy.wait_send()


def summed_over(x, axis, number):
    count = lax.axis_size(axis)
    return pl.pallas_call(
        functools.partial(sum_kernel, axis, count),
        out_shape=jax.ShapeDtypeStruct(x.shape, f32),
        in_specs=[pl.BlockSpec(memory_space=pltpu.VMEM)],
        out_specs=pl.BlockSpec(memory_space=pltpu.VMEM),
        scratch_shapes=[
            pltpu.VMEM(x.shape, bf16),
            pltpu.VMEM(x.shape, bf16),
            pltpu.VMEM((count // 2 - 1,) + x.shape, bf16),
            pltpu.SemaphoreType.DMA((count // 2,)),
            pltpu.SemaphoreType.DMA((count // 2,)),
        ],
        compiler_params=pltpu.CompilerParams(
            collective_id=number, has_side_effects=True, vmem_limit_bytes=16 * MIB
        ),
    )(x)


class Share:
    def __init__(self, axis, count, size, x_ref, near_in, pairs, far_in, near_send, near_recv, far_send, far_recv):
        self.groups, self.size, self.x = count // size, size, x_ref
        self.near_in, self.pairs, self.far_in = near_in, pairs, far_in
        me = lax.axis_index(axis)
        side, place = lax.rem(me, size), me // size
        self.rows, self.near, self.far = [], [], []
        for k in range(self.groups):
            group = flipped(place, (order_of(self.groups) + [0])[k])
            self.rows.append(group * size + side)
            self.near.append(
                [
                    pltpu.make_async_remote_copy(
                        src_ref=x_ref.at[group * size + lax.rem(side + j, size)],
                        dst_ref=near_in.at[k, j - 1],
                        send_sem=near_send.at[k, j - 1],
                        recv_sem=near_recv.at[k, j - 1],
                        device_id={axis: place * size + lax.rem(side + j, size)},
                        device_id_type=MESH,
                    )
                    for j in range(1, size)
                ]
            )
            if k < self.groups - 1:
                self.far.append(
                    pltpu.make_async_remote_copy(
                        src_ref=pairs.at[k],
                        dst_ref=far_in.at[k],
                        send_sem=far_send.at[k],
                        recv_sem=far_recv.at[k],
                        device_id={axis: self.rows[k]},
                        device_id_type=MESH,
                    )
                )

    def begin(self, k):
        for copy in self.near[k]:
            copy.start()

    def near_sum(self, k, wait=True):
        total = self.x[self.rows[k]].astype(f32)
        for j, copy in enumerate(self.near[k]):
            if wait:
                copy.wait_recv()
            total = total + self.near_in[k, j].astype(f32)
        return total

    def pass_on(self, k):
        if k < self.groups - 1:
            self.pairs[k] = self.near_sum(k).astype(self.pairs.dtype)
            self.far[k].start()
        else:
            for copy in self.near[k]:
                copy.wait_recv()

    def total(self):
        total = self.near_sum(self.groups - 1, False)
        for k, copy in enumerate(self.far):
            copy.wait_recv()
            total = total + self.far_in[k].astype(f32)
        return total

    def close(self):
        for copy in [copy for copies in self.near for copy in copies] + self.far:
            copy.wait_send()


def share_kernel(shares, items, *refs):
    many, number = len(shares), len(items)
    at = 0

    def take(k):
        nonlocal at
        at += k
        return refs[at - k : at]

    xs, riders, outs, rider_outs = take(many), take(number), take(many), take(number)
    tasks = [Share(axis, count, size, x, *take(7)) for (axis, count, size), x in zip(shares, xs)]
    axes = set(axes_of(items)) | {(axis, count) for axis, count, _ in shares}
    pl.semaphore_wait(pltpu.get_barrier_semaphore(), greet(sorted(axes)))
    turns = {}
    for (axis, _, _), task in zip(shares, tasks):
        turns.setdefault(axis, []).extend((task, k) for k in range(task.groups))
    for turn in turns.values():
        for task, k in turn[:AHEAD]:
            task.begin(k)
    under_way = Riders(items, riders, rider_outs, take(3 * number)).start()
    for i in range(max(len(turn) for turn in turns.values())):
        for turn in turns.values():
            if i < len(turn):
                task, k = turn[i]
                task.pass_on(k)
                if i + AHEAD < len(turn):
                    task, k = turn[i + AHEAD]
                    task.begin(k)
        under_way.step()
    for task, out in zip(tasks, outs):
        out[...] = task.total().astype(out.dtype)
    for task in tasks:
        task.close()
    under_way.finish()


def share_of(number, shares, *exchanges):
    items = items_of(exchanges)
    anywhere = [pl.BlockSpec(memory_space=pl.ANY)] * len(items)
    held = [pl.BlockSpec(memory_space=pltpu.VMEM)] * len(shares)
    scratch = []
    for x, axis, size, _ in shares:
        scratch += share_scratch(x, axis, size)
    return pl.pallas_call(
        functools.partial(
            share_kernel, [(axis, lax.axis_size(axis), size) for _, axis, size, _ in shares], items
        ),
        out_shape=[jax.ShapeDtypeStruct(x.shape[1:], kind) for x, _, _, kind in shares]
        + [landed(x, item) for (x, _, _), item in zip(exchanges, items)],
        in_specs=held + anywhere,
        out_specs=held + anywhere,
        scratch_shapes=scratch + [sem for item in items for sem in sems_of(item)],
        compiler_params=pltpu.CompilerParams(
            collective_id=number, has_side_effects=True, vmem_limit_bytes=32 * MIB
        ),
    )(*[share[0] for share in shares], *[x for x, _, _ in exchanges])


def turned(value):
    return pltpu.roll(value, value.shape[0] // 2, 0)


def carry_kernel(axis, count, back, items, *refs):
    number = len(items)
    local_ref, sums_ref, rate_ref = refs[:3]
    xs, o_ref, outs = refs[3 : 3 + number], refs[3 + number], refs[4 + number : 4 + 2 * number]
    send, got, send_sum, got_sum, total, enter = refs[4 + 2 * number : 10 + 2 * number]
    send_sem, recv_sem, send_sum_sem, recv_sum_sem = refs[10 + 2 * number : 14 + 2 * number]
    sems = refs[14 + 2 * number :]
    me = lax.axis_index(axis)
    states, rows, width = local_ref.shape
    half = rows // 2
    spans = []
    span = 1
    while span < count:
        spans.append(span)
        span *= 2
    sign = -1 if back else 1
    barrier = pltpu.get_barrier_semaphore()
    greeted = greet(axes_of(items))
    for span in spans:
        for by in (span, -span):
            there = me + by
            greeted = greeted + jnp.where((there >= 0) & (there < count), 1, 0)

            @pl.when((there >= 0) & (there < count))
            def _():
                pl.semaphore_signal(barrier, inc=1, device_id={axis: there}, device_id_type=MESH)

    upper = lax.broadcasted_iota(jnp.int32, (rows, width), 0) >= half
    first = upper if back else jnp.logical_not(upper)
    sums = sums_ref[...]
    sums_turned = turned(sums)
    sums_both = sums + sums_turned
    sums_first = jnp.where(first, sums, sums_turned)
    sums_last = jnp.where(first, sums_turned, sums)

    def packed_rate(j):
        return jnp.where(upper, rate_ref[pl.ds(2 * j + 1, 1), :], rate_ref[pl.ds(2 * j, 1), :])

    def both(j):
        even, odd = local_ref[2 * j], local_ref[2 * j + 1]
        low = jnp.where(upper, turned(odd), even)
        high = jnp.where(upper, odd, turned(even))
        return (high, low) if back else (low, high)

    for j in range(states // 2):
        opening, closing = both(j)
        total[j] = jnp.exp2(packed_rate(j) * sums_last) * opening + closing
        enter[j] = jnp.zeros((rows, width), f32)

    pl.semaphore_wait(barrier, greeted)
    under_way = Riders(items, xs, outs, sems).start()
    sums_total = sums_both
    sums_enter = jnp.zeros((rows, width), f32)
    for turn, span in enumerate(spans):
        to = me + sign * span
        origin = me - sign * span
        sends = (to >= 0) & (to < count)
        takes = (origin >= 0) & (origin < count)
        for j in range(0, states // 2, 2):
            send[turn, pl.ds(j * rows, 2 * rows), :] = jnp.concatenate([total[j], total[j + 1]], axis=0).astype(bf16)
        send_sum[turn] = sums_total
        copies = [
            pltpu.make_async_remote_copy(
                src_ref=source.at[turn],
                dst_ref=target.at[turn],
                send_sem=ssem.at[turn],
                recv_sem=rsem.at[turn],
                device_id={axis: to},
                device_id_type=MESH,
            )
            for source, target, ssem, rsem in (
                (send, got, send_sem, recv_sem),
                (send_sum, got_sum, send_sum_sem, recv_sum_sem),
            )
        ]

        @pl.when(sends)
        def _():
            for copy in copies:
                copy.start()

        @pl.when(jnp.logical_not(takes))
        def _():
            got[turn] = jnp.zeros(got.shape[1:], bf16)
            got_sum[turn] = jnp.zeros(got_sum.shape[1:], f32)

        @pl.when(takes)
        def _():
            for copy in copies:
                copy.wait_recv()

        for j in range(0, states // 2, 2):
            pair = got[turn, pl.ds(j * rows, 2 * rows), :].astype(f32)
            for i in (j, j + 1):
                came = pair[(i - j) * rows : (i - j + 1) * rows]
                rate = packed_rate(i)
                enter[i] = jnp.exp2(rate * sums_enter) * came + enter[i]
                total[i] = jnp.exp2(rate * sums_total) * came + total[i]
        sums_enter = sums_enter + got_sum[turn]
        sums_total = sums_total + got_sum[turn]

        @pl.when(sends)
        def _():
            for copy in copies:
                copy.wait_send()

    for j in range(states // 2):
        opening, _ = both(j)
        outer = enter[j]
        inner = jnp.exp2(packed_rate(j) * sums_first) * outer + opening
        low, high = (inner, outer) if back else (outer, inner)
        o_ref[2 * j] = jnp.where(upper, turned(high), low)
        o_ref[2 * j + 1] = jnp.where(upper, high, turned(low))
    under_way.finish()


def carried(local, sums, rate, axis, back, number, *exchanges):
    count = lax.axis_size(axis)
    states, rows, width = local.shape
    turns = max(1, (count - 1).bit_length())
    items = items_of(exchanges)
    anywhere = [pl.BlockSpec(memory_space=pl.ANY)] * len(items)
    return pl.pallas_call(
        functools.partial(carry_kernel, axis, count, back, items),
        out_shape=[jax.ShapeDtypeStruct(local.shape, f32)]
        + [landed(x, item) for (x, _, _), item in zip(exchanges, items)],
        in_specs=[pl.BlockSpec(memory_space=pltpu.VMEM)] * 3 + anywhere,
        out_specs=[pl.BlockSpec(memory_space=pltpu.VMEM)] + anywhere,
        scratch_shapes=[
            pltpu.VMEM((turns, states // 2 * rows, width), bf16),
            pltpu.VMEM((turns, states // 2 * rows, width), bf16),
            pltpu.VMEM((turns, rows, width), f32),
            pltpu.VMEM((turns, rows, width), f32),
            pltpu.VMEM((states // 2, rows, width), f32),
            pltpu.VMEM((states // 2, rows, width), f32),
            pltpu.SemaphoreType.DMA((turns,)),
            pltpu.SemaphoreType.DMA((turns,)),
            pltpu.SemaphoreType.DMA((turns,)),
            pltpu.SemaphoreType.DMA((turns,)),
        ]
        + [sem for item in items for sem in sems_of(item)],
        compiler_params=pltpu.CompilerParams(
            collective_id=number, has_side_effects=True, vmem_limit_bytes=24 * MIB
        ),
    )(local, sums, rate, *[x for x, _, _ in exchanges])


def spread(mapped_ref, first, wide_ref):
    count, steps, rows, lanes = wide_ref.shape
    column = lax.broadcasted_iota(jnp.int32, (mapped_ref.shape[1], lanes), 0)
    values = mapped_ref[...]
    for n in range(count):
        pick = (column == first + n).astype(bf16)
        wide_ref[n] = jnp.dot(values, pick, preferred_element_type=f32).reshape(steps, rows, lanes)


def rows_of(rate_ref, n, rows):
    return jnp.broadcast_to(rate_ref[n : n + 1, :], (rows, rate_ref.shape[1]))


def perm_of(steps, lines, seqs):
    rows = steps * lines
    laid = lax.broadcasted_iota(jnp.int32, (rows, rows), 0)
    natural = lax.broadcasted_iota(jnp.int32, (rows, rows), 1)
    line = laid % lines
    wanted = (line % seqs) * (rows // seqs) + (line // seqs) * steps + laid // lines
    return (natural == wanted).astype(bf16)


def unit_of(rows):
    return rows * lax.rsqrt(jnp.mean(rows * rows, axis=-1, keepdims=True) + epsilon)


def softplus(x):
    return jnp.maximum(x, 0.0) + jnp.log1p(jnp.exp(-jnp.abs(x)))


def sigmoid(x):
    return 1.0 / (1.0 + jnp.exp(-x))


def silu_slope(values, sigma):
    return sigma * (1.0 + values * (1.0 - sigma))


def dot(a, b):
    return jnp.dot(a, b, preferred_element_type=f32)


def dot_nt(a, b):
    return lax.dot_general(a, b, (((1,), (1,)), ((), ())), preferred_element_type=f32)


def dot_tn(a, b):
    return lax.dot_general(a, b, (((0,), (0,)), ((), ())), preferred_element_type=f32)


def front_kernel(seq_count, chan_count, tokens_ref, gain_ref, w_ref, taps_ref, bias_ref, xproj_ref, valid_ref,
                 normed_ref, ext_ref, pre_ref, gate_ref, mapped_ref,
                 halo, part, beside_in, pair, far_in, halo_send, halo_recv, send_sem, recv_sem):
    seqs, group, width = tokens_ref.shape
    steps, lines, full = pre_ref.shape
    taps, inner = taps_ref.shape[0], w_ref.shape[1]
    rim, rows, tail = taps - 1, steps * lines, halo.shape[1]
    here, me = lax.axis_index("seq"), lax.axis_index("chan")
    beside = me + 1 - 2 * lax.rem(me, 2)
    barrier = pltpu.get_barrier_semaphore()
    told = chan_count // 2
    for by in (1, -1):
        there = here + by
        near = (there >= 0) & (there < seq_count)
        told = told + jnp.where(near, 1, 0)

        @pl.when(near)
        def _():
            pl.semaphore_signal(barrier, inc=1, device_id={"seq": there}, device_id_type=MESH)

    pl.semaphore_signal(barrier, inc=1, device_id={"chan": beside}, device_id_type=MESH)
    for k in range(1, chan_count // 2):
        to = lax.rem(me + 2 * k, chan_count)
        pl.semaphore_signal(barrier, inc=1, device_id={"chan": to}, device_id_type=MESH)
    pl.semaphore_wait(barrier, told)
    ends = pltpu.make_async_remote_copy(
        src_ref=tokens_ref.at[:, pl.ds(group - tail, tail), :],
        dst_ref=halo,
        send_sem=halo_send,
        recv_sem=halo_recv,
        device_id={"seq": here + 1},
        device_id_type=MESH,
    )

    @pl.when(here + 1 < seq_count)
    def _():
        ends.start()

    def normed_of(rows_low):
        return (unit_of(rows_low.astype(f32)) * gain_ref[...]).astype(bf16)

    perm = perm_of(steps, lines, seqs)
    normed = dot(perm, normed_of(tokens_ref[...].reshape(rows, width))).astype(bf16)
    normed_ref[...] = normed
    conv_in = dot_nt(normed, w_ref[0]).astype(bf16).astype(f32)
    ext_ref[pl.ds(rim, steps), :, pl.ds(0, inner)] = conv_in.reshape(steps, lines, inner)
    gate_ref[:, :, pl.ds(0, inner)] = dot_nt(normed, w_ref[1]).reshape(steps, lines, inner)
    if full > inner:
        ext_ref[:, :, pl.ds(inner, full - inner)] = jnp.zeros((steps + rim, lines, full - inner), f32)
        gate_ref[:, :, pl.ds(inner, full - inner)] = jnp.zeros((steps, lines, full - inner), f32)

    @pl.when(here == 0)
    def _():
        halo[...] = jnp.zeros(halo.shape, bf16)

    @pl.when(here > 0)
    def _():
        ends.wait_recv()

    prior = dot_nt(normed_of(halo[...].reshape(seqs * tail, width)), w_ref[0]).astype(bf16)
    to = lax.broadcasted_iota(jnp.int32, (rim * lines, seqs * tail), 0)
    origin = lax.broadcasted_iota(jnp.int32, (rim * lines, seqs * tail), 1)
    pick = (to % lines < seqs) & (origin == (to % lines) * tail + tail - rim + to // lines)
    prior = dot(pick.astype(bf16), prior).reshape(rim, lines, inner)
    upper = lax.broadcasted_iota(jnp.int32, (lines, inner), 0) >= seqs
    for j in range(rim):
        own = turned(ext_ref[steps + j, :, pl.ds(0, inner)])
        ext_ref[j, :, pl.ds(0, inner)] = jnp.where(upper, own, prior[j])
    pre = jnp.broadcast_to(bias_ref[...], (steps, lines, full))
    for k in range(taps):
        pre = pre + taps_ref[k : k + 1, :] * ext_ref[pl.ds(k, steps)] * valid_ref[:, :, k : k + 1]
    pre_ref[...] = pre
    act_low = (pre * sigmoid(pre)).astype(bf16).reshape(rows, full)
    part[...] = dot_nt(act_low, xproj_ref[...]).astype(bf16)
    near = pltpu.make_async_remote_copy(
        src_ref=part,
        dst_ref=beside_in,
        send_sem=send_sem.at[0],
        recv_sem=recv_sem.at[0],
        device_id={"chan": beside},
        device_id_type=MESH,
    )
    near.start()
    near.wait_recv()
    pair[...] = (part[...].astype(f32) + beside_in[...].astype(f32)).astype(bf16)
    copies = []
    for k in range(1, chan_count // 2):
        copies.append(
            pltpu.make_async_remote_copy(
                src_ref=pair,
                dst_ref=far_in.at[k - 1],
                send_sem=send_sem.at[k],
                recv_sem=recv_sem.at[k],
                device_id={"chan": lax.rem(me + 2 * k, chan_count)},
                device_id_type=MESH,
            )
        )
        copies[-1].start()
    for copy in copies:
        copy.wait_recv()
    total = pair[...].astype(f32)
    for k in range(chan_count // 2 - 1):
        total = total + far_in[k].astype(f32)
    mapped_ref[...] = total.astype(bf16)
    near.wait_send()
    for copy in copies:
        copy.wait_send()

    @pl.when(here + 1 < seq_count)
    def _():
        ends.wait_send()


def front(tokens, gain, w_in, taps, bias, xproj, valid, full, number):
    seqs, group, width = tokens.shape
    steps, lines = valid.shape[:2]
    count, rows, maps = lax.axis_size("chan"), steps * lines, xproj.shape[0]
    tail = min(16, group)
    return pl.pallas_call(
        functools.partial(front_kernel, lax.axis_size("seq"), count),
        out_shape=[
            jax.ShapeDtypeStruct((rows, width), bf16),
            jax.ShapeDtypeStruct((steps + taps.shape[0] - 1, lines, full), f32),
            jax.ShapeDtypeStruct((steps, lines, full), f32),
            jax.ShapeDtypeStruct((steps, lines, full), f32),
            jax.ShapeDtypeStruct((rows, maps), bf16),
        ],
        in_specs=[pl.BlockSpec(memory_space=pltpu.VMEM)] * 7,
        out_specs=[pl.BlockSpec(memory_space=pltpu.VMEM)] * 5,
        scratch_shapes=[
            pltpu.VMEM((seqs, tail, width), bf16),
            pltpu.VMEM((rows, maps), bf16),
            pltpu.VMEM((rows, maps), bf16),
            pltpu.VMEM((rows, maps), bf16),
            pltpu.VMEM((count // 2 - 1, rows, maps), bf16),
            pltpu.SemaphoreType.DMA,
            pltpu.SemaphoreType.DMA,
            pltpu.SemaphoreType.DMA((count // 2,)),
            pltpu.SemaphoreType.DMA((count // 2,)),
        ],
        compiler_params=pltpu.CompilerParams(
            collective_id=number, has_side_effects=True, vmem_limit_bytes=48 * MIB
        ),
    )(tokens, gain, w_in, taps, bias, xproj, valid)


def totals_kernel(rank, taps, pre_ref, mapped_ref, dtw_ref, bias_ref, valid_ref, rate_ref,
                  dt_ref, step_ref, drive_ref, last_ref, sums_ref, wide):
    count, steps, rows, lanes = wide.shape

    @pl.when(pl.program_id(0) == 0)
    def _():
        spread(mapped_ref, rank, wide)

    dt_pre = (dot(mapped_ref[...], dtw_ref[...]) + bias_ref[...]).reshape(steps, rows, lanes)
    delta = softplus(dt_pre)
    pre = pre_ref[...]
    dt_ref[...] = dt_pre
    step_ref[...] = jnp.where(valid_ref[:, :, taps : taps + 1] > 0.5, delta, cut)
    drive_ref[...] = delta * pre * sigmoid(pre)
    rates = [rows_of(rate_ref, n, rows) for n in range(count)]
    zero = jnp.zeros((rows, lanes), f32)

    def one(p, held):
        states, sums = held
        step, drive = step_ref[p], drive_ref[p]
        states = tuple(
            jnp.exp2(step * rates[n]) * states[n] + drive * wide[n, p] for n in range(count)
        )
        return states, sums + step

    states, sums = lax.fori_loop(0, steps, one, ((zero,) * count, zero), unroll=2)
    for n in range(count):
        last_ref[n] = states[n]
    sums_ref[...] = sums


def states_kernel(rank, seqs, step_ref, drive_ref, mapped_ref, rate_ref, enter_ref, pre_ref, gate_ref, skip_ref, out_w_ref,
                  y_ref, gated_ref, state_ref, out_ref, wide_in, wide_read, total):
    count, steps, rows, lanes = wide_in.shape
    place = pl.program_id(0)

    @pl.when(place == 0)
    def _():
        spread(mapped_ref, rank, wide_in)
        spread(mapped_ref, rank + count, wide_read)
        total[...] = jnp.zeros_like(total)

    rates = [rows_of(rate_ref, n, rows) for n in range(count)]

    def one(p, states):
        step, drive = step_ref[p], drive_ref[p]
        states = tuple(
            jnp.exp2(step * rates[n]) * states[n] + drive * wide_in[n, p] for n in range(count)
        )
        terms = [states[n] * wide_read[n, p] for n in range(count)]
        while len(terms) > 1:
            terms = [a + b for a, b in zip(terms[::2], terms[1::2])]
        y_ref[p] = terms[0]
        for n in range(count):
            state_ref[p, n] = states[n]
        return states

    lax.fori_loop(0, steps, one, tuple(enter_ref[n] for n in range(count)), unroll=2)
    pre, gate = pre_ref[...], gate_ref[...]
    y_full = y_ref[...] + skip_ref[...] * (pre * sigmoid(pre))
    y_ref[...] = y_full
    gated = (y_full * (gate * sigmoid(gate))).astype(bf16).reshape(steps * rows, lanes)
    gated_ref[...] = gated
    total[...] += dot(gated, out_w_ref[...])

    @pl.when(place == pl.num_programs(0) - 1)
    def _():
        perm = perm_of(steps, rows, seqs)
        out_ref[...] = dot_tn(perm, total[...].astype(bf16)).astype(bf16)


def back_totals_kernel(rank, seqs, step_ref, mapped_ref, rate_ref, mixed_ref, normed_ref, out_w_ref, gate_ref, y_ref, gated_ref,
                       pre_ref, grad_y_ref, grad_z_ref, grad_out_ref, grad_gate_ref, skip_ref, last_ref,
                       wide, mixed):
    count, steps, rows, lanes = wide.shape

    @pl.when(pl.program_id(0) == 0)
    def _():
        spread(mapped_ref, rank + count, wide)
        mixed[...] = dot(perm_of(steps, rows, seqs), mixed_ref[...]).astype(bf16)

    grad_gated = dot_nt(mixed[...], out_w_ref[...]).reshape(steps, rows, lanes)
    gate, pre = gate_ref[...], pre_ref[...]
    sigma = sigmoid(gate)
    grad_y = grad_gated * (gate * sigma)
    grad_y_ref[...] = grad_y
    grad_z = (grad_gated * y_ref[...] * silu_slope(gate, sigma)).astype(bf16)
    grad_z = grad_z.reshape(steps * rows, lanes)
    grad_z_ref[...] = grad_z
    skip_ref[...] = jnp.sum(grad_y * (pre * sigmoid(pre)), axis=0)
    grad_out_ref[...] = dot_tn(gated_ref[...], mixed[...]).astype(bf16)
    grad_gate_ref[...] = dot_tn(grad_z, normed_ref[...]).astype(bf16)
    rates = [rows_of(rate_ref, n, rows) for n in range(count)]
    zero = jnp.zeros((rows, lanes), f32)

    def one(turn, held):
        p = steps - 1 - turn
        step, grad_y = step_ref[p], grad_y_ref[p]
        return tuple(
            jnp.exp2(step * rates[n]) * (held[n] + grad_y * wide[n, p]) for n in range(count)
        )

    held = lax.fori_loop(0, steps, one, (zero,) * count, unroll=2)
    for n in range(count):
        last_ref[n] = held[n]


def back_kernel(rank, pieces, shares, items, step_ref, drive_ref, grad_y_ref, mapped_ref, rate_ref, first_ref, state_ref, enter_ref, dt_ref,
                pre_ref, dtw_ref, *refs):
    many, number = len(shares), len(items)
    at = 0

    def take(k):
        nonlocal at
        at += k
        return refs[at - k : at]

    xs, riders = take(many), take(number)
    side_ref, log_ref, bias_ref, grad_dtw_ref, low_ref = take(5)
    parts, rider_outs = take(many), take(number)
    wide_in, wide_read, sum_in, sum_read, to_input, to_decay, total = take(7)
    count, steps, rows, lanes = wide_in.shape
    place, tiles = pl.program_id(0), pl.num_programs(0)
    kept, kept_sem = take(many), take(1)[0]
    tasks = [Share(*share, held, *take(7)) for share, held in zip(shares, kept)]
    under_way = Riders(items, riders, rider_outs, take(3 * number))
    turn = [(task, k) for task in tasks for k in range(task.groups)]

    @pl.when(place == 0)
    def _():
        copies = [
            pltpu.make_async_copy(x, held, kept_sem.at[i]) for i, (x, held) in enumerate(zip(xs, kept))
        ]
        for copy in copies:
            copy.start()
        axes = {share[:2] for share in shares} | set(axes_of(items))
        pl.semaphore_wait(pltpu.get_barrier_semaphore(), greet(sorted(axes)))
        for copy in copies:
            copy.wait()
        for task, k in turn[:3]:
            task.begin(k)
        under_way.start()
        spread(mapped_ref, rank, wide_in)
        spread(mapped_ref, rank + count, wide_read)
        sum_in[...] = jnp.zeros_like(sum_in)
        sum_read[...] = jnp.zeros_like(sum_read)
        total[...] = jnp.zeros_like(total)

    moments = 2 * (pieces - 1)
    each = -(-len(turn) // moments)

    def pass_on(late):
        for piece in range(1, pieces):
            moment = 2 * (piece - 1) + late

            @pl.when(place == piece)
            def _():
                for i in range(moment * each, min((moment + 1) * each, len(turn))):
                    turn[i][0].pass_on(turn[i][1])
                    if i + 3 < len(turn):
                        turn[i + 3][0].begin(turn[i + 3][1])

    pass_on(0)
    rates = [rows_of(rate_ref, n, rows) for n in range(count)]
    for n in range(count):
        log_ref[n] = jnp.zeros((rows, lanes), f32)

    def step_back(p, carry, prior_of):
        step, drive, grad_y = step_ref[p], drive_ref[p], grad_y_ref[p]
        inputs = jnp.zeros((rows, lanes), f32)
        decays = jnp.zeros((rows, lanes), f32)
        new, grads = [], []
        for n in range(count):
            grad = grad_y * wide_read[n, p] + carry[n]
            passed = jnp.exp2(step * rates[n]) * grad
            new.append(passed)
            grad_decay = passed * prior_of(n)
            decays = decays + grad_decay * rates[n]
            log_ref[n] += grad_decay * step
            inputs = inputs + grad * wide_in[n, p]
            grads.append(grad)
        to_input[p] = inputs
        to_decay[p] = decays
        grads = jnp.concatenate(grads, axis=0).astype(bf16)
        held_states = state_ref[p].reshape(count * rows, lanes).astype(bf16)
        sum_in[p] += dot_nt(drive.astype(bf16), grads)
        sum_read[p] += dot_nt(grad_y.astype(bf16), held_states)
        return tuple(new)

    def one(turn, carry):
        p = steps - 1 - turn
        return step_back(p, carry, lambda n: state_ref[p - 1, n])

    carry = tuple(enter_ref[n] for n in range(count))
    unroll = 7 if (steps - 1) % 7 == 0 else 1
    middle = (steps - 1) // unroll // 2 * unroll
    carry = lax.fori_loop(0, middle, one, carry, unroll=unroll)
    pass_on(1)
    carry = lax.fori_loop(middle, steps - 1, one, carry, unroll=unroll)
    step_back(0, carry, lambda n: first_ref[n])
    dt_pre, pre = dt_ref[...], pre_ref[...]
    inputs = to_input[...]
    side_ref[...] = inputs * softplus(dt_pre)
    grad_delta = to_decay[...] * (1.0 / log2e) + inputs * (pre * sigmoid(pre))
    grad_dt = grad_delta * sigmoid(dt_pre)
    bias_ref[...] = jnp.sum(grad_dt, axis=0)
    grad_dt = grad_dt.astype(bf16).reshape(steps * rows, lanes)
    grad_dtw_ref[...] = dot_tn(mapped_ref[...], grad_dt)
    total[...] += dot_nt(grad_dt, dtw_ref[...])

    @pl.when(place == tiles - 1)
    def _():
        wide = count * rows
        line = lax.broadcasted_iota(jnp.int32, (steps * rows, wide), 0) % rows
        lane = lax.broadcasted_iota(jnp.int32, (steps * rows, wide), 1)
        state = lax.broadcasted_iota(jnp.int32, (wide, total.shape[1]), 0) // rows
        column = lax.broadcasted_iota(jnp.int32, (wide, total.shape[1]), 1)
        sums = total[...]
        for which, source in enumerate((sum_in, sum_read)):
            values = jnp.where(lane % rows == line, source[...].reshape(steps * rows, wide), 0.0)
            pick = (column == rank + which * count + state).astype(bf16)
            sums = sums + dot(values.astype(bf16), pick)
        low_ref[...] = sums.astype(bf16)
        for task, part in zip(tasks, parts):
            part[...] = task.total().astype(bf16)
            task.close()
        under_way.finish()


def conv_back_kernel(taps, grad_mapped_ref, grad_y_ref, side_ref, pre_ref, ext_ref, skip_ref, xproj_ref, taps_ref, valid_ref,
                     grad_ref, rim_ref, grad_xproj_ref, sums_ref, ext_grad):
    steps, rows, lanes = pre_ref.shape
    rim = taps - 1
    pre = pre_ref[...]
    sigma = sigmoid(pre)
    grad_act = dot(grad_mapped_ref[...], xproj_ref[...]).reshape(steps, rows, lanes)
    grad_act = grad_act + grad_y_ref[...] * skip_ref[...] + side_ref[...]
    grad_pre = grad_act * silu_slope(pre, sigma)
    act_low = (pre * sigma).astype(bf16).reshape(steps * rows, lanes)
    grad_xproj_ref[...] = dot_tn(grad_mapped_ref[...], act_low)
    ext_grad[...] = jnp.zeros_like(ext_grad)
    for k in range(taps):
        masked = grad_pre * valid_ref[:, :, k : k + 1]
        sums_ref[k] = jnp.sum(masked * ext_ref[pl.ds(k, steps)], axis=0)
        ext_grad[pl.ds(k, steps)] += masked * taps_ref[k : k + 1, :]
    sums_ref[taps] = jnp.sum(grad_pre, axis=0)
    upper = lax.broadcasted_iota(jnp.int32, (rows, lanes), 0) >= rows // 2
    for j in range(rim):
        edge = ext_grad[j]
        rim_ref[j] = edge
        ext_grad[steps + j] += jnp.where(upper, 0.0, turned(edge))
    grad_ref[...] = ext_grad[pl.ds(rim, steps)]


def ends_kernel(count, items, tokens_ref, grad_ref, rim_ref, grad_z_ref, normed_ref, w_ref, *refs):
    number = len(items)
    xs, refs = refs[:number], refs[number:]
    grad_conv_ref, part_ref, gain_ref = refs[:3]
    outs, (came, send_sem, recv_sem), sems = refs[3 : 3 + number], refs[3 + number : 6 + number], refs[6 + number :]
    steps, lines, full = grad_ref.shape
    seqs, group, width = tokens_ref.shape
    rows, inner, rim = steps * lines, w_ref.shape[1], rim_ref.shape[0]
    here = lax.axis_index("seq")
    told = greet(sorted({("seq", count)} | set(axes_of(items))))
    pl.semaphore_wait(pltpu.get_barrier_semaphore(), told)
    edge = pltpu.make_async_remote_copy(
        src_ref=rim_ref,
        dst_ref=came,
        send_sem=send_sem,
        recv_sem=recv_sem,
        device_id={"seq": here - 1},
        device_id_type=MESH,
    )

    @pl.when(here > 0)
    def _():
        edge.start()

    under_way = Riders(items, xs, outs, sems).start()
    unit = unit_of(tokens_ref[...].reshape(rows, width).astype(f32))
    under_way.step()
    by_gate = dot(grad_z_ref[:, pl.ds(0, inner)], w_ref[1])
    under_way.step()

    @pl.when(here == count - 1)
    def _():
        came[...] = jnp.zeros(came.shape, f32)

    @pl.when(here < count - 1)
    def _():
        edge.wait_recv()

    upper = lax.broadcasted_iota(jnp.int32, (lines, full), 0) >= lines // 2
    last = [
        (grad_ref[steps - rim + j] + jnp.where(upper, turned(came[j]), 0.0))[None] for j in range(rim)
    ]
    grad = jnp.concatenate([grad_ref[pl.ds(0, steps - rim)]] + last, axis=0)
    grad = grad.reshape(rows, full).astype(bf16)
    for j in range(0, inner, LANES):
        many = min(LANES, inner - j)
        piece = dot_tn(grad[:, j : j + many], normed_ref[...])
        grad_conv_ref[pl.ds(j, many), :] = piece.astype(bf16)
        under_way.step()
    perm = perm_of(steps, lines, seqs)
    tile = next(t for t in (384, LANES, width) if width % t == 0)
    for j in range(0, width, tile):
        piece = dot(grad[:, :inner], w_ref[0, :, pl.ds(j, tile)]) + by_gate[:, j : j + tile]
        piece = dot_tn(perm, piece.astype(bf16))
        part_ref[:, pl.ds(j, tile)] = piece.astype(bf16)
        gain_ref[:, pl.ds(j, tile)] = jnp.sum(piece * unit[:, j : j + tile], axis=0, keepdims=True)
        under_way.step()
    under_way.finish()

    @pl.when(here > 0)
    def _():
        edge.wait_send()


def ends(tokens, grad, rim, grad_z, normed, w_in, number, *exchanges):
    steps, lines, full = grad.shape
    rows, width = normed.shape
    items = items_of(exchanges)
    anywhere = [pl.BlockSpec(memory_space=pl.ANY)] * len(items)
    return pl.pallas_call(
        functools.partial(ends_kernel, lax.axis_size("seq"), items),
        out_shape=[
            jax.ShapeDtypeStruct((w_in.shape[1], width), bf16),
            jax.ShapeDtypeStruct((rows, width), bf16),
            jax.ShapeDtypeStruct((1, width), f32),
        ]
        + [landed(x, item) for (x, _, _), item in zip(exchanges, items)],
        in_specs=[pl.BlockSpec(memory_space=pltpu.VMEM)] * 6 + anywhere,
        out_specs=[pl.BlockSpec(memory_space=pltpu.VMEM)] * 3 + anywhere,
        scratch_shapes=[
            pltpu.VMEM(rim.shape, f32),
            pltpu.SemaphoreType.DMA,
            pltpu.SemaphoreType.DMA,
        ]
        + [sem for item in items for sem in sems_of(item)],
        compiler_params=pltpu.CompilerParams(
            collective_id=number, has_side_effects=True, vmem_limit_bytes=48 * MIB
        ),
    )(tokens, grad, rim, grad_z, normed, w_in, *[x for x, _, _ in exchanges])


def hits_of(routes, experts, part, most, slots):
    rows = routes.shape[0]
    chosen = (lax.broadcasted_iota(jnp.int32, (rows, experts), 1) == routes).astype(f32)
    row = lax.broadcasted_iota(jnp.int32, (rows, rows), 0)
    other = lax.broadcasted_iota(jnp.int32, (rows, rows), 1)
    earlier = (other < row) & (row // part == other // part)
    ranks = jnp.sum(dot(earlier.astype(bf16), chosen.astype(bf16)) * chosen, axis=1, keepdims=True)
    slot = lax.broadcasted_iota(jnp.int32, (rows, 1), 0) // part * most + ranks.astype(jnp.int32)
    column = lax.broadcasted_iota(jnp.int32, (rows, experts * slots), 1)
    return chosen, (column == routes * slots + slot).astype(bf16)


def route_kernel(part, most, slots, tokens_ref, mixed_ref, gain_ref, routes_ref, router_ref,
                 hidden_ref, normed_ref, probs_ref, chosen_ref, hit_ref, packed_ref):
    hidden = tokens_ref[...].astype(f32) + mixed_ref[...]
    hidden_ref[...] = hidden
    normed = (unit_of(hidden) * gain_ref[...]).astype(bf16)
    normed_ref[...] = normed
    logits = dot_nt(normed, router_ref[...])
    raised = jnp.exp(logits - jnp.max(logits, axis=1, keepdims=True))
    probs_ref[...] = raised / jnp.sum(raised, axis=1, keepdims=True)
    chosen, hit = hits_of(routes_ref[...], router_ref.shape[0], part, most, slots)
    chosen_ref[...] = chosen
    hit_ref[...] = hit
    packed_ref[...] = dot_tn(hit, normed).astype(bf16)


def loss_kernel(group, lengths_ref, came_ref, back_ref, hit_ref, hidden_ref, probs_ref, chosen_ref, teacher_ref,
                layer_ref, grad_layer_ref, grad_logit_ref, loss_ref, packed_ref):
    rows, width = hidden_ref.shape
    seqs = lengths_ref.shape[0]
    expert = dot(back_ref[...], came_ref[...])
    probs, chosen = probs_ref[...], chosen_ref[...]
    gate = jnp.sum(probs * chosen, axis=1, keepdims=True)
    layer = hidden_ref[...] + gate * expert
    layer_ref[...] = layer.astype(bf16)
    flat_row = lax.axis_index("chan") * rows + lax.broadcasted_iota(jnp.int32, (rows, 1), 0)
    length = jnp.zeros((rows, 1), jnp.int32)
    total = 0
    for s in range(seqs):
        length = jnp.where(flat_row // group == s, lengths_ref[s], length)
        total = total + lengths_ref[s]
    scale = 1.0 / jnp.broadcast_to(total, (rows, 1)).astype(f32)
    at = lax.axis_index("seq") * group + flat_row % group
    mask = jnp.where(at < length, scale, 0.0)
    error = layer - teacher_ref[...].astype(f32)
    scaled = mask * error
    lost = jnp.sum(scaled * error, axis=0, keepdims=True)
    loss_ref[...] = jnp.broadcast_to(jnp.sum(lost, axis=1, keepdims=True), (1, width))
    grad_layer = 2.0 * scaled
    grad_layer_ref[...] = grad_layer
    grad_gate = jnp.sum(grad_layer * expert, axis=1, keepdims=True)
    grad_logit_ref[...] = grad_gate * gate * (chosen - probs)
    packed_ref[...] = dot_tn(hit_ref[...], (gate * grad_layer).astype(bf16)).astype(bf16)


def norm_back_kernel(came_ref, back_ref, grad_logit_ref, router_ref, normed_ref, hidden_ref, grad_layer_ref, gain_ref, loss_ref,
                     grad_ref, low_ref, shared_ref):
    experts = router_ref.shape[0]
    grad_logit = grad_logit_ref[...].astype(bf16)
    grad_normed = dot(back_ref[...], came_ref[...]) + dot(grad_logit, router_ref[...])
    hidden = hidden_ref[...]
    inverse = lax.rsqrt(jnp.mean(hidden * hidden, axis=1, keepdims=True) + epsilon)
    unit = hidden * inverse
    shared_ref[...] = jnp.zeros_like(shared_ref)
    shared_ref[pl.ds(0, experts), :] = dot_tn(grad_logit, normed_ref[...])
    shared_ref[pl.ds(experts, 1), :] = jnp.sum(grad_normed * unit, axis=0, keepdims=True)
    shared_ref[pl.ds(experts + 1, 1), :] = loss_ref[...]
    grad = grad_layer_ref[...] + norm_back(grad_normed, unit, inverse, gain_ref[...])
    grad_ref[...] = grad
    low_ref[...] = grad.astype(bf16)


def at_once(kernel, ins, outs, scalars=0):
    spaces = [pltpu.SMEM] * scalars + [pltpu.VMEM] * (len(ins) - scalars)
    return pl.pallas_call(
        kernel,
        in_specs=[pl.BlockSpec(memory_space=space) for space in spaces],
        out_specs=[pl.BlockSpec(memory_space=pltpu.VMEM)] * len(outs),
        out_shape=[jax.ShapeDtypeStruct(shape, dtype) for shape, dtype in outs],
        compiler_params=pltpu.CompilerParams(vmem_limit_bytes=32 * MIB),
        cost_estimate=pl.CostEstimate(flops=1000, bytes_accessed=1000, transcendentals=0),
    )(*ins)


def expert_kernel(x_ref, first_ref, second_ref, hidden_ref, slope_ref, result_ref, total):
    place = pl.program_id(0)

    @pl.when(place == 0)
    def _():
        total[...] = jnp.zeros_like(total)

    pre = dot(x_ref[...], first_ref[...])
    cdf = 0.5 * (1.0 + lax.erf(pre * 0.7071067811865476))
    hidden = (pre * cdf).astype(bf16)
    hidden_ref[0] = hidden
    slope = cdf + pre * (jnp.exp(-0.5 * pre * pre) * 0.3989422804014327)
    slope_ref[...] = slope.astype(bf16)
    total[...] += dot(hidden, second_ref[...])

    @pl.when(place == pl.num_programs(0) - 1)
    def _():
        result_ref[...] = total[...].astype(bf16)


def expert_back_kernel(grad_ref, first_ref, second_ref, slope_ref, grad_pre_ref, result_ref, total):
    place = pl.program_id(0)

    @pl.when(place == 0)
    def _():
        total[...] = jnp.zeros_like(total)

    grad = dot_nt(grad_ref[...], second_ref[...]) * slope_ref[...].astype(f32)
    grad = grad.astype(bf16)
    grad_pre_ref[0] = grad
    total[...] += dot_nt(grad, first_ref[...])

    @pl.when(place == pl.num_programs(0) - 1)
    def _():
        result_ref[...] = total[...].astype(bf16)


def expert(x, first, second, parts, slope=None):
    rows, width = x.shape
    units = first.shape[1] // parts
    tile = next((t for t in (768, 384, 256, 128) if units % t == 0), None)
    low = jax.ShapeDtypeStruct((rows, width), bf16)
    if tile is None:

        def split(h):
            return h.reshape(rows, parts, units).transpose(1, 0, 2)

        if slope is not None:
            grad = (dot_nt(x, second) * slope.astype(f32)).astype(bf16)
            return split(grad), dot_nt(grad, first).astype(bf16)
        pre = dot(x, first)
        cdf = 0.5 * (1.0 + lax.erf(pre * 0.7071067811865476))
        hidden = (pre * cdf).astype(bf16)
        slope = cdf + pre * (jnp.exp(-0.5 * pre * pre) * 0.3989422804014327)
        return split(hidden), slope.astype(bf16), dot(hidden, second).astype(bf16)
    each = units // tile
    columns = pl.BlockSpec((width, tile), lambda i: (0, i))
    lines = pl.BlockSpec((tile, width), lambda i: (i, 0))
    everything = pl.BlockSpec((rows, width), lambda i: (0, 0))
    slopes = pl.BlockSpec((rows, tile), lambda i: (0, i))
    hiddens = pl.BlockSpec((1, rows, tile), lambda i: (i // each, 0, i % each))
    hidden_shape = jax.ShapeDtypeStruct((parts, rows, units), bf16)
    back = slope is not None
    return pl.pallas_call(
        expert_back_kernel if back else expert_kernel,
        grid=(parts * each,),
        in_specs=[everything, columns, lines] + ([slopes] if back else []),
        out_specs=[hiddens] + ([] if back else [slopes]) + [everything],
        out_shape=[hidden_shape]
        + ([] if back else [jax.ShapeDtypeStruct((rows, first.shape[1]), bf16)])
        + [low],
        scratch_shapes=[pltpu.VMEM((rows, width), f32)],
        compiler_params=pltpu.CompilerParams(vmem_limit_bytes=60 * MIB),
        cost_estimate=pl.CostEstimate(flops=1000, bytes_accessed=1000, transcendentals=0),
    )(x, first, second, *([slope] if back else []))


def widen_kernel(conv_ref, gate_ref, out_ref, tokens_ref, grad_in_ref, grad_out_ref, grad_tokens_ref):
    grad_in_ref[0] = conv_ref[...].astype(f32)
    grad_in_ref[1] = gate_ref[...].astype(f32)
    grad_out_ref[...] = out_ref[...].astype(f32)
    grad_tokens_ref[...] = tokens_ref[...].astype(f32)


def widened(conv, gate, out, tokens, inner):
    width, rows = conv.shape[1], tokens.shape[0]
    pieces = next(n for n in (4, 2, 1) if inner % (16 * n) == 0 and rows % (16 * n) == 0)
    each, lines = inner // pieces, rows // pieces
    block = pl.BlockSpec((each, width), lambda i: (i, 0))
    row_block = pl.BlockSpec((lines, width), lambda i: (i, 0))
    return pl.pallas_call(
        widen_kernel,
        grid=(pieces,),
        in_specs=[block] * 3 + [row_block],
        out_specs=[pl.BlockSpec((2, each, width), lambda i: (0, i, 0)), block, row_block],
        out_shape=[
            jax.ShapeDtypeStruct((2, inner, width), f32),
            jax.ShapeDtypeStruct((inner, width), f32),
            jax.ShapeDtypeStruct((rows, width), f32),
        ],
        compiler_params=pltpu.CompilerParams(vmem_limit_bytes=48 * MIB),
        cost_estimate=pl.CostEstimate(flops=1000, bytes_accessed=1000, transcendentals=0),
    )(conv, gate, out, tokens)


def block_of(shape, kind):
    if kind == "tile":
        return pl.BlockSpec(shape[:-1] + (LANES,), lambda i: (0,) * (len(shape) - 1) + (i,))
    if kind == "rows":
        return pl.BlockSpec((LANES,) + shape[1:], lambda i: (i,) + (0,) * (len(shape) - 1))
    if kind == "any":
        return pl.BlockSpec(memory_space=pl.ANY)
    return pl.BlockSpec(shape, lambda i: (0,) * len(shape))


def share_scratch(x, axis, size):
    groups = lax.axis_size(axis) // size
    part = x.shape[1:]
    return [
        pltpu.VMEM((groups, size - 1) + part, x.dtype),
        pltpu.VMEM((groups - 1,) + part, x.dtype),
        pltpu.VMEM((groups - 1,) + part, x.dtype),
        pltpu.SemaphoreType.DMA((groups, size - 1)),
        pltpu.SemaphoreType.DMA((groups, size - 1)),
        pltpu.SemaphoreType.DMA((groups - 1,)),
        pltpu.SemaphoreType.DMA((groups - 1,)),
    ]


def by_tiles(kernel, full, ins, outs, scratch, more=(), params=None):
    return pl.pallas_call(
        kernel,
        grid=(full // LANES,),
        in_specs=[block_of(a.shape, kind) for a, kind in ins],
        out_specs=[block_of(shape, kind) for shape, _, kind in outs],
        out_shape=[jax.ShapeDtypeStruct(shape, dtype) for shape, dtype, _ in outs],
        scratch_shapes=[pltpu.VMEM(shape, dtype) for shape, dtype in scratch] + list(more),
        compiler_params=pltpu.CompilerParams(vmem_limit_bytes=58 * MIB, **(params or {})),
        cost_estimate=pl.CostEstimate(flops=1000, bytes_accessed=1000, transcendentals=0),
    )(*[a for a, _ in ins])


def norm_back(grad_normed, unit_rows, inverse, weight_gain):
    scaled = grad_normed * weight_gain
    return inverse * (scaled - unit_rows * jnp.mean(scaled * unit_rows, axis=-1, keepdims=True))


def local(
    tokens,
    teacher,
    true_lengths,
    doc_lengths,
    routes,
    norm1_gain,
    in_weight,
    conv_weight,
    conv_bias,
    xproj_weight,
    dt_weight,
    dt_bias,
    a_log,
    skip_weight,
    out_weight,
    norm2_gain,
    router_weight,
    expert_in,
    expert_out,
):
    seqs, group, width = tokens.shape
    inner = in_weight.shape[2]
    rank = dt_weight.shape[0]
    states = a_log.shape[1]
    experts = router_weight.shape[1]
    n_seq = lax.axis_size("seq")
    n_chan = lax.axis_size("chan")
    shards = n_seq // experts
    most = group // 4
    taps = conv_weight.shape[0]
    rim = taps - 1
    lines = 8
    chunks = lines // seqs
    steps = group // chunks
    owned = seqs * group // n_chan
    part = min(group, owned)
    most = min(most, part)
    parts = owned // part
    place = lax.axis_index("chan")
    first_pos = lax.axis_index("seq") * group

    full = -(-inner // LANES) * LANES
    rows = steps * lines
    maps = rank + 2 * states

    def padded(x):
        return jnp.pad(x, ((0, 0),) * (x.ndim - 1) + ((0, full - inner),))

    at = (
        first_pos
        + jnp.arange(steps, dtype=jnp.int32)[:, None]
        + (jnp.arange(lines, dtype=jnp.int32) // seqs * steps)[None, :]
    )
    stops = []
    for k in range(doc_lengths.shape[1] - 1):
        stops.append(doc_lengths[:, k] + (stops[-1] if stops else 0))
    stops = [jnp.tile(stop, chunks)[None, :] for stop in stops]

    def doc_at(pos):
        return sum((pos >= stop).astype(jnp.int32) for stop in stops)

    doc_ids = doc_at(at)
    keep = (doc_ids == doc_at(at - 1)) & (at > 0)
    valid = [doc_at(at - rim + k) == doc_ids for k in range(taps)] + [keep]
    valid = jnp.stack(valid + [keep] * (lines - taps - 1), axis=-1).astype(f32)

    w_in = in_weight.transpose(1, 2, 0)
    router_rows = router_weight.T
    gain_one = norm1_gain.astype(f32)
    taps_full = padded(conv_weight.astype(f32))
    xproj_rows = padded(xproj_weight.T)
    dt_rows = jnp.pad(padded(dt_weight), ((0, maps - rank), (0, 0)))
    skip_row = padded(skip_weight[None])
    out_rows = jnp.pad(out_weight, ((0, full - inner), (0, 0)))
    rate = -jnp.exp(a_log.T)
    rate_two = padded(rate * log2e)
    normed_one, extended, pre_act, gate_z, mapped = front(
        tokens,
        gain_one[None],
        w_in,
        taps_full,
        padded(conv_bias.astype(f32)[None]),
        xproj_rows,
        valid,
        full,
        1,
    )
    act_shape, state_shape, wide_shape = (steps, lines, full), (states, lines, full), (states, steps, lines, LANES)
    dt_pre, step_size, drive, own_states, sums = by_tiles(
        functools.partial(totals_kernel, rank, taps),
        full,
        [
            (pre_act, "tile"),
            (mapped, "whole"),
            (dt_rows, "tile"),
            (padded(dt_bias[None]), "tile"),
            (valid, "whole"),
            (rate_two, "tile"),
        ],
        [
            (act_shape, f32, "tile"),
            (act_shape, f32, "tile"),
            (act_shape, f32, "tile"),
            (state_shape, f32, "tile"),
            ((lines, full), f32, "tile"),
        ],
        [(wide_shape, f32)],
    )
    (enter,) = carried(own_states, sums, rate_two, "seq", False, 2)
    y_full, gated, state, out_part = by_tiles(
        functools.partial(states_kernel, rank, seqs),
        full,
        [
            (step_size, "tile"),
            (drive, "tile"),
            (mapped, "whole"),
            (rate_two, "tile"),
            (enter, "tile"),
            (pre_act, "tile"),
            (gate_z, "tile"),
            (skip_row, "tile"),
            (out_rows, "rows"),
        ],
        [
            (act_shape, f32, "tile"),
            ((rows, full), bf16, "tile"),
            ((steps, states, lines, full), f32, "tile"),
            ((rows, width), bf16, "whole"),
        ],
        [(wide_shape, f32)] * 2 + [((rows, width), f32)],
    )
    (mixed,) = share_of(3, [(out_part.reshape(n_chan, owned, width), "chan", 2, f32)])

    def own(x):
        return lax.dynamic_slice_in_dim(x.reshape((rows,) + x.shape[2:]), place * owned, owned, 0)

    slots = parts * most
    tokens_own, gain_two = own(tokens), norm2_gain.astype(f32)[None]
    line, low = (owned, width), ((owned, width), bf16)
    hidden_one, normed_two, probs, chosen, hit, packed = at_once(
        functools.partial(route_kernel, part, most, slots),
        [tokens_own, mixed, gain_two, own(routes)[:, None], router_rows],
        [
            (line, f32),
            low,
            ((owned, experts), f32),
            ((owned, experts), f32),
            ((owned, experts * slots), bf16),
            ((experts * slots, width), bf16),
        ],
    )
    hit_back = hit
    if shards > 1:
        hit_back = hit.reshape(owned, experts, slots)
        hit_back = jnp.repeat(hit_back, shards, axis=1).reshape(owned, n_seq * slots)

    def to_slabs(x):
        x = x.reshape(experts, slots, width)
        return x if shards == 1 else jnp.repeat(x, shards, axis=0), "scatter", "seq"

    def to_rows(x):
        return x.reshape(n_seq, slots, width), "scatter", "seq"

    def flat(x):
        return x.reshape(-1, x.shape[-1])

    first_slab, second_slab = expert_in[0], expert_out[0]
    arrived = flat(exchange(4, to_slabs(packed))[0])
    hidden, slope, result = expert(arrived, first_slab, second_slab, n_chan)
    (result_rows,) = exchange(5, to_rows(result))
    layer_low, grad_layer, grad_logit, loss_row, packed = at_once(
        functools.partial(loss_kernel, group),
        [
            true_lengths,
            flat(result_rows),
            hit_back,
            hit,
            hidden_one,
            probs,
            chosen,
            own(teacher),
        ],
        [
            low,
            (line, f32),
            ((owned, experts), f32),
            ((1, width), f32),
            ((experts * slots, width), bf16),
        ],
        scalars=1,
    )
    grad_rows = flat(exchange(6, to_slabs(packed))[0])
    grad_pre, grad_slab_rows = expert(grad_rows, first_slab, second_slab, n_chan, slope)
    (grad_expert,) = exchange(7, to_rows(grad_slab_rows))
    shared_rows = -(-(experts + 2) // 8) * 8
    grad_hidden_one, grad_low, shared = at_once(
        norm_back_kernel,
        [
            flat(grad_expert),
            hit_back,
            grad_logit,
            router_rows,
            normed_two,
            hidden_one,
            grad_layer,
            gain_two,
            loss_row,
        ],
        [(line, f32), low, ((shared_rows, width), f32)],
    )

    (grad_mixed,) = exchange(8, (grad_low, 2, "chan"))
    grad_y, grad_z, grad_out_w, grad_in_gate, skip_sums, back_last = by_tiles(
        functools.partial(back_totals_kernel, rank, seqs),
        full,
        [
            (step_size, "tile"),
            (mapped, "whole"),
            (rate_two, "tile"),
            (grad_mixed.reshape(rows, width), "whole"),
            (normed_one, "whole"),
            (out_rows, "rows"),
            (gate_z, "tile"),
            (y_full, "tile"),
            (gated, "tile"),
            (pre_act, "tile"),
        ],
        [
            (act_shape, f32, "tile"),
            ((rows, full), bf16, "tile"),
            ((inner, width), bf16, "rows"),
            ((inner, width), bf16, "rows"),
            ((lines, full), f32, "tile"),
            (state_shape, f32, "tile"),
        ],
        [(wide_shape, f32), ((rows, width), bf16)],
    )
    back_enter, shared = carried(
        back_last, sums, rate_two, "seq", True, 9, (shared, "gather", "chan")
    )
    shared = jnp.sum(shared, axis=0).reshape(-1, LANES)
    def cut_rows(x, unit):
        each = -(-x.shape[0] // (unit * n_seq)) * unit
        return jnp.pad(x, ((0, each * n_seq - x.shape[0]), (0, 0))).reshape(n_seq, each, -1)

    across = n_chan // 2
    by_out, by_gate = cut_rows(grad_out_w, 8), cut_rows(grad_in_gate, 8)
    riders = [(hidden, "scatter", "chan"), (grad_pre, "scatter", "chan")]
    items = items_of(riders)
    side, log_sums, bias_sums, grad_dt_w, low_part, by_out, by_gate, hidden_all, grad_pre_all = by_tiles(
        functools.partial(back_kernel, rank, full // LANES, [("seq", n_seq, across)] * 2, items),
        full,
        [
            (step_size, "tile"),
            (drive, "tile"),
            (grad_y, "tile"),
            (mapped, "whole"),
            (rate_two, "tile"),
            (enter, "tile"),
            (state, "tile"),
            (back_enter, "tile"),
            (dt_pre, "tile"),
            (pre_act, "tile"),
            (dt_rows, "tile"),
            (by_out, "any"),
            (by_gate, "any"),
            (hidden, "any"),
            (grad_pre, "any"),
        ],
        [
            (act_shape, f32, "tile"),
            (state_shape, f32, "tile"),
            ((lines, full), f32, "tile"),
            ((maps, full), f32, "tile"),
            ((rows, maps), bf16, "whole"),
            (by_out.shape[1:], bf16, "whole"),
            (by_gate.shape[1:], bf16, "whole"),
            (hidden.shape, bf16, "any"),
            (grad_pre.shape, bf16, "any"),
        ],
        [(wide_shape, f32)] * 2
        + [((steps, lines, states * lines), f32)] * 2
        + [((steps, lines, LANES), f32)] * 2
        + [((rows, maps), f32)]
        + [(by_out.shape, bf16)] * 2,
        [pltpu.SemaphoreType.DMA((2,))]
        + share_scratch(by_out, "seq", across)
        + share_scratch(by_gate, "seq", across)
        + [sem for item in items for sem in sems_of(item)],
        {"collective_id": 15, "has_side_effects": True},
    )
    grad_mapped = summed_over(low_part, "chan", 10).astype(bf16)
    grad_conv_in, rims, grad_xproj, conv_sums = by_tiles(
        functools.partial(conv_back_kernel, taps),
        full,
        [
            (grad_mapped, "whole"),
            (grad_y, "tile"),
            (side, "tile"),
            (pre_act, "tile"),
            (extended, "tile"),
            (skip_row, "tile"),
            (xproj_rows, "tile"),
            (taps_full, "tile"),
            (valid, "whole"),
        ],
        [
            (act_shape, f32, "tile"),
            ((rim, lines, full), f32, "tile"),
            ((maps, full), f32, "tile"),
            ((taps + 1, lines, full), f32, "tile"),
        ],
        [((steps + rim, lines, LANES), f32)],
    )
    grad_in_conv, normed_part, grad_gain_one, by_gate, rows_all = ends(
        tokens,
        grad_conv_in,
        rims,
        grad_z,
        normed_one,
        w_in,
        14,
        (by_gate, across, "seq"),
        (arrived, 2, "chan"),
    )
    normed_part = normed_part.reshape(n_chan, owned, width)
    sums_all = jnp.concatenate([conv_sums, bias_sums[None], skip_sums[None], log_sums], axis=0)
    sums_all = jnp.sum(sums_all, axis=1)
    small_rows = sums_all.shape[0] * full // LANES
    small = jnp.concatenate([sums_all.reshape(small_rows, LANES), shared], axis=0)

    by_conv = cut_rows(grad_in_conv, 8)
    middle = cut_rows(jnp.concatenate([grad_xproj, grad_dt_w[:rank]], axis=0).astype(bf16), 16)
    grad_normed_one, small, middle, by_conv, grad_gain_one, by_out, grad_rows_all = share_of(
        11,
        [
            (normed_part, "chan", 2, f32),
            (cut_rows(small, 8), "seq", across, f32),
            (middle, "seq", across, bf16),
            (by_conv, "seq", across, bf16),
        ],
        (grad_gain_one, "gather", "chan"),
        (by_out, across, "seq"),
        (grad_rows, 2, "chan"),
    )
    grad_gain_one = jnp.sum(grad_gain_one, axis=0)
    tokens_full = tokens_own.astype(f32)
    inverse_one = lax.rsqrt(jnp.mean(tokens_full * tokens_full, axis=-1, keepdims=True) + epsilon)
    grad_own = grad_hidden_one + norm_back(
        grad_normed_one, tokens_full * inverse_one, inverse_one, gain_one
    )
    moved = [
        (grad_own.astype(bf16), 2, "chan"),
        (layer_low, 2, "chan"),
        (small, across, "seq"),
        (middle, across, "seq"),
        (by_conv, across, "seq"),
        (grad_gain_one, "gather", "seq"),
    ]
    moved = exchange(12, *moved)
    grad_first = dot_tn(flat(rows_all), flat(grad_pre_all))
    grad_second = dot_tn(flat(hidden_all), flat(grad_rows_all))
    grad_tokens, layer_out, small, middle, by_conv, grad_gain_one = moved
    grad_gain_one = jnp.sum(grad_gain_one, axis=(0, 1))
    summed_in, summed_out, grad_tokens = widened(
        flat(by_conv), flat(by_gate), flat(by_out), flat(grad_tokens), inner
    )
    middle = flat(middle)[:, :inner].astype(f32)
    small = flat(small)
    shared = small[small_rows : small_rows + shared_rows * width // LANES].reshape(shared_rows, width)
    small = small[:small_rows].reshape(-1, full)[:, :inner]
    return (
        layer_out.reshape(seqs, group, width),
        shared[experts + 1, 0],
        grad_tokens.reshape(seqs, group, width),
        grad_gain_one,
        summed_in.transpose(2, 0, 1),
        small[:taps],
        small[taps],
        middle[:maps].T,
        middle[maps : maps + rank],
        small[taps + 1],
        (small[taps + 3 : taps + 3 + states] * rate).T,
        small[taps + 2],
        summed_out,
        shared[experts],
        shared[:experts].T,
        grad_first[None],
        grad_second[None],
    )


def solution(mesh):
    placed = (
        P(None, "seq", None),
        P(None, "seq", None),
        P(),
        P(),
        P(None, "seq"),
        P(),
        P(None, None, "chan"),
        P(None, "chan"),
        P("chan"),
        P("chan", None),
        P(None, "chan"),
        P("chan"),
        P("chan", None),
        P("chan"),
        P("chan", None),
        P(),
        P(),
        P("seq", None, None),
        P("seq", None, None),
    )
    return jax.shard_map(
        local,
        mesh=mesh,
        in_specs=placed,
        out_specs=(
            P(None, "seq", None),
            P(),
            P(None, "seq", None),
            P(),
            P(None, None, "chan"),
            P(None, "chan"),
            P("chan"),
            P("chan", None),
            P(None, "chan"),
            P("chan"),
            P("chan", None),
            P("chan"),
            P("chan", None),
            P(),
            P(),
            P("seq", None, "chan"),
            P("seq", "chan", None),
        ),
        check_vma=False,
    )
```

```python
import functools

import jax
import jax.numpy as jnp
from jax import lax
from jax.experimental import pallas as pl
from jax.experimental.pallas import tpu as pltpu
from jax.sharding import PartitionSpec as P

epsilon = 1e-05
log2e = 1.4426950408889634
cut = 1e30
MESH = pl.DeviceIdType.MESH
f32 = jnp.float32
bf16 = jnp.bfloat16
LANES = 128
MIB = 1024 * 1024
AHEAD = 12


def greet(axes):
    barrier = pltpu.get_barrier_semaphore()
    told = 0
    for axis, count in axes:
        me = lax.axis_index(axis)
        for k in range(1, count):
            pl.semaphore_signal(
                barrier, inc=1, device_id={axis: lax.rem(me + k, count)}, device_id_type=MESH
            )
        told += count - 1
    return told


def cuts_of(size):
    half = -(-size // 32) * 16
    return [(0, half), (half, size - half)] if half < size and size % 16 == 0 else [(0, size)]


def sems_of(item):
    copies = 2 * (item[2] - 1)
    return [pltpu.SemaphoreType.DMA] + [pltpu.SemaphoreType.DMA((copies,))] * 2


def flipped(i, mask):
    bit = 1
    while bit <= mask:
        if mask & bit:
            i = i + bit - 2 * bit * lax.rem(i // bit, 2)
        bit *= 2
    return i


def order_of(groups):
    masks, low, high = [], 1, groups - 1
    while low <= high:
        masks += [high] if low == high else [high, low]
        low, high = low + 1, high - 1
    return masks


class Riders:
    def __init__(self, items, xs, outs, sems):
        self.own, self.copies, self.chains = [], [], {}
        for i, item in enumerate(items):
            self.add(item, xs[i], outs[i], *sems[3 * i : 3 * i + 3])
        self.at = {axis: 0 for axis in self.chains}

    def start(self):
        for copy in self.copies + self.own:
            copy.start()
        for chain in self.chains.values():
            for first, _ in chain[:AHEAD]:
                first.start()
        return self

    def add(self, item, x_ref, o_ref, own_sem, send_sem, recv_sem):
        mode, axis, count = item
        me = lax.axis_index(axis)

        def remote(source, row, slot, to, cut=None):
            target = o_ref.at[row]
            if cut is not None:
                source, target = source.at[pl.ds(*cut)], o_ref.at[row, pl.ds(*cut)]
            return pltpu.make_async_remote_copy(
                src_ref=source,
                dst_ref=target,
                send_sem=send_sem.at[slot],
                recv_sem=recv_sem.at[slot],
                device_id={axis: to},
                device_id_type=MESH,
            )

        source = x_ref.at[me] if mode == "scatter" else x_ref
        self.own.append(pltpu.make_async_copy(source, o_ref.at[me], own_sem))
        if mode in ("gather", "scatter"):
            for mask in range(count - 1, 0, -1):
                to = flipped(me, mask)
                source = x_ref.at[to] if mode == "scatter" else x_ref
                self.copies.append(remote(source, me, mask - 1, to))
            return
        groups = count // mode
        side, place = lax.rem(me, mode), me // mode
        mates = [place * mode + lax.rem(side + j, mode) for j in range(1, mode)]
        slot = 0
        for mate in mates:
            self.copies.append(remote(x_ref, me, slot, mate))
            slot += 1
        chain = self.chains.setdefault(axis, [])
        for mask in order_of(groups):
            row = flipped(place, mask) * mode + side
            for cut in cuts_of(x_ref.shape[0]):
                first = remote(x_ref, me, slot, row, cut)
                slot += 1
                passed = []
                for mate in mates:
                    passed.append(remote(o_ref.at[row], row, slot, mate, cut))
                    slot += 1
                chain.append((first, passed))

    def left(self):
        return any(self.at[axis] < len(chain) for axis, chain in self.chains.items())

    def step(self):
        for axis in sorted(self.chains, reverse=True):
            i, chain = self.at[axis], self.chains[axis]
            if i == len(chain):
                continue
            self.at[axis] = i + 1
            first, passed = chain[i]
            first.wait_recv()
            for copy in passed:
                copy.start()
            if i + AHEAD < len(chain):
                chain[i + AHEAD][0].start()
            return

    def finish(self):
        while self.left():
            self.step()
        for copy in self.own + self.copies:
            copy.wait()
        for chain in self.chains.values():
            for first, passed in chain:
                first.wait_send()
                for copy in passed:
                    copy.wait()


def items_of(exchanges):
    return [(mode, axis, lax.axis_size(axis)) for _, mode, axis in exchanges]


def axes_of(items):
    return sorted({(axis, count) for _, axis, count in items})


def landed(x, item):
    shape = x.shape if item[0] == "scatter" else (item[2],) + x.shape
    return jax.ShapeDtypeStruct(shape, x.dtype)


def exchange_kernel(items, *refs):
    number = len(items)
    sems = refs[2 * number :]
    pl.semaphore_wait(pltpu.get_barrier_semaphore(), greet(axes_of(items)))
    Riders(items, refs[:number], refs[number : 2 * number], sems).start().finish()


def exchange(number, *exchanges):
    items = items_of(exchanges)
    return pl.pallas_call(
        functools.partial(exchange_kernel, items),
        out_shape=[landed(x, item) for (x, _, _), item in zip(exchanges, items)],
        in_specs=[pl.BlockSpec(memory_space=pl.ANY)] * len(items),
        out_specs=[pl.BlockSpec(memory_space=pl.ANY)] * len(items),
        scratch_shapes=[sem for item in items for sem in sems_of(item)],
        compiler_params=pltpu.CompilerParams(
            collective_id=number, has_side_effects=True, vmem_limit_bytes=4 * MIB
        ),
    )(*[x for x, _, _ in exchanges])


def greet_near(axis, count):
    barrier = pltpu.get_barrier_semaphore()
    me = lax.axis_index(axis)
    beside = me + 1 - 2 * lax.rem(me, 2)
    pl.semaphore_signal(barrier, inc=1, device_id={axis: beside}, device_id_type=MESH)
    for k in range(1, count // 2):
        pl.semaphore_signal(
            barrier, inc=1, device_id={axis: lax.rem(me + 2 * k, count)}, device_id_type=MESH
        )
    pl.semaphore_wait(barrier, count // 2)


def sum_kernel(axis, count, x_ref, o_ref, beside_in, pair, far_in, send_sem, recv_sem):
    me = lax.axis_index(axis)
    beside = me + 1 - 2 * lax.rem(me, 2)
    greet_near(axis, count)
    near = pltpu.make_async_remote_copy(
        src_ref=x_ref,
        dst_ref=beside_in,
        send_sem=send_sem.at[0],
        recv_sem=recv_sem.at[0],
        device_id={axis: beside},
        device_id_type=MESH,
    )
    near.start()
    near.wait_recv()
    pair[...] = (x_ref[...].astype(f32) + beside_in[...].astype(f32)).astype(bf16)
    copies = []
    for k in range(1, count // 2):
        copies.append(
            pltpu.make_async_remote_copy(
                src_ref=pair,
                dst_ref=far_in.at[k - 1],
                send_sem=send_sem.at[k],
                recv_sem=recv_sem.at[k],
                device_id={axis: lax.rem(me + 2 * k, count)},
                device_id_type=MESH,
            )
        )
        copies[-1].start()
    for copy in copies:
        copy.wait_recv()
    total = pair[...].astype(f32)
    for k in range(count // 2 - 1):
        total = total + far_in[k].astype(f32)
    o_ref[...] = total
    near.wait_send()
    for copy in copies:
        copy.wait_send()


def summed_over(x, axis, number):
    count = lax.axis_size(axis)
    return pl.pallas_call(
        functools.partial(sum_kernel, axis, count),
        out_shape=jax.ShapeDtypeStruct(x.shape, f32),
        in_specs=[pl.BlockSpec(memory_space=pltpu.VMEM)],
        out_specs=pl.BlockSpec(memory_space=pltpu.VMEM),
        scratch_shapes=[
            pltpu.VMEM(x.shape, bf16),
            pltpu.VMEM(x.shape, bf16),
            pltpu.VMEM((count // 2 - 1,) + x.shape, bf16),
            pltpu.SemaphoreType.DMA((count // 2,)),
            pltpu.SemaphoreType.DMA((count // 2,)),
        ],
        compiler_params=pltpu.CompilerParams(
            collective_id=number, has_side_effects=True, vmem_limit_bytes=8 * MIB
        ),
    )(x)


class Share:
    def __init__(self, axis, count, size, x_ref, near_in, pairs, far_in, near_send, near_recv, far_send, far_recv):
        self.groups, self.size, self.x = count // size, size, x_ref
        self.near_in, self.pairs, self.far_in = near_in, pairs, far_in
        me = lax.axis_index(axis)
        side, place = lax.rem(me, size), me // size
        self.rows, self.near, self.far = [], [], []
        for k in range(self.groups):
            group = flipped(place, (order_of(self.groups) + [0])[k])
            self.rows.append(group * size + side)
            self.near.append(
                [
                    pltpu.make_async_remote_copy(
                        src_ref=x_ref.at[group * size + lax.rem(side + j, size)],
                        dst_ref=near_in.at[k, j - 1],
                        send_sem=near_send.at[k, j - 1],
                        recv_sem=near_recv.at[k, j - 1],
                        device_id={axis: place * size + lax.rem(side + j, size)},
                        device_id_type=MESH,
                    )
                    for j in range(1, size)
                ]
            )
            if k < self.groups - 1:
                self.far.append(
                    pltpu.make_async_remote_copy(
                        src_ref=pairs.at[k],
                        dst_ref=far_in.at[k],
                        send_sem=far_send.at[k],
                        recv_sem=far_recv.at[k],
                        device_id={axis: self.rows[k]},
                        device_id_type=MESH,
                    )
                )

    def begin(self, k):
        for copy in self.near[k]:
            copy.start()

    def near_sum(self, k, wait=True):
        total = self.x[self.rows[k]].astype(f32)
        for j, copy in enumerate(self.near[k]):
            if wait:
                copy.wait_recv()
            total = total + self.near_in[k, j].astype(f32)
        return total

    def pass_on(self, k):
        if k < self.groups - 1:
            self.pairs[k] = self.near_sum(k).astype(self.pairs.dtype)
            self.far[k].start()
        else:
            for copy in self.near[k]:
                copy.wait_recv()

    def total(self):
        total = self.near_sum(self.groups - 1, False)
        for k, copy in enumerate(self.far):
            copy.wait_recv()
            total = total + self.far_in[k].astype(f32)
        return total

    def close(self):
        for copy in [copy for copies in self.near for copy in copies] + self.far:
            copy.wait_send()


def share_kernel(shares, items, *refs):
    many, number = len(shares), len(items)
    at = 0

    def take(k):
        nonlocal at
        at += k
        return refs[at - k : at]

    xs, riders, outs, rider_outs = take(many), take(number), take(many), take(number)
    tasks = [Share(axis, count, size, x, *take(7)) for (axis, count, size), x in zip(shares, xs)]
    axes = set(axes_of(items)) | {(axis, count) for axis, count, _ in shares}
    told = greet(sorted(axes))
    rider_sems = take(3 * number)
    pl.semaphore_wait(pltpu.get_barrier_semaphore(), told)
    turns = {}
    for (axis, _, _), task in zip(shares, tasks):
        turns.setdefault(axis, []).extend((task, k) for k in range(task.groups))
    for turn in turns.values():
        for task, k in turn[:AHEAD]:
            task.begin(k)
    under_way = Riders(items, riders, rider_outs, rider_sems).start()
    for i in range(max(len(turn) for turn in turns.values())):
        for turn in turns.values():
            if i < len(turn):
                task, k = turn[i]
                task.pass_on(k)
                if i + AHEAD < len(turn):
                    task, k = turn[i + AHEAD]
                    task.begin(k)
        under_way.step()
    for task, out in zip(tasks, outs):
        out[...] = task.total().astype(out.dtype)
    for task in tasks:
        task.close()
    under_way.finish()


def share_of(number, shares, *exchanges):
    items = items_of(exchanges)
    anywhere = [pl.BlockSpec(memory_space=pl.ANY)] * len(items)
    held = [pl.BlockSpec(memory_space=pltpu.VMEM)] * len(shares)
    scratch = []
    for x, axis, size, _ in shares:
        scratch += share_scratch(x, axis, size)
    outs = [jax.ShapeDtypeStruct(x.shape[1:], kind) for x, _, _, kind in shares]
    outs += [landed(x, item) for (x, _, _), item in zip(exchanges, items)]
    scratch += [sem for item in items for sem in sems_of(item)]
    return pl.pallas_call(
        functools.partial(
            share_kernel, [(axis, lax.axis_size(axis), size) for _, axis, size, _ in shares], items
        ),
        out_shape=outs,
        in_specs=held + anywhere,
        out_specs=held + anywhere,
        scratch_shapes=scratch,
        compiler_params=pltpu.CompilerParams(
            collective_id=number, has_side_effects=True, vmem_limit_bytes=18 * MIB
        ),
    )(*[share[0] for share in shares], *[x for x, _, _ in exchanges])


def turned(value):
    return pltpu.roll(value, value.shape[0] // 2, 0)


def carry_kernel(axis, count, back, items, *refs):
    number = len(items)
    local_ref, sums_ref, rate_ref = refs[:3]
    xs, o_ref, outs = refs[3 : 3 + number], refs[3 + number], refs[4 + number : 4 + 2 * number]
    send, got, send_sum, got_sum, total, enter = refs[4 + 2 * number : 10 + 2 * number]
    send_sem, recv_sem, send_sum_sem, recv_sum_sem = refs[10 + 2 * number : 14 + 2 * number]
    sems = refs[14 + 2 * number :]
    me = lax.axis_index(axis)
    states, rows, width = local_ref.shape
    half = rows // 2
    spans = []
    span = 1
    while span < count:
        spans.append(span)
        span *= 2
    sign = -1 if back else 1
    barrier = pltpu.get_barrier_semaphore()
    greeted = greet(axes_of(items))
    for span in spans:
        for by in (span, -span):
            there = me + by
            greeted = greeted + jnp.where((there >= 0) & (there < count), 1, 0)

            @pl.when((there >= 0) & (there < count))
            def _():
                pl.semaphore_signal(barrier, inc=1, device_id={axis: there}, device_id_type=MESH)

    upper = lax.broadcasted_iota(jnp.int32, (rows, width), 0) >= half
    first = upper if back else jnp.logical_not(upper)
    sums = sums_ref[...]
    sums_turned = turned(sums)
    sums_both = sums + sums_turned
    sums_first = jnp.where(first, sums, sums_turned)
    sums_last = jnp.where(first, sums_turned, sums)

    def packed_rate(j):
        return jnp.where(upper, rate_ref[pl.ds(2 * j + 1, 1), :], rate_ref[pl.ds(2 * j, 1), :])

    def both(j):
        even, odd = local_ref[2 * j], local_ref[2 * j + 1]
        low = jnp.where(upper, turned(odd), even)
        high = jnp.where(upper, odd, turned(even))
        return (high, low) if back else (low, high)

    for j in range(states // 2):
        opening, closing = both(j)
        total[j] = jnp.exp2(packed_rate(j) * sums_last) * opening + closing
        enter[j] = jnp.zeros((rows, width), f32)

    pl.semaphore_wait(barrier, greeted)
    under_way = Riders(items, xs, outs, sems).start()
    sums_total = sums_both
    sums_enter = jnp.zeros((rows, width), f32)
    for turn, span in enumerate(spans):
        to = me + sign * span
        origin = me - sign * span
        sends = (to >= 0) & (to < count)
        takes = (origin >= 0) & (origin < count)
        for j in range(0, states // 2, 2):
            send[turn, pl.ds(j * rows, 2 * rows), :] = jnp.concatenate([total[j], total[j + 1]], axis=0).astype(bf16)
        send_sum[turn] = sums_total
        copies = [
            pltpu.make_async_remote_copy(
                src_ref=source.at[turn],
                dst_ref=target.at[turn],
                send_sem=ssem.at[turn],
                recv_sem=rsem.at[turn],
                device_id={axis: to},
                device_id_type=MESH,
            )
            for source, target, ssem, rsem in (
                (send, got, send_sem, recv_sem),
                (send_sum, got_sum, send_sum_sem, recv_sum_sem),
            )
        ]

        @pl.when(sends)
        def _():
            for copy in copies:
                copy.start()

        @pl.when(jnp.logical_not(takes))
        def _():
            got[turn] = jnp.zeros(got.shape[1:], bf16)
            got_sum[turn] = jnp.zeros(got_sum.shape[1:], f32)

        @pl.when(takes)
        def _():
            for copy in copies:
                copy.wait_recv()

        for j in range(0, states // 2, 2):
            pair = got[turn, pl.ds(j * rows, 2 * rows), :].astype(f32)
            for i in (j, j + 1):
                came = pair[(i - j) * rows : (i - j + 1) * rows]
                rate = packed_rate(i)
                enter[i] = jnp.exp2(rate * sums_enter) * came + enter[i]
                total[i] = jnp.exp2(rate * sums_total) * came + total[i]
        sums_enter = sums_enter + got_sum[turn]
        sums_total = sums_total + got_sum[turn]

        @pl.when(sends)
        def _():
            for copy in copies:
                copy.wait_send()

    for j in range(states // 2):
        opening, _ = both(j)
        outer = enter[j]
        inner = jnp.exp2(packed_rate(j) * sums_first) * outer + opening
        low, high = (inner, outer) if back else (outer, inner)
        o_ref[2 * j] = jnp.where(upper, turned(high), low)
        o_ref[2 * j + 1] = jnp.where(upper, high, turned(low))
    under_way.finish()


def carried(local, sums, rate, axis, back, number, *exchanges):
    count = lax.axis_size(axis)
    states, rows, width = local.shape
    turns = max(1, (count - 1).bit_length())
    items = items_of(exchanges)
    anywhere = [pl.BlockSpec(memory_space=pl.ANY)] * len(items)
    return pl.pallas_call(
        functools.partial(carry_kernel, axis, count, back, items),
        out_shape=[jax.ShapeDtypeStruct(local.shape, f32)]
        + [landed(x, item) for (x, _, _), item in zip(exchanges, items)],
        in_specs=[pl.BlockSpec(memory_space=pltpu.VMEM)] * 3 + anywhere,
        out_specs=[pl.BlockSpec(memory_space=pltpu.VMEM)] + anywhere,
        scratch_shapes=[
            pltpu.VMEM((turns, states // 2 * rows, width), bf16),
            pltpu.VMEM((turns, states // 2 * rows, width), bf16),
            pltpu.VMEM((turns, rows, width), f32),
            pltpu.VMEM((turns, rows, width), f32),
            pltpu.VMEM((states // 2, rows, width), f32),
            pltpu.VMEM((states // 2, rows, width), f32),
            pltpu.SemaphoreType.DMA((turns,)),
            pltpu.SemaphoreType.DMA((turns,)),
            pltpu.SemaphoreType.DMA((turns,)),
            pltpu.SemaphoreType.DMA((turns,)),
        ]
        + [sem for item in items for sem in sems_of(item)],
        compiler_params=pltpu.CompilerParams(
            collective_id=number, has_side_effects=True, vmem_limit_bytes=10 * MIB
        ),
    )(local, sums, rate, *[x for x, _, _ in exchanges])


def spread(mapped_ref, first, wide_ref):
    count, steps, rows, lanes = wide_ref.shape
    column = lax.broadcasted_iota(jnp.int32, (mapped_ref.shape[1], lanes), 0)
    values = mapped_ref[...]
    for n in range(count):
        pick = (column == first + n).astype(bf16)
        wide_ref[n] = jnp.dot(values, pick, preferred_element_type=f32).reshape(steps, rows, lanes)


def rows_of(rate_ref, n, rows):
    return jnp.broadcast_to(rate_ref[n : n + 1, :], (rows, rate_ref.shape[1]))


def perm_of(steps, lines, seqs):
    rows = steps * lines
    laid = lax.broadcasted_iota(jnp.int32, (rows, rows), 0)
    natural = lax.broadcasted_iota(jnp.int32, (rows, rows), 1)
    line = laid % lines
    wanted = (line % seqs) * (rows // seqs) + (line // seqs) * steps + laid // lines
    return (natural == wanted).astype(bf16)


def unit_of(rows):
    return rows * lax.rsqrt(jnp.mean(rows * rows, axis=-1, keepdims=True) + epsilon)


def softplus(x):
    return jnp.maximum(x, 0.0) + jnp.log1p(jnp.exp(-jnp.abs(x)))


def sigmoid(x):
    return 1.0 / (1.0 + jnp.exp(-x))


def silu_slope(values, sigma):
    return sigma * (1.0 + values * (1.0 - sigma))


def dot(a, b):
    return jnp.dot(a, b, preferred_element_type=f32)


def dot_nt(a, b):
    return lax.dot_general(a, b, (((1,), (1,)), ((), ())), preferred_element_type=f32)


def dot_tn(a, b):
    return lax.dot_general(a, b, (((0,), (0,)), ((), ())), preferred_element_type=f32)


def front_kernel(seq_count, chan_count, states, taps, tokens_ref, gain_ref, w_ref, params_ref, xproj_ref, valid_ref,
                 normed_ref, ext_ref, pre_ref, gate_ref, mapped_ref,
                 halo, part, beside_in, pair, far_in, halo_send, halo_recv, send_sem, recv_sem):
    seqs, group, width = tokens_ref.shape
    steps, lines, full = pre_ref.shape
    inner = w_ref.shape[1]
    rim, rows, tail = taps - 1, steps * lines, halo.shape[1]
    here, me = lax.axis_index("seq"), lax.axis_index("chan")
    beside = me + 1 - 2 * lax.rem(me, 2)
    barrier = pltpu.get_barrier_semaphore()
    told = chan_count // 2
    for by in (1, -1):
        there = here + by
        near = (there >= 0) & (there < seq_count)
        told = told + jnp.where(near, 1, 0)

        @pl.when(near)
        def _():
            pl.semaphore_signal(barrier, inc=1, device_id={"seq": there}, device_id_type=MESH)

    pl.semaphore_signal(barrier, inc=1, device_id={"chan": beside}, device_id_type=MESH)
    for k in range(1, chan_count // 2):
        to = lax.rem(me + 2 * k, chan_count)
        pl.semaphore_signal(barrier, inc=1, device_id={"chan": to}, device_id_type=MESH)
    pl.semaphore_wait(barrier, told)
    ends = pltpu.make_async_remote_copy(
        src_ref=tokens_ref.at[:, pl.ds(group - tail, tail), :],
        dst_ref=halo,
        send_sem=halo_send,
        recv_sem=halo_recv,
        device_id={"seq": here + 1},
        device_id_type=MESH,
    )

    @pl.when(here + 1 < seq_count)
    def _():
        ends.start()

    def normed_of(rows_low):
        return (unit_of(rows_low.astype(f32)) * gain_ref[...]).astype(bf16)

    perm = perm_of(steps, lines, seqs)
    normed = dot(perm, normed_of(tokens_ref[...].reshape(rows, width))).astype(bf16)
    normed_ref[...] = normed
    conv_in = dot_nt(normed, w_ref[0]).astype(bf16).astype(f32)
    ext_ref[pl.ds(rim, steps), :, pl.ds(0, inner)] = conv_in.reshape(steps, lines, inner)
    gate_ref[:, :, pl.ds(0, inner)] = dot_nt(normed, w_ref[1]).reshape(steps, lines, inner)
    if full > inner:
        ext_ref[:, :, pl.ds(inner, full - inner)] = jnp.zeros((steps + rim, lines, full - inner), f32)
        gate_ref[:, :, pl.ds(inner, full - inner)] = jnp.zeros((steps, lines, full - inner), f32)

    @pl.when(here == 0)
    def _():
        halo[...] = jnp.zeros(halo.shape, bf16)

    @pl.when(here > 0)
    def _():
        ends.wait_recv()

    prior = dot_nt(normed_of(halo[...].reshape(seqs * tail, width)), w_ref[0]).astype(bf16)
    to = lax.broadcasted_iota(jnp.int32, (rim * lines, seqs * tail), 0)
    origin = lax.broadcasted_iota(jnp.int32, (rim * lines, seqs * tail), 1)
    pick = (to % lines < seqs) & (origin == (to % lines) * tail + tail - rim + to // lines)
    prior = dot(pick.astype(bf16), prior).reshape(rim, lines, inner)
    upper = lax.broadcasted_iota(jnp.int32, (lines, inner), 0) >= seqs
    for j in range(rim):
        own = turned(ext_ref[steps + j, :, pl.ds(0, inner)])
        ext_ref[j, :, pl.ds(0, inner)] = jnp.where(upper, own, prior[j])
    pre = jnp.broadcast_to(params_ref[pl.ds(states + taps, 1), :], (steps, lines, full))
    for k in range(taps):
        tap = params_ref[pl.ds(states + k, 1), :]
        pre = pre + tap * ext_ref[pl.ds(k, steps)] * valid_ref[:, :, k : k + 1]
    pre_ref[...] = pre
    act_low = (pre * sigmoid(pre)).astype(bf16).reshape(rows, full)
    part[...] = dot_nt(act_low, xproj_ref[...]).astype(bf16)
    near = pltpu.make_async_remote_copy(
        src_ref=part,
        dst_ref=beside_in,
        send_sem=send_sem.at[0],
        recv_sem=recv_sem.at[0],
        device_id={"chan": beside},
        device_id_type=MESH,
    )
    near.start()
    near.wait_recv()
    pair[...] = (part[...].astype(f32) + beside_in[...].astype(f32)).astype(bf16)
    copies = []
    for k in range(1, chan_count // 2):
        copies.append(
            pltpu.make_async_remote_copy(
                src_ref=pair,
                dst_ref=far_in.at[k - 1],
                send_sem=send_sem.at[k],
                recv_sem=recv_sem.at[k],
                device_id={"chan": lax.rem(me + 2 * k, chan_count)},
                device_id_type=MESH,
            )
        )
        copies[-1].start()
    for copy in copies:
        copy.wait_recv()
    total = pair[...].astype(f32)
    for k in range(chan_count // 2 - 1):
        total = total + far_in[k].astype(f32)
    mapped_ref[...] = total.astype(bf16)
    near.wait_send()
    for copy in copies:
        copy.wait_send()

    @pl.when(here + 1 < seq_count)
    def _():
        ends.wait_send()


def front(tokens, gain, w_in, params, states, taps, xproj, valid, full, number):
    seqs, group, width = tokens.shape
    steps, lines = valid.shape[:2]
    count, rows, maps = lax.axis_size("chan"), steps * lines, xproj.shape[0]
    tail = min(16, group)
    return pl.pallas_call(
        functools.partial(front_kernel, lax.axis_size("seq"), count, states, taps),
        out_shape=[
            jax.ShapeDtypeStruct((rows, width), bf16),
            jax.ShapeDtypeStruct((steps + taps - 1, lines, full), f32),
            jax.ShapeDtypeStruct((steps, lines, full), f32),
            jax.ShapeDtypeStruct((steps, lines, full), f32),
            jax.ShapeDtypeStruct((rows, maps), bf16),
        ],
        in_specs=[pl.BlockSpec(memory_space=pltpu.VMEM)] * 6,
        out_specs=[pl.BlockSpec(memory_space=pltpu.VMEM)] * 5,
        scratch_shapes=[
            pltpu.VMEM((seqs, tail, width), bf16),
            pltpu.VMEM((rows, maps), bf16),
            pltpu.VMEM((rows, maps), bf16),
            pltpu.VMEM((rows, maps), bf16),
            pltpu.VMEM((count // 2 - 1, rows, maps), bf16),
            pltpu.SemaphoreType.DMA,
            pltpu.SemaphoreType.DMA,
            pltpu.SemaphoreType.DMA((count // 2,)),
            pltpu.SemaphoreType.DMA((count // 2,)),
        ],
        compiler_params=pltpu.CompilerParams(
            collective_id=number, has_side_effects=True, vmem_limit_bytes=36 * MIB
        ),
    )(tokens, gain, w_in, params, xproj, valid)


def totals_kernel(rank, taps, pre_ref, mapped_ref, dtw_ref, valid_ref, rate_ref,
                  dt_ref, step_ref, drive_ref, last_ref, sums_ref, wide):
    count, steps, rows, lanes = wide.shape

    @pl.when(pl.program_id(0) == 0)
    def _():
        spread(mapped_ref, rank, wide)

    bias = rate_ref[pl.ds(count + taps + 1, 1), :]
    dt_pre = (dot(mapped_ref[...], dtw_ref[...]) + bias).reshape(steps, rows, lanes)
    delta = softplus(dt_pre)
    pre = pre_ref[...]
    dt_ref[...] = dt_pre
    step_ref[...] = jnp.where(valid_ref[:, :, taps : taps + 1] > 0.5, delta, cut)
    drive_ref[...] = delta * pre * sigmoid(pre)
    rates = [rows_of(rate_ref, n, rows) for n in range(count)]
    zero = jnp.zeros((rows, lanes), f32)

    def one(p, held):
        states, sums = held
        step, drive = step_ref[p], drive_ref[p]
        states = tuple(
            jnp.exp2(step * rates[n]) * states[n] + drive * wide[n, p] for n in range(count)
        )
        return states, sums + step

    states, sums = lax.fori_loop(0, steps, one, ((zero,) * count, zero), unroll=2)
    for n in range(count):
        last_ref[n] = states[n]
    sums_ref[...] = sums


def known(rows_ref, size):
    row = pl.program_id(0) * rows_ref.shape[0] + lax.broadcasted_iota(jnp.int32, rows_ref.shape, 0)
    return jnp.where(row < size, rows_ref[...].astype(f32), 0.0).astype(rows_ref.dtype)


def states_kernel(rank, seqs, taps, inner, step_ref, drive_ref, mapped_ref, rate_ref, enter_ref, pre_ref, gate_ref, out_w_ref,
                  y_ref, gated_ref, state_ref, out_ref, wide_in, wide_read, total):
    count, steps, rows, lanes = wide_in.shape
    place = pl.program_id(0)

    @pl.when(place == 0)
    def _():
        spread(mapped_ref, rank, wide_in)
        spread(mapped_ref, rank + count, wide_read)
        total[...] = jnp.zeros_like(total)

    rates = [rows_of(rate_ref, n, rows) for n in range(count)]

    def one(p, states):
        step, drive = step_ref[p], drive_ref[p]
        states = tuple(
            jnp.exp2(step * rates[n]) * states[n] + drive * wide_in[n, p] for n in range(count)
        )
        terms = [states[n] * wide_read[n, p] for n in range(count)]
        while len(terms) > 1:
            terms = [a + b for a, b in zip(terms[::2], terms[1::2])]
        y_ref[p] = terms[0]
        for n in range(count):
            state_ref[p, n] = states[n]
        return states

    lax.fori_loop(0, steps, one, tuple(enter_ref[n] for n in range(count)), unroll=2)
    pre, gate = pre_ref[...], gate_ref[...]
    y_full = y_ref[...] + rate_ref[pl.ds(count + taps + 2, 1), :] * (pre * sigmoid(pre))
    y_ref[...] = y_full
    gated = (y_full * (gate * sigmoid(gate))).astype(bf16).reshape(steps * rows, lanes)
    gated_ref[...] = gated
    total[...] += dot(gated, known(out_w_ref, inner))

    @pl.when(place == pl.num_programs(0) - 1)
    def _():
        perm = perm_of(steps, rows, seqs)
        out_ref[...] = dot_tn(perm, total[...].astype(bf16)).astype(bf16)


def back_totals_kernel(rank, seqs, inner, step_ref, mapped_ref, rate_ref, mixed_ref, normed_ref, out_w_ref, gate_ref, y_ref, gated_ref,
                       pre_ref, grad_y_ref, grad_z_ref, grad_out_ref, grad_gate_ref, skip_ref, last_ref,
                       wide, mixed):
    count, steps, rows, lanes = wide.shape

    @pl.when(pl.program_id(0) == 0)
    def _():
        spread(mapped_ref, rank + count, wide)
        mixed[...] = dot(perm_of(steps, rows, seqs), mixed_ref[...]).astype(bf16)

    grad_gated = dot_nt(mixed[...], known(out_w_ref, inner)).reshape(steps, rows, lanes)
    gate, pre = gate_ref[...], pre_ref[...]
    sigma = sigmoid(gate)
    grad_y = grad_gated * (gate * sigma)
    grad_y_ref[...] = grad_y
    grad_z = (grad_gated * y_ref[...] * silu_slope(gate, sigma)).astype(bf16)
    grad_z = grad_z.reshape(steps * rows, lanes)
    grad_z_ref[...] = grad_z
    skip_ref[...] = jnp.sum(grad_y * (pre * sigmoid(pre)), axis=0)
    grad_out_ref[...] = dot_tn(gated_ref[...], mixed[...]).astype(bf16)
    grad_gate_ref[...] = dot_tn(grad_z, normed_ref[...]).astype(bf16)
    rates = [rows_of(rate_ref, n, rows) for n in range(count)]
    zero = jnp.zeros((rows, lanes), f32)

    def one(turn, held):
        p = steps - 1 - turn
        step, grad_y = step_ref[p], grad_y_ref[p]
        return tuple(
            jnp.exp2(step * rates[n]) * (held[n] + grad_y * wide[n, p]) for n in range(count)
        )

    held = lax.fori_loop(0, steps, one, (zero,) * count, unroll=2)
    for n in range(count):
        last_ref[n] = held[n]


def back_kernel(rank, pieces, shares, items, step_ref, drive_ref, grad_y_ref, mapped_ref, rate_ref, first_ref, state_ref, enter_ref, dt_ref,
                pre_ref, dtw_ref, *refs):
    many, number = len(shares), len(items)
    at = 0

    def take(k):
        nonlocal at
        at += k
        return refs[at - k : at]

    xs, riders = take(many), take(number)
    side_ref, log_ref, bias_ref, grad_dtw_ref, low_ref = take(5)
    parts, rider_outs = take(many), take(number)
    wide_in, wide_read, sum_in, sum_read, to_input, to_decay, total = take(7)
    count, steps, rows, lanes = wide_in.shape
    place, tiles = pl.program_id(0), pl.num_programs(0)
    kept, kept_sem = take(many), take(1)[0]
    tasks = [Share(*share, held, *take(7)) for share, held in zip(shares, kept)]
    under_way = Riders(items, riders, rider_outs, take(3 * number))
    turn = [(task, k) for task in tasks for k in range(task.groups)]

    @pl.when(place == 0)
    def _():
        copies = [
            pltpu.make_async_copy(x, held, kept_sem.at[i]) for i, (x, held) in enumerate(zip(xs, kept))
        ]
        for copy in copies:
            copy.start()
        axes = {share[:2] for share in shares} | set(axes_of(items))
        pl.semaphore_wait(pltpu.get_barrier_semaphore(), greet(sorted(axes)))
        for copy in copies:
            copy.wait()
        for task, k in turn[:3]:
            task.begin(k)
        under_way.start()
        spread(mapped_ref, rank, wide_in)
        spread(mapped_ref, rank + count, wide_read)
        sum_in[...] = jnp.zeros_like(sum_in)
        sum_read[...] = jnp.zeros_like(sum_read)
        total[...] = jnp.zeros_like(total)

    moments = 2 * (pieces - 1)
    each = -(-len(turn) // moments)

    def pass_on(late):
        for piece in range(1, pieces):
            moment = 2 * (piece - 1) + late

            @pl.when(place == piece)
            def _():
                for i in range(moment * each, min((moment + 1) * each, len(turn))):
                    turn[i][0].pass_on(turn[i][1])
                    if i + 3 < len(turn):
                        turn[i + 3][0].begin(turn[i + 3][1])

    pass_on(0)
    rates = [rows_of(rate_ref, n, rows) for n in range(count)]
    for n in range(count):
        log_ref[n] = jnp.zeros((rows, lanes), f32)

    def step_back(p, carry, prior_of):
        step, drive, grad_y = step_ref[p], drive_ref[p], grad_y_ref[p]
        inputs = jnp.zeros((rows, lanes), f32)
        decays = jnp.zeros((rows, lanes), f32)
        new, grads = [], []
        for n in range(count):
            grad = grad_y * wide_read[n, p] + carry[n]
            passed = jnp.exp2(step * rates[n]) * grad
            new.append(passed)
            grad_decay = passed * prior_of(n)
            decays = decays + grad_decay * rates[n]
            log_ref[n] += grad_decay * step
            inputs = inputs + grad * wide_in[n, p]
            grads.append(grad)
        to_input[p] = inputs
        to_decay[p] = decays
        grads = jnp.concatenate(grads, axis=0).astype(bf16)
        held_states = state_ref[p].reshape(count * rows, lanes).astype(bf16)
        sum_in[p] += dot_nt(drive.astype(bf16), grads)
        sum_read[p] += dot_nt(grad_y.astype(bf16), held_states)
        return tuple(new)

    def one(turn, carry):
        p = steps - 1 - turn
        return step_back(p, carry, lambda n: state_ref[p - 1, n])

    carry = tuple(enter_ref[n] for n in range(count))
    unroll = 7 if (steps - 1) % 7 == 0 else 1
    middle = (steps - 1) // unroll // 2 * unroll
    carry = lax.fori_loop(0, middle, one, carry, unroll=unroll)
    pass_on(1)
    carry = lax.fori_loop(middle, steps - 1, one, carry, unroll=unroll)
    step_back(0, carry, lambda n: first_ref[n])
    dt_pre, pre = dt_ref[...], pre_ref[...]
    inputs = to_input[...]
    side_ref[...] = inputs * softplus(dt_pre)
    grad_delta = to_decay[...] * (1.0 / log2e) + inputs * (pre * sigmoid(pre))
    grad_dt = grad_delta * sigmoid(dt_pre)
    bias_ref[...] = jnp.sum(grad_dt, axis=0)
    grad_dt = grad_dt.astype(bf16).reshape(steps * rows, lanes)
    grad_dtw_ref[...] = dot_tn(mapped_ref[...], grad_dt)
    total[...] += dot_nt(grad_dt, dtw_ref[...])

    @pl.when(place == tiles - 1)
    def _():
        wide = count * rows
        line = lax.broadcasted_iota(jnp.int32, (steps * rows, wide), 0) % rows
        lane = lax.broadcasted_iota(jnp.int32, (steps * rows, wide), 1)
        state = lax.broadcasted_iota(jnp.int32, (wide, total.shape[1]), 0) // rows
        column = lax.broadcasted_iota(jnp.int32, (wide, total.shape[1]), 1)
        sums = total[...]
        for which, source in enumerate((sum_in, sum_read)):
            values = jnp.where(lane % rows == line, source[...].reshape(steps * rows, wide), 0.0)
            pick = (column == rank + which * count + state).astype(bf16)
            sums = sums + dot(values.astype(bf16), pick)
        low_ref[...] = sums.astype(bf16)
        for task, part in zip(tasks, parts):
            part[...] = task.total().astype(bf16)
            task.close()
        under_way.finish()


def conv_back_kernel(states, taps, grad_mapped_ref, grad_y_ref, side_ref, pre_ref, ext_ref, params_ref, xproj_ref, valid_ref,
                     grad_ref, rim_ref, grad_xproj_ref, sums_ref, ext_grad):
    steps, rows, lanes = pre_ref.shape
    rim = taps - 1
    pre = pre_ref[...]
    sigma = sigmoid(pre)
    grad_act = dot(grad_mapped_ref[...], xproj_ref[...]).reshape(steps, rows, lanes)
    grad_act = grad_act + grad_y_ref[...] * params_ref[pl.ds(states + taps + 2, 1), :] + side_ref[...]
    grad_pre = grad_act * silu_slope(pre, sigma)
    act_low = (pre * sigma).astype(bf16).reshape(steps * rows, lanes)
    grad_xproj_ref[...] = dot_tn(grad_mapped_ref[...], act_low)
    ext_grad[...] = jnp.zeros_like(ext_grad)
    for k in range(taps):
        masked = grad_pre * valid_ref[:, :, k : k + 1]
        sums_ref[k] = jnp.sum(masked * ext_ref[pl.ds(k, steps)], axis=0)
        ext_grad[pl.ds(k, steps)] += masked * params_ref[pl.ds(states + k, 1), :]
    sums_ref[taps] = jnp.sum(grad_pre, axis=0)
    upper = lax.broadcasted_iota(jnp.int32, (rows, lanes), 0) >= rows // 2
    for j in range(rim):
        edge = ext_grad[j]
        rim_ref[j] = edge
        ext_grad[steps + j] += jnp.where(upper, 0.0, turned(edge))
    grad_ref[...] = ext_grad[pl.ds(rim, steps)]


def ends_kernel(count, items, tokens_ref, grad_ref, rim_ref, grad_z_ref, normed_ref, w_ref, *refs):
    number = len(items)
    xs, refs = refs[:number], refs[number:]
    grad_conv_ref, part_ref, gain_ref = refs[:3]
    outs, (came, send_sem, recv_sem), sems = refs[3 : 3 + number], refs[3 + number : 6 + number], refs[6 + number :]
    steps, lines, full = grad_ref.shape
    seqs, group, width = tokens_ref.shape
    rows, inner, rim = steps * lines, w_ref.shape[1], rim_ref.shape[0]
    here = lax.axis_index("seq")
    told = greet(sorted({("seq", count)} | set(axes_of(items))))
    pl.semaphore_wait(pltpu.get_barrier_semaphore(), told)
    edge = pltpu.make_async_remote_copy(
        src_ref=rim_ref,
        dst_ref=came,
        send_sem=send_sem,
        recv_sem=recv_sem,
        device_id={"seq": here - 1},
        device_id_type=MESH,
    )

    @pl.when(here > 0)
    def _():
        edge.start()

    under_way = Riders(items, xs, outs, sems).start()
    unit = unit_of(tokens_ref[...].reshape(rows, width).astype(f32))
    under_way.step()
    by_gate = dot(grad_z_ref[:, pl.ds(0, inner)], w_ref[1])
    under_way.step()

    @pl.when(here == count - 1)
    def _():
        came[...] = jnp.zeros(came.shape, f32)

    @pl.when(here < count - 1)
    def _():
        edge.wait_recv()

    upper = lax.broadcasted_iota(jnp.int32, (lines, full), 0) >= lines // 2
    last = [
        (grad_ref[steps - rim + j] + jnp.where(upper, turned(came[j]), 0.0))[None] for j in range(rim)
    ]
    grad = jnp.concatenate([grad_ref[pl.ds(0, steps - rim)]] + last, axis=0)
    grad = grad.reshape(rows, full).astype(bf16)
    for j in range(0, inner, LANES):
        many = min(LANES, inner - j)
        piece = dot_tn(grad[:, j : j + many], normed_ref[...])
        grad_conv_ref[pl.ds(j, many), :] = piece.astype(bf16)
        under_way.step()
    perm = perm_of(steps, lines, seqs)
    tile = next(t for t in (384, LANES, width) if width % t == 0)
    for j in range(0, width, tile):
        piece = dot(grad[:, :inner], w_ref[0, :, pl.ds(j, tile)]) + by_gate[:, j : j + tile]
        piece = dot_tn(perm, piece.astype(bf16))
        part_ref[:, pl.ds(j, tile)] = piece.astype(bf16)
        gain_ref[:, pl.ds(j, tile)] = jnp.sum(piece * unit[:, j : j + tile], axis=0, keepdims=True)
        under_way.step()
    under_way.finish()

    @pl.when(here > 0)
    def _():
        edge.wait_send()


def ends(tokens, grad, rim, grad_z, normed, w_in, number, *exchanges):
    steps, lines, full = grad.shape
    rows, width = normed.shape
    items = items_of(exchanges)
    anywhere = [pl.BlockSpec(memory_space=pl.ANY)] * len(items)
    return pl.pallas_call(
        functools.partial(ends_kernel, lax.axis_size("seq"), items),
        out_shape=[
            jax.ShapeDtypeStruct((w_in.shape[1], width), bf16),
            jax.ShapeDtypeStruct((rows, width), bf16),
            jax.ShapeDtypeStruct((1, width), f32),
        ]
        + [landed(x, item) for (x, _, _), item in zip(exchanges, items)],
        in_specs=[pl.BlockSpec(memory_space=pltpu.VMEM)] * 6 + anywhere,
        out_specs=[pl.BlockSpec(memory_space=pltpu.VMEM)] * 3 + anywhere,
        scratch_shapes=[
            pltpu.VMEM(rim.shape, f32),
            pltpu.SemaphoreType.DMA,
            pltpu.SemaphoreType.DMA,
        ]
        + [sem for item in items for sem in sems_of(item)],
        compiler_params=pltpu.CompilerParams(
            collective_id=number, has_side_effects=True, vmem_limit_bytes=36 * MIB
        ),
    )(tokens, grad, rim, grad_z, normed, w_in, *[x for x, _, _ in exchanges])


def hits_of(routes, experts, part, most, slots):
    rows = routes.shape[0]
    chosen = (lax.broadcasted_iota(jnp.int32, (rows, experts), 1) == routes).astype(f32)
    row = lax.broadcasted_iota(jnp.int32, (rows, rows), 0)
    other = lax.broadcasted_iota(jnp.int32, (rows, rows), 1)
    earlier = (other < row) & (row // part == other // part)
    ranks = jnp.sum(dot(earlier.astype(bf16), chosen.astype(bf16)) * chosen, axis=1, keepdims=True)
    slot = lax.broadcasted_iota(jnp.int32, (rows, 1), 0) // part * most + ranks.astype(jnp.int32)
    column = lax.broadcasted_iota(jnp.int32, (rows, experts * slots), 1)
    return chosen, (column == routes * slots + slot).astype(bf16)


def route_kernel(part, most, slots, tokens_ref, mixed_ref, gain_ref, routes_ref, router_ref,
                 hidden_ref, normed_ref, probs_ref, chosen_ref, hit_ref, packed_ref):
    hidden = tokens_ref[...].astype(f32) + mixed_ref[...]
    hidden_ref[...] = hidden
    normed = (unit_of(hidden) * gain_ref[...]).astype(bf16)
    normed_ref[...] = normed
    logits = dot_nt(normed, router_ref[...])
    raised = jnp.exp(logits - jnp.max(logits, axis=1, keepdims=True))
    probs_ref[...] = raised / jnp.sum(raised, axis=1, keepdims=True)
    chosen, hit = hits_of(routes_ref[...], router_ref.shape[0], part, most, slots)
    chosen_ref[...] = chosen
    hit_ref[...] = hit
    packed_ref[...] = dot_tn(hit, normed).astype(bf16)


def loss_kernel(group, lengths_ref, came_ref, back_ref, hit_ref, hidden_ref, probs_ref, chosen_ref, teacher_ref,
                layer_ref, grad_layer_ref, grad_logit_ref, loss_ref, packed_ref):
    rows, width = hidden_ref.shape
    seqs = lengths_ref.shape[0]
    expert = dot(back_ref[...], came_ref[...])
    probs, chosen = probs_ref[...], chosen_ref[...]
    gate = jnp.sum(probs * chosen, axis=1, keepdims=True)
    layer = hidden_ref[...] + gate * expert
    layer_ref[...] = layer.astype(bf16)
    flat_row = lax.axis_index("chan") * rows + lax.broadcasted_iota(jnp.int32, (rows, 1), 0)
    length = jnp.zeros((rows, 1), jnp.int32)
    total = 0
    for s in range(seqs):
        length = jnp.where(flat_row // group == s, lengths_ref[s], length)
        total = total + lengths_ref[s]
    scale = 1.0 / jnp.broadcast_to(total, (rows, 1)).astype(f32)
    at = lax.axis_index("seq") * group + flat_row % group
    mask = jnp.where(at < length, scale, 0.0)
    error = layer - teacher_ref[...].astype(f32)
    scaled = mask * error
    lost = jnp.sum(scaled * error, axis=0, keepdims=True)
    loss_ref[...] = jnp.broadcast_to(jnp.sum(lost, axis=1, keepdims=True), (1, width))
    grad_layer = 2.0 * scaled
    grad_layer_ref[...] = grad_layer
    grad_gate = jnp.sum(grad_layer * expert, axis=1, keepdims=True)
    grad_logit_ref[...] = grad_gate * gate * (chosen - probs)
    packed_ref[...] = dot_tn(hit_ref[...], (gate * grad_layer).astype(bf16)).astype(bf16)


def norm_back_kernel(came_ref, back_ref, grad_logit_ref, router_ref, normed_ref, hidden_ref, grad_layer_ref, gain_ref, loss_ref,
                     grad_ref, low_ref, shared_ref):
    experts = router_ref.shape[0]
    grad_logit = grad_logit_ref[...].astype(bf16)
    grad_normed = dot(back_ref[...], came_ref[...]) + dot(grad_logit, router_ref[...])
    hidden = hidden_ref[...]
    inverse = lax.rsqrt(jnp.mean(hidden * hidden, axis=1, keepdims=True) + epsilon)
    unit = hidden * inverse
    shared_ref[...] = jnp.zeros_like(shared_ref)
    shared_ref[pl.ds(0, experts), :] = dot_tn(grad_logit, normed_ref[...])
    shared_ref[pl.ds(experts, 1), :] = jnp.sum(grad_normed * unit, axis=0, keepdims=True)
    shared_ref[pl.ds(experts + 1, 1), :] = loss_ref[...]
    grad = grad_layer_ref[...] + norm_back(grad_normed, unit, inverse, gain_ref[...])
    grad_ref[...] = grad
    low_ref[...] = grad.astype(bf16)


def at_once(kernel, ins, outs, scalars=0):
    spaces = [pltpu.SMEM] * scalars + [pltpu.VMEM] * (len(ins) - scalars)
    return pl.pallas_call(
        kernel,
        in_specs=[pl.BlockSpec(memory_space=space) for space in spaces],
        out_specs=[pl.BlockSpec(memory_space=pltpu.VMEM)] * len(outs),
        out_shape=[jax.ShapeDtypeStruct(shape, dtype) for shape, dtype in outs],
        compiler_params=pltpu.CompilerParams(vmem_limit_bytes=12 * MIB),
        cost_estimate=pl.CostEstimate(flops=1000, bytes_accessed=1000, transcendentals=0),
    )(*ins)


def expert_kernel(x_ref, first_ref, second_ref, hidden_ref, slope_ref, result_ref, total):
    place = pl.program_id(0)

    @pl.when(place == 0)
    def _():
        total[...] = jnp.zeros_like(total)

    pre = dot(x_ref[...], first_ref[...])
    cdf = 0.5 * (1.0 + lax.erf(pre * 0.7071067811865476))
    hidden = (pre * cdf).astype(bf16)
    hidden_ref[0] = hidden
    slope = cdf + pre * (jnp.exp(-0.5 * pre * pre) * 0.3989422804014327)
    slope_ref[...] = slope.astype(bf16)
    total[...] += dot(hidden, second_ref[...])

    @pl.when(place == pl.num_programs(0) - 1)
    def _():
        result_ref[...] = total[...].astype(bf16)


def expert_back_kernel(grad_ref, first_ref, second_ref, slope_ref, grad_pre_ref, result_ref, total):
    place = pl.program_id(0)

    @pl.when(place == 0)
    def _():
        total[...] = jnp.zeros_like(total)

    grad = dot_nt(grad_ref[...], second_ref[...]) * slope_ref[...].astype(f32)
    grad = grad.astype(bf16)
    grad_pre_ref[0] = grad
    total[...] += dot_nt(grad, first_ref[...])

    @pl.when(place == pl.num_programs(0) - 1)
    def _():
        result_ref[...] = total[...].astype(bf16)


def expert(x, first, second, parts, slope=None):
    rows, width = x.shape
    units = first.shape[1] // parts
    tile = next((t for t in (768, 384, 256, 128) if units % t == 0), None)
    low = jax.ShapeDtypeStruct((rows, width), bf16)
    if tile is None:

        def split(h):
            return h.reshape(rows, parts, units).transpose(1, 0, 2)

        if slope is not None:
            grad = (dot_nt(x, second) * slope.astype(f32)).astype(bf16)
            return split(grad), dot_nt(grad, first).astype(bf16)
        pre = dot(x, first)
        cdf = 0.5 * (1.0 + lax.erf(pre * 0.7071067811865476))
        hidden = (pre * cdf).astype(bf16)
        slope = cdf + pre * (jnp.exp(-0.5 * pre * pre) * 0.3989422804014327)
        return split(hidden), slope.astype(bf16), dot(hidden, second).astype(bf16)
    each = units // tile
    columns = pl.BlockSpec((width, tile), lambda i: (0, i))
    lines = pl.BlockSpec((tile, width), lambda i: (i, 0))
    everything = pl.BlockSpec((rows, width), lambda i: (0, 0))
    slopes = pl.BlockSpec((rows, tile), lambda i: (0, i))
    hiddens = pl.BlockSpec((1, rows, tile), lambda i: (i // each, 0, i % each))
    hidden_shape = jax.ShapeDtypeStruct((parts, rows, units), bf16)
    back = slope is not None
    return pl.pallas_call(
        expert_back_kernel if back else expert_kernel,
        grid=(parts * each,),
        in_specs=[everything, columns, lines] + ([slopes] if back else []),
        out_specs=[hiddens] + ([] if back else [slopes]) + [everything],
        out_shape=[hidden_shape]
        + ([] if back else [jax.ShapeDtypeStruct((rows, first.shape[1]), bf16)])
        + [low],
        scratch_shapes=[pltpu.VMEM((rows, width), f32)],
        compiler_params=pltpu.CompilerParams(vmem_limit_bytes=60 * MIB),
        cost_estimate=pl.CostEstimate(flops=1000, bytes_accessed=1000, transcendentals=0),
    )(x, first, second, *([slope] if back else []))


def widen_kernel(conv_ref, gate_ref, *refs):
    half = len(refs) // 2
    refs[half][0] = conv_ref[...].astype(f32)
    refs[half][1] = gate_ref[...].astype(f32)
    for x_ref, o_ref in zip(refs[:half], refs[half + 1 :]):
        o_ref[...] = x_ref[...].astype(f32)


def widened(conv, gate, *arrays):
    sizes = [x.shape[0] for x in (conv, *arrays)]
    pieces = next(n for n in (6, 4, 3, 2, 1) if all(size % (16 * n) == 0 for size in sizes) or n == 1)

    def block(x):
        return pl.BlockSpec((x.shape[0] // pieces, x.shape[1]), lambda i: (i, 0))

    each, width = conv.shape[0] // pieces, conv.shape[1]
    return pl.pallas_call(
        widen_kernel,
        grid=(pieces,),
        in_specs=[block(x) for x in (conv, gate, *arrays)],
        out_specs=[pl.BlockSpec((2, each, width), lambda i: (0, i, 0))] + [block(x) for x in arrays],
        out_shape=[jax.ShapeDtypeStruct((2,) + conv.shape, f32)]
        + [jax.ShapeDtypeStruct(x.shape, f32) for x in arrays],
        compiler_params=pltpu.CompilerParams(vmem_limit_bytes=20 * MIB),
        cost_estimate=pl.CostEstimate(flops=1000, bytes_accessed=1000, transcendentals=0),
    )(conv, gate, *arrays)


def block_of(shape, kind):
    if kind == "tile":
        return pl.BlockSpec(shape[:-1] + (LANES,), lambda i: (0,) * (len(shape) - 1) + (i,))
    if kind == "rows":
        return pl.BlockSpec((LANES,) + shape[1:], lambda i: (i,) + (0,) * (len(shape) - 1))
    if kind == "any":
        return pl.BlockSpec(memory_space=pl.ANY)
    return pl.BlockSpec(shape, lambda i: (0,) * len(shape))


def share_scratch(x, axis, size):
    groups = lax.axis_size(axis) // size
    part = x.shape[1:]
    return [
        pltpu.VMEM((groups, size - 1) + part, x.dtype),
        pltpu.VMEM((groups - 1,) + part, x.dtype),
        pltpu.VMEM((groups - 1,) + part, x.dtype),
        pltpu.SemaphoreType.DMA((groups, size - 1)),
        pltpu.SemaphoreType.DMA((groups, size - 1)),
        pltpu.SemaphoreType.DMA((groups - 1,)),
        pltpu.SemaphoreType.DMA((groups - 1,)),
    ]


def by_tiles(kernel, room, full, ins, outs, scratch, more=(), params=None):
    return pl.pallas_call(
        kernel,
        grid=(full // LANES,),
        in_specs=[block_of(a.shape, kind) for a, kind in ins],
        out_specs=[block_of(shape, kind) for shape, _, kind in outs],
        out_shape=[jax.ShapeDtypeStruct(shape, dtype) for shape, dtype, _ in outs],
        scratch_shapes=[pltpu.VMEM(shape, dtype) for shape, dtype in scratch] + list(more),
        compiler_params=pltpu.CompilerParams(vmem_limit_bytes=room * MIB, **(params or {})),
        cost_estimate=pl.CostEstimate(flops=1000, bytes_accessed=1000, transcendentals=0),
    )(*[a for a, _ in ins])


def norm_back(grad_normed, unit_rows, inverse, weight_gain):
    scaled = grad_normed * weight_gain
    return inverse * (scaled - unit_rows * jnp.mean(scaled * unit_rows, axis=-1, keepdims=True))


def local(
    tokens,
    teacher,
    true_lengths,
    doc_lengths,
    routes,
    norm1_gain,
    in_weight,
    conv_weight,
    conv_bias,
    xproj_weight,
    dt_weight,
    dt_bias,
    a_log,
    skip_weight,
    out_weight,
    norm2_gain,
    router_weight,
    expert_in,
    expert_out,
):
    seqs, group, width = tokens.shape
    inner = in_weight.shape[2]
    rank = dt_weight.shape[0]
    states = a_log.shape[1]
    experts = router_weight.shape[1]
    n_seq = lax.axis_size("seq")
    n_chan = lax.axis_size("chan")
    shards = n_seq // experts
    most = group // 4
    taps = conv_weight.shape[0]
    rim = taps - 1
    lines = 8
    chunks = lines // seqs
    steps = group // chunks
    owned = seqs * group // n_chan
    part = min(group, owned)
    most = min(most, part)
    parts = owned // part
    place = lax.axis_index("chan")
    first_pos = lax.axis_index("seq") * group

    full = -(-inner // LANES) * LANES
    rows = steps * lines
    maps = rank + 2 * states

    def padded(x):
        return jnp.pad(x, ((0, 0),) * (x.ndim - 1) + ((0, full - inner),))

    at = (
        first_pos
        + jnp.arange(steps, dtype=jnp.int32)[:, None]
        + (jnp.arange(lines, dtype=jnp.int32) // seqs * steps)[None, :]
    )
    stops = []
    for k in range(doc_lengths.shape[1] - 1):
        stops.append(doc_lengths[:, k] + (stops[-1] if stops else 0))
    stops = [jnp.tile(stop, chunks)[None, :] for stop in stops]

    def doc_at(pos):
        return sum((pos >= stop).astype(jnp.int32) for stop in stops)

    doc_ids = doc_at(at)
    keep = (doc_ids == doc_at(at - 1)) & (at > 0)
    valid = [doc_at(at - rim + k) == doc_ids for k in range(taps)] + [keep]
    valid = jnp.stack(valid + [keep] * (lines - taps - 1), axis=-1).astype(f32)

    w_in = in_weight.transpose(1, 2, 0)
    router_rows = router_weight.T
    gain_one = norm1_gain.astype(f32)
    xproj_rows = padded(xproj_weight.T)
    dt_rows = jnp.pad(padded(dt_weight), ((0, maps - rank), (0, 0)))
    rate = -jnp.exp(a_log.T)
    params = [rate * log2e, conv_weight, conv_bias[None], dt_bias[None], skip_weight[None]]
    params = jnp.concatenate([x.astype(f32) for x in params], axis=0)
    params = jnp.pad(params, ((0, -params.shape[0] % 8), (0, full - inner)))
    normed_one, extended, pre_act, gate_z, mapped = front(
        tokens,
        gain_one[None],
        w_in,
        params,
        states,
        taps,
        xproj_rows,
        valid,
        full,
        1,
    )
    act_shape, state_shape, wide_shape = (steps, lines, full), (states, lines, full), (states, steps, lines, LANES)
    dt_pre, step_size, drive, own_states, sums = by_tiles(
        functools.partial(totals_kernel, rank, taps),
        20,
        full,
        [
            (pre_act, "tile"),
            (mapped, "whole"),
            (dt_rows, "tile"),
            (valid, "whole"),
            (params, "tile"),
        ],
        [
            (act_shape, f32, "tile"),
            (act_shape, f32, "tile"),
            (act_shape, f32, "tile"),
            (state_shape, f32, "tile"),
            ((lines, full), f32, "tile"),
        ],
        [(wide_shape, f32)],
    )
    (enter,) = carried(own_states, sums, params, "seq", False, 2)
    y_full, gated, state, out_part = by_tiles(
        functools.partial(states_kernel, rank, seqs, taps, inner),
        36,
        full,
        [
            (step_size, "tile"),
            (drive, "tile"),
            (mapped, "whole"),
            (params, "tile"),
            (enter, "tile"),
            (pre_act, "tile"),
            (gate_z, "tile"),
            (out_weight, "rows"),
        ],
        [
            (act_shape, f32, "tile"),
            ((rows, full), bf16, "tile"),
            ((steps, states, lines, full), f32, "tile"),
            ((rows, width), bf16, "whole"),
        ],
        [(wide_shape, f32)] * 2 + [((rows, width), f32)],
    )
    (mixed,) = share_of(3, [(out_part.reshape(n_chan, owned, width), "chan", 2, f32)])

    def own(x):
        return lax.dynamic_slice_in_dim(x.reshape((rows,) + x.shape[2:]), place * owned, owned, 0)

    slots = parts * most
    tokens_own, gain_two = own(tokens), norm2_gain.astype(f32)[None]
    line, low = (owned, width), ((owned, width), bf16)
    hidden_one, normed_two, probs, chosen, hit, packed = at_once(
        functools.partial(route_kernel, part, most, slots),
        [tokens_own, mixed, gain_two, own(routes)[:, None], router_rows],
        [
            (line, f32),
            low,
            ((owned, experts), f32),
            ((owned, experts), f32),
            ((owned, experts * slots), bf16),
            ((experts * slots, width), bf16),
        ],
    )
    hit_back = hit
    if shards > 1:
        hit_back = hit.reshape(owned, experts, slots)
        hit_back = jnp.repeat(hit_back, shards, axis=1).reshape(owned, n_seq * slots)

    def to_slabs(x):
        x = x.reshape(experts, slots, width)
        return x if shards == 1 else jnp.repeat(x, shards, axis=0), "scatter", "seq"

    def to_rows(x):
        return x.reshape(n_seq, slots, width), "scatter", "seq"

    def flat(x):
        return x.reshape(-1, x.shape[-1])

    first_slab, second_slab = expert_in[0], expert_out[0]
    arrived = flat(exchange(4, to_slabs(packed))[0])
    hidden, slope, result = expert(arrived, first_slab, second_slab, n_chan)
    (result_rows,) = exchange(5, to_rows(result))
    layer_low, grad_layer, grad_logit, loss_row, packed = at_once(
        functools.partial(loss_kernel, group),
        [
            true_lengths,
            flat(result_rows),
            hit_back,
            hit,
            hidden_one,
            probs,
            chosen,
            own(teacher),
        ],
        [
            low,
            (line, f32),
            ((owned, experts), f32),
            ((1, width), f32),
            ((experts * slots, width), bf16),
        ],
        scalars=1,
    )
    grad_rows = flat(exchange(6, to_slabs(packed))[0])
    grad_pre, grad_slab_rows = expert(grad_rows, first_slab, second_slab, n_chan, slope)
    (grad_expert,) = exchange(7, to_rows(grad_slab_rows))
    shared_rows = -(-(experts + 2) // 8) * 8
    grad_hidden_one, grad_low, shared = at_once(
        norm_back_kernel,
        [
            flat(grad_expert),
            hit_back,
            grad_logit,
            router_rows,
            normed_two,
            hidden_one,
            grad_layer,
            gain_two,
            loss_row,
        ],
        [(line, f32), low, ((shared_rows, width), f32)],
    )

    (grad_mixed,) = exchange(8, (grad_low, 2, "chan"))
    grad_y, grad_z, grad_out_w, grad_in_gate, skip_sums, back_last = by_tiles(
        functools.partial(back_totals_kernel, rank, seqs, inner),
        28,
        full,
        [
            (step_size, "tile"),
            (mapped, "whole"),
            (params, "tile"),
            (grad_mixed.reshape(rows, width), "whole"),
            (normed_one, "whole"),
            (out_weight, "rows"),
            (gate_z, "tile"),
            (y_full, "tile"),
            (gated, "tile"),
            (pre_act, "tile"),
        ],
        [
            (act_shape, f32, "tile"),
            ((rows, full), bf16, "tile"),
            ((inner, width), bf16, "rows"),
            ((inner, width), bf16, "rows"),
            ((lines, full), f32, "tile"),
            (state_shape, f32, "tile"),
        ],
        [(wide_shape, f32), ((rows, width), bf16)],
    )
    back_enter, shared = carried(
        back_last, sums, params, "seq", True, 9, (shared, "gather", "chan")
    )
    shared = jnp.sum(shared, axis=0).reshape(-1, LANES)
    def cut_rows(x, unit):
        each = -(-x.shape[0] // (unit * n_seq)) * unit
        return jnp.pad(x, ((0, each * n_seq - x.shape[0]), (0, 0))).reshape(n_seq, each, -1)

    across = n_chan // 2
    by_out, by_gate = cut_rows(grad_out_w, 8), cut_rows(grad_in_gate, 8)
    riders = [(hidden, "scatter", "chan"), (grad_pre, "scatter", "chan")]
    items = items_of(riders)
    side, log_sums, bias_sums, grad_dt_w, low_part, by_out, by_gate, hidden_all, grad_pre_all = by_tiles(
        functools.partial(back_kernel, rank, full // LANES, [("seq", n_seq, across)] * 2, items),
        46,
        full,
        [
            (step_size, "tile"),
            (drive, "tile"),
            (grad_y, "tile"),
            (mapped, "whole"),
            (params, "tile"),
            (enter, "tile"),
            (state, "tile"),
            (back_enter, "tile"),
            (dt_pre, "tile"),
            (pre_act, "tile"),
            (dt_rows, "tile"),
            (by_out, "any"),
            (by_gate, "any"),
            (hidden, "any"),
            (grad_pre, "any"),
        ],
        [
            (act_shape, f32, "tile"),
            (state_shape, f32, "tile"),
            ((lines, full), f32, "tile"),
            ((maps, full), f32, "tile"),
            ((rows, maps), bf16, "whole"),
            (by_out.shape[1:], bf16, "whole"),
            (by_gate.shape[1:], bf16, "whole"),
            (hidden.shape, bf16, "any"),
            (grad_pre.shape, bf16, "any"),
        ],
        [(wide_shape, f32)] * 2
        + [((steps, lines, states * lines), f32)] * 2
        + [((steps, lines, LANES), f32)] * 2
        + [((rows, maps), f32)]
        + [(by_out.shape, bf16)] * 2,
        [pltpu.SemaphoreType.DMA((2,))]
        + share_scratch(by_out, "seq", across)
        + share_scratch(by_gate, "seq", across)
        + [sem for item in items for sem in sems_of(item)],
        {"collective_id": 15, "has_side_effects": True},
    )
    grad_mapped = summed_over(low_part, "chan", 10).astype(bf16)
    grad_conv_in, rims, grad_xproj, conv_sums = by_tiles(
        functools.partial(conv_back_kernel, states, taps),
        20,
        full,
        [
            (grad_mapped, "whole"),
            (grad_y, "tile"),
            (side, "tile"),
            (pre_act, "tile"),
            (extended, "tile"),
            (params, "tile"),
            (xproj_rows, "tile"),
            (valid, "whole"),
        ],
        [
            (act_shape, f32, "tile"),
            ((rim, lines, full), f32, "tile"),
            ((maps, full), f32, "tile"),
            ((taps + 1, lines, full), f32, "tile"),
        ],
        [((steps + rim, lines, LANES), f32)],
    )
    grad_in_conv, normed_part, grad_gain_one, by_gate, rows_all = ends(
        tokens,
        grad_conv_in,
        rims,
        grad_z,
        normed_one,
        w_in,
        14,
        (by_gate, across, "seq"),
        (arrived, 2, "chan"),
    )
    normed_part = normed_part.reshape(n_chan, owned, width)
    sums_all = jnp.concatenate([conv_sums, bias_sums[None], skip_sums[None], log_sums], axis=0)
    sums_all = jnp.sum(sums_all, axis=1)
    small_rows = sums_all.shape[0] * full // LANES
    small = jnp.concatenate([sums_all.reshape(small_rows, LANES), shared], axis=0)

    by_conv = cut_rows(grad_in_conv, 8)
    middle = cut_rows(jnp.concatenate([grad_xproj, grad_dt_w[:rank]], axis=0).astype(bf16), 16)
    grad_normed_one, small, middle, by_conv, grad_gain_one, by_out, grad_rows_all = share_of(
        11,
        [
            (normed_part, "chan", 2, f32),
            (cut_rows(small, 8), "seq", across, f32),
            (middle, "seq", across, bf16),
            (by_conv, "seq", across, bf16),
        ],
        (grad_gain_one, "gather", "chan"),
        (by_out, across, "seq"),
        (grad_rows, 2, "chan"),
    )
    grad_first = dot_tn(flat(rows_all), flat(grad_pre_all))
    grad_second = dot_tn(flat(hidden_all), flat(grad_rows_all))
    grad_gain_one = jnp.sum(grad_gain_one, axis=0)
    tokens_full = tokens_own.astype(f32)
    inverse_one = lax.rsqrt(jnp.mean(tokens_full * tokens_full, axis=-1, keepdims=True) + epsilon)
    grad_own = grad_hidden_one + norm_back(
        grad_normed_one, tokens_full * inverse_one, inverse_one, gain_one
    )
    moved = [
        (grad_own.astype(bf16), 2, "chan"),
        (layer_low, 2, "chan"),
        (small, across, "seq"),
        (middle, across, "seq"),
        (by_conv, across, "seq"),
        (grad_gain_one, "gather", "seq"),
    ]
    grad_first, grad_second, grad_low = lax.optimization_barrier((grad_first, grad_second, moved[0][0]))
    moved[0] = (grad_low,) + moved[0][1:]
    moved = exchange(12, *moved)
    grad_tokens, layer_out, small, middle, by_conv, grad_gain_one = moved
    grad_gain_one = jnp.sum(grad_gain_one, axis=(0, 1))
    summed_in, summed_out, grad_tokens = widened(
        flat(by_conv)[:inner], flat(by_gate)[:inner], flat(by_out)[:inner], flat(grad_tokens)
    )
    middle = flat(middle)[:, :inner].astype(f32)
    small = flat(small)
    shared = small[small_rows : small_rows + shared_rows * width // LANES].reshape(shared_rows, width)
    small = small[:small_rows].reshape(-1, full)[:, :inner]
    return (
        layer_out.reshape(seqs, group, width),
        shared[experts + 1, 0],
        grad_tokens.reshape(seqs, group, width),
        grad_gain_one,
        summed_in.transpose(2, 0, 1),
        small[:taps],
        small[taps],
        middle[:maps].T,
        middle[maps : maps + rank],
        small[taps + 1],
        (small[taps + 3 : taps + 3 + states] * rate).T,
        small[taps + 2],
        summed_out,
        shared[experts],
        shared[:experts].T,
        grad_first[None],
        grad_second[None],
    )


def solution(mesh):
    placed = (
        P(None, "seq", None),
        P(None, "seq", None),
        P(),
        P(),
        P(None, "seq"),
        P(),
        P(None, None, "chan"),
        P(None, "chan"),
        P("chan"),
        P("chan", None),
        P(None, "chan"),
        P("chan"),
        P("chan", None),
        P("chan"),
        P("chan", None),
        P(),
        P(),
        P("seq", None, None),
        P("seq", None, None),
    )
    return jax.shard_map(
        local,
        mesh=mesh,
        in_specs=placed,
        out_specs=(
            P(None, "seq", None),
            P(),
            P(None, "seq", None),
            P(),
            P(None, None, "chan"),
            P(None, "chan"),
            P("chan"),
            P("chan", None),
            P(None, "chan"),
            P("chan"),
            P("chan", None),
            P("chan"),
            P("chan", None),
            P(),
            P(),
            P("seq", None, "chan"),
            P("seq", "chan", None),
        ),
        check_vma=False,
    )
```

```python
import functools

import jax
import jax.numpy as jnp
from jax import lax
from jax.experimental import pallas as pl
from jax.experimental.pallas import tpu as pltpu
from jax.sharding import PartitionSpec as P

epsilon = 1e-05
log2e = 1.4426950408889634
cut = 1e30
MESH = pl.DeviceIdType.MESH
f32 = jnp.float32
bf16 = jnp.bfloat16
LANES = 128
MIB = 1024 * 1024
AHEAD = 12


def greet(axes):
    barrier = pltpu.get_barrier_semaphore()
    told = 0
    for axis, count in axes:
        me = lax.axis_index(axis)
        for k in range(1, count):
            pl.semaphore_signal(
                barrier, inc=1, device_id={axis: lax.rem(me + k, count)}, device_id_type=MESH
            )
        told += count - 1
    return told


def cuts_of(size):
    half = -(-size // 32) * 16
    return [(0, half), (half, size - half)] if half < size and size % 16 == 0 else [(0, size)]


def sems_of(item):
    copies = 2 * (item[2] - 1)
    return [pltpu.SemaphoreType.DMA] + [pltpu.SemaphoreType.DMA((copies,))] * 2


def flipped(i, mask):
    bit = 1
    while bit <= mask:
        if mask & bit:
            i = i + bit - 2 * bit * lax.rem(i // bit, 2)
        bit *= 2
    return i


def order_of(groups):
    masks, low, high = [], 1, groups - 1
    while low <= high:
        masks += [high] if low == high else [high, low]
        low, high = low + 1, high - 1
    return masks


class Riders:
    def __init__(self, items, xs, outs, sems):
        self.own, self.copies, self.chains = [], [], {}
        for i, item in enumerate(items):
            self.add(item, xs[i], outs[i], *sems[3 * i : 3 * i + 3])
        self.at = {axis: 0 for axis in self.chains}

    def start(self):
        for copy in self.copies + self.own:
            copy.start()
        for chain in self.chains.values():
            for first, _ in chain[:AHEAD]:
                first.start()
        return self

    def add(self, item, x_ref, o_ref, own_sem, send_sem, recv_sem):
        mode, axis, count = item
        me = lax.axis_index(axis)

        def remote(source, row, slot, to, cut=None):
            target = o_ref.at[row]
            if cut is not None:
                source, target = source.at[pl.ds(*cut)], o_ref.at[row, pl.ds(*cut)]
            return pltpu.make_async_remote_copy(
                src_ref=source,
                dst_ref=target,
                send_sem=send_sem.at[slot],
                recv_sem=recv_sem.at[slot],
                device_id={axis: to},
                device_id_type=MESH,
            )

        source = x_ref.at[me] if mode == "scatter" else x_ref
        self.own.append(pltpu.make_async_copy(source, o_ref.at[me], own_sem))
        if mode in ("gather", "scatter"):
            for mask in range(count - 1, 0, -1):
                to = flipped(me, mask)
                source = x_ref.at[to] if mode == "scatter" else x_ref
                self.copies.append(remote(source, me, mask - 1, to))
            return
        groups = count // mode
        side, place = lax.rem(me, mode), me // mode
        mates = [place * mode + lax.rem(side + j, mode) for j in range(1, mode)]
        slot = 0
        for mate in mates:
            self.copies.append(remote(x_ref, me, slot, mate))
            slot += 1
        chain = self.chains.setdefault(axis, [])
        masks = order_of(groups)
        for mask in masks[1::2] + masks[::2]:
            row = flipped(place, mask) * mode + side
            for cut in cuts_of(x_ref.shape[0]):
                first = remote(x_ref, me, slot, row, cut)
                slot += 1
                passed = []
                for mate in mates:
                    passed.append(remote(o_ref.at[row], row, slot, mate, cut))
                    slot += 1
                chain.append((first, passed))

    def left(self):
        return any(self.at[axis] < len(chain) for axis, chain in self.chains.items())

    def step(self):
        for axis in sorted(self.chains, reverse=True):
            i, chain = self.at[axis], self.chains[axis]
            if i == len(chain):
                continue
            self.at[axis] = i + 1
            first, passed = chain[i]
            first.wait_recv()
            for copy in passed:
                copy.start()
            if i + AHEAD < len(chain):
                chain[i + AHEAD][0].start()
            return

    def finish(self):
        while self.left():
            self.step()
        for copy in self.own + self.copies:
            copy.wait()
        for chain in self.chains.values():
            for first, passed in chain:
                first.wait_send()
                for copy in passed:
                    copy.wait()


def items_of(exchanges):
    return [(mode, axis, lax.axis_size(axis)) for _, mode, axis in exchanges]


def axes_of(items):
    return sorted({(axis, count) for _, axis, count in items})


def landed(x, item):
    shape = x.shape if item[0] == "scatter" else (item[2],) + x.shape
    return jax.ShapeDtypeStruct(shape, x.dtype)


def exchange_kernel(items, *refs):
    number = len(items)
    sems = refs[2 * number :]
    pl.semaphore_wait(pltpu.get_barrier_semaphore(), greet(axes_of(items)))
    Riders(items, refs[:number], refs[number : 2 * number], sems).start().finish()


def exchange(number, *exchanges):
    items = items_of(exchanges)
    return pl.pallas_call(
        functools.partial(exchange_kernel, items),
        out_shape=[landed(x, item) for (x, _, _), item in zip(exchanges, items)],
        in_specs=[pl.BlockSpec(memory_space=pl.ANY)] * len(items),
        out_specs=[pl.BlockSpec(memory_space=pl.ANY)] * len(items),
        scratch_shapes=[sem for item in items for sem in sems_of(item)],
        compiler_params=pltpu.CompilerParams(
            collective_id=number, has_side_effects=True, vmem_limit_bytes=4 * MIB
        ),
    )(*[x for x, _, _ in exchanges])


def greet_near(axis, count):
    barrier = pltpu.get_barrier_semaphore()
    me = lax.axis_index(axis)
    beside = me + 1 - 2 * lax.rem(me, 2)
    pl.semaphore_signal(barrier, inc=1, device_id={axis: beside}, device_id_type=MESH)
    for k in range(1, count // 2):
        pl.semaphore_signal(
            barrier, inc=1, device_id={axis: lax.rem(me + 2 * k, count)}, device_id_type=MESH
        )
    pl.semaphore_wait(barrier, count // 2)


def sum_kernel(axis, count, x_ref, o_ref, beside_in, pair, far_in, send_sem, recv_sem):
    me = lax.axis_index(axis)
    beside = me + 1 - 2 * lax.rem(me, 2)
    greet_near(axis, count)
    near = pltpu.make_async_remote_copy(
        src_ref=x_ref,
        dst_ref=beside_in,
        send_sem=send_sem.at[0],
        recv_sem=recv_sem.at[0],
        device_id={axis: beside},
        device_id_type=MESH,
    )
    near.start()
    near.wait_recv()
    pair[...] = (x_ref[...].astype(f32) + beside_in[...].astype(f32)).astype(bf16)
    copies = []
    for k in range(1, count // 2):
        copies.append(
            pltpu.make_async_remote_copy(
                src_ref=pair,
                dst_ref=far_in.at[k - 1],
                send_sem=send_sem.at[k],
                recv_sem=recv_sem.at[k],
                device_id={axis: lax.rem(me + 2 * k, count)},
                device_id_type=MESH,
            )
        )
        copies[-1].start()
    for copy in copies:
        copy.wait_recv()
    total = pair[...].astype(f32)
    for k in range(count // 2 - 1):
        total = total + far_in[k].astype(f32)
    o_ref[...] = total
    near.wait_send()
    for copy in copies:
        copy.wait_send()


def summed_over(x, axis, number):
    count = lax.axis_size(axis)
    return pl.pallas_call(
        functools.partial(sum_kernel, axis, count),
        out_shape=jax.ShapeDtypeStruct(x.shape, f32),
        in_specs=[pl.BlockSpec(memory_space=pltpu.VMEM)],
        out_specs=pl.BlockSpec(memory_space=pltpu.VMEM),
        scratch_shapes=[
            pltpu.VMEM(x.shape, bf16),
            pltpu.VMEM(x.shape, bf16),
            pltpu.VMEM((count // 2 - 1,) + x.shape, bf16),
            pltpu.SemaphoreType.DMA((count // 2,)),
            pltpu.SemaphoreType.DMA((count // 2,)),
        ],
        compiler_params=pltpu.CompilerParams(
            collective_id=number, has_side_effects=True, vmem_limit_bytes=8 * MIB
        ),
    )(x)


class Share:
    def __init__(self, axis, count, size, x_ref, near_in, pairs, far_in, near_send, near_recv, far_send, far_recv):
        self.groups, self.size, self.x = count // size, size, x_ref
        self.near_in, self.pairs, self.far_in = near_in, pairs, far_in
        me = lax.axis_index(axis)
        side, place = lax.rem(me, size), me // size
        self.rows, self.near, self.far = [], [], []
        for k in range(self.groups):
            group = flipped(place, (order_of(self.groups) + [0])[k])
            self.rows.append(group * size + side)
            self.near.append(
                [
                    pltpu.make_async_remote_copy(
                        src_ref=x_ref.at[group * size + lax.rem(side + j, size)],
                        dst_ref=near_in.at[k, j - 1],
                        send_sem=near_send.at[k, j - 1],
                        recv_sem=near_recv.at[k, j - 1],
                        device_id={axis: place * size + lax.rem(side + j, size)},
                        device_id_type=MESH,
                    )
                    for j in range(1, size)
                ]
            )
            if k < self.groups - 1:
                self.far.append(
                    pltpu.make_async_remote_copy(
                        src_ref=pairs.at[k],
                        dst_ref=far_in.at[k],
                        send_sem=far_send.at[k],
                        recv_sem=far_recv.at[k],
                        device_id={axis: self.rows[k]},
                        device_id_type=MESH,
                    )
                )

    def begin(self, k):
        for copy in self.near[k]:
            copy.start()

    def near_sum(self, k, wait=True):
        total = self.x[self.rows[k]].astype(f32)
        for j, copy in enumerate(self.near[k]):
            if wait:
                copy.wait_recv()
            total = total + self.near_in[k, j].astype(f32)
        return total

    def pass_on(self, k):
        if k < self.groups - 1:
            self.pairs[k] = self.near_sum(k).astype(self.pairs.dtype)
            self.far[k].start()
        else:
            for copy in self.near[k]:
                copy.wait_recv()

    def total(self):
        total = self.near_sum(self.groups - 1, False)
        for k, copy in enumerate(self.far):
            copy.wait_recv()
            total = total + self.far_in[k].astype(f32)
        return total

    def close(self):
        for copy in [copy for copies in self.near for copy in copies] + self.far:
            copy.wait_send()


def share_kernel(shares, items, *refs):
    many, number = len(shares), len(items)
    at = 0

    def take(k):
        nonlocal at
        at += k
        return refs[at - k : at]

    xs, riders, outs, rider_outs = take(many), take(number), take(many), take(number)
    tasks = [Share(axis, count, size, x, *take(7)) for (axis, count, size), x in zip(shares, xs)]
    axes = set(axes_of(items)) | {(axis, count) for axis, count, _ in shares}
    told = greet(sorted(axes))
    rider_sems = take(3 * number)
    pl.semaphore_wait(pltpu.get_barrier_semaphore(), told)
    turns = {}
    for (axis, _, _), task in zip(shares, tasks):
        turns.setdefault(axis, []).extend((task, k) for k in range(task.groups))
    for turn in turns.values():
        for task, k in turn[:AHEAD]:
            task.begin(k)
    under_way = Riders(items, riders, rider_outs, rider_sems).start()
    for i in range(max(len(turn) for turn in turns.values())):
        for turn in turns.values():
            if i < len(turn):
                task, k = turn[i]
                task.pass_on(k)
                if i + AHEAD < len(turn):
                    task, k = turn[i + AHEAD]
                    task.begin(k)
        under_way.step()
    for task, out in zip(tasks, outs):
        out[...] = task.total().astype(out.dtype)
    for task in tasks:
        task.close()
    under_way.finish()


def share_of(number, shares, *exchanges):
    items = items_of(exchanges)
    anywhere = [pl.BlockSpec(memory_space=pl.ANY)] * len(items)
    held = [pl.BlockSpec(memory_space=pltpu.VMEM)] * len(shares)
    scratch = []
    for x, axis, size, _ in shares:
        scratch += share_scratch(x, axis, size)
    outs = [jax.ShapeDtypeStruct(x.shape[1:], kind) for x, _, _, kind in shares]
    outs += [landed(x, item) for (x, _, _), item in zip(exchanges, items)]
    scratch += [sem for item in items for sem in sems_of(item)]
    return pl.pallas_call(
        functools.partial(
            share_kernel, [(axis, lax.axis_size(axis), size) for _, axis, size, _ in shares], items
        ),
        out_shape=outs,
        in_specs=held + anywhere,
        out_specs=held + anywhere,
        scratch_shapes=scratch,
        compiler_params=pltpu.CompilerParams(
            collective_id=number, has_side_effects=True, vmem_limit_bytes=18 * MIB
        ),
    )(*[share[0] for share in shares], *[x for x, _, _ in exchanges])


def turned(value):
    return pltpu.roll(value, value.shape[0] // 2, 0)


def carry_kernel(axis, count, back, items, *refs):
    number = len(items)
    local_ref, sums_ref, rate_ref = refs[:3]
    xs, o_ref, outs = refs[3 : 3 + number], refs[3 + number], refs[4 + number : 4 + 2 * number]
    send, got, send_sum, got_sum, total, enter = refs[4 + 2 * number : 10 + 2 * number]
    send_sem, recv_sem, send_sum_sem, recv_sum_sem = refs[10 + 2 * number : 14 + 2 * number]
    sems = refs[14 + 2 * number :]
    me = lax.axis_index(axis)
    states, rows, width = local_ref.shape
    half = rows // 2
    spans = []
    span = 1
    while span < count:
        spans.append(span)
        span *= 2
    sign = -1 if back else 1
    barrier = pltpu.get_barrier_semaphore()
    greeted = greet(axes_of(items))
    for span in spans:
        for by in (span, -span):
            there = me + by
            greeted = greeted + jnp.where((there >= 0) & (there < count), 1, 0)

            @pl.when((there >= 0) & (there < count))
            def _():
                pl.semaphore_signal(barrier, inc=1, device_id={axis: there}, device_id_type=MESH)

    upper = lax.broadcasted_iota(jnp.int32, (rows, width), 0) >= half
    first = upper if back else jnp.logical_not(upper)
    sums = sums_ref[...]
    sums_turned = turned(sums)
    sums_both = sums + sums_turned
    sums_first = jnp.where(first, sums, sums_turned)
    sums_last = jnp.where(first, sums_turned, sums)

    def packed_rate(j):
        return jnp.where(upper, rate_ref[pl.ds(2 * j + 1, 1), :], rate_ref[pl.ds(2 * j, 1), :])

    def both(j):
        even, odd = local_ref[2 * j], local_ref[2 * j + 1]
        low = jnp.where(upper, turned(odd), even)
        high = jnp.where(upper, odd, turned(even))
        return (high, low) if back else (low, high)

    for j in range(states // 2):
        opening, closing = both(j)
        total[j] = jnp.exp2(packed_rate(j) * sums_last) * opening + closing
        enter[j] = jnp.zeros((rows, width), f32)

    pl.semaphore_wait(barrier, greeted)
    under_way = Riders(items, xs, outs, sems).start()
    sums_total = sums_both
    sums_enter = jnp.zeros((rows, width), f32)
    for turn, span in enumerate(spans):
        to = me + sign * span
        origin = me - sign * span
        sends = (to >= 0) & (to < count)
        takes = (origin >= 0) & (origin < count)
        for j in range(0, states // 2, 2):
            send[turn, pl.ds(j * rows, 2 * rows), :] = jnp.concatenate([total[j], total[j + 1]], axis=0).astype(bf16)
        send_sum[turn] = sums_total
        copies = [
            pltpu.make_async_remote_copy(
                src_ref=source.at[turn],
                dst_ref=target.at[turn],
                send_sem=ssem.at[turn],
                recv_sem=rsem.at[turn],
                device_id={axis: to},
                device_id_type=MESH,
            )
            for source, target, ssem, rsem in (
                (send, got, send_sem, recv_sem),
                (send_sum, got_sum, send_sum_sem, recv_sum_sem),
            )
        ]

        @pl.when(sends)
        def _():
            for copy in copies:
                copy.start()

        @pl.when(jnp.logical_not(takes))
        def _():
            got[turn] = jnp.zeros(got.shape[1:], bf16)
            got_sum[turn] = jnp.zeros(got_sum.shape[1:], f32)

        @pl.when(takes)
        def _():
            for copy in copies:
                copy.wait_recv()

        for j in range(0, states // 2, 2):
            pair = got[turn, pl.ds(j * rows, 2 * rows), :].astype(f32)
            for i in (j, j + 1):
                came = pair[(i - j) * rows : (i - j + 1) * rows]
                rate = packed_rate(i)
                enter[i] = jnp.exp2(rate * sums_enter) * came + enter[i]
                total[i] = jnp.exp2(rate * sums_total) * came + total[i]
        sums_enter = sums_enter + got_sum[turn]
        sums_total = sums_total + got_sum[turn]

        @pl.when(sends)
        def _():
            for copy in copies:
                copy.wait_send()

    for j in range(states // 2):
        opening, _ = both(j)
        outer = enter[j]
        inner = jnp.exp2(packed_rate(j) * sums_first) * outer + opening
        low, high = (inner, outer) if back else (outer, inner)
        o_ref[2 * j] = jnp.where(upper, turned(high), low)
        o_ref[2 * j + 1] = jnp.where(upper, high, turned(low))
    under_way.finish()


def carried(local, sums, rate, axis, back, number, *exchanges):
    count = lax.axis_size(axis)
    states, rows, width = local.shape
    turns = max(1, (count - 1).bit_length())
    items = items_of(exchanges)
    anywhere = [pl.BlockSpec(memory_space=pl.ANY)] * len(items)
    return pl.pallas_call(
        functools.partial(carry_kernel, axis, count, back, items),
        out_shape=[jax.ShapeDtypeStruct(local.shape, f32)]
        + [landed(x, item) for (x, _, _), item in zip(exchanges, items)],
        in_specs=[pl.BlockSpec(memory_space=pltpu.VMEM)] * 3 + anywhere,
        out_specs=[pl.BlockSpec(memory_space=pltpu.VMEM)] + anywhere,
        scratch_shapes=[
            pltpu.VMEM((turns, states // 2 * rows, width), bf16),
            pltpu.VMEM((turns, states // 2 * rows, width), bf16),
            pltpu.VMEM((turns, rows, width), f32),
            pltpu.VMEM((turns, rows, width), f32),
            pltpu.VMEM((states // 2, rows, width), f32),
            pltpu.VMEM((states // 2, rows, width), f32),
            pltpu.SemaphoreType.DMA((turns,)),
            pltpu.SemaphoreType.DMA((turns,)),
            pltpu.SemaphoreType.DMA((turns,)),
            pltpu.SemaphoreType.DMA((turns,)),
        ]
        + [sem for item in items for sem in sems_of(item)],
        compiler_params=pltpu.CompilerParams(
            collective_id=number, has_side_effects=True, vmem_limit_bytes=10 * MIB
        ),
    )(local, sums, rate, *[x for x, _, _ in exchanges])


def spread(mapped_ref, first, wide_ref):
    count, steps, rows, lanes = wide_ref.shape
    column = lax.broadcasted_iota(jnp.int32, (mapped_ref.shape[1], lanes), 0)
    values = mapped_ref[...]
    for n in range(count):
        pick = (column == first + n).astype(bf16)
        wide_ref[n] = jnp.dot(values, pick, preferred_element_type=f32).reshape(steps, rows, lanes)


def rows_of(rate_ref, n, rows):
    return jnp.broadcast_to(rate_ref[n : n + 1, :], (rows, rate_ref.shape[1]))


def perm_of(steps, lines, seqs):
    rows = steps * lines
    laid = lax.broadcasted_iota(jnp.int32, (rows, rows), 0)
    natural = lax.broadcasted_iota(jnp.int32, (rows, rows), 1)
    line = laid % lines
    wanted = (line % seqs) * (rows // seqs) + (line // seqs) * steps + laid // lines
    return (natural == wanted).astype(bf16)


def unit_of(rows):
    return rows * lax.rsqrt(jnp.mean(rows * rows, axis=-1, keepdims=True) + epsilon)


def softplus(x):
    return jnp.maximum(x, 0.0) + jnp.log1p(jnp.exp(-jnp.abs(x)))


def sigmoid(x):
    return 1.0 / (1.0 + jnp.exp(-x))


def silu_slope(values, sigma):
    return sigma * (1.0 + values * (1.0 - sigma))


def dot(a, b):
    return jnp.dot(a, b, preferred_element_type=f32)


def dot_nt(a, b):
    return lax.dot_general(a, b, (((1,), (1,)), ((), ())), preferred_element_type=f32)


def dot_tn(a, b):
    return lax.dot_general(a, b, (((0,), (0,)), ((), ())), preferred_element_type=f32)


def front_kernel(seq_count, chan_count, states, taps, tokens_ref, gain_ref, w_ref, params_ref, xproj_ref, valid_ref,
                 normed_ref, ext_ref, pre_ref, gate_ref, mapped_ref,
                 halo, part, beside_in, pair, far_in, halo_send, halo_recv, send_sem, recv_sem):
    seqs, group, width = tokens_ref.shape
    steps, lines, full = pre_ref.shape
    inner = w_ref.shape[1]
    rim, rows, tail = taps - 1, steps * lines, halo.shape[1]
    here, me = lax.axis_index("seq"), lax.axis_index("chan")
    beside = me + 1 - 2 * lax.rem(me, 2)
    barrier = pltpu.get_barrier_semaphore()
    told = chan_count // 2
    for by in (1, -1):
        there = here + by
        near = (there >= 0) & (there < seq_count)
        told = told + jnp.where(near, 1, 0)

        @pl.when(near)
        def _():
            pl.semaphore_signal(barrier, inc=1, device_id={"seq": there}, device_id_type=MESH)

    pl.semaphore_signal(barrier, inc=1, device_id={"chan": beside}, device_id_type=MESH)
    for k in range(1, chan_count // 2):
        to = lax.rem(me + 2 * k, chan_count)
        pl.semaphore_signal(barrier, inc=1, device_id={"chan": to}, device_id_type=MESH)
    pl.semaphore_wait(barrier, told)
    ends = pltpu.make_async_remote_copy(
        src_ref=tokens_ref.at[:, pl.ds(group - tail, tail), :],
        dst_ref=halo,
        send_sem=halo_send,
        recv_sem=halo_recv,
        device_id={"seq": here + 1},
        device_id_type=MESH,
    )

    @pl.when(here + 1 < seq_count)
    def _():
        ends.start()

    def normed_of(rows_low):
        return (unit_of(rows_low.astype(f32)) * gain_ref[...]).astype(bf16)

    perm = perm_of(steps, lines, seqs)
    normed = dot(perm, normed_of(tokens_ref[...].reshape(rows, width))).astype(bf16)
    normed_ref[...] = normed
    conv_in = dot_nt(normed, w_ref[0]).astype(bf16).astype(f32)
    ext_ref[pl.ds(rim, steps), :, pl.ds(0, inner)] = conv_in.reshape(steps, lines, inner)
    gate_ref[:, :, pl.ds(0, inner)] = dot_nt(normed, w_ref[1]).reshape(steps, lines, inner)
    if full > inner:
        ext_ref[:, :, pl.ds(inner, full - inner)] = jnp.zeros((steps + rim, lines, full - inner), f32)
        gate_ref[:, :, pl.ds(inner, full - inner)] = jnp.zeros((steps, lines, full - inner), f32)

    @pl.when(here == 0)
    def _():
        halo[...] = jnp.zeros(halo.shape, bf16)

    @pl.when(here > 0)
    def _():
        ends.wait_recv()

    prior = dot_nt(normed_of(halo[...].reshape(seqs * tail, width)), w_ref[0]).astype(bf16)
    to = lax.broadcasted_iota(jnp.int32, (rim * lines, seqs * tail), 0)
    origin = lax.broadcasted_iota(jnp.int32, (rim * lines, seqs * tail), 1)
    pick = (to % lines < seqs) & (origin == (to % lines) * tail + tail - rim + to // lines)
    prior = dot(pick.astype(bf16), prior).reshape(rim, lines, inner)
    upper = lax.broadcasted_iota(jnp.int32, (lines, inner), 0) >= seqs
    for j in range(rim):
        own = turned(ext_ref[steps + j, :, pl.ds(0, inner)])
        ext_ref[j, :, pl.ds(0, inner)] = jnp.where(upper, own, prior[j])
    pre = jnp.broadcast_to(params_ref[pl.ds(states + taps, 1), :], (steps, lines, full))
    for k in range(taps):
        tap = params_ref[pl.ds(states + k, 1), :]
        pre = pre + tap * ext_ref[pl.ds(k, steps)] * valid_ref[:, :, k : k + 1]
    pre_ref[...] = pre
    act_low = (pre * sigmoid(pre)).astype(bf16).reshape(rows, full)
    part[...] = dot_nt(act_low, xproj_ref[...]).astype(bf16)
    near = pltpu.make_async_remote_copy(
        src_ref=part,
        dst_ref=beside_in,
        send_sem=send_sem.at[0],
        recv_sem=recv_sem.at[0],
        device_id={"chan": beside},
        device_id_type=MESH,
    )
    near.start()
    near.wait_recv()
    pair[...] = (part[...].astype(f32) + beside_in[...].astype(f32)).astype(bf16)
    copies = []
    for k in range(1, chan_count // 2):
        copies.append(
            pltpu.make_async_remote_copy(
                src_ref=pair,
                dst_ref=far_in.at[k - 1],
                send_sem=send_sem.at[k],
                recv_sem=recv_sem.at[k],
                device_id={"chan": lax.rem(me + 2 * k, chan_count)},
                device_id_type=MESH,
            )
        )
        copies[-1].start()
    for copy in copies:
        copy.wait_recv()
    total = pair[...].astype(f32)
    for k in range(chan_count // 2 - 1):
        total = total + far_in[k].astype(f32)
    mapped_ref[...] = total.astype(bf16)
    near.wait_send()
    for copy in copies:
        copy.wait_send()

    @pl.when(here + 1 < seq_count)
    def _():
        ends.wait_send()


def front(tokens, gain, w_in, params, states, taps, xproj, valid, full, number):
    seqs, group, width = tokens.shape
    steps, lines = valid.shape[:2]
    count, rows, maps = lax.axis_size("chan"), steps * lines, xproj.shape[0]
    tail = min(16, group)
    return pl.pallas_call(
        functools.partial(front_kernel, lax.axis_size("seq"), count, states, taps),
        out_shape=[
            jax.ShapeDtypeStruct((rows, width), bf16),
            jax.ShapeDtypeStruct((steps + taps - 1, lines, full), f32),
            jax.ShapeDtypeStruct((steps, lines, full), f32),
            jax.ShapeDtypeStruct((steps, lines, full), f32),
            jax.ShapeDtypeStruct((rows, maps), bf16),
        ],
        in_specs=[pl.BlockSpec(memory_space=pltpu.VMEM)] * 6,
        out_specs=[pl.BlockSpec(memory_space=pltpu.VMEM)] * 5,
        scratch_shapes=[
            pltpu.VMEM((seqs, tail, width), bf16),
            pltpu.VMEM((rows, maps), bf16),
            pltpu.VMEM((rows, maps), bf16),
            pltpu.VMEM((rows, maps), bf16),
            pltpu.VMEM((count // 2 - 1, rows, maps), bf16),
            pltpu.SemaphoreType.DMA,
            pltpu.SemaphoreType.DMA,
            pltpu.SemaphoreType.DMA((count // 2,)),
            pltpu.SemaphoreType.DMA((count // 2,)),
        ],
        compiler_params=pltpu.CompilerParams(
            collective_id=number, has_side_effects=True, vmem_limit_bytes=30 * MIB
        ),
    )(tokens, gain, w_in, params, xproj, valid)


def totals_kernel(rank, taps, pre_ref, mapped_ref, dtw_ref, valid_ref, rate_ref,
                  dt_ref, step_ref, drive_ref, last_ref, sums_ref, wide):
    count, steps, rows, lanes = wide.shape

    @pl.when(pl.program_id(0) == 0)
    def _():
        spread(mapped_ref, rank, wide)

    bias = rate_ref[pl.ds(count + taps + 1, 1), :]
    dt_pre = (dot(mapped_ref[...], dtw_ref[...]) + bias).reshape(steps, rows, lanes)
    delta = softplus(dt_pre)
    pre = pre_ref[...]
    dt_ref[...] = dt_pre
    step_ref[...] = jnp.where(valid_ref[:, :, taps : taps + 1] > 0.5, delta, cut)
    drive_ref[...] = delta * pre * sigmoid(pre)
    rates = [rows_of(rate_ref, n, rows) for n in range(count)]
    zero = jnp.zeros((rows, lanes), f32)

    def one(p, held):
        states, sums = held
        step, drive = step_ref[p], drive_ref[p]
        states = tuple(
            jnp.exp2(step * rates[n]) * states[n] + drive * wide[n, p] for n in range(count)
        )
        return states, sums + step

    states, sums = lax.fori_loop(0, steps, one, ((zero,) * count, zero), unroll=2)
    for n in range(count):
        last_ref[n] = states[n]
    sums_ref[...] = sums


def known(rows_ref, size):
    row = pl.program_id(0) * rows_ref.shape[0] + lax.broadcasted_iota(jnp.int32, rows_ref.shape, 0)
    return jnp.where(row < size, rows_ref[...].astype(f32), 0.0).astype(rows_ref.dtype)


def states_kernel(rank, seqs, taps, inner, step_ref, drive_ref, mapped_ref, rate_ref, enter_ref, pre_ref, gate_ref, out_w_ref,
                  y_ref, gated_ref, state_ref, out_ref, wide_in, wide_read, total):
    count, steps, rows, lanes = wide_in.shape
    place = pl.program_id(0)

    @pl.when(place == 0)
    def _():
        spread(mapped_ref, rank, wide_in)
        spread(mapped_ref, rank + count, wide_read)
        total[...] = jnp.zeros_like(total)

    rates = [rows_of(rate_ref, n, rows) for n in range(count)]

    def one(p, states):
        step, drive = step_ref[p], drive_ref[p]
        states = tuple(
            jnp.exp2(step * rates[n]) * states[n] + drive * wide_in[n, p] for n in range(count)
        )
        terms = [states[n] * wide_read[n, p] for n in range(count)]
        while len(terms) > 1:
            terms = [a + b for a, b in zip(terms[::2], terms[1::2])]
        y_ref[p] = terms[0]
        for n in range(count):
            state_ref[p, n] = states[n]
        return states

    lax.fori_loop(0, steps, one, tuple(enter_ref[n] for n in range(count)), unroll=2)
    pre, gate = pre_ref[...], gate_ref[...]
    y_full = y_ref[...] + rate_ref[pl.ds(count + taps + 2, 1), :] * (pre * sigmoid(pre))
    y_ref[...] = y_full
    gated = (y_full * (gate * sigmoid(gate))).astype(bf16).reshape(steps * rows, lanes)
    gated_ref[...] = gated
    total[...] += dot(gated, known(out_w_ref, inner))

    @pl.when(place == pl.num_programs(0) - 1)
    def _():
        perm = perm_of(steps, rows, seqs)
        out_ref[...] = dot_tn(perm, total[...].astype(bf16)).astype(bf16)


def back_totals_kernel(rank, seqs, inner, step_ref, mapped_ref, rate_ref, mixed_ref, normed_ref, out_w_ref, gate_ref, y_ref, gated_ref,
                       pre_ref, grad_y_ref, grad_z_ref, grad_out_ref, grad_gate_ref, skip_ref, last_ref,
                       wide, mixed):
    count, steps, rows, lanes = wide.shape

    @pl.when(pl.program_id(0) == 0)
    def _():
        spread(mapped_ref, rank + count, wide)
        mixed[...] = dot(perm_of(steps, rows, seqs), mixed_ref[...]).astype(bf16)

    grad_gated = dot_nt(mixed[...], known(out_w_ref, inner)).reshape(steps, rows, lanes)
    gate, pre = gate_ref[...], pre_ref[...]
    sigma = sigmoid(gate)
    grad_y = grad_gated * (gate * sigma)
    grad_y_ref[...] = grad_y
    grad_z = (grad_gated * y_ref[...] * silu_slope(gate, sigma)).astype(bf16)
    grad_z = grad_z.reshape(steps * rows, lanes)
    grad_z_ref[...] = grad_z
    skip_ref[...] = jnp.sum(grad_y * (pre * sigmoid(pre)), axis=0)
    grad_out_ref[...] = dot_tn(gated_ref[...], mixed[...]).astype(bf16)
    grad_gate_ref[...] = dot_tn(grad_z, normed_ref[...]).astype(bf16)
    rates = [rows_of(rate_ref, n, rows) for n in range(count)]
    zero = jnp.zeros((rows, lanes), f32)

    def one(turn, held):
        p = steps - 1 - turn
        step, grad_y = step_ref[p], grad_y_ref[p]
        return tuple(
            jnp.exp2(step * rates[n]) * (held[n] + grad_y * wide[n, p]) for n in range(count)
        )

    held = lax.fori_loop(0, steps, one, (zero,) * count, unroll=2)
    for n in range(count):
        last_ref[n] = held[n]


def back_kernel(rank, pieces, shares, items, step_ref, drive_ref, grad_y_ref, mapped_ref, rate_ref, first_ref, state_ref, enter_ref, dt_ref,
                pre_ref, dtw_ref, *refs):
    many, number = len(shares), len(items)
    at = 0

    def take(k):
        nonlocal at
        at += k
        return refs[at - k : at]

    xs, riders = take(many), take(number)
    side_ref, log_ref, bias_ref, grad_dtw_ref, low_ref = take(5)
    parts, rider_outs = take(many), take(number)
    wide_in, wide_read, sum_in, sum_read, to_input, to_decay, total = take(7)
    count, steps, rows, lanes = wide_in.shape
    place, tiles = pl.program_id(0), pl.num_programs(0)
    kept, kept_sem = take(many), take(1)[0]
    tasks = [Share(*share, held, *take(7)) for share, held in zip(shares, kept)]
    under_way = Riders(items, riders, rider_outs, take(3 * number))
    turn = [(task, k) for task in tasks for k in range(task.groups)]

    @pl.when(place == 0)
    def _():
        copies = [
            pltpu.make_async_copy(x, held, kept_sem.at[i]) for i, (x, held) in enumerate(zip(xs, kept))
        ]
        for copy in copies:
            copy.start()
        axes = {share[:2] for share in shares} | set(axes_of(items))
        pl.semaphore_wait(pltpu.get_barrier_semaphore(), greet(sorted(axes)))
        for copy in copies:
            copy.wait()
        for task, k in turn[:3]:
            task.begin(k)
        under_way.start()
        spread(mapped_ref, rank, wide_in)
        spread(mapped_ref, rank + count, wide_read)
        sum_in[...] = jnp.zeros_like(sum_in)
        sum_read[...] = jnp.zeros_like(sum_read)
        total[...] = jnp.zeros_like(total)

    moments = 2 * (pieces - 1)
    each = -(-len(turn) // moments)

    def pass_on(late):
        for piece in range(1, pieces):
            moment = 2 * (piece - 1) + late

            @pl.when(place == piece)
            def _():
                for i in range(moment * each, min((moment + 1) * each, len(turn))):
                    turn[i][0].pass_on(turn[i][1])
                    if i + 3 < len(turn):
                        turn[i + 3][0].begin(turn[i + 3][1])

    pass_on(0)
    rates = [rows_of(rate_ref, n, rows) for n in range(count)]
    for n in range(count):
        log_ref[n] = jnp.zeros((rows, lanes), f32)

    def step_back(p, carry, prior_of):
        step, drive, grad_y = step_ref[p], drive_ref[p], grad_y_ref[p]
        inputs = jnp.zeros((rows, lanes), f32)
        decays = jnp.zeros((rows, lanes), f32)
        new, grads = [], []
        for n in range(count):
            grad = grad_y * wide_read[n, p] + carry[n]
            passed = jnp.exp2(step * rates[n]) * grad
            new.append(passed)
            grad_decay = passed * prior_of(n)
            decays = decays + grad_decay * rates[n]
            log_ref[n] += grad_decay * step
            inputs = inputs + grad * wide_in[n, p]
            grads.append(grad)
        to_input[p] = inputs
        to_decay[p] = decays
        grads = jnp.concatenate(grads, axis=0).astype(bf16)
        held_states = state_ref[p].reshape(count * rows, lanes).astype(bf16)
        sum_in[p] += dot_nt(drive.astype(bf16), grads)
        sum_read[p] += dot_nt(grad_y.astype(bf16), held_states)
        return tuple(new)

    def one(turn, carry):
        p = steps - 1 - turn
        return step_back(p, carry, lambda n: state_ref[p - 1, n])

    carry = tuple(enter_ref[n] for n in range(count))
    unroll = 7 if (steps - 1) % 7 == 0 else 1
    middle = (steps - 1) // unroll // 2 * unroll
    carry = lax.fori_loop(0, middle, one, carry, unroll=unroll)
    pass_on(1)
    carry = lax.fori_loop(middle, steps - 1, one, carry, unroll=unroll)
    step_back(0, carry, lambda n: first_ref[n])
    dt_pre, pre = dt_ref[...], pre_ref[...]
    inputs = to_input[...]
    side_ref[...] = inputs * softplus(dt_pre)
    grad_delta = to_decay[...] * (1.0 / log2e) + inputs * (pre * sigmoid(pre))
    grad_dt = grad_delta * sigmoid(dt_pre)
    bias_ref[...] = jnp.sum(grad_dt, axis=0)
    grad_dt = grad_dt.astype(bf16).reshape(steps * rows, lanes)
    grad_dtw_ref[...] = dot_tn(mapped_ref[...], grad_dt)
    total[...] += dot_nt(grad_dt, dtw_ref[...])

    @pl.when(place == tiles - 1)
    def _():
        wide = count * rows
        line = lax.broadcasted_iota(jnp.int32, (steps * rows, wide), 0) % rows
        lane = lax.broadcasted_iota(jnp.int32, (steps * rows, wide), 1)
        state = lax.broadcasted_iota(jnp.int32, (wide, total.shape[1]), 0) // rows
        column = lax.broadcasted_iota(jnp.int32, (wide, total.shape[1]), 1)
        sums = total[...]
        for which, source in enumerate((sum_in, sum_read)):
            values = jnp.where(lane % rows == line, source[...].reshape(steps * rows, wide), 0.0)
            pick = (column == rank + which * count + state).astype(bf16)
            sums = sums + dot(values.astype(bf16), pick)
        low_ref[...] = sums.astype(bf16)
        for task, part in zip(tasks, parts):
            part[...] = task.total().astype(bf16)
            task.close()
        under_way.finish()


def conv_back_kernel(states, taps, grad_mapped_ref, grad_y_ref, side_ref, pre_ref, ext_ref, params_ref, xproj_ref, valid_ref,
                     grad_ref, rim_ref, grad_xproj_ref, sums_ref, ext_grad):
    steps, rows, lanes = pre_ref.shape
    rim = taps - 1
    pre = pre_ref[...]
    sigma = sigmoid(pre)
    grad_act = dot(grad_mapped_ref[...], xproj_ref[...]).reshape(steps, rows, lanes)
    grad_act = grad_act + grad_y_ref[...] * params_ref[pl.ds(states + taps + 2, 1), :] + side_ref[...]
    grad_pre = grad_act * silu_slope(pre, sigma)
    act_low = (pre * sigma).astype(bf16).reshape(steps * rows, lanes)
    grad_xproj_ref[...] = dot_tn(grad_mapped_ref[...], act_low)
    ext_grad[...] = jnp.zeros_like(ext_grad)
    for k in range(taps):
        masked = grad_pre * valid_ref[:, :, k : k + 1]
        sums_ref[k] = jnp.sum(masked * ext_ref[pl.ds(k, steps)], axis=0)
        ext_grad[pl.ds(k, steps)] += masked * params_ref[pl.ds(states + k, 1), :]
    sums_ref[taps] = jnp.sum(grad_pre, axis=0)
    upper = lax.broadcasted_iota(jnp.int32, (rows, lanes), 0) >= rows // 2
    for j in range(rim):
        edge = ext_grad[j]
        rim_ref[j] = edge
        ext_grad[steps + j] += jnp.where(upper, 0.0, turned(edge))
    grad_ref[...] = ext_grad[pl.ds(rim, steps)]


def ends_kernel(count, items, tokens_ref, grad_ref, rim_ref, grad_z_ref, normed_ref, w_ref, *refs):
    number = len(items)
    xs, refs = refs[:number], refs[number:]
    grad_conv_ref, part_ref, gain_ref = refs[:3]
    outs, (came, send_sem, recv_sem), sems = refs[3 : 3 + number], refs[3 + number : 6 + number], refs[6 + number :]
    steps, lines, full = grad_ref.shape
    seqs, group, width = tokens_ref.shape
    rows, inner, rim = steps * lines, w_ref.shape[1], rim_ref.shape[0]
    here = lax.axis_index("seq")
    told = greet(sorted({("seq", count)} | set(axes_of(items))))
    pl.semaphore_wait(pltpu.get_barrier_semaphore(), told)
    edge = pltpu.make_async_remote_copy(
        src_ref=rim_ref,
        dst_ref=came,
        send_sem=send_sem,
        recv_sem=recv_sem,
        device_id={"seq": here - 1},
        device_id_type=MESH,
    )

    @pl.when(here > 0)
    def _():
        edge.start()

    under_way = Riders(items, xs, outs, sems).start()
    unit = unit_of(tokens_ref[...].reshape(rows, width).astype(f32))
    under_way.step()
    by_gate = dot(grad_z_ref[:, pl.ds(0, inner)], w_ref[1])
    under_way.step()

    @pl.when(here == count - 1)
    def _():
        came[...] = jnp.zeros(came.shape, f32)

    @pl.when(here < count - 1)
    def _():
        edge.wait_recv()

    upper = lax.broadcasted_iota(jnp.int32, (lines, full), 0) >= lines // 2
    last = [
        (grad_ref[steps - rim + j] + jnp.where(upper, turned(came[j]), 0.0))[None] for j in range(rim)
    ]
    grad = jnp.concatenate([grad_ref[pl.ds(0, steps - rim)]] + last, axis=0)
    grad = grad.reshape(rows, full).astype(bf16)
    for j in range(0, inner, LANES):
        many = min(LANES, inner - j)
        piece = dot_tn(grad[:, j : j + many], normed_ref[...])
        grad_conv_ref[pl.ds(j, many), :] = piece.astype(bf16)
        under_way.step()
    perm = perm_of(steps, lines, seqs)
    tile = next(t for t in (384, LANES, width) if width % t == 0)
    for j in range(0, width, tile):
        piece = dot(grad[:, :inner], w_ref[0, :, pl.ds(j, tile)]) + by_gate[:, j : j + tile]
        piece = dot_tn(perm, piece.astype(bf16))
        part_ref[:, pl.ds(j, tile)] = piece.astype(bf16)
        gain_ref[:, pl.ds(j, tile)] = jnp.sum(piece * unit[:, j : j + tile], axis=0, keepdims=True)
        under_way.step()
    under_way.finish()

    @pl.when(here > 0)
    def _():
        edge.wait_send()


def ends(tokens, grad, rim, grad_z, normed, w_in, number, *exchanges):
    steps, lines, full = grad.shape
    rows, width = normed.shape
    items = items_of(exchanges)
    anywhere = [pl.BlockSpec(memory_space=pl.ANY)] * len(items)
    return pl.pallas_call(
        functools.partial(ends_kernel, lax.axis_size("seq"), items),
        out_shape=[
            jax.ShapeDtypeStruct((w_in.shape[1], width), bf16),
            jax.ShapeDtypeStruct((rows, width), bf16),
            jax.ShapeDtypeStruct((1, width), f32),
        ]
        + [landed(x, item) for (x, _, _), item in zip(exchanges, items)],
        in_specs=[pl.BlockSpec(memory_space=pltpu.VMEM)] * 6 + anywhere,
        out_specs=[pl.BlockSpec(memory_space=pltpu.VMEM)] * 3 + anywhere,
        scratch_shapes=[
            pltpu.VMEM(rim.shape, f32),
            pltpu.SemaphoreType.DMA,
            pltpu.SemaphoreType.DMA,
        ]
        + [sem for item in items for sem in sems_of(item)],
        compiler_params=pltpu.CompilerParams(
            collective_id=number, has_side_effects=True, vmem_limit_bytes=30 * MIB
        ),
    )(tokens, grad, rim, grad_z, normed, w_in, *[x for x, _, _ in exchanges])


def hits_of(routes, experts, part, most, slots):
    rows = routes.shape[0]
    chosen = (lax.broadcasted_iota(jnp.int32, (rows, experts), 1) == routes).astype(f32)
    row = lax.broadcasted_iota(jnp.int32, (rows, rows), 0)
    other = lax.broadcasted_iota(jnp.int32, (rows, rows), 1)
    earlier = (other < row) & (row // part == other // part)
    ranks = jnp.sum(dot(earlier.astype(bf16), chosen.astype(bf16)) * chosen, axis=1, keepdims=True)
    slot = lax.broadcasted_iota(jnp.int32, (rows, 1), 0) // part * most + ranks.astype(jnp.int32)
    column = lax.broadcasted_iota(jnp.int32, (rows, experts * slots), 1)
    return chosen, (column == routes * slots + slot).astype(bf16)


def route_kernel(part, most, slots, tokens_ref, mixed_ref, gain_ref, routes_ref, router_ref,
                 hidden_ref, normed_ref, probs_ref, chosen_ref, hit_ref, packed_ref):
    hidden = tokens_ref[...].astype(f32) + mixed_ref[...]
    hidden_ref[...] = hidden
    normed = (unit_of(hidden) * gain_ref[...]).astype(bf16)
    normed_ref[...] = normed
    logits = dot_nt(normed, router_ref[...])
    raised = jnp.exp(logits - jnp.max(logits, axis=1, keepdims=True))
    probs_ref[...] = raised / jnp.sum(raised, axis=1, keepdims=True)
    chosen, hit = hits_of(routes_ref[...], router_ref.shape[0], part, most, slots)
    chosen_ref[...] = chosen
    hit_ref[...] = hit
    packed_ref[...] = dot_tn(hit, normed).astype(bf16)


def loss_kernel(group, lengths_ref, came_ref, back_ref, hit_ref, hidden_ref, probs_ref, chosen_ref, teacher_ref,
                layer_ref, grad_layer_ref, grad_logit_ref, loss_ref, packed_ref):
    rows, width = hidden_ref.shape
    seqs = lengths_ref.shape[0]
    expert = dot(back_ref[...], came_ref[...])
    probs, chosen = probs_ref[...], chosen_ref[...]
    gate = jnp.sum(probs * chosen, axis=1, keepdims=True)
    layer = hidden_ref[...] + gate * expert
    layer_ref[...] = layer.astype(bf16)
    flat_row = lax.axis_index("chan") * rows + lax.broadcasted_iota(jnp.int32, (rows, 1), 0)
    length = jnp.zeros((rows, 1), jnp.int32)
    total = 0
    for s in range(seqs):
        length = jnp.where(flat_row // group == s, lengths_ref[s], length)
        total = total + lengths_ref[s]
    scale = 1.0 / jnp.broadcast_to(total, (rows, 1)).astype(f32)
    at = lax.axis_index("seq") * group + flat_row % group
    mask = jnp.where(at < length, scale, 0.0)
    error = layer - teacher_ref[...].astype(f32)
    scaled = mask * error
    lost = jnp.sum(scaled * error, axis=0, keepdims=True)
    loss_ref[...] = jnp.broadcast_to(jnp.sum(lost, axis=1, keepdims=True), (1, width))
    grad_layer = 2.0 * scaled
    grad_layer_ref[...] = grad_layer
    grad_gate = jnp.sum(grad_layer * expert, axis=1, keepdims=True)
    grad_logit_ref[...] = grad_gate * gate * (chosen - probs)
    packed_ref[...] = dot_tn(hit_ref[...], (gate * grad_layer).astype(bf16)).astype(bf16)


def norm_back_kernel(came_ref, back_ref, grad_logit_ref, router_ref, normed_ref, hidden_ref, grad_layer_ref, gain_ref, loss_ref,
                     grad_ref, low_ref, shared_ref):
    experts = router_ref.shape[0]
    grad_logit = grad_logit_ref[...].astype(bf16)
    grad_normed = dot(back_ref[...], came_ref[...]) + dot(grad_logit, router_ref[...])
    hidden = hidden_ref[...]
    inverse = lax.rsqrt(jnp.mean(hidden * hidden, axis=1, keepdims=True) + epsilon)
    unit = hidden * inverse
    shared_ref[...] = jnp.zeros_like(shared_ref)
    shared_ref[pl.ds(0, experts), :] = dot_tn(grad_logit, normed_ref[...])
    shared_ref[pl.ds(experts, 1), :] = jnp.sum(grad_normed * unit, axis=0, keepdims=True)
    shared_ref[pl.ds(experts + 1, 1), :] = loss_ref[...]
    grad = grad_layer_ref[...] + norm_back(grad_normed, unit, inverse, gain_ref[...])
    grad_ref[...] = grad
    low_ref[...] = grad.astype(bf16)


def at_once(kernel, ins, outs, scalars=0):
    spaces = [pltpu.SMEM] * scalars + [pltpu.VMEM] * (len(ins) - scalars)
    return pl.pallas_call(
        kernel,
        in_specs=[pl.BlockSpec(memory_space=space) for space in spaces],
        out_specs=[pl.BlockSpec(memory_space=pltpu.VMEM)] * len(outs),
        out_shape=[jax.ShapeDtypeStruct(shape, dtype) for shape, dtype in outs],
        compiler_params=pltpu.CompilerParams(vmem_limit_bytes=12 * MIB),
        cost_estimate=pl.CostEstimate(flops=1000, bytes_accessed=1000, transcendentals=0),
    )(*ins)


def expert_kernel(x_ref, first_ref, second_ref, hidden_ref, slope_ref, result_ref, total):
    place = pl.program_id(0)

    @pl.when(place == 0)
    def _():
        total[...] = jnp.zeros_like(total)

    pre = dot(x_ref[...], first_ref[...])
    cdf = 0.5 * (1.0 + lax.erf(pre * 0.7071067811865476))
    hidden = (pre * cdf).astype(bf16)
    hidden_ref[0] = hidden
    slope = cdf + pre * (jnp.exp(-0.5 * pre * pre) * 0.3989422804014327)
    slope_ref[...] = slope.astype(bf16)
    total[...] += dot(hidden, second_ref[...])

    @pl.when(place == pl.num_programs(0) - 1)
    def _():
        result_ref[...] = total[...].astype(bf16)


def expert_back_kernel(grad_ref, first_ref, second_ref, slope_ref, grad_pre_ref, result_ref, total):
    place = pl.program_id(0)

    @pl.when(place == 0)
    def _():
        total[...] = jnp.zeros_like(total)

    grad = dot_nt(grad_ref[...], second_ref[...]) * slope_ref[...].astype(f32)
    grad = grad.astype(bf16)
    grad_pre_ref[0] = grad
    total[...] += dot_nt(grad, first_ref[...])

    @pl.when(place == pl.num_programs(0) - 1)
    def _():
        result_ref[...] = total[...].astype(bf16)


def expert(x, first, second, parts, slope=None):
    rows, width = x.shape
    units = first.shape[1] // parts
    tile = next((t for t in (768, 384, 256, 128) if units % t == 0), None)
    low = jax.ShapeDtypeStruct((rows, width), bf16)
    if tile is None:

        def split(h):
            return h.reshape(rows, parts, units).transpose(1, 0, 2)

        if slope is not None:
            grad = (dot_nt(x, second) * slope.astype(f32)).astype(bf16)
            return split(grad), dot_nt(grad, first).astype(bf16)
        pre = dot(x, first)
        cdf = 0.5 * (1.0 + lax.erf(pre * 0.7071067811865476))
        hidden = (pre * cdf).astype(bf16)
        slope = cdf + pre * (jnp.exp(-0.5 * pre * pre) * 0.3989422804014327)
        return split(hidden), slope.astype(bf16), dot(hidden, second).astype(bf16)
    each = units // tile
    columns = pl.BlockSpec((width, tile), lambda i: (0, i))
    lines = pl.BlockSpec((tile, width), lambda i: (i, 0))
    everything = pl.BlockSpec((rows, width), lambda i: (0, 0))
    slopes = pl.BlockSpec((rows, tile), lambda i: (0, i))
    hiddens = pl.BlockSpec((1, rows, tile), lambda i: (i // each, 0, i % each))
    hidden_shape = jax.ShapeDtypeStruct((parts, rows, units), bf16)
    back = slope is not None
    return pl.pallas_call(
        expert_back_kernel if back else expert_kernel,
        grid=(parts * each,),
        in_specs=[everything, columns, lines] + ([slopes] if back else []),
        out_specs=[hiddens] + ([] if back else [slopes]) + [everything],
        out_shape=[hidden_shape]
        + ([] if back else [jax.ShapeDtypeStruct((rows, first.shape[1]), bf16)])
        + [low],
        scratch_shapes=[pltpu.VMEM((rows, width), f32)],
        compiler_params=pltpu.CompilerParams(vmem_limit_bytes=60 * MIB),
        cost_estimate=pl.CostEstimate(flops=1000, bytes_accessed=1000, transcendentals=0),
    )(x, first, second, *([slope] if back else []))


def widen_kernel(conv_ref, gate_ref, *refs):
    half = len(refs) // 2
    refs[half][0] = conv_ref[...].astype(f32)
    refs[half][1] = gate_ref[...].astype(f32)
    for x_ref, o_ref in zip(refs[:half], refs[half + 1 :]):
        o_ref[...] = x_ref[...].astype(f32)


def widened(conv, gate, *arrays):
    sizes = [x.shape[0] for x in (conv, *arrays)]
    pieces = next(n for n in (6, 4, 3, 2, 1) if all(size % (16 * n) == 0 for size in sizes) or n == 1)

    def block(x):
        return pl.BlockSpec((x.shape[0] // pieces, x.shape[1]), lambda i: (i, 0))

    each, width = conv.shape[0] // pieces, conv.shape[1]
    return pl.pallas_call(
        widen_kernel,
        grid=(pieces,),
        in_specs=[block(x) for x in (conv, gate, *arrays)],
        out_specs=[pl.BlockSpec((2, each, width), lambda i: (0, i, 0))] + [block(x) for x in arrays],
        out_shape=[jax.ShapeDtypeStruct((2,) + conv.shape, f32)]
        + [jax.ShapeDtypeStruct(x.shape, f32) for x in arrays],
        compiler_params=pltpu.CompilerParams(vmem_limit_bytes=20 * MIB),
        cost_estimate=pl.CostEstimate(flops=1000, bytes_accessed=1000, transcendentals=0),
    )(conv, gate, *arrays)


def block_of(shape, kind):
    if kind == "tile":
        return pl.BlockSpec(shape[:-1] + (LANES,), lambda i: (0,) * (len(shape) - 1) + (i,))
    if kind == "rows":
        return pl.BlockSpec((LANES,) + shape[1:], lambda i: (i,) + (0,) * (len(shape) - 1))
    if kind == "any":
        return pl.BlockSpec(memory_space=pl.ANY)
    return pl.BlockSpec(shape, lambda i: (0,) * len(shape))


def share_scratch(x, axis, size):
    groups = lax.axis_size(axis) // size
    part = x.shape[1:]
    return [
        pltpu.VMEM((groups, size - 1) + part, x.dtype),
        pltpu.VMEM((groups - 1,) + part, x.dtype),
        pltpu.VMEM((groups - 1,) + part, x.dtype),
        pltpu.SemaphoreType.DMA((groups, size - 1)),
        pltpu.SemaphoreType.DMA((groups, size - 1)),
        pltpu.SemaphoreType.DMA((groups - 1,)),
        pltpu.SemaphoreType.DMA((groups - 1,)),
    ]


def by_tiles(kernel, room, full, ins, outs, scratch, more=(), params=None):
    return pl.pallas_call(
        kernel,
        grid=(full // LANES,),
        in_specs=[block_of(a.shape, kind) for a, kind in ins],
        out_specs=[block_of(shape, kind) for shape, _, kind in outs],
        out_shape=[jax.ShapeDtypeStruct(shape, dtype) for shape, dtype, _ in outs],
        scratch_shapes=[pltpu.VMEM(shape, dtype) for shape, dtype in scratch] + list(more),
        compiler_params=pltpu.CompilerParams(vmem_limit_bytes=room * MIB, **(params or {})),
        cost_estimate=pl.CostEstimate(flops=1000, bytes_accessed=1000, transcendentals=0),
    )(*[a for a, _ in ins])


def norm_back(grad_normed, unit_rows, inverse, weight_gain):
    scaled = grad_normed * weight_gain
    return inverse * (scaled - unit_rows * jnp.mean(scaled * unit_rows, axis=-1, keepdims=True))


def local(
    tokens,
    teacher,
    true_lengths,
    doc_lengths,
    routes,
    norm1_gain,
    in_weight,
    conv_weight,
    conv_bias,
    xproj_weight,
    dt_weight,
    dt_bias,
    a_log,
    skip_weight,
    out_weight,
    norm2_gain,
    router_weight,
    expert_in,
    expert_out,
):
    seqs, group, width = tokens.shape
    inner = in_weight.shape[2]
    rank = dt_weight.shape[0]
    states = a_log.shape[1]
    experts = router_weight.shape[1]
    n_seq = lax.axis_size("seq")
    n_chan = lax.axis_size("chan")
    shards = n_seq // experts
    most = group // 4
    taps = conv_weight.shape[0]
    rim = taps - 1
    lines = 8
    chunks = lines // seqs
    steps = group // chunks
    owned = seqs * group // n_chan
    part = min(group, owned)
    most = min(most, part)
    parts = owned // part
    place = lax.axis_index("chan")
    first_pos = lax.axis_index("seq") * group

    full = -(-inner // LANES) * LANES
    rows = steps * lines
    maps = rank + 2 * states

    def padded(x):
        return jnp.pad(x, ((0, 0),) * (x.ndim - 1) + ((0, full - inner),))

    at = (
        first_pos
        + jnp.arange(steps, dtype=jnp.int32)[:, None]
        + (jnp.arange(lines, dtype=jnp.int32) // seqs * steps)[None, :]
    )
    stops = []
    for k in range(doc_lengths.shape[1] - 1):
        stops.append(doc_lengths[:, k] + (stops[-1] if stops else 0))
    stops = [jnp.tile(stop, chunks)[None, :] for stop in stops]

    def doc_at(pos):
        return sum((pos >= stop).astype(jnp.int32) for stop in stops)

    doc_ids = doc_at(at)
    keep = (doc_ids == doc_at(at - 1)) & (at > 0)
    valid = [doc_at(at - rim + k) == doc_ids for k in range(taps)] + [keep]
    valid = jnp.stack(valid + [keep] * (lines - taps - 1), axis=-1).astype(f32)

    w_in = in_weight.transpose(1, 2, 0)
    router_rows = router_weight.T
    gain_one = norm1_gain.astype(f32)
    xproj_rows = padded(xproj_weight.T)
    dt_rows = jnp.pad(padded(dt_weight), ((0, maps - rank), (0, 0)))
    rate = -jnp.exp(a_log.T)
    params = [rate * log2e, conv_weight, conv_bias[None], dt_bias[None], skip_weight[None]]
    params = jnp.concatenate([x.astype(f32) for x in params], axis=0)
    params = jnp.pad(params, ((0, -params.shape[0] % 8), (0, full - inner)))
    normed_one, extended, pre_act, gate_z, mapped = front(
        tokens,
        gain_one[None],
        w_in,
        params,
        states,
        taps,
        xproj_rows,
        valid,
        full,
        1,
    )
    act_shape, state_shape, wide_shape = (steps, lines, full), (states, lines, full), (states, steps, lines, LANES)
    dt_pre, step_size, drive, own_states, sums = by_tiles(
        functools.partial(totals_kernel, rank, taps),
        16,
        full,
        [
            (pre_act, "tile"),
            (mapped, "whole"),
            (dt_rows, "tile"),
            (valid, "whole"),
            (params, "tile"),
        ],
        [
            (act_shape, f32, "tile"),
            (act_shape, f32, "tile"),
            (act_shape, f32, "tile"),
            (state_shape, f32, "tile"),
            ((lines, full), f32, "tile"),
        ],
        [(wide_shape, f32)],
    )
    (enter,) = carried(own_states, sums, params, "seq", False, 2)
    y_full, gated, state, out_part = by_tiles(
        functools.partial(states_kernel, rank, seqs, taps, inner),
        30,
        full,
        [
            (step_size, "tile"),
            (drive, "tile"),
            (mapped, "whole"),
            (params, "tile"),
            (enter, "tile"),
            (pre_act, "tile"),
            (gate_z, "tile"),
            (out_weight, "rows"),
        ],
        [
            (act_shape, f32, "tile"),
            ((rows, full), bf16, "tile"),
            ((steps, states, lines, full), f32, "tile"),
            ((rows, width), bf16, "whole"),
        ],
        [(wide_shape, f32)] * 2 + [((rows, width), f32)],
    )
    (mixed,) = share_of(3, [(out_part.reshape(n_chan, owned, width), "chan", 2, f32)])

    def own(x):
        return lax.dynamic_slice_in_dim(x.reshape((rows,) + x.shape[2:]), place * owned, owned, 0)

    slots = parts * most
    tokens_own, gain_two = own(tokens), norm2_gain.astype(f32)[None]
    line, low = (owned, width), ((owned, width), bf16)
    hidden_one, normed_two, probs, chosen, hit, packed = at_once(
        functools.partial(route_kernel, part, most, slots),
        [tokens_own, mixed, gain_two, own(routes)[:, None], router_rows],
        [
            (line, f32),
            low,
            ((owned, experts), f32),
            ((owned, experts), f32),
            ((owned, experts * slots), bf16),
            ((experts * slots, width), bf16),
        ],
    )
    hit_back = hit
    if shards > 1:
        hit_back = hit.reshape(owned, experts, slots)
        hit_back = jnp.repeat(hit_back, shards, axis=1).reshape(owned, n_seq * slots)

    def to_slabs(x):
        x = x.reshape(experts, slots, width)
        return x if shards == 1 else jnp.repeat(x, shards, axis=0), "scatter", "seq"

    def to_rows(x):
        return x.reshape(n_seq, slots, width), "scatter", "seq"

    def flat(x):
        return x.reshape(-1, x.shape[-1])

    first_slab, second_slab = expert_in[0], expert_out[0]
    arrived = flat(exchange(4, to_slabs(packed))[0])
    hidden, slope, result = expert(arrived, first_slab, second_slab, n_chan)
    (result_rows,) = exchange(5, to_rows(result))
    layer_low, grad_layer, grad_logit, loss_row, packed = at_once(
        functools.partial(loss_kernel, group),
        [
            true_lengths,
            flat(result_rows),
            hit_back,
            hit,
            hidden_one,
            probs,
            chosen,
            own(teacher),
        ],
        [
            low,
            (line, f32),
            ((owned, experts), f32),
            ((1, width), f32),
            ((experts * slots, width), bf16),
        ],
        scalars=1,
    )
    grad_rows = flat(exchange(6, to_slabs(packed))[0])
    grad_pre, grad_slab_rows = expert(grad_rows, first_slab, second_slab, n_chan, slope)
    (grad_expert,) = exchange(7, to_rows(grad_slab_rows))
    shared_rows = -(-(experts + 2) // 8) * 8
    grad_hidden_one, grad_low, shared = at_once(
        norm_back_kernel,
        [
            flat(grad_expert),
            hit_back,
            grad_logit,
            router_rows,
            normed_two,
            hidden_one,
            grad_layer,
            gain_two,
            loss_row,
        ],
        [(line, f32), low, ((shared_rows, width), f32)],
    )

    (grad_mixed,) = exchange(8, (grad_low, 2, "chan"))
    grad_y, grad_z, grad_out_w, grad_in_gate, skip_sums, back_last = by_tiles(
        functools.partial(back_totals_kernel, rank, seqs, inner),
        22,
        full,
        [
            (step_size, "tile"),
            (mapped, "whole"),
            (params, "tile"),
            (grad_mixed.reshape(rows, width), "whole"),
            (normed_one, "whole"),
            (out_weight, "rows"),
            (gate_z, "tile"),
            (y_full, "tile"),
            (gated, "tile"),
            (pre_act, "tile"),
        ],
        [
            (act_shape, f32, "tile"),
            ((rows, full), bf16, "tile"),
            ((inner, width), bf16, "rows"),
            ((inner, width), bf16, "rows"),
            ((lines, full), f32, "tile"),
            (state_shape, f32, "tile"),
        ],
        [(wide_shape, f32), ((rows, width), bf16)],
    )
    back_enter, shared = carried(
        back_last, sums, params, "seq", True, 9, (shared, "gather", "chan")
    )
    shared = jnp.sum(shared, axis=0).reshape(-1, LANES)
    def cut_rows(x, unit):
        each = -(-x.shape[0] // (unit * n_seq)) * unit
        return jnp.pad(x, ((0, each * n_seq - x.shape[0]), (0, 0))).reshape(n_seq, each, -1)

    across = n_chan // 2
    by_out, by_gate = cut_rows(grad_out_w, 8), cut_rows(grad_in_gate, 8)
    riders = [(hidden, "scatter", "chan"), (grad_pre, "scatter", "chan")]
    items = items_of(riders)
    side, log_sums, bias_sums, grad_dt_w, low_part, by_out, by_gate, hidden_all, grad_pre_all = by_tiles(
        functools.partial(back_kernel, rank, full // LANES, [("seq", n_seq, across)] * 2, items),
        38,
        full,
        [
            (step_size, "tile"),
            (drive, "tile"),
            (grad_y, "tile"),
            (mapped, "whole"),
            (params, "tile"),
            (enter, "tile"),
            (state, "tile"),
            (back_enter, "tile"),
            (dt_pre, "tile"),
            (pre_act, "tile"),
            (dt_rows, "tile"),
            (by_out, "any"),
            (by_gate, "any"),
            (hidden, "any"),
            (grad_pre, "any"),
        ],
        [
            (act_shape, f32, "tile"),
            (state_shape, f32, "tile"),
            ((lines, full), f32, "tile"),
            ((maps, full), f32, "tile"),
            ((rows, maps), bf16, "whole"),
            (by_out.shape[1:], bf16, "whole"),
            (by_gate.shape[1:], bf16, "whole"),
            (hidden.shape, bf16, "any"),
            (grad_pre.shape, bf16, "any"),
        ],
        [(wide_shape, f32)] * 2
        + [((steps, lines, states * lines), f32)] * 2
        + [((steps, lines, LANES), f32)] * 2
        + [((rows, maps), f32)]
        + [(by_out.shape, bf16)] * 2,
        [pltpu.SemaphoreType.DMA((2,))]
        + share_scratch(by_out, "seq", across)
        + share_scratch(by_gate, "seq", across)
        + [sem for item in items for sem in sems_of(item)],
        {"collective_id": 15, "has_side_effects": True},
    )
    grad_mapped = summed_over(low_part, "chan", 10).astype(bf16)
    grad_conv_in, rims, grad_xproj, conv_sums = by_tiles(
        functools.partial(conv_back_kernel, states, taps),
        14,
        full,
        [
            (grad_mapped, "whole"),
            (grad_y, "tile"),
            (side, "tile"),
            (pre_act, "tile"),
            (extended, "tile"),
            (params, "tile"),
            (xproj_rows, "tile"),
            (valid, "whole"),
        ],
        [
            (act_shape, f32, "tile"),
            ((rim, lines, full), f32, "tile"),
            ((maps, full), f32, "tile"),
            ((taps + 1, lines, full), f32, "tile"),
        ],
        [((steps + rim, lines, LANES), f32)],
    )
    grad_in_conv, normed_part, grad_gain_one, by_gate, rows_all = ends(
        tokens,
        grad_conv_in,
        rims,
        grad_z,
        normed_one,
        w_in,
        14,
        (by_gate, across, "seq"),
        (arrived, 2, "chan"),
    )
    normed_part = normed_part.reshape(n_chan, owned, width)
    sums_all = jnp.concatenate([conv_sums, bias_sums[None], skip_sums[None], log_sums], axis=0)
    sums_all = jnp.sum(sums_all, axis=1)
    small_rows = sums_all.shape[0] * full // LANES
    small = jnp.concatenate([sums_all.reshape(small_rows, LANES), shared], axis=0)

    by_conv = cut_rows(grad_in_conv, 8)
    middle = cut_rows(jnp.concatenate([grad_xproj, grad_dt_w[:rank]], axis=0).astype(bf16), 16)
    grad_normed_one, small, middle, by_conv, grad_gain_one, by_out, grad_rows_all = share_of(
        11,
        [
            (normed_part, "chan", 2, f32),
            (cut_rows(small, 8), "seq", across, f32),
            (middle, "seq", across, bf16),
            (by_conv, "seq", across, bf16),
        ],
        (grad_gain_one, "gather", "chan"),
        (by_out, across, "seq"),
        (grad_rows, 2, "chan"),
    )
    grad_first = dot_tn(flat(rows_all), flat(grad_pre_all))
    grad_second = dot_tn(flat(hidden_all), flat(grad_rows_all))
    grad_gain_one = jnp.sum(grad_gain_one, axis=0)
    tokens_full = tokens_own.astype(f32)
    inverse_one = lax.rsqrt(jnp.mean(tokens_full * tokens_full, axis=-1, keepdims=True) + epsilon)
    grad_own = grad_hidden_one + norm_back(
        grad_normed_one, tokens_full * inverse_one, inverse_one, gain_one
    )
    moved = [
        (grad_own.astype(bf16), 2, "chan"),
        (layer_low, 2, "chan"),
        (small, across, "seq"),
        (middle, across, "seq"),
        (by_conv, across, "seq"),
        (grad_gain_one, "gather", "seq"),
    ]
    grad_first, grad_second, grad_low = lax.optimization_barrier((grad_first, grad_second, moved[0][0]))
    moved[0] = (grad_low,) + moved[0][1:]
    moved = exchange(12, *moved)
    grad_tokens, layer_out, small, middle, by_conv, grad_gain_one = moved
    grad_gain_one = jnp.sum(grad_gain_one, axis=(0, 1))
    summed_in, summed_out, grad_tokens = widened(
        flat(by_conv)[:inner], flat(by_gate)[:inner], flat(by_out)[:inner], flat(grad_tokens)
    )
    middle = flat(middle)[:, :inner].astype(f32)
    small = flat(small)
    shared = small[small_rows : small_rows + shared_rows * width // LANES].reshape(shared_rows, width)
    small = small[:small_rows].reshape(-1, full)[:, :inner]
    return (
        layer_out.reshape(seqs, group, width),
        shared[experts + 1, 0],
        grad_tokens.reshape(seqs, group, width),
        grad_gain_one,
        summed_in.transpose(2, 0, 1),
        small[:taps],
        small[taps],
        middle[:maps].T,
        middle[maps : maps + rank],
        small[taps + 1],
        (small[taps + 3 : taps + 3 + states] * rate).T,
        small[taps + 2],
        summed_out,
        shared[experts],
        shared[:experts].T,
        grad_first[None],
        grad_second[None],
    )


def solution(mesh):
    placed = (
        P(None, "seq", None),
        P(None, "seq", None),
        P(),
        P(),
        P(None, "seq"),
        P(),
        P(None, None, "chan"),
        P(None, "chan"),
        P("chan"),
        P("chan", None),
        P(None, "chan"),
        P("chan"),
        P("chan", None),
        P("chan"),
        P("chan", None),
        P(),
        P(),
        P("seq", None, None),
        P("seq", None, None),
    )
    return jax.shard_map(
        local,
        mesh=mesh,
        in_specs=placed,
        out_specs=(
            P(None, "seq", None),
            P(),
            P(None, "seq", None),
            P(),
            P(None, None, "chan"),
            P(None, "chan"),
            P("chan"),
            P("chan", None),
            P(None, "chan"),
            P("chan"),
            P("chan", None),
            P("chan"),
            P("chan", None),
            P(),
            P(),
            P("seq", None, "chan"),
            P("seq", "chan", None),
        ),
        check_vma=False,
    )
```
